32 devices in a mesh: dp: 8 (over z, x), seq: 4 (over y, core).
Axes of the slice: x: 2, y: 2, z: 4, core: 2. Of those that a mesh axis runs over, the one named last changes fastest.
Arguments:
- tokens: bfloat16 [64, 512, 768], P('dp', 'seq'), may hold values from -6 to 6
- lengths: int32 [64], P('dp'), may hold values from 1 to 512, as said below
- w_query: bfloat16 [768, 768], replicated, may hold values from -0.21875 to 0.21875
- b_query: bfloat16 [768], replicated, may hold values from -3 to 3
- w_key: bfloat16 [768, 768], replicated, may hold values from -0.21875 to 0.21875
- w_value: bfloat16 [768, 768], replicated, may hold values from -0.21875 to 0.21875
- b_value: bfloat16 [768], replicated, may hold values from -3 to 3
- w_out: bfloat16 [768, 768], replicated, may hold values from -0.875 to 0.875
- b_out: bfloat16 [768], replicated, may hold values from -2 to 2
- gain_one: bfloat16 [768], replicated, may hold values from 0.5 to 1.5
- shift_one: bfloat16 [768], replicated, may hold values from -2 to 2
- w_up: bfloat16 [768, 3072], replicated, may hold values from -0.21875 to 0.21875
- b_up: bfloat16 [3072], replicated, may hold values from -3 to 3
- w_down: bfloat16 [3072, 768], replicated, may hold values from -0.109375 to 0.109375
- b_down: bfloat16 [768], replicated, may hold values from -2 to 2
- gain_two: bfloat16 [768], replicated, may hold values from 0.5 to 1.5
- shift_two: bfloat16 [768], replicated, may hold values from -2 to 2
- out_grad: bfloat16 [64, 512, 768], P('dp', 'seq'), may hold values from -6 to 6
- pooled_grad: float32 [64, 768], P('dp'), may hold values from -6 to 6
Outputs:
- block_out: bfloat16 [64, 512, 768], P('dp', 'seq')
- pooled: float32 [64, 768], P('dp')
- tokens_grad: bfloat16 [64, 512, 768], P('dp', 'seq')
- w_query_grad: float32 [768, 768], replicated
- b_query_grad: float32 [768], replicated
- w_key_grad: float32 [768, 768], replicated
- w_value_grad: float32 [768, 768], replicated
- b_value_grad: float32 [768], replicated
- w_out_grad: float32 [768, 768], replicated
- b_out_grad: float32 [768], replicated
- gain_one_grad: float32 [768], replicated
- shift_one_grad: float32 [768], replicated
- w_up_grad: float32 [768, 3072], replicated
- b_up_grad: float32 [3072], replicated
- w_down_grad: float32 [3072, 768], replicated
- b_down_grad: float32 [768], replicated
- gain_two_grad: float32 [768], replicated
- shift_two_grad: float32 [768], replicated
The draws below stay inside these ranges and needn't reach their ends.
Inputs may be any that keep to these rules, and one draw needn't show every extreme that they name: `lengths`: in every aligned block of 8 consecutive passages at least one passage has length 512; the others are heavy-tailed, mostly short.
All inputs are finite; a program needn't handle non-finite values.
Results may differ from the reference program's by a relative error of at most 0.015.
Values may be sent and summed in bfloat16 or wider, within the bound.
No kernel may reach another device: no remote copies, remote signals or barrier semaphores. Data moves between devices by JAX's collectives and lax.ppermute only.
A program may use at most 256 MiB of HBM per device.

```python
import jax
import jax.numpy as jnp
from jax import lax

D = 768
HEADS = 12
HEAD_DIM = 64
FF = 3072
SEQ_DEV = 8
LENGTH = 512
PASSAGES = 64


def draw_lengths(key, part):
    key = jax.random.fold_in(key, 11)
    key_scale, key_raw, key_pick = jax.random.split(key, 3)
    exponent = jax.random.randint(key_scale, (PASSAGES,), 2, 10)
    spread = jnp.left_shift(jnp.ones((PASSAGES,), jnp.int32), exponent)
    raw_draw = jax.random.randint(key_raw, (PASSAGES,), 0, 1048576)
    drawn = jnp.minimum(1 + raw_draw % spread, LENGTH)
    chosen = jax.random.randint(key_pick, (PASSAGES // SEQ_DEV,), 0, SEQ_DEV)
    slot_index = jnp.arange(PASSAGES) % SEQ_DEV
    longest = slot_index == jnp.repeat(chosen, SEQ_DEV)
    return jnp.where(longest, LENGTH, drawn).astype(jnp.int32)


def block_scale(rng, extent, shards, smallest, top_value):
    def one(axis_at, shards_of):
        steps = jax.random.uniform(jax.random.fold_in(jax.random.fold_in(rng, 6), axis_at), (shards_of,), jnp.float32, smallest / len(shards), top_value / len(shards))
        return jnp.repeat(jnp.exp(steps), extent[axis_at] // shards_of).reshape((-1,) + (1,) * (len(extent) - axis_at - 1))

    gain = one(*shards[0])
    for cut in shards[1:]:
        gain = gain * one(*cut)
    return gain


def noise(rng, dims, deviation, most, shards=(), held_as=jnp.bfloat16):
    values = jax.random.normal(rng, dims, jnp.float32) * deviation
    if len(shards) > 0:
        values = block_scale(rng, dims, shards, -0.22, 0.18) * values
    return jnp.clip(values, min=-most, max=most).astype(held_as)


def setup_inputs(seed: int = 0) -> dict:
    streams_of = jax.random.split(jax.random.key(seed), 20)
    tokens = noise(streams_of[0], (PASSAGES, LENGTH, D), 1.0, 6.0, ((0, 8), (1, 4)))
    lengths = draw_lengths(jax.random.fold_in(streams_of[19], 71), 0)
    w_query = noise(streams_of[2], (D, D), D ** -0.5, 0.21875)
    b_query = noise(streams_of[3], (D,), 0.5, 3.0)
    w_key = noise(streams_of[4], (D, D), D ** -0.5, 0.21875)
    w_value = noise(streams_of[5], (D, D), D ** -0.5, 0.21875)
    b_value = noise(streams_of[6], (D,), 0.5, 3.0)
    w_out = noise(streams_of[7], (D, D), (D // 16) ** -0.5, 0.875)
    b_out = noise(streams_of[8], (D,), 0.3, 2.0)
    gain_one = jnp.clip(1.0 + 0.1 * jax.random.normal(streams_of[9], (D,), jnp.float32), 0.5, 1.5).astype(jnp.bfloat16)
    shift_one = noise(streams_of[10], (D,), 0.3, 2.0)
    w_up = noise(streams_of[11], (D, FF), D ** -0.5, 0.21875)
    b_up = noise(streams_of[12], (FF,), 0.5, 3.0)
    w_down = noise(streams_of[13], (FF, D), FF ** -0.5, 0.109375)
    b_down = noise(streams_of[14], (D,), 0.3, 2.0)
    gain_two = jnp.clip(1.0 + 0.1 * jax.random.normal(streams_of[15], (D,), jnp.float32), 0.5, 1.5).astype(jnp.bfloat16)
    shift_two = noise(streams_of[16], (D,), 0.3, 2.0)
    out_grad = noise(streams_of[17], (PASSAGES, LENGTH, D), 1.0, 6.0, ((0, 8), (1, 4)))
    pooled_grad = noise(streams_of[18], (PASSAGES, D), 1.0, 6.0, ((0, 8),), jnp.float32)
    return {"tokens": tokens, "lengths": lengths, "w_query": w_query, "b_query": b_query, "w_key": w_key, "w_value": w_value, "b_value": b_value, "w_out": w_out, "b_out": b_out, "gain_one": gain_one, "shift_one": shift_one, "w_up": w_up, "b_up": b_up, "w_down": w_down, "b_down": b_down, "gain_two": gain_two, "shift_two": shift_two, "out_grad": out_grad, "pooled_grad": pooled_grad}


@jax.custom_vjp
def low(v):
    return lax.optimization_barrier(v.astype(jnp.bfloat16)).astype(jnp.float32)

@jax.custom_vjp
def low_back(v):
    return v

def low_keep(v):
    return (low(v), None)

def low_pass(kept, grad):
    return (grad,)

def back_keep(v):
    return (v, None)

def back_low(kept, grad):
    return (low(grad),)
low.defvjp(low_keep, low_pass)
low_back.defvjp(back_keep, back_low)
eps = 1e-06

def matmul_high(left, right):
    return jnp.dot(left, right, precision=lax.Precision.HIGHEST)

def layer_norm(hidden, gain_vec, shift_vec):
    row_mean = lax.optimization_barrier(jnp.mean(hidden, axis=-1, keepdims=True))
    centred = hidden - row_mean
    variance = lax.optimization_barrier(jnp.mean(centred * centred, axis=-1, keepdims=True))
    return centred * lax.rsqrt(variance + eps) * gain_vec + shift_vec

def forward(inputs, params, passage_len):
    w_query, b_query, w_key, w_value, b_value, w_out, b_out, gain_one, shift_one, w_up, b_up, w_down, b_down, gain_two, shift_two = params
    passages = inputs.shape[0]
    token_rows = inputs.reshape(passages * LENGTH, D)

    def split_heads(matrix):
        return matrix.reshape(passages, LENGTH, HEADS, HEAD_DIM)
    queries = split_heads(low_back(low(matmul_high(token_rows, w_query) + b_query)))
    key_heads = split_heads(low_back(low(matmul_high(token_rows, w_key))))
    value_heads = split_heads(low_back(low(matmul_high(token_rows, w_value) + b_value)))
    raw_scores = jnp.einsum('bqhe,bkhe->bhqk', queries, key_heads, precision=lax.Precision.HIGHEST) * HEAD_DIM ** (-0.5)
    positions = jnp.arange(LENGTH)
    key_live = positions[None, :] < passage_len[:, None]
    scores = jnp.where(key_live[:, None, None, :], low_back(raw_scores), -1e+30)
    attn_probs = jax.nn.softmax(scores, axis=-1)
    mixed_heads = jnp.einsum('bhqk,bkhe->bqhe', low(attn_probs), value_heads, precision=lax.Precision.HIGHEST)
    mixed_rows = low_back(low(mixed_heads)).reshape(passages * LENGTH, D)
    branch = low_back(matmul_high(mixed_rows, w_out) + b_out)
    normed_one = layer_norm(token_rows + branch, gain_one, shift_one)
    inner_pre = low_back(matmul_high(low(normed_one), w_up) + b_up)
    second = low_back(matmul_high(low(jax.nn.gelu(inner_pre, approximate=False)), w_down) + b_down)
    result = layer_norm(normed_one + second, gain_two, shift_two).reshape(passages, LENGTH, D)
    live_mask = key_live.astype(jnp.float32)
    pooled = lax.optimization_barrier(jnp.sum(result * live_mask[:, :, None], axis=1)) / passage_len[:, None].astype(jnp.float32)
    return (result, pooled)

def reference(tokens, lengths, w_query, b_query, w_key, w_value, b_value, w_out, b_out, gain_one, shift_one, w_up, b_up, w_down, b_down, gain_two, shift_two, out_grad, pooled_grad):
    params = tuple((weight.astype(jnp.float32) for weight in (w_query, b_query, w_key, w_value, b_value, w_out, b_out, gain_one, shift_one, w_up, b_up, w_down, b_down, gain_two, shift_two)))
    blocks = PASSAGES // SEQ_DEV
    inputs = tokens.astype(jnp.float32).reshape(blocks, SEQ_DEV, LENGTH, D)
    block_len = lengths.reshape(blocks, SEQ_DEV)
    token_cot = out_grad.astype(jnp.float32).reshape(blocks, SEQ_DEV, LENGTH, D)
    pool_cot = pooled_grad.astype(jnp.float32).reshape(blocks, SEQ_DEV, D)

    def one_block(summed, block_item):
        block_in, block_lens, block_cot, block_pool = block_item

        def local_layer(values, weights):
            return forward(values, weights, block_lens)
        (result, pooled), pullback = jax.vjp(local_layer, block_in, params)
        input_grad, weight_grads = pullback((block_cot, block_pool))
        summed = tuple((running + extra for running, extra in zip(summed, weight_grads)))
        return (summed, (result.astype(jnp.bfloat16), pooled, input_grad.astype(jnp.bfloat16)))
    zero_grads = tuple((jnp.zeros_like(weight) for weight in params))
    summed, (results, pooled, input_grad) = lax.scan(one_block, zero_grads, (inputs, block_len, token_cot, pool_cot))
    return (results.reshape(PASSAGES, LENGTH, D), pooled.reshape(PASSAGES, D), input_grad.reshape(PASSAGES, LENGTH, D), summed[0], summed[1], summed[2], summed[3], summed[4], summed[5], summed[6], summed[7], summed[8], summed[9], summed[10], summed[11], summed[12], summed[13], summed[14])
```

```python
import jax
import jax.numpy as jnp
from jax import lax
from jax.sharding import PartitionSpec as P

HEADS = 12
HEAD_DIM = 64


eps = 1e-06
root_half = 0.7071067811865476
inv_root_two_pi = 0.3989422804014327


def norm_forward(hidden, gain_vec, shift_vec):
    row_mean = jnp.mean(hidden, axis=-1, keepdims=True)
    centred = hidden - row_mean
    variance = jnp.mean(centred * centred, axis=-1, keepdims=True)
    inv_scale = lax.rsqrt(variance + eps)
    normed = centred * inv_scale
    return (normed * gain_vec + shift_vec, normed, inv_scale)


def norm_backward(upstream, normed, inv_scale, gain_vec):
    scaled = upstream * gain_vec
    centred = scaled - jnp.mean(scaled, axis=-1, keepdims=True)
    centred = centred - normed * jnp.mean(scaled * normed, axis=-1, keepdims=True)
    return (centred * inv_scale, jnp.sum(upstream * normed, axis=0), jnp.sum(upstream, axis=0))


def score_block(queries, key_heads, key_live):
    scores = jnp.einsum(
        "bqhe,bkhe->bhqk", queries, key_heads, preferred_element_type=jnp.float32
    ) * HEAD_DIM ** (-0.5)
    return jnp.where(key_live[:, None, None, :], scores, -1e30)


def attend(queries, key_heads, value_heads, key_live):
    scores = score_block(queries, key_heads, key_live)
    highest = jnp.max(scores, axis=-1, keepdims=True)
    expo_terms = jnp.exp(scores - highest)
    totals = jnp.sum(expo_terms, axis=-1, keepdims=True)
    attn_probs = (expo_terms / totals).astype(jnp.bfloat16)
    mixed_heads = jnp.einsum(
        "bhqk,bkhe->bqhe", attn_probs, value_heads, preferred_element_type=jnp.float32
    )
    return (mixed_heads, highest + jnp.log(totals))


def attend_back(queries, key_heads, value_heads, key_live, log_total, mixed_grad):
    attn_probs = jnp.exp(score_block(queries, key_heads, key_live) - log_total)
    prob_grad = jnp.einsum(
        "bqhe,bkhe->bhqk", mixed_grad, value_heads, preferred_element_type=jnp.float32
    )
    row_along = jnp.sum(attn_probs * prob_grad, axis=-1, keepdims=True)
    score_grad = (attn_probs * (prob_grad - row_along)).astype(jnp.bfloat16)
    score_scale = HEAD_DIM ** (-0.5)
    query_grad = (
        jnp.einsum("bhqk,bkhe->bqhe", score_grad, key_heads, preferred_element_type=jnp.float32)
        * score_scale
    )
    key_grad = (
        jnp.einsum("bhqk,bqhe->bkhe", score_grad, queries, preferred_element_type=jnp.float32)
        * score_scale
    )
    value_grad = jnp.einsum(
        "bhqk,bqhe->bkhe",
        attn_probs.astype(jnp.bfloat16),
        mixed_grad,
        preferred_element_type=jnp.float32,
    )
    return (query_grad, key_grad, value_grad)


def outer_sum(left, right):
    return jnp.einsum("ra,rb->ab", left, right, preferred_element_type=jnp.float32)


def back_project(grads, weight):
    return jnp.einsum("rb,ab->ra", grads, weight, preferred_element_type=jnp.float32)


def exchange(value, axis, mask):
    count = lax.axis_size(axis)
    return lax.ppermute(value, axis, [(i, i ^ mask) for i in range(count)])


def to_passages(value):
    count = lax.axis_size("seq")
    mine = lax.axis_index("seq")
    held, piece, width = value.shape
    own = held // count
    whole = jnp.zeros((own, piece * count, width), value.dtype)
    for mask in range(count):
        peer = mine ^ mask
        part = lax.dynamic_slice_in_dim(value, peer * own, own, 0)
        if mask:
            part = exchange(part, "seq", mask)
        whole = lax.dynamic_update_slice_in_dim(whole, part, peer * piece, 1)
    return whole


def to_positions(value):
    count = lax.axis_size("seq")
    mine = lax.axis_index("seq")
    own, full, width = value.shape
    piece = full // count
    result = jnp.zeros((own * count, piece, width), value.dtype)
    for mask in range(count):
        peer = mine ^ mask
        part = lax.dynamic_slice_in_dim(value, peer * piece, piece, 1)
        if mask:
            part = exchange(part, "seq", mask)
        result = lax.dynamic_update_slice_in_dim(result, part, peer * own, 0)
    return result


def axis_bits(axis):
    return [(axis, 1 << i) for i in range(lax.axis_size(axis).bit_length() - 1)]


def orders():
    seq_bits = axis_bits("seq")
    dp_bits = axis_bits("dp")
    first = seq_bits[:1] + dp_bits[:1] + seq_bits[1:] + dp_bits[1:]
    second = seq_bits[:2] + dp_bits[:1] + seq_bits[2:] + dp_bits[1:]
    return first, second


def upper(axis, mask):
    return (lax.axis_index(axis) & mask) // mask


def halve(value, order):
    for axis, mask in order:
        half = value.shape[0] // 2
        bit = upper(axis, mask)
        send = lax.dynamic_slice_in_dim(value, (1 - bit) * half, half, 0)
        keep = lax.dynamic_slice_in_dim(value, bit * half, half, 0)
        got = exchange(send, axis, mask)
        value = (keep.astype(jnp.float32) + got.astype(jnp.float32)).astype(jnp.bfloat16)
    return value


def double(value, order):
    for axis, mask in reversed(order):
        got = exchange(value, axis, mask)
        bit = upper(axis, mask)
        value = jnp.where(
            bit == 1,
            jnp.concatenate([got, value], axis=0),
            jnp.concatenate([value, got], axis=0),
        )
    return value


def butterfly(value):
    for axis, mask in axis_bits("seq") + axis_bits("dp"):
        value = value + exchange(value, axis, mask)
    return value


def sum_blocks(blocks):
    stacked = jnp.concatenate([b.astype(jnp.bfloat16) for b in blocks], axis=0)
    first, second = orders()
    half = stacked.shape[0] // 2
    return jnp.concatenate(
        [double(halve(stacked[:half], first), first), double(halve(stacked[half:], second), second)],
        axis=0,
    ).astype(jnp.float32)


def shards(
    tokens,
    lengths,
    w_query,
    b_query,
    w_key,
    w_value,
    b_value,
    w_out,
    b_out,
    gain_one,
    shift_one,
    w_up,
    b_up,
    w_down,
    b_down,
    gain_two,
    shift_two,
    out_grad,
    pooled_grad,
):
    seq_count = lax.axis_size("seq")
    held, piece_len, model_width = tokens.shape
    full_len = piece_len * seq_count
    passages = held // seq_count
    mine = lax.axis_index("seq")
    local_in = to_passages(tokens)
    local_cot = to_passages(out_grad)
    local_len = lax.dynamic_slice_in_dim(lengths, mine * passages, passages, 0)
    local_pool = lax.dynamic_slice_in_dim(pooled_grad, mine * passages, passages, 0)
    span_len = full_len
    total_rows = passages * span_len
    token_rows = local_in.reshape(total_rows, model_width)
    key_live = jnp.arange(full_len)[None, :] < local_len[:, None]
    len_float = local_len.astype(jnp.float32)[:, None]
    heads_shape = (passages, -1, HEADS, HEAD_DIM)
    query_rows = (
        jnp.dot(token_rows, w_query, preferred_element_type=jnp.float32) + b_query
    ).astype(jnp.bfloat16)
    key_rows = jnp.dot(token_rows, w_key, preferred_element_type=jnp.float32).astype(jnp.bfloat16)
    value_rows = (
        jnp.dot(token_rows, w_value, preferred_element_type=jnp.float32) + b_value
    ).astype(jnp.bfloat16)
    queries = query_rows.reshape(heads_shape)
    key_heads = key_rows.reshape(heads_shape)
    value_heads = value_rows.reshape(heads_shape)
    mixed_heads, log_total = attend(queries, key_heads, value_heads, key_live)
    mixed_rows = mixed_heads.astype(jnp.bfloat16).reshape(total_rows, model_width)
    branch = jnp.dot(mixed_rows, w_out, preferred_element_type=jnp.float32) + b_out
    normed_out, normed_one, scale_one = norm_forward(
        token_rows.astype(jnp.float32) + branch, gain_one, shift_one
    )
    first_low = normed_out.astype(jnp.bfloat16)
    inner_pre = jnp.dot(first_low, w_up, preferred_element_type=jnp.float32) + b_up
    activated = jax.nn.gelu(inner_pre, approximate=False).astype(jnp.bfloat16)
    second = jnp.dot(activated, w_down, preferred_element_type=jnp.float32) + b_down
    result, normed_two, scale_two = norm_forward(normed_out + second, gain_two, shift_two)
    result_low = result.astype(jnp.bfloat16).reshape(passages, span_len, model_width)
    block_out = to_positions(result_low)
    live_float = key_live.astype(jnp.float32)
    pooled_mine = (
        jnp.sum(result.reshape(passages, span_len, model_width) * live_float[:, :, None], axis=1)
        / len_float
    )
    pooled = jnp.zeros((held, model_width), jnp.float32)
    for mask in range(seq_count):
        part = exchange(pooled_mine, "seq", mask) if mask else pooled_mine
        pooled = lax.dynamic_update_slice_in_dim(pooled, part, (mine ^ mask) * passages, 0)
    upstream = (
        local_cot.astype(jnp.float32)
        + live_float[:, :, None] * (local_pool / len_float)[:, None, :]
    )
    upstream = upstream.reshape(total_rows, model_width)
    second_in, gain_two_grad, shift_two_grad = norm_backward(
        upstream, normed_two, scale_two, gain_two
    )
    second_grad = second_in.astype(jnp.bfloat16)
    down_grad = outer_sum(activated, second_grad)
    down_bias_grad = jnp.sum(second_grad.astype(jnp.float32), axis=0)
    act_grad = back_project(second_grad, w_down)
    gelu_slope = 0.5 * (
        1.0 + lax.erf(inner_pre * root_half)
    ) + inner_pre * inv_root_two_pi * jnp.exp(-0.5 * inner_pre * inner_pre)
    inner_grad = (act_grad * gelu_slope).astype(jnp.bfloat16)
    up_bias_grad = jnp.sum(inner_grad.astype(jnp.float32), axis=0)
    wide = w_up.shape[1] // model_width
    up_blocks = [
        outer_sum(first_low, inner_grad[:, i * model_width : (i + 1) * model_width])
        for i in range(wide)
    ]
    down_sum = sum_blocks([down_grad])
    up_sum = sum_blocks(up_blocks)
    first_up = second_in + back_project(inner_grad, w_up)
    branch_in, gain_one_grad, shift_one_grad = norm_backward(
        first_up, normed_one, scale_one, gain_one
    )
    branch_grad = branch_in.astype(jnp.bfloat16)
    out_weight_grad = outer_sum(mixed_rows, branch_grad)
    out_bias_grad = jnp.sum(branch_grad.astype(jnp.float32), axis=0)
    mixed_grad = back_project(branch_grad, w_out).astype(jnp.bfloat16).reshape(heads_shape)
    query_grad, key_grad, value_grad = attend_back(
        queries, key_heads, value_heads, key_live, log_total, mixed_grad
    )
    query_low = query_grad.astype(jnp.bfloat16).reshape(total_rows, model_width)
    key_low = key_grad.astype(jnp.bfloat16).reshape(total_rows, model_width)
    value_low = value_grad.astype(jnp.bfloat16).reshape(total_rows, model_width)
    query_weight_grad = outer_sum(token_rows, query_low)
    query_bias_grad = jnp.sum(query_low.astype(jnp.float32), axis=0)
    key_weight_grad = outer_sum(token_rows, key_low)
    value_weight_grad = outer_sum(token_rows, value_low)
    value_bias_grad = jnp.sum(value_low.astype(jnp.float32), axis=0)
    input_grad = (
        branch_in
        + back_project(query_low, w_query)
        + back_project(key_low, w_key)
        + back_project(value_low, w_value)
    )
    input_low = input_grad.astype(jnp.bfloat16).reshape(passages, span_len, model_width)
    tokens_grad = to_positions(input_low)
    attn_sum = sum_blocks(
        [query_weight_grad, key_weight_grad, value_weight_grad, out_weight_grad]
    )
    vectors = jnp.concatenate(
        [
            query_bias_grad[None],
            value_bias_grad[None],
            out_bias_grad[None],
            gain_one_grad[None],
            shift_one_grad[None],
            down_bias_grad[None],
            gain_two_grad[None],
            shift_two_grad[None],
            up_bias_grad.reshape(wide, model_width),
        ],
        axis=0,
    )
    vectors = butterfly(vectors)
    attn_sum = attn_sum.reshape(4, model_width, model_width)
    up_sum = up_sum.reshape(wide, model_width, model_width)
    up_sum = jnp.concatenate([up_sum[i] for i in range(wide)], axis=1)
    return (
        block_out,
        pooled,
        tokens_grad,
        attn_sum[0],
        vectors[0],
        attn_sum[1],
        attn_sum[2],
        vectors[1],
        attn_sum[3],
        vectors[2],
        vectors[3],
        vectors[4],
        up_sum,
        vectors[8:].reshape(-1),
        down_sum,
        vectors[5],
        vectors[6],
        vectors[7],
    )


def solution(mesh):
    in_specs = (
        (P("dp", "seq", None), P("dp"))
        + (P(),) * 15
        + (P("dp", "seq", None), P("dp", None))
    )
    out_specs = (P("dp", "seq", None), P("dp", None), P("dp", "seq", None)) + (P(),) * 15
    return jax.shard_map(shards, mesh=mesh, in_specs=in_specs, out_specs=out_specs, check_vma=False)
```

```python
import jax
import jax.numpy as jnp
from jax import lax
from jax.sharding import PartitionSpec as P

HEADS = 12
HEAD_DIM = 64


eps = 1e-06
root_half = 0.7071067811865476
inv_root_two_pi = 0.3989422804014327


def norm_forward(hidden, gain_vec, shift_vec):
    row_mean = jnp.mean(hidden, axis=-1, keepdims=True)
    centred = hidden - row_mean
    variance = jnp.mean(centred * centred, axis=-1, keepdims=True)
    inv_scale = lax.rsqrt(variance + eps)
    normed = centred * inv_scale
    return (normed * gain_vec + shift_vec, normed, inv_scale)


def norm_backward(upstream, normed, inv_scale, gain_vec):
    scaled = upstream * gain_vec
    centred = scaled - jnp.mean(scaled, axis=-1, keepdims=True)
    centred = centred - normed * jnp.mean(scaled * normed, axis=-1, keepdims=True)
    return (centred * inv_scale, jnp.sum(upstream * normed, axis=0), jnp.sum(upstream, axis=0))


def score_block(queries, key_heads, key_live):
    scores = jnp.einsum(
        "bqhe,bkhe->bhqk", queries, key_heads, preferred_element_type=jnp.float32
    ) * HEAD_DIM ** (-0.5)
    return jnp.where(key_live[:, None, None, :], scores, -1e30)


def attend(queries, key_heads, value_heads, key_live):
    scores = score_block(queries, key_heads, key_live)
    highest = jnp.max(scores, axis=-1, keepdims=True)
    expo_terms = jnp.exp(scores - highest)
    totals = jnp.sum(expo_terms, axis=-1, keepdims=True)
    attn_probs = (expo_terms / totals).astype(jnp.bfloat16)
    mixed_heads = jnp.einsum(
        "bhqk,bkhe->bqhe", attn_probs, value_heads, preferred_element_type=jnp.float32
    )
    return (mixed_heads, highest + jnp.log(totals))


def attend_back(queries, key_heads, value_heads, key_live, log_total, mixed_grad):
    attn_probs = jnp.exp(score_block(queries, key_heads, key_live) - log_total)
    prob_grad = jnp.einsum(
        "bqhe,bkhe->bhqk", mixed_grad, value_heads, preferred_element_type=jnp.float32
    )
    row_along = jnp.sum(attn_probs * prob_grad, axis=-1, keepdims=True)
    score_grad = (attn_probs * (prob_grad - row_along)).astype(jnp.bfloat16)
    score_scale = HEAD_DIM ** (-0.5)
    query_grad = (
        jnp.einsum("bhqk,bkhe->bqhe", score_grad, key_heads, preferred_element_type=jnp.float32)
        * score_scale
    )
    key_grad = (
        jnp.einsum("bhqk,bqhe->bkhe", score_grad, queries, preferred_element_type=jnp.float32)
        * score_scale
    )
    value_grad = jnp.einsum(
        "bhqk,bqhe->bkhe",
        attn_probs.astype(jnp.bfloat16),
        mixed_grad,
        preferred_element_type=jnp.float32,
    )
    return (query_grad, key_grad, value_grad)


def outer_sum(left, right):
    return jnp.einsum("ra,rb->ab", left, right, preferred_element_type=jnp.float32)


def back_project(grads, weight):
    return jnp.einsum("rb,ab->ra", grads, weight, preferred_element_type=jnp.float32)


def exchange(value, axis, mask):
    count = lax.axis_size(axis)
    return lax.ppermute(value, axis, [(i, i ^ mask) for i in range(count)])


def to_passages(value):
    count = lax.axis_size("seq")
    mine = lax.axis_index("seq")
    held, piece, width = value.shape
    own = held // count
    whole = jnp.zeros((own, piece * count, width), value.dtype)
    for mask in range(count):
        peer = mine ^ mask
        part = lax.dynamic_slice_in_dim(value, peer * own, own, 0)
        if mask:
            part = exchange(part, "seq", mask)
        whole = lax.dynamic_update_slice_in_dim(whole, part, peer * piece, 1)
    return whole


def to_positions(value):
    count = lax.axis_size("seq")
    mine = lax.axis_index("seq")
    own, full, width = value.shape
    piece = full // count
    result = jnp.zeros((own * count, piece, width), value.dtype)
    for mask in range(count):
        peer = mine ^ mask
        part = lax.dynamic_slice_in_dim(value, peer * piece, piece, 1)
        if mask:
            part = exchange(part, "seq", mask)
        result = lax.dynamic_update_slice_in_dim(result, part, peer * own, 0)
    return result


def axis_bits(axis):
    return [(axis, 1 << i) for i in range(lax.axis_size(axis).bit_length() - 1)]


def orders():
    seq_bits = axis_bits("seq")
    dp_bits = axis_bits("dp")
    first = seq_bits[:1] + dp_bits[:1] + seq_bits[1:] + dp_bits[1:]
    second = seq_bits[:2] + dp_bits[:1] + seq_bits[2:] + dp_bits[1:]
    return first, second


def upper(axis, mask):
    return (lax.axis_index(axis) & mask) // mask


def halve(value, order):
    for axis, mask in order:
        half = value.shape[0] // 2
        bit = upper(axis, mask)
        send = lax.dynamic_slice_in_dim(value, (1 - bit) * half, half, 0)
        keep = lax.dynamic_slice_in_dim(value, bit * half, half, 0)
        got = exchange(send, axis, mask)
        value = (keep.astype(jnp.float32) + got.astype(jnp.float32)).astype(jnp.bfloat16)
    return value


def double(value, order):
    for axis, mask in reversed(order):
        got = exchange(value, axis, mask)
        bit = upper(axis, mask)
        value = jnp.where(
            bit == 1,
            jnp.concatenate([got, value], axis=0),
            jnp.concatenate([value, got], axis=0),
        )
    return value


def butterfly(value):
    for axis, mask in axis_bits("seq") + axis_bits("dp"):
        value = value + exchange(value, axis, mask)
    return value


def sum_blocks(blocks):
    stacked = jnp.concatenate([b.astype(jnp.bfloat16) for b in blocks], axis=0)
    return lax.psum(stacked, ("dp", "seq")).astype(jnp.float32)


def shards(
    tokens,
    lengths,
    w_query,
    b_query,
    w_key,
    w_value,
    b_value,
    w_out,
    b_out,
    gain_one,
    shift_one,
    w_up,
    b_up,
    w_down,
    b_down,
    gain_two,
    shift_two,
    out_grad,
    pooled_grad,
):
    seq_count = lax.axis_size("seq")
    held, piece_len, model_width = tokens.shape
    full_len = piece_len * seq_count
    passages = held // seq_count
    mine = lax.axis_index("seq")
    local_in = to_passages(tokens)
    local_cot = to_passages(out_grad)
    local_len = lax.dynamic_slice_in_dim(lengths, mine * passages, passages, 0)
    local_pool = lax.dynamic_slice_in_dim(pooled_grad, mine * passages, passages, 0)
    span_len = full_len
    total_rows = passages * span_len
    token_rows = local_in.reshape(total_rows, model_width)
    key_live = jnp.arange(full_len)[None, :] < local_len[:, None]
    len_float = local_len.astype(jnp.float32)[:, None]
    heads_shape = (passages, -1, HEADS, HEAD_DIM)
    query_rows = (
        jnp.dot(token_rows, w_query, preferred_element_type=jnp.float32) + b_query
    ).astype(jnp.bfloat16)
    key_rows = jnp.dot(token_rows, w_key, preferred_element_type=jnp.float32).astype(jnp.bfloat16)
    value_rows = (
        jnp.dot(token_rows, w_value, preferred_element_type=jnp.float32) + b_value
    ).astype(jnp.bfloat16)
    queries = query_rows.reshape(heads_shape)
    key_heads = key_rows.reshape(heads_shape)
    value_heads = value_rows.reshape(heads_shape)
    mixed_heads, log_total = attend(queries, key_heads, value_heads, key_live)
    mixed_rows = mixed_heads.astype(jnp.bfloat16).reshape(total_rows, model_width)
    branch = jnp.dot(mixed_rows, w_out, preferred_element_type=jnp.float32) + b_out
    normed_out, normed_one, scale_one = norm_forward(
        token_rows.astype(jnp.float32) + branch, gain_one, shift_one
    )
    first_low = normed_out.astype(jnp.bfloat16)
    inner_pre = jnp.dot(first_low, w_up, preferred_element_type=jnp.float32) + b_up
    activated = jax.nn.gelu(inner_pre, approximate=False).astype(jnp.bfloat16)
    second = jnp.dot(activated, w_down, preferred_element_type=jnp.float32) + b_down
    result, normed_two, scale_two = norm_forward(normed_out + second, gain_two, shift_two)
    result_low = result.astype(jnp.bfloat16).reshape(passages, span_len, model_width)
    block_out = to_positions(result_low)
    live_float = key_live.astype(jnp.float32)
    pooled_mine = (
        jnp.sum(result.reshape(passages, span_len, model_width) * live_float[:, :, None], axis=1)
        / len_float
    )
    pooled = jnp.zeros((held, model_width), jnp.float32)
    for mask in range(seq_count):
        part = exchange(pooled_mine, "seq", mask) if mask else pooled_mine
        pooled = lax.dynamic_update_slice_in_dim(pooled, part, (mine ^ mask) * passages, 0)
    upstream = (
        local_cot.astype(jnp.float32)
        + live_float[:, :, None] * (local_pool / len_float)[:, None, :]
    )
    upstream = upstream.reshape(total_rows, model_width)
    second_in, gain_two_grad, shift_two_grad = norm_backward(
        upstream, normed_two, scale_two, gain_two
    )
    second_grad = second_in.astype(jnp.bfloat16)
    down_grad = outer_sum(activated, second_grad)
    down_bias_grad = jnp.sum(second_grad.astype(jnp.float32), axis=0)
    act_grad = back_project(second_grad, w_down)
    gelu_slope = 0.5 * (
        1.0 + lax.erf(inner_pre * root_half)
    ) + inner_pre * inv_root_two_pi * jnp.exp(-0.5 * inner_pre * inner_pre)
    inner_grad = (act_grad * gelu_slope).astype(jnp.bfloat16)
    up_bias_grad = jnp.sum(inner_grad.astype(jnp.float32), axis=0)
    wide = w_up.shape[1] // model_width
    up_blocks = [
        outer_sum(first_low, inner_grad[:, i * model_width : (i + 1) * model_width])
        for i in range(wide)
    ]
    down_sum = sum_blocks([down_grad])
    up_sum = sum_blocks(up_blocks)
    first_up = second_in + back_project(inner_grad, w_up)
    branch_in, gain_one_grad, shift_one_grad = norm_backward(
        first_up, normed_one, scale_one, gain_one
    )
    branch_grad = branch_in.astype(jnp.bfloat16)
    out_weight_grad = outer_sum(mixed_rows, branch_grad)
    out_bias_grad = jnp.sum(branch_grad.astype(jnp.float32), axis=0)
    mixed_grad = back_project(branch_grad, w_out).astype(jnp.bfloat16).reshape(heads_shape)
    query_grad, key_grad, value_grad = attend_back(
        queries, key_heads, value_heads, key_live, log_total, mixed_grad
    )
    query_low = query_grad.astype(jnp.bfloat16).reshape(total_rows, model_width)
    key_low = key_grad.astype(jnp.bfloat16).reshape(total_rows, model_width)
    value_low = value_grad.astype(jnp.bfloat16).reshape(total_rows, model_width)
    query_weight_grad = outer_sum(token_rows, query_low)
    query_bias_grad = jnp.sum(query_low.astype(jnp.float32), axis=0)
    key_weight_grad = outer_sum(token_rows, key_low)
    value_weight_grad = outer_sum(token_rows, value_low)
    value_bias_grad = jnp.sum(value_low.astype(jnp.float32), axis=0)
    input_grad = (
        branch_in
        + back_project(query_low, w_query)
        + back_project(key_low, w_key)
        + back_project(value_low, w_value)
    )
    input_low = input_grad.astype(jnp.bfloat16).reshape(passages, span_len, model_width)
    tokens_grad = to_positions(input_low)
    attn_sum = sum_blocks(
        [query_weight_grad, key_weight_grad, value_weight_grad, out_weight_grad]
    )
    vectors = jnp.concatenate(
        [
            query_bias_grad[None],
            value_bias_grad[None],
            out_bias_grad[None],
            gain_one_grad[None],
            shift_one_grad[None],
            down_bias_grad[None],
            gain_two_grad[None],
            shift_two_grad[None],
            up_bias_grad.reshape(wide, model_width),
        ],
        axis=0,
    )
    vectors = butterfly(vectors)
    attn_sum = attn_sum.reshape(4, model_width, model_width)
    up_sum = up_sum.reshape(wide, model_width, model_width)
    up_sum = jnp.concatenate([up_sum[i] for i in range(wide)], axis=1)
    return (
        block_out,
        pooled,
        tokens_grad,
        attn_sum[0],
        vectors[0],
        attn_sum[1],
        attn_sum[2],
        vectors[1],
        attn_sum[3],
        vectors[2],
        vectors[3],
        vectors[4],
        up_sum,
        vectors[8:].reshape(-1),
        down_sum,
        vectors[5],
        vectors[6],
        vectors[7],
    )


def solution(mesh):
    in_specs = (
        (P("dp", "seq", None), P("dp"))
        + (P(),) * 15
        + (P("dp", "seq", None), P("dp", None))
    )
    out_specs = (P("dp", "seq", None), P("dp", None), P("dp", "seq", None)) + (P(),) * 15
    return jax.shard_map(shards, mesh=mesh, in_specs=in_specs, out_specs=out_specs, check_vma=False)
```

```python
import functools

import jax
import jax.numpy as jnp
from jax import lax
from jax.experimental import pallas as pl
from jax.experimental.pallas import tpu as pltpu
from jax.sharding import PartitionSpec as P

HEADS = 12
HEAD_DIM = 64
PAIR = 2 * HEAD_DIM
PAIRS = HEADS // 2
SCALE = HEAD_DIM ** (-0.5)
ROWS = 256
KEY_STEP = 128
MIB = 1024 * 1024

eps = 1e-06
root_half = 0.7071067811865476
inv_root_two_pi = 0.3989422804014327

f32 = jnp.float32
bf16 = jnp.bfloat16

NN = (((1,), (0,)), ((), ()))
NT = (((1,), (1,)), ((), ()))
TN = (((0,), (0,)), ((), ()))


def mul(left, right, dims=NN):
    return lax.dot_general(left, right, dims, preferred_element_type=f32)


def fixed(shape):
    return pl.BlockSpec(shape, lambda *_: (0,) * len(shape), pipeline_mode=pl.Buffered(1))


def params(mib):
    return pltpu.CompilerParams(
        dimension_semantics=("arbitrary",), vmem_limit_bytes=mib * MIB
    )


def cost(flops, moved, exps=0):
    return pl.CostEstimate(flops=int(flops), bytes_accessed=int(moved), transcendentals=int(exps))


def over_extents(length, full, body):
    for extent in range(KEY_STEP, full + 1, KEY_STEP):
        pl.when((length > extent - KEY_STEP) & (length <= extent))(functools.partial(body, extent))


def attend_kernel(
    len_ref, x_ref, wq_ref, bq_ref, wk_ref, wv_ref, bv_ref, q_ref, k_ref, v_ref, mix_ref, stat_ref
):
    full = x_ref.shape[1]
    length = len_ref[pl.program_id(0)]
    q_ref[0] = (mul(x_ref[0], wq_ref[...]) + bq_ref[...]).astype(bf16)
    stat_ref[0] = jnp.zeros(stat_ref.shape[1:], f32)
    lane = lax.broadcasted_iota(jnp.int32, (1, PAIR), 1)

    def run(extent):
        x = x_ref[0, :extent]
        k_ref[0, :extent] = mul(x, wk_ref[...]).astype(bf16)
        v_ref[0, :extent] = (mul(x, wv_ref[...]) + bv_ref[...]).astype(bf16)
        key_at = lax.broadcasted_iota(jnp.int32, (1, extent), 1)
        dead = jnp.where(key_at < length, 0.0, -1e30)

        def pair_step(pair, carry):
            at = pl.ds(pl.multiple_of(pair * PAIR, PAIR), PAIR)
            q, k, v = q_ref[0, :, at], k_ref[0, :extent, at], v_ref[0, :extent, at]
            mixed = []
            stat = stat_ref[0]
            for half in range(2):
                own = (lane >= half * HEAD_DIM) & (lane < (half + 1) * HEAD_DIM)
                q_own = jnp.where(own, q * SCALE, 0).astype(bf16)
                scores = mul(q_own, k, NT) + dead
                top = jnp.max(scores, axis=1, keepdims=True)
                expo = jnp.exp(scores - top)
                total = jnp.sum(expo, axis=1, keepdims=True)
                probs = (expo * (1.0 / total)).astype(bf16)
                mixed.append(mul(probs, v))
                stat = jnp.where(lane == pair * 2 + half, top + jnp.log(total), stat)
            stat_ref[0] = stat
            mix_ref[0, :, at] = jnp.where(lane < HEAD_DIM, mixed[0], mixed[1]).astype(bf16)
            return carry

        lax.fori_loop(0, PAIRS, pair_step, 0)

    over_extents(length, full, run)


def attend(lengths, x, w_query, b_query, w_key, w_value, b_value):
    count, full, width = x.shape
    rows = pl.BlockSpec((1, full, width), lambda i, *_: (i, 0, 0))
    act = jax.ShapeDtypeStruct((count, full, width), bf16)
    return pl.pallas_call(
        attend_kernel,
        grid_spec=pltpu.PrefetchScalarGridSpec(
            num_scalar_prefetch=1,
            grid=(count,),
            in_specs=[
                rows,
                fixed((width, width)),
                fixed((1, width)),
                fixed((width, width)),
                fixed((width, width)),
                fixed((1, width)),
            ],
            out_specs=[rows] * 4 + [pl.BlockSpec((1, full, PAIR), lambda i, *_: (i, 0, 0))],
        ),
        out_shape=[act] * 4 + [jax.ShapeDtypeStruct((count, full, PAIR), f32)],
        compiler_params=params(48),
        cost_estimate=cost(
            2 * count * full * (3 * width * width + 4 * 2 * full * width),
            10 * count * full * width + 6 * width * width,
        ),
    )(lengths, x, w_query, b_query, w_key, w_value, b_value)


def attend_back_kernel(
    len_ref, q_ref, k_ref, v_ref, mg_ref, stat_ref, dq_ref, dk_ref, dv_ref, bias_ref, log_ref
):
    full = q_ref.shape[1]
    length = len_ref[pl.program_id(0)]
    lane = lax.broadcasted_iota(jnp.int32, (1, PAIR), 1)
    log_ref[...] = stat_ref[0].T
    row = lax.broadcasted_iota(jnp.int32, (8, 1), 0)

    @pl.when(pl.program_id(0) == 0)
    def _():
        bias_ref[...] = jnp.zeros(bias_ref.shape, f32)

    def run(extent):
        key_at = lax.broadcasted_iota(jnp.int32, (extent, 1), 0)
        dead = jnp.where(key_at < length, 0.0, -1e30)
        if extent < full:
            dk_ref[0, extent:] = jnp.zeros((full - extent, dk_ref.shape[2]), bf16)
            dv_ref[0, extent:] = jnp.zeros((full - extent, dv_ref.shape[2]), bf16)

        def pair_step(pair, carry):
            at = pl.ds(pl.multiple_of(pair * PAIR, PAIR), PAIR)
            q, mg = q_ref[0, :, at], mg_ref[0, :, at]
            k, v = k_ref[0, :extent, at], v_ref[0, :extent, at]
            dq, dk, dv = [], [], []
            for half in range(2):
                own = (lane >= half * HEAD_DIM) & (lane < (half + 1) * HEAD_DIM)
                k_own = jnp.where(own, k * SCALE, 0).astype(bf16)
                v_own = jnp.where(own, v, 0).astype(bf16)
                log_row = log_ref[pl.ds(pair * 2 + half, 1), :]
                probs = jnp.exp(mul(k_own, q, NT) + dead - log_row)
                prob_grad = mul(v_own, mg, NT)
                along = jnp.sum(probs * prob_grad, axis=0, keepdims=True)
                score_grad = (probs * (prob_grad - along)).astype(bf16)
                dv.append(mul(probs.astype(bf16), mg))
                dk.append(mul(score_grad, q))
                dq.append(mul(score_grad, k, TN))
            first = lane < HEAD_DIM
            dq_pair = jnp.where(first, dq[0], dq[1]) * SCALE
            dk_pair = jnp.where(first, dk[0], dk[1]) * SCALE
            dv_pair = jnp.where(first, dv[0], dv[1])
            dq_ref[0, :, at] = dq_pair.astype(bf16)
            dk_ref[0, :extent, at] = dk_pair.astype(bf16)
            dv_ref[0, :extent, at] = dv_pair.astype(bf16)
            sums = jnp.where(
                row == 0,
                jnp.sum(dq_pair, axis=0, keepdims=True),
                jnp.where(row == 1, jnp.sum(dv_pair, axis=0, keepdims=True), 0.0),
            )
            bias_ref[:, at] += sums
            return carry

        lax.fori_loop(0, PAIRS, pair_step, 0)

    over_extents(length, full, run)


def attend_back(lengths, q, k, v, mixed_grad, stat):
    count, full, width = q.shape
    rows = pl.BlockSpec((1, full, width), lambda i, *_: (i, 0, 0))
    act = jax.ShapeDtypeStruct((count, full, width), bf16)
    return pl.pallas_call(
        attend_back_kernel,
        grid_spec=pltpu.PrefetchScalarGridSpec(
            num_scalar_prefetch=1,
            grid=(count,),
            in_specs=[rows] * 4 + [pl.BlockSpec((1, full, PAIR), lambda i, *_: (i, 0, 0))],
            out_specs=[rows] * 3 + [pl.BlockSpec((8, width), lambda i, *_: (0, 0))],
            scratch_shapes=[pltpu.VMEM((PAIR, full), f32)],
        ),
        out_shape=[act] * 3 + [jax.ShapeDtypeStruct((8, width), f32)],
        compiler_params=params(48),
        cost_estimate=cost(
            2 * count * full * 10 * 2 * full * width, 14 * count * full * width
        ),
    )(lengths, q, k, v, mixed_grad, stat)


def norm_parts(hidden):
    centred = hidden - jnp.mean(hidden, axis=1, keepdims=True)
    inv_scale = lax.rsqrt(jnp.mean(centred * centred, axis=1, keepdims=True) + eps)
    return centred * inv_scale, inv_scale


def norm_back(scaled, normed, inv_scale):
    mean = jnp.mean(scaled, axis=1, keepdims=True)
    along = jnp.mean(scaled * normed, axis=1, keepdims=True)
    return (scaled - mean - normed * along) * inv_scale


def gelu_parts(u):
    expo = jnp.exp(u * u * -0.5)
    base = 1.0 + jnp.abs(u) * (0.3275911 * root_half)
    t = pl.reciprocal(base, approx=True)
    t = t * (2.0 - base * t)
    poly = t * (
        0.5 * 0.254829592
        + t
        * (
            0.5 * -0.284496736
            + t * (0.5 * 1.421413741 + t * (0.5 * -1.453152027 + t * (0.5 * 1.061405429)))
        )
    )
    tail = poly * expo
    return jnp.where(u >= 0, 1.0 - tail, tail), expo


def rows_kernel(
    blocks,
    len_ref,
    x_ref,
    mix_ref,
    cot_ref,
    pool_ref,
    wo_ref,
    wu_ref,
    wd_ref,
    vec_ref,
    bu_ref,
    out_ref,
    pooled_ref,
    low_ref,
    act_ref,
    second_ref,
    inner_ref,
    branch_ref,
    mg_ref,
    sum_ref,
    slope_ref,
):
    step = pl.program_id(0)
    rows, width = x_ref.shape
    wide = bu_ref.shape[0]
    b_out, gain_one, shift_one, b_down, gain_two, shift_two = (vec_ref[i : i + 1] for i in range(6))
    length = len_ref[step // blocks]
    row_at = lax.broadcasted_iota(jnp.int32, (rows, 1), 0) + (step % blocks) * rows
    live = jnp.where(row_at < length, 1.0, 0.0)

    @pl.when(step == 0)
    def _():
        sum_ref[...] = jnp.zeros(sum_ref.shape, f32)

    @pl.when(step % blocks == 0)
    def _():
        pooled_ref[...] = jnp.zeros(pooled_ref.shape, f32)

    def tally(at, value):
        sum_ref[at : at + 1] += jnp.sum(value, axis=0, keepdims=True)

    part = [slice(i * width, (i + 1) * width) for i in range(wide)]
    hidden = x_ref[...].astype(f32) + mul(mix_ref[...], wo_ref[...]) + b_out
    normed_one, scale_one = norm_parts(hidden)
    first = normed_one * gain_one + shift_one
    first_low = first.astype(bf16)
    low_ref[...] = first_low
    hidden = first + b_down
    for i in range(wide):
        pre = mul(first_low, wu_ref[:, part[i]]) + bu_ref[i : i + 1]
        phi, expo = gelu_parts(pre)
        act = (pre * phi).astype(bf16)
        act_ref[:, part[i]] = act
        slope_ref[:, part[i]] = phi + pre * expo * inv_root_two_pi
        hidden += mul(act, wd_ref[part[i], :])
    normed_two, scale_two = norm_parts(hidden)
    result = normed_two * gain_two + shift_two
    out_ref[...] = result.astype(bf16)
    pooled_ref[0] += jnp.sum(result * live, axis=0, keepdims=True)
    upstream = cot_ref[...].astype(f32) + live * pool_ref[0]
    tally(6, upstream * normed_two)
    tally(7, upstream)
    second_in = norm_back(upstream * gain_two, normed_two, scale_two)
    tally(5, second_in)
    second = second_in.astype(bf16)
    second_ref[...] = second
    first_up = second_in
    for i in range(wide):
        inner = mul(second, wd_ref[part[i], :], NT) * slope_ref[:, part[i]]
        tally(8 + i, inner)
        inner = inner.astype(bf16)
        inner_ref[:, part[i]] = inner
        first_up += mul(inner, wu_ref[:, part[i]], NT)
    tally(3, first_up * normed_one)
    tally(4, first_up)
    branch_in = norm_back(first_up * gain_one, normed_one, scale_one)
    tally(2, branch_in)
    branch_ref[...] = branch_in
    mg_ref[...] = mul(branch_in.astype(bf16), wo_ref[...], NT).astype(bf16)


def row_work(lengths, x, mixed, cot, pool, w_out, w_up, w_down, vecs, b_up):
    total, width = x.shape
    count = lengths.shape[0]
    full = total // count
    hidden = w_up.shape[1]
    wide = hidden // width
    blocks = full // ROWS
    narrow = pl.BlockSpec((ROWS, width), lambda i, *_: (i, 0))
    broad = pl.BlockSpec((ROWS, hidden), lambda i, *_: (i, 0))
    single = pl.BlockSpec((1, 1, width), lambda i, *_: (i // blocks, 0, 0))
    thin = jax.ShapeDtypeStruct((total, width), bf16)
    thick = jax.ShapeDtypeStruct((total, hidden), bf16)
    return pl.pallas_call(
        functools.partial(rows_kernel, blocks),
        grid_spec=pltpu.PrefetchScalarGridSpec(
            num_scalar_prefetch=1,
            grid=(total // ROWS,),
            in_specs=[
                narrow,
                narrow,
                narrow,
                single,
                fixed((width, width)),
                fixed((width, hidden)),
                fixed((hidden, width)),
                fixed(vecs.shape),
                fixed((wide, width)),
            ],
            out_specs=[
                narrow,
                single,
                narrow,
                broad,
                narrow,
                broad,
                narrow,
                narrow,
                pl.BlockSpec((16, width), lambda i, *_: (0, 0)),
            ],
            scratch_shapes=[pltpu.VMEM((ROWS, hidden), f32)],
        ),
        out_shape=[
            thin,
            jax.ShapeDtypeStruct((count, 1, width), f32),
            thin,
            thick,
            thin,
            thick,
            jax.ShapeDtypeStruct((total, width), f32),
            thin,
            jax.ShapeDtypeStruct((16, width), f32),
        ],
        compiler_params=params(56),
        cost_estimate=cost(
            4 * total * width * (width + 2 * hidden),
            2 * total * (8 * width + 2 * hidden) + 2 * width * (width + 2 * hidden),
        ),
    )(lengths, x, mixed, cot, pool, w_out, w_up, w_down, vecs, b_up)


def outer_kernel(left_ref, right_ref, out_ref):
    out_ref[0] = mul(left_ref[...], right_ref[...], TN).astype(bf16)


def outer_blocks(left, right, side):
    total, width = left.shape[0], min(left.shape[1], right.shape[1])
    steps = (left if side == 0 else right).shape[1] // width
    whole = fixed((total, width))
    moving = pl.BlockSpec((total, width), lambda i: (0, i))
    return pl.pallas_call(
        outer_kernel,
        grid=(steps,),
        in_specs=[moving, whole] if side == 0 else [whole, moving],
        out_specs=pl.BlockSpec((1, width, width), lambda i: (i, 0, 0)),
        out_shape=jax.ShapeDtypeStruct((steps, width, width), bf16),
        compiler_params=params(48),
        cost_estimate=cost(
            2 * total * width * width * steps, 2 * (steps + 1) * total * width + 2 * steps * width * width
        ),
    )(left, right)


def attend_outer_kernel(x_ref, dq_ref, dk_ref, dv_ref, mix_ref, branch_ref, out_ref):
    step = pl.program_id(0)
    for at, grad_ref in enumerate((dq_ref, dk_ref, dv_ref)):

        @pl.when(step == at)
        def _(grad_ref=grad_ref):
            out_ref[0] = mul(x_ref[...], grad_ref[...], TN).astype(bf16)

    @pl.when(step == 3)
    def _():
        out_ref[0] = mul(mix_ref[...], branch_ref[...].astype(bf16), TN).astype(bf16)


def attend_outer(x, dq, dk, dv, mixed, branch_in):
    total, width = x.shape
    whole = fixed((total, width))
    return pl.pallas_call(
        attend_outer_kernel,
        grid=(4,),
        in_specs=[whole] * 6,
        out_specs=pl.BlockSpec((1, width, width), lambda i: (i, 0, 0)),
        out_shape=jax.ShapeDtypeStruct((4, width, width), bf16),
        compiler_params=params(48),
        cost_estimate=cost(8 * total * width * width, 14 * total * width + 8 * width * width),
    )(x, dq, dk, dv, mixed, branch_in)


def input_kernel(branch_ref, dq_ref, dk_ref, dv_ref, wq_ref, wk_ref, wv_ref, out_ref):
    total = branch_ref[...] + mul(dq_ref[...], wq_ref[...], NT)
    total += mul(dk_ref[...], wk_ref[...], NT)
    total += mul(dv_ref[...], wv_ref[...], NT)
    out_ref[...] = total.astype(bf16)


def input_grad(branch_in, dq, dk, dv, w_query, w_key, w_value):
    total, width = branch_in.shape
    rows = pl.BlockSpec((ROWS, width), lambda i: (i, 0))
    return pl.pallas_call(
        input_kernel,
        grid=(total // ROWS,),
        in_specs=[rows] * 4 + [fixed((width, width))] * 3,
        out_specs=rows,
        out_shape=jax.ShapeDtypeStruct((total, width), bf16),
        compiler_params=params(48),
        cost_estimate=cost(6 * total * width * width, 12 * total * width + 6 * width * width),
    )(branch_in, dq, dk, dv, w_query, w_key, w_value)


def exchange(value, axis, mask):
    count = lax.axis_size(axis)
    return lax.ppermute(value, axis, [(i, i ^ mask) for i in range(count)])


def to_passages(value):
    count = lax.axis_size("seq")
    mine = lax.axis_index("seq")
    held, piece, width = value.shape
    own = held // count
    whole = jnp.zeros((own, piece * count, width), value.dtype)
    for mask in range(count):
        peer = mine ^ mask
        part = lax.dynamic_slice_in_dim(value, peer * own, own, 0)
        if mask:
            part = exchange(part, "seq", mask)
        whole = lax.dynamic_update_slice_in_dim(whole, part, peer * piece, 1)
    return whole


def to_positions(value):
    count = lax.axis_size("seq")
    mine = lax.axis_index("seq")
    own, full, width = value.shape
    piece = full // count
    result = jnp.zeros((own * count, piece, width), value.dtype)
    for mask in range(count):
        peer = mine ^ mask
        part = lax.dynamic_slice_in_dim(value, peer * piece, piece, 1)
        if mask:
            part = exchange(part, "seq", mask)
        result = lax.dynamic_update_slice_in_dim(result, part, peer * own, 0)
    return result


def axis_bits(axis):
    return [(axis, 1 << i) for i in range(lax.axis_size(axis).bit_length() - 1)]


def orders():
    seq_bits = axis_bits("seq")
    dp_bits = axis_bits("dp")
    first = seq_bits[:1] + dp_bits[:1] + seq_bits[1:] + dp_bits[1:]
    second = seq_bits[:2] + dp_bits[:1] + seq_bits[2:] + dp_bits[1:]
    return first, second


def upper(axis, mask):
    return (lax.axis_index(axis) & mask) // mask


def halve(value, order):
    for axis, mask in order:
        half = value.shape[0] // 2
        bit = upper(axis, mask)
        send = lax.dynamic_slice_in_dim(value, (1 - bit) * half, half, 0)
        keep = lax.dynamic_slice_in_dim(value, bit * half, half, 0)
        got = exchange(send, axis, mask)
        value = (keep.astype(jnp.float32) + got.astype(jnp.float32)).astype(jnp.bfloat16)
    return value


def double(value, order):
    for axis, mask in reversed(order):
        got = exchange(value, axis, mask)
        bit = upper(axis, mask)
        value = jnp.where(
            bit == 1,
            jnp.concatenate([got, value], axis=0),
            jnp.concatenate([value, got], axis=0),
        )
    return value


def butterfly(value):
    for axis, mask in axis_bits("seq") + axis_bits("dp"):
        value = value + exchange(value, axis, mask)
    return value


def shards(
    tokens,
    lengths,
    w_query,
    b_query,
    w_key,
    w_value,
    b_value,
    w_out,
    b_out,
    gain_one,
    shift_one,
    w_up,
    b_up,
    w_down,
    b_down,
    gain_two,
    shift_two,
    out_grad,
    pooled_grad,
):
    seq_count = lax.axis_size("seq")
    held, piece, width = tokens.shape
    full = piece * seq_count
    count = held // seq_count
    mine = lax.axis_index("seq")
    wide = w_up.shape[1] // width
    total = count * full

    def flat(value):
        return value.reshape(total, width)

    def split(value):
        return value.reshape(count, full, width)

    x = to_passages(tokens)
    cot = to_passages(out_grad)
    local_len = lax.dynamic_slice_in_dim(lengths, mine * count, count, 0)
    len_float = local_len.astype(f32)[:, None, None]
    pool = lax.dynamic_slice_in_dim(pooled_grad, mine * count, count, 0)[:, None, :] / len_float

    q, k, v, mixed, stat = attend(
        local_len, x, w_query, b_query.astype(f32)[None], w_key, w_value, b_value.astype(f32)[None]
    )
    vecs = jnp.stack([b_out, gain_one, shift_one, b_down, gain_two, shift_two]).astype(f32)
    vecs = jnp.pad(vecs, ((0, 2), (0, 0)))
    result, pooled_sum, first_low, act, second, inner, branch_in, mixed_grad, sums = row_work(
        local_len,
        flat(x),
        flat(mixed),
        flat(cot),
        pool,
        w_out,
        w_up,
        w_down,
        vecs,
        b_up.astype(f32).reshape(wide, width),
    )
    down = outer_blocks(act, second, 0).reshape(-1, width)
    up = outer_blocks(first_low, inner, 1).reshape(-1, width)
    dense = lax.psum(jnp.concatenate([down, up], axis=0), ("dp", "seq"))
    block_out = to_positions(split(result))
    pooled_mine = pooled_sum[:, 0] / len_float[:, 0]
    pooled = jnp.zeros((held, width), f32)
    for mask in range(seq_count):
        got = exchange(pooled_mine, "seq", mask) if mask else pooled_mine
        pooled = lax.dynamic_update_slice_in_dim(pooled, got, (mine ^ mask) * count, 0)

    dq, dk, dv, bias_sums = attend_back(local_len, q, k, v, split(mixed_grad), stat)
    dq, dk, dv = flat(dq), flat(dk), flat(dv)
    outer = attend_outer(flat(x), dq, dk, dv, flat(mixed), branch_in).reshape(-1, width)
    tokens_grad = to_positions(split(input_grad(branch_in, dq, dk, dv, w_query, w_key, w_value)))
    vectors = butterfly(sums + jnp.pad(bias_sums, ((0, 8), (0, 0))))
    outer, dense = lax.optimization_barrier((outer, dense))
    outer = lax.psum(outer, ("dp", "seq")).astype(f32).reshape(4, width, width)
    dense = dense.astype(f32)
    down_sum = dense[: wide * width]
    up_sum = dense[wide * width :].reshape(wide, width, width)
    up_sum = jnp.concatenate([up_sum[i] for i in range(wide)], axis=1)
    return (
        block_out,
        pooled,
        tokens_grad,
        outer[0],
        vectors[0],
        outer[1],
        outer[2],
        vectors[1],
        outer[3],
        vectors[2],
        vectors[3],
        vectors[4],
        up_sum,
        vectors[8 : 8 + wide].reshape(-1),
        down_sum,
        vectors[5],
        vectors[6],
        vectors[7],
    )


def solution(mesh):
    in_specs = (
        (P("dp", "seq", None), P("dp"))
        + (P(),) * 15
        + (P("dp", "seq", None), P("dp", None))
    )
    out_specs = (P("dp", "seq", None), P("dp", None), P("dp", "seq", None)) + (P(),) * 15
    return jax.shard_map(shards, mesh=mesh, in_specs=in_specs, out_specs=out_specs, check_vma=False)
```

```python
import functools

import jax
import jax.numpy as jnp
from jax import lax
from jax.experimental import pallas as pl
from jax.experimental.pallas import tpu as pltpu
from jax.sharding import PartitionSpec as P

HEADS = 12
HEAD_DIM = 64
PAIR = 2 * HEAD_DIM
PAIRS = HEADS // 2
SCALE = HEAD_DIM ** (-0.5)
ROWS = 256
KEY_STEP = 128
MIB = 1024 * 1024

eps = 1e-06
root_half = 0.7071067811865476
inv_root_two_pi = 0.3989422804014327

f32 = jnp.float32
bf16 = jnp.bfloat16

NN = (((1,), (0,)), ((), ()))
NT = (((1,), (1,)), ((), ()))
TN = (((0,), (0,)), ((), ()))


def mul(left, right, dims=NN):
    return lax.dot_general(left, right, dims, preferred_element_type=f32)


def fixed(shape):
    return pl.BlockSpec(shape, lambda *_: (0,) * len(shape), pipeline_mode=pl.Buffered(1))


def params(mib):
    return pltpu.CompilerParams(
        dimension_semantics=("arbitrary",), vmem_limit_bytes=mib * MIB
    )


def cost(flops, moved, exps=0):
    return pl.CostEstimate(flops=int(flops), bytes_accessed=int(moved), transcendentals=int(exps))


def over_extents(length, full, body):
    for extent in range(KEY_STEP, full + 1, KEY_STEP):
        pl.when((length > extent - KEY_STEP) & (length <= extent))(functools.partial(body, extent))


def attend_kernel(
    len_ref, x_ref, wq_ref, bq_ref, wk_ref, wv_ref, bv_ref, q_ref, k_ref, v_ref, mix_ref, stat_ref
):
    full = x_ref.shape[1]
    length = len_ref[pl.program_id(0)]
    q_ref[0] = (mul(x_ref[0], wq_ref[...]) + bq_ref[...]).astype(bf16)
    stat_ref[0] = jnp.zeros(stat_ref.shape[1:], f32)
    lane = lax.broadcasted_iota(jnp.int32, (1, PAIR), 1)

    def run(extent):
        x = x_ref[0, :extent]
        k_ref[0, :extent] = mul(x, wk_ref[...]).astype(bf16)
        v_ref[0, :extent] = (mul(x, wv_ref[...]) + bv_ref[...]).astype(bf16)
        key_at = lax.broadcasted_iota(jnp.int32, (1, extent), 1)
        dead = jnp.where(key_at < length, 0.0, -1e30)

        def pair_step(pair, carry):
            at = pl.ds(pl.multiple_of(pair * PAIR, PAIR), PAIR)
            q, k, v = q_ref[0, :, at], k_ref[0, :extent, at], v_ref[0, :extent, at]
            mixed = []
            stat = stat_ref[0]
            for half in range(2):
                own = (lane >= half * HEAD_DIM) & (lane < (half + 1) * HEAD_DIM)
                q_own = jnp.where(own, q * SCALE, 0).astype(bf16)
                scores = mul(q_own, k, NT) + dead
                top = jnp.max(scores, axis=1, keepdims=True)
                expo = jnp.exp(scores - top)
                total = jnp.sum(expo, axis=1, keepdims=True)
                probs = (expo * (1.0 / total)).astype(bf16)
                mixed.append(mul(probs, v))
                stat = jnp.where(lane == pair * 2 + half, top + jnp.log(total), stat)
            stat_ref[0] = stat
            mix_ref[0, :, at] = jnp.where(lane < HEAD_DIM, mixed[0], mixed[1]).astype(bf16)
            return carry

        lax.fori_loop(0, PAIRS, pair_step, 0)

    over_extents(length, full, run)


def attend(lengths, x, w_query, b_query, w_key, w_value, b_value):
    count, full, width = x.shape
    rows = pl.BlockSpec((1, full, width), lambda i, *_: (i, 0, 0))
    act = jax.ShapeDtypeStruct((count, full, width), bf16)
    return pl.pallas_call(
        attend_kernel,
        grid_spec=pltpu.PrefetchScalarGridSpec(
            num_scalar_prefetch=1,
            grid=(count,),
            in_specs=[
                rows,
                fixed((width, width)),
                fixed((1, width)),
                fixed((width, width)),
                fixed((width, width)),
                fixed((1, width)),
            ],
            out_specs=[rows] * 4 + [pl.BlockSpec((1, full, PAIR), lambda i, *_: (i, 0, 0))],
        ),
        out_shape=[act] * 4 + [jax.ShapeDtypeStruct((count, full, PAIR), f32)],
        compiler_params=params(48),
        cost_estimate=cost(
            2 * count * full * (3 * width * width + 4 * 2 * full * width),
            10 * count * full * width + 6 * width * width,
        ),
    )(lengths, x, w_query, b_query, w_key, w_value, b_value)


def attend_back_kernel(
    len_ref, q_ref, k_ref, v_ref, mg_ref, stat_ref, dq_ref, dk_ref, dv_ref, bias_ref, log_ref
):
    full = q_ref.shape[1]
    length = len_ref[pl.program_id(0)]
    lane = lax.broadcasted_iota(jnp.int32, (1, PAIR), 1)
    log_ref[...] = stat_ref[0].T
    row = lax.broadcasted_iota(jnp.int32, (8, 1), 0)

    @pl.when(pl.program_id(0) == 0)
    def _():
        bias_ref[...] = jnp.zeros(bias_ref.shape, f32)

    def run(extent):
        key_at = lax.broadcasted_iota(jnp.int32, (extent, 1), 0)
        dead = jnp.where(key_at < length, 0.0, -1e30)
        if extent < full:
            dk_ref[0, extent:] = jnp.zeros((full - extent, dk_ref.shape[2]), bf16)
            dv_ref[0, extent:] = jnp.zeros((full - extent, dv_ref.shape[2]), bf16)

        def pair_step(pair, carry):
            at = pl.ds(pl.multiple_of(pair * PAIR, PAIR), PAIR)
            q, mg = q_ref[0, :, at], mg_ref[0, :, at]
            k, v = k_ref[0, :extent, at], v_ref[0, :extent, at]
            dq, dk, dv = [], [], []
            for half in range(2):
                own = (lane >= half * HEAD_DIM) & (lane < (half + 1) * HEAD_DIM)
                k_own = jnp.where(own, k * SCALE, 0).astype(bf16)
                v_own = jnp.where(own, v, 0).astype(bf16)
                log_row = log_ref[pl.ds(pair * 2 + half, 1), :]
                probs = jnp.exp(mul(k_own, q, NT) + dead - log_row)
                prob_grad = mul(v_own, mg, NT)
                along = jnp.sum(probs * prob_grad, axis=0, keepdims=True)
                score_grad = (probs * (prob_grad - along)).astype(bf16)
                dv.append(mul(probs.astype(bf16), mg))
                dk.append(mul(score_grad, q))
                dq.append(mul(score_grad, k, TN))
            first = lane < HEAD_DIM
            dq_pair = jnp.where(first, dq[0], dq[1]) * SCALE
            dk_pair = jnp.where(first, dk[0], dk[1]) * SCALE
            dv_pair = jnp.where(first, dv[0], dv[1])
            dq_ref[0, :, at] = dq_pair.astype(bf16)
            dk_ref[0, :extent, at] = dk_pair.astype(bf16)
            dv_ref[0, :extent, at] = dv_pair.astype(bf16)
            sums = jnp.where(
                row == 0,
                jnp.sum(dq_pair, axis=0, keepdims=True),
                jnp.where(row == 1, jnp.sum(dv_pair, axis=0, keepdims=True), 0.0),
            )
            bias_ref[:, at] += sums
            return carry

        lax.fori_loop(0, PAIRS, pair_step, 0)

    over_extents(length, full, run)


def attend_back(lengths, q, k, v, mixed_grad, stat):
    count, full, width = q.shape
    rows = pl.BlockSpec((1, full, width), lambda i, *_: (i, 0, 0))
    act = jax.ShapeDtypeStruct((count, full, width), bf16)
    return pl.pallas_call(
        attend_back_kernel,
        grid_spec=pltpu.PrefetchScalarGridSpec(
            num_scalar_prefetch=1,
            grid=(count,),
            in_specs=[rows] * 4 + [pl.BlockSpec((1, full, PAIR), lambda i, *_: (i, 0, 0))],
            out_specs=[rows] * 3 + [pl.BlockSpec((8, width), lambda i, *_: (0, 0))],
            scratch_shapes=[pltpu.VMEM((PAIR, full), f32)],
        ),
        out_shape=[act] * 3 + [jax.ShapeDtypeStruct((8, width), f32)],
        compiler_params=params(48),
        cost_estimate=cost(
            2 * count * full * 10 * 2 * full * width, 14 * count * full * width
        ),
    )(lengths, q, k, v, mixed_grad, stat)


def norm_parts(hidden):
    centred = hidden - jnp.mean(hidden, axis=1, keepdims=True)
    inv_scale = lax.rsqrt(jnp.mean(centred * centred, axis=1, keepdims=True) + eps)
    return centred * inv_scale, inv_scale


def norm_back(scaled, normed, inv_scale):
    mean = jnp.mean(scaled, axis=1, keepdims=True)
    along = jnp.mean(scaled * normed, axis=1, keepdims=True)
    return (scaled - mean - normed * along) * inv_scale


def gelu_parts(u):
    expo = jnp.exp(u * u * -0.5)
    base = 1.0 + jnp.abs(u) * (0.3275911 * root_half)
    t = pl.reciprocal(base, approx=True)
    t = t * (2.0 - base * t)
    poly = t * (
        0.5 * 0.254829592
        + t
        * (
            0.5 * -0.284496736
            + t * (0.5 * 1.421413741 + t * (0.5 * -1.453152027 + t * (0.5 * 1.061405429)))
        )
    )
    tail = poly * expo
    return jnp.where(u >= 0, 1.0 - tail, tail), expo


def rows_kernel(
    blocks,
    len_ref,
    x_ref,
    mix_ref,
    cot_ref,
    pool_ref,
    wo_ref,
    wu_ref,
    wd_ref,
    vec_ref,
    bu_ref,
    out_ref,
    pooled_ref,
    low_ref,
    act_ref,
    second_ref,
    inner_ref,
    branch_ref,
    mg_ref,
    sum_ref,
    slope_ref,
):
    step = pl.program_id(0)
    rows, width = x_ref.shape
    wide = bu_ref.shape[0]
    b_out, gain_one, shift_one, b_down, gain_two, shift_two = (vec_ref[i : i + 1] for i in range(6))
    length = len_ref[step // blocks]
    row_at = lax.broadcasted_iota(jnp.int32, (rows, 1), 0) + (step % blocks) * rows
    live = jnp.where(row_at < length, 1.0, 0.0)

    @pl.when(step == 0)
    def _():
        sum_ref[...] = jnp.zeros(sum_ref.shape, f32)

    @pl.when(step % blocks == 0)
    def _():
        pooled_ref[...] = jnp.zeros(pooled_ref.shape, f32)

    def tally(at, value):
        sum_ref[at : at + 1] += jnp.sum(value, axis=0, keepdims=True)

    part = [slice(i * width, (i + 1) * width) for i in range(wide)]
    hidden = x_ref[...].astype(f32) + mul(mix_ref[...], wo_ref[...]) + b_out
    normed_one, scale_one = norm_parts(hidden)
    first = normed_one * gain_one + shift_one
    first_low = first.astype(bf16)
    low_ref[...] = first_low
    hidden = first + b_down
    for i in range(wide):
        pre = mul(first_low, wu_ref[:, part[i]]) + bu_ref[i : i + 1]
        phi, expo = gelu_parts(pre)
        act = (pre * phi).astype(bf16)
        act_ref[:, part[i]] = act
        slope_ref[:, part[i]] = phi + pre * expo * inv_root_two_pi
        hidden += mul(act, wd_ref[part[i], :])
    normed_two, scale_two = norm_parts(hidden)
    result = normed_two * gain_two + shift_two
    out_ref[...] = result.astype(bf16)
    pooled_ref[0] += jnp.sum(result * live, axis=0, keepdims=True)
    upstream = cot_ref[...].astype(f32) + live * pool_ref[0]
    tally(6, upstream * normed_two)
    tally(7, upstream)
    second_in = norm_back(upstream * gain_two, normed_two, scale_two)
    tally(5, second_in)
    second = second_in.astype(bf16)
    second_ref[...] = second
    first_up = second_in
    for i in range(wide):
        inner = mul(second, wd_ref[part[i], :], NT) * slope_ref[:, part[i]]
        tally(8 + i, inner)
        inner = inner.astype(bf16)
        inner_ref[:, part[i]] = inner
        first_up += mul(inner, wu_ref[:, part[i]], NT)
    tally(3, first_up * normed_one)
    tally(4, first_up)
    branch_in = norm_back(first_up * gain_one, normed_one, scale_one)
    tally(2, branch_in)
    branch_ref[...] = branch_in
    mg_ref[...] = mul(branch_in.astype(bf16), wo_ref[...], NT).astype(bf16)


def row_work(lengths, x, mixed, cot, pool, w_out, w_up, w_down, vecs, b_up):
    total, width = x.shape
    count = lengths.shape[0]
    full = total // count
    hidden = w_up.shape[1]
    wide = hidden // width
    blocks = full // ROWS
    narrow = pl.BlockSpec((ROWS, width), lambda i, *_: (i, 0))
    broad = pl.BlockSpec((ROWS, hidden), lambda i, *_: (i, 0))
    single = pl.BlockSpec((1, 1, width), lambda i, *_: (i // blocks, 0, 0))
    thin = jax.ShapeDtypeStruct((total, width), bf16)
    thick = jax.ShapeDtypeStruct((total, hidden), bf16)
    return pl.pallas_call(
        functools.partial(rows_kernel, blocks),
        grid_spec=pltpu.PrefetchScalarGridSpec(
            num_scalar_prefetch=1,
            grid=(total // ROWS,),
            in_specs=[
                narrow,
                narrow,
                narrow,
                single,
                fixed((width, width)),
                fixed((width, hidden)),
                fixed((hidden, width)),
                fixed(vecs.shape),
                fixed((wide, width)),
            ],
            out_specs=[
                narrow,
                single,
                narrow,
                broad,
                narrow,
                broad,
                narrow,
                narrow,
                pl.BlockSpec((16, width), lambda i, *_: (0, 0)),
            ],
            scratch_shapes=[pltpu.VMEM((ROWS, hidden), f32)],
        ),
        out_shape=[
            thin,
            jax.ShapeDtypeStruct((count, 1, width), f32),
            thin,
            thick,
            thin,
            thick,
            jax.ShapeDtypeStruct((total, width), f32),
            thin,
            jax.ShapeDtypeStruct((16, width), f32),
        ],
        compiler_params=params(56),
        cost_estimate=cost(
            4 * total * width * (width + 2 * hidden),
            2 * total * (8 * width + 2 * hidden) + 2 * width * (width + 2 * hidden),
        ),
    )(lengths, x, mixed, cot, pool, w_out, w_up, w_down, vecs, b_up)


def dense_outer_kernel(side_ref, act_ref, second_ref, low_ref, inner_ref, out_ref):
    step = pl.program_id(0)
    half = pl.num_programs(0) // 2

    @pl.when(step < half)
    def _():
        out_ref[0] = mul(act_ref[...], second_ref[...], TN).astype(bf16)

    @pl.when(step >= half)
    def _():
        out_ref[0] = mul(low_ref[...], inner_ref[...], TN).astype(bf16)


def dense_outer(side, act, second, low, inner):
    total, width = second.shape
    wide = act.shape[1] // width
    half = wide // 2
    return pl.pallas_call(
        dense_outer_kernel,
        grid_spec=pltpu.PrefetchScalarGridSpec(
            num_scalar_prefetch=1,
            grid=(wide,),
            in_specs=[
                pl.BlockSpec(
                    (total, width), lambda i, s: (0, s[0] * half + jnp.minimum(i, half - 1))
                ),
                fixed((total, width)),
                fixed((total, width)),
                pl.BlockSpec(
                    (total, width), lambda i, s: (0, s[0] * half + jnp.maximum(i - half, 0))
                ),
            ],
            out_specs=pl.BlockSpec((1, width, width), lambda i, s: (i, 0, 0)),
        ),
        out_shape=jax.ShapeDtypeStruct((wide, width, width), bf16),
        compiler_params=params(48),
        cost_estimate=cost(
            2 * total * width * width * wide, 2 * (wide + 2) * total * width + 2 * wide * width * width
        ),
    )(side, act, second, low, inner).reshape(wide * width, width)


def attend_outer_kernel(side_ref, x_ref, dq_ref, dk_ref, dv_ref, mix_ref, branch_ref, out_ref):
    block = side_ref[0] * 2 + pl.program_id(0)
    for at, grad_ref in enumerate((dq_ref, dk_ref, dv_ref)):

        @pl.when(block == at)
        def _(grad_ref=grad_ref):
            out_ref[0] = mul(x_ref[...], grad_ref[...], TN).astype(bf16)

    @pl.when(block == 3)
    def _():
        out_ref[0] = mul(mix_ref[...], branch_ref[...].astype(bf16), TN).astype(bf16)


def attend_outer(side, x, dq, dk, dv, mixed, branch_in):
    total, width = x.shape
    whole = fixed((total, width))
    return pl.pallas_call(
        attend_outer_kernel,
        grid_spec=pltpu.PrefetchScalarGridSpec(
            num_scalar_prefetch=1,
            grid=(2,),
            in_specs=[whole] * 6,
            out_specs=pl.BlockSpec((1, width, width), lambda i, s: (i, 0, 0)),
        ),
        out_shape=jax.ShapeDtypeStruct((2, width, width), bf16),
        compiler_params=params(48),
        cost_estimate=cost(4 * total * width * width, 14 * total * width + 4 * width * width),
    )(side, x, dq, dk, dv, mixed, branch_in).reshape(2 * width, width)


def input_kernel(branch_ref, dq_ref, dk_ref, dv_ref, wq_ref, wk_ref, wv_ref, out_ref):
    total = branch_ref[...] + mul(dq_ref[...], wq_ref[...], NT)
    total += mul(dk_ref[...], wk_ref[...], NT)
    total += mul(dv_ref[...], wv_ref[...], NT)
    out_ref[...] = total.astype(bf16)


def input_grad(branch_in, dq, dk, dv, w_query, w_key, w_value):
    total, width = branch_in.shape
    rows = pl.BlockSpec((ROWS, width), lambda i: (i, 0))
    return pl.pallas_call(
        input_kernel,
        grid=(total // ROWS,),
        in_specs=[rows] * 4 + [fixed((width, width))] * 3,
        out_specs=rows,
        out_shape=jax.ShapeDtypeStruct((total, width), bf16),
        compiler_params=params(48),
        cost_estimate=cost(6 * total * width * width, 12 * total * width + 6 * width * width),
    )(branch_in, dq, dk, dv, w_query, w_key, w_value)


def exchange(value, axis, mask):
    count = lax.axis_size(axis)
    return lax.ppermute(value, axis, [(i, i ^ mask) for i in range(count)])


def to_passages(value):
    count = lax.axis_size("seq")
    mine = lax.axis_index("seq")
    held, piece, width = value.shape
    own = held // count
    whole = jnp.zeros((own, piece * count, width), value.dtype)
    for mask in range(count):
        peer = mine ^ mask
        part = lax.dynamic_slice_in_dim(value, peer * own, own, 0)
        if mask:
            part = exchange(part, "seq", mask)
        whole = lax.dynamic_update_slice_in_dim(whole, part, peer * piece, 1)
    return whole


def to_positions(value):
    count = lax.axis_size("seq")
    mine = lax.axis_index("seq")
    own, full, width = value.shape
    piece = full // count
    result = jnp.zeros((own * count, piece, width), value.dtype)
    for mask in range(count):
        peer = mine ^ mask
        part = lax.dynamic_slice_in_dim(value, peer * piece, piece, 1)
        if mask:
            part = exchange(part, "seq", mask)
        result = lax.dynamic_update_slice_in_dim(result, part, peer * own, 0)
    return result


def axis_bits(axis):
    return [(axis, 1 << i) for i in range(lax.axis_size(axis).bit_length() - 1)]


def upper(dim):
    axis, mask = dim
    return (lax.axis_index(axis) & mask) // mask


def swap(value, dim):
    return exchange(value, dim[0], dim[1])


def total_of(parts):
    total = parts[0].astype(f32)
    for part in parts[1:]:
        total += part.astype(f32)
    return total.astype(bf16)


PARTS = 3
SHARD_STEP = 16


class Plan:
    def __init__(self, rows):
        dims = axis_bits("seq") + axis_bits("dp")
        self.first = dims[0]
        rest = dims[1:]
        self.rows = rows // PARTS
        halved = 0
        while halved < len(rest) and (self.rows >> (halved + 1)) % SHARD_STEP == 0:
            halved += 1
        self.last = rest[halved - 1]
        self.plain = rest[halved:]
        split = rest[: halved - 1]
        self.orders = [split[i % len(split) :] + split[: i % len(split)] for i in range(PARTS)]
        self.shards = 1 << halved
        self.shard = self.rows >> halved

    def codes(self):
        found = []
        for order in self.orders:
            code = upper(self.last)
            for at, dim in enumerate(reversed(order)):
                code += upper(dim) << (at + 1)
            found.append(code)
        return jnp.stack(found).astype(jnp.int32)


def scatter_sum(plan, keep, got):
    parts = []
    for i, order in enumerate(plan.orders):
        base, size = i * plan.rows, plan.rows
        pair = [keep, got]
        for dim in order:
            size //= 2
            bit = upper(dim)
            send = total_of(
                [lax.dynamic_slice_in_dim(p, base + (1 - bit) * size, size, 0) for p in pair]
            )
            mine = total_of([lax.dynamic_slice_in_dim(p, base + bit * size, size, 0) for p in pair])
            pair = [mine, swap(send, dim)]
            base = 0
        parts.append(pair)
    size = plan.shard
    bit = upper(plan.last)

    def side(at):
        return jnp.concatenate(
            [total_of([lax.dynamic_slice_in_dim(p, at * size, size, 0) for p in pair]) for pair in parts],
            axis=0,
        )

    shard = total_of([side(bit), swap(side(1 - bit), plan.last)])
    for dim in plan.plain:
        shard = total_of([shard, swap(shard, dim)])
    return shard


def gather_parts(plan, shard):
    got = swap(shard, plan.last)
    found = []
    size = plan.shard
    for i, order in enumerate(plan.orders):
        at = slice(i * size, (i + 1) * size)
        value, more = shard[at], got[at]
        for dim in reversed(order):
            value = jnp.concatenate([value, more], axis=0)
            more = swap(value, dim)
        found += [value, more]
    return found


def place(plan, refs, code_ref, row, store):
    part = row // plan.rows
    shard = ((row % plan.rows) // plan.shard) ^ code_ref[part]
    half = plan.shards // 2
    at = pl.ds(pl.multiple_of((shard & (half - 1)) * plan.shard, plan.shard), plan.shard)
    low, high = refs[2 * part][at, :], refs[2 * part + 1][at, :]
    store(jnp.where(shard >= half, high.astype(f32), low.astype(f32)))


def dense_place_kernel(plan, half, code_ref, *refs):
    sources, (down_ref, up_ref) = refs[: 4 * PARTS], refs[4 * PARTS :]
    width = down_ref.shape[1]
    for step in range(4 * half):

        @pl.when(pl.program_id(0) == step)
        def _(step=step):
            side, block = step // (2 * half), step % (2 * half)
            own = sources[2 * PARTS * side : 2 * PARTS * (side + 1)]
            out_ref = down_ref if block < half else up_ref
            for row in range(0, width, plan.shard):

                def store(value, row=row):
                    out_ref[row : row + plan.shard, :] = value

                place(plan, own, code_ref, block * width + row, store)


def dense_place(plan, info, sources, width, wide):
    half = wide // 2

    def spot(i, info, shift):
        step = jnp.clip(i - shift, 0, 4 * half - 1)
        turn = step // (2 * half)
        side = jnp.where(turn == 0, info[PARTS], 1 - info[PARTS])
        return side * half + jnp.minimum(step % (2 * half), half - 1)

    return pl.pallas_call(
        functools.partial(dense_place_kernel, plan, half),
        grid_spec=pltpu.PrefetchScalarGridSpec(
            num_scalar_prefetch=1,
            grid=(4 * half,),
            in_specs=[fixed(x.shape) for x in sources],
            out_specs=[
                pl.BlockSpec((width, width), lambda i, s: (spot(i, s, 0), 0)),
                pl.BlockSpec((width, width), lambda i, s: (0, spot(i, s, half))),
            ],
        ),
        out_shape=[
            jax.ShapeDtypeStruct((wide * width, width), f32),
            jax.ShapeDtypeStruct((width, wide * width), f32),
        ],
        compiler_params=params(48),
        cost_estimate=cost(0, 12 * wide * width * width),
    )(info, *sources)


def attend_place_kernel(plan, code_ref, *refs):
    sources, outs = refs[: 4 * PARTS], refs[4 * PARTS :]
    width = outs[0].shape[1]
    for step in range(4):

        @pl.when(pl.program_id(0) == step)
        def _(step=step):
            turn, block = step // 2, step % 2
            own = sources[2 * PARTS * turn : 2 * PARTS * (turn + 1)]
            for row in range(0, width, plan.shard):

                def store(value, row=row):
                    for side in range(2):

                        @pl.when(code_ref[PARTS] == (side if turn == 0 else 1 - side))
                        def _():
                            outs[2 * side + block][row : row + plan.shard, :] = value

                place(plan, own, code_ref, block * width + row, store)


def attend_place(plan, info, sources, width):
    return pl.pallas_call(
        functools.partial(attend_place_kernel, plan),
        grid_spec=pltpu.PrefetchScalarGridSpec(
            num_scalar_prefetch=1,
            grid=(4,),
            in_specs=[fixed(x.shape) for x in sources],
            out_specs=[pl.BlockSpec((width, width), lambda i, s: (0, 0))] * 4,
        ),
        out_shape=[jax.ShapeDtypeStruct((width, width), f32)] * 4,
        compiler_params=params(48),
        cost_estimate=cost(0, 24 * width * width),
    )(info, *sources)


def sum_halves(plan, send, keep):
    shard = scatter_sum(plan, keep, swap(send, plan.first))
    own = gather_parts(plan, shard)
    return own + [swap(value, plan.first) for value in own]


def shards(
    tokens,
    lengths,
    w_query,
    b_query,
    w_key,
    w_value,
    b_value,
    w_out,
    b_out,
    gain_one,
    shift_one,
    w_up,
    b_up,
    w_down,
    b_down,
    gain_two,
    shift_two,
    out_grad,
    pooled_grad,
):
    seq_count = lax.axis_size("seq")
    held, piece, width = tokens.shape
    full = piece * seq_count
    count = held // seq_count
    mine = lax.axis_index("seq")
    wide = w_up.shape[1] // width
    total = count * full

    def flat(value):
        return value.reshape(total, width)

    def split(value):
        return value.reshape(count, full, width)

    x = to_passages(tokens)
    cot = to_passages(lax.optimization_barrier((out_grad, x))[0])
    local_len = lax.dynamic_slice_in_dim(lengths, mine * count, count, 0)
    len_float = local_len.astype(f32)[:, None, None]
    pool = lax.dynamic_slice_in_dim(pooled_grad, mine * count, count, 0)[:, None, :] / len_float

    q, k, v, mixed, stat = attend(
        local_len, x, w_query, b_query.astype(f32)[None], w_key, w_value, b_value.astype(f32)[None]
    )
    vecs = jnp.stack([b_out, gain_one, shift_one, b_down, gain_two, shift_two]).astype(f32)
    vecs = jnp.pad(vecs, ((0, 2), (0, 0)))
    result, pooled_sum, first_low, act, second, inner, branch_in, mixed_grad, sums = row_work(
        local_len,
        flat(x),
        flat(mixed),
        flat(cot),
        pool,
        w_out,
        w_up,
        w_down,
        vecs,
        b_up.astype(f32).reshape(wide, width),
    )
    first = axis_bits("seq")[0]
    own = upper(first).astype(jnp.int32)[None]
    dense_plan = Plan(wide * width)
    outer_plan = Plan(2 * width)
    send = dense_outer(1 - own, act, second, first_low, inner)
    keep = dense_outer(own, act, second, first_low, inner)
    dense = sum_halves(dense_plan, send, keep)
    block_out = to_positions(split(result))
    pooled_mine = pooled_sum[:, 0] / len_float[:, 0]
    pooled = lax.all_gather(pooled_mine, "seq", axis=0, tiled=True)

    dq, dk, dv, bias_sums = attend_back(local_len, q, k, v, split(mixed_grad), stat)
    dq, dk, dv = flat(dq), flat(dk), flat(dv)
    send = attend_outer(1 - own, flat(x), dq, dk, dv, flat(mixed), branch_in)
    keep = attend_outer(own, flat(x), dq, dk, dv, flat(mixed), branch_in)
    vectors = sums + jnp.pad(bias_sums, ((0, 8), (0, 0)))
    vectors = jnp.sum(lax.all_gather(vectors, ("dp", "seq"), axis=0), axis=0)
    tokens_grad = to_positions(split(input_grad(branch_in, dq, dk, dv, w_query, w_key, w_value)))
    down_sum, up_sum = dense_place(
        dense_plan, jnp.concatenate([dense_plan.codes(), own]), dense, width, wide
    )
    outer = attend_place(
        outer_plan,
        jnp.concatenate([outer_plan.codes(), own]),
        sum_halves(outer_plan, send, keep),
        width,
    )
    return (
        block_out,
        pooled,
        tokens_grad,
        outer[0],
        vectors[0],
        outer[1],
        outer[2],
        vectors[1],
        outer[3],
        vectors[2],
        vectors[3],
        vectors[4],
        up_sum,
        vectors[8 : 8 + wide].reshape(-1),
        down_sum,
        vectors[5],
        vectors[6],
        vectors[7],
    )


def solution(mesh):
    in_specs = (
        (P("dp", "seq", None), P("dp"))
        + (P(),) * 15
        + (P("dp", "seq", None), P("dp", None))
    )
    out_specs = (P("dp", "seq", None), P("dp", None), P("dp", "seq", None)) + (P(),) * 15
    return jax.shard_map(shards, mesh=mesh, in_specs=in_specs, out_specs=out_specs, check_vma=False)
```

```python
import functools

import jax
import jax.numpy as jnp
from jax import lax
from jax.experimental import pallas as pl
from jax.experimental.pallas import tpu as pltpu
from jax.sharding import PartitionSpec as P

HEADS = 12
HEAD_DIM = 64
PAIR = 2 * HEAD_DIM
PAIRS = HEADS // 2
SCALE = HEAD_DIM ** (-0.5)
ROWS = 256
KEY_STEP = 128
MIB = 1024 * 1024

eps = 1e-06
root_half = 0.7071067811865476
inv_root_two_pi = 0.3989422804014327

f32 = jnp.float32
bf16 = jnp.bfloat16

NN = (((1,), (0,)), ((), ()))
NT = (((1,), (1,)), ((), ()))
TN = (((0,), (0,)), ((), ()))


def mul(left, right, dims=NN):
    return lax.dot_general(left, right, dims, preferred_element_type=f32)


def fixed(shape):
    return pl.BlockSpec(shape, lambda *_: (0,) * len(shape), pipeline_mode=pl.Buffered(1))


def params(mib):
    return pltpu.CompilerParams(
        dimension_semantics=("arbitrary",), vmem_limit_bytes=mib * MIB
    )


def cost(flops, moved, exps=0):
    return pl.CostEstimate(flops=int(flops), bytes_accessed=int(moved), transcendentals=int(exps))


def over_extents(length, full, body):
    for extent in range(KEY_STEP, full + 1, KEY_STEP):
        pl.when((length > extent - KEY_STEP) & (length <= extent))(functools.partial(body, extent))


def attend_kernel(
    len_ref, x_ref, wq_ref, bq_ref, wk_ref, wv_ref, bv_ref, q_ref, k_ref, v_ref, mix_ref, stat_ref
):
    full = x_ref.shape[1]
    length = len_ref[pl.program_id(0)]
    q_ref[0] = (mul(x_ref[0], wq_ref[...]) + bq_ref[...]).astype(bf16)
    stat_ref[0] = jnp.zeros(stat_ref.shape[1:], f32)
    lane = lax.broadcasted_iota(jnp.int32, (1, PAIR), 1)

    def run(extent):
        x = x_ref[0, :extent]
        k_ref[0, :extent] = mul(x, wk_ref[...]).astype(bf16)
        v_ref[0, :extent] = (mul(x, wv_ref[...]) + bv_ref[...]).astype(bf16)
        key_at = lax.broadcasted_iota(jnp.int32, (1, extent), 1)
        dead = jnp.where(key_at < length, 0.0, -1e30)

        def pair_step(pair, carry):
            at = pl.ds(pl.multiple_of(pair * PAIR, PAIR), PAIR)
            q, k, v = q_ref[0, :, at], k_ref[0, :extent, at], v_ref[0, :extent, at]
            mixed = []
            stat = stat_ref[0]
            for half in range(2):
                own = (lane >= half * HEAD_DIM) & (lane < (half + 1) * HEAD_DIM)
                q_own = jnp.where(own, q * SCALE, 0).astype(bf16)
                scores = mul(q_own, k, NT) + dead
                top = jnp.max(scores, axis=1, keepdims=True)
                expo = jnp.exp(scores - top)
                total = jnp.sum(expo, axis=1, keepdims=True)
                probs = (expo * (1.0 / total)).astype(bf16)
                mixed.append(mul(probs, v))
                stat = jnp.where(lane == pair * 2 + half, top + jnp.log(total), stat)
            stat_ref[0] = stat
            mix_ref[0, :, at] = jnp.where(lane < HEAD_DIM, mixed[0], mixed[1]).astype(bf16)
            return carry

        lax.fori_loop(0, PAIRS, pair_step, 0)

    over_extents(length, full, run)


def attend(lengths, x, w_query, b_query, w_key, w_value, b_value):
    count, full, width = x.shape
    rows = pl.BlockSpec((1, full, width), lambda i, *_: (i, 0, 0))
    act = jax.ShapeDtypeStruct((count, full, width), bf16)
    return pl.pallas_call(
        attend_kernel,
        grid_spec=pltpu.PrefetchScalarGridSpec(
            num_scalar_prefetch=1,
            grid=(count,),
            in_specs=[
                rows,
                fixed((width, width)),
                fixed((1, width)),
                fixed((width, width)),
                fixed((width, width)),
                fixed((1, width)),
            ],
            out_specs=[rows] * 4 + [pl.BlockSpec((1, full, PAIR), lambda i, *_: (i, 0, 0))],
        ),
        out_shape=[act] * 4 + [jax.ShapeDtypeStruct((count, full, PAIR), f32)],
        compiler_params=params(48),
        cost_estimate=cost(
            2 * count * full * (3 * width * width + 4 * 2 * full * width),
            10 * count * full * width + 6 * width * width,
        ),
    )(lengths, x, w_query, b_query, w_key, w_value, b_value)


def attend_back_kernel(
    len_ref, q_ref, k_ref, v_ref, mg_ref, stat_ref, dq_ref, dk_ref, dv_ref, bias_ref, log_ref
):
    full = q_ref.shape[1]
    length = len_ref[pl.program_id(0)]
    lane = lax.broadcasted_iota(jnp.int32, (1, PAIR), 1)
    log_ref[...] = stat_ref[0].T
    row = lax.broadcasted_iota(jnp.int32, (8, 1), 0)

    @pl.when(pl.program_id(0) == 0)
    def _():
        bias_ref[...] = jnp.zeros(bias_ref.shape, f32)

    def run(extent):
        key_at = lax.broadcasted_iota(jnp.int32, (extent, 1), 0)
        dead = jnp.where(key_at < length, 0.0, -1e30)
        if extent < full:
            dk_ref[0, extent:] = jnp.zeros((full - extent, dk_ref.shape[2]), bf16)
            dv_ref[0, extent:] = jnp.zeros((full - extent, dv_ref.shape[2]), bf16)

        def pair_step(pair, carry):
            at = pl.ds(pl.multiple_of(pair * PAIR, PAIR), PAIR)
            q, mg = q_ref[0, :, at], mg_ref[0, :, at]
            k, v = k_ref[0, :extent, at], v_ref[0, :extent, at]
            dq, dk, dv = [], [], []
            for half in range(2):
                own = (lane >= half * HEAD_DIM) & (lane < (half + 1) * HEAD_DIM)
                k_own = jnp.where(own, k * SCALE, 0).astype(bf16)
                v_own = jnp.where(own, v, 0).astype(bf16)
                log_row = log_ref[pl.ds(pair * 2 + half, 1), :]
                probs = jnp.exp(mul(k_own, q, NT) + dead - log_row)
                prob_grad = mul(v_own, mg, NT)
                along = jnp.sum(probs * prob_grad, axis=0, keepdims=True)
                score_grad = (probs * (prob_grad - along)).astype(bf16)
                dv.append(mul(probs.astype(bf16), mg))
                dk.append(mul(score_grad, q))
                dq.append(mul(score_grad, k, TN))
            first = lane < HEAD_DIM
            dq_pair = jnp.where(first, dq[0], dq[1]) * SCALE
            dk_pair = jnp.where(first, dk[0], dk[1]) * SCALE
            dv_pair = jnp.where(first, dv[0], dv[1])
            dq_ref[0, :, at] = dq_pair.astype(bf16)
            dk_ref[0, :extent, at] = dk_pair.astype(bf16)
            dv_ref[0, :extent, at] = dv_pair.astype(bf16)
            sums = jnp.where(
                row == 0,
                jnp.sum(dq_pair, axis=0, keepdims=True),
                jnp.where(row == 1, jnp.sum(dv_pair, axis=0, keepdims=True), 0.0),
            )
            bias_ref[:, at] += sums
            return carry

        lax.fori_loop(0, PAIRS, pair_step, 0)

    over_extents(length, full, run)


def attend_back(lengths, q, k, v, mixed_grad, stat):
    count, full, width = q.shape
    rows = pl.BlockSpec((1, full, width), lambda i, *_: (i, 0, 0))
    act = jax.ShapeDtypeStruct((count, full, width), bf16)
    return pl.pallas_call(
        attend_back_kernel,
        grid_spec=pltpu.PrefetchScalarGridSpec(
            num_scalar_prefetch=1,
            grid=(count,),
            in_specs=[rows] * 4 + [pl.BlockSpec((1, full, PAIR), lambda i, *_: (i, 0, 0))],
            out_specs=[rows] * 3 + [pl.BlockSpec((8, width), lambda i, *_: (0, 0))],
            scratch_shapes=[pltpu.VMEM((PAIR, full), f32)],
        ),
        out_shape=[act] * 3 + [jax.ShapeDtypeStruct((8, width), f32)],
        compiler_params=params(48),
        cost_estimate=cost(
            2 * count * full * 10 * 2 * full * width, 14 * count * full * width
        ),
    )(lengths, q, k, v, mixed_grad, stat)


def norm_parts(hidden):
    centred = hidden - jnp.mean(hidden, axis=1, keepdims=True)
    inv_scale = lax.rsqrt(jnp.mean(centred * centred, axis=1, keepdims=True) + eps)
    return centred * inv_scale, inv_scale


def norm_back(scaled, normed, inv_scale):
    mean = jnp.mean(scaled, axis=1, keepdims=True)
    along = jnp.mean(scaled * normed, axis=1, keepdims=True)
    return (scaled - mean - normed * along) * inv_scale


def gelu_parts(u):
    expo = jnp.exp(u * u * -0.5)
    base = 1.0 + jnp.abs(u) * (0.3275911 * root_half)
    t = pl.reciprocal(base, approx=True)
    t = t * (2.0 - base * t)
    poly = t * (
        0.5 * 0.254829592
        + t
        * (
            0.5 * -0.284496736
            + t * (0.5 * 1.421413741 + t * (0.5 * -1.453152027 + t * (0.5 * 1.061405429)))
        )
    )
    tail = poly * expo
    return jnp.where(u >= 0, 1.0 - tail, tail), expo


def rows_kernel(
    blocks,
    len_ref,
    x_ref,
    mix_ref,
    cot_ref,
    pool_ref,
    wo_ref,
    wu_ref,
    wd_ref,
    vec_ref,
    bu_ref,
    out_ref,
    pooled_ref,
    low_ref,
    act_ref,
    second_ref,
    inner_ref,
    branch_ref,
    mg_ref,
    sum_ref,
    slope_ref,
):
    step = pl.program_id(0)
    rows, width = x_ref.shape
    wide = bu_ref.shape[0]
    b_out, gain_one, shift_one, b_down, gain_two, shift_two = (vec_ref[i : i + 1] for i in range(6))
    length = len_ref[step // blocks]
    row_at = lax.broadcasted_iota(jnp.int32, (rows, 1), 0) + (step % blocks) * rows
    live = jnp.where(row_at < length, 1.0, 0.0)

    @pl.when(step == 0)
    def _():
        sum_ref[...] = jnp.zeros(sum_ref.shape, f32)

    @pl.when(step % blocks == 0)
    def _():
        pooled_ref[...] = jnp.zeros(pooled_ref.shape, f32)

    def tally(at, value):
        sum_ref[at : at + 1] += jnp.sum(value, axis=0, keepdims=True)

    part = [slice(i * width, (i + 1) * width) for i in range(wide)]
    hidden = x_ref[...].astype(f32) + mul(mix_ref[...], wo_ref[...]) + b_out
    normed_one, scale_one = norm_parts(hidden)
    first = normed_one * gain_one + shift_one
    first_low = first.astype(bf16)
    low_ref[...] = first_low
    hidden = first + b_down
    for i in range(wide):
        pre = mul(first_low, wu_ref[:, part[i]]) + bu_ref[i : i + 1]
        phi, expo = gelu_parts(pre)
        act = (pre * phi).astype(bf16)
        act_ref[:, part[i]] = act
        slope_ref[:, part[i]] = phi + pre * expo * inv_root_two_pi
        hidden += mul(act, wd_ref[part[i], :])
    normed_two, scale_two = norm_parts(hidden)
    result = normed_two * gain_two + shift_two
    out_ref[...] = result.astype(bf16)
    pooled_ref[0] += jnp.sum(result * live, axis=0, keepdims=True)
    upstream = cot_ref[...].astype(f32) + live * pool_ref[0]
    tally(6, upstream * normed_two)
    tally(7, upstream)
    second_in = norm_back(upstream * gain_two, normed_two, scale_two)
    tally(5, second_in)
    second = second_in.astype(bf16)
    second_ref[...] = second
    first_up = second_in
    for i in range(wide):
        inner = mul(second, wd_ref[part[i], :], NT) * slope_ref[:, part[i]]
        tally(8 + i, inner)
        inner = inner.astype(bf16)
        inner_ref[:, part[i]] = inner
        first_up += mul(inner, wu_ref[:, part[i]], NT)
    tally(3, first_up * normed_one)
    tally(4, first_up)
    branch_in = norm_back(first_up * gain_one, normed_one, scale_one)
    tally(2, branch_in)
    branch_ref[...] = branch_in
    mg_ref[...] = mul(branch_in.astype(bf16), wo_ref[...], NT).astype(bf16)


def row_work(lengths, x, mixed, cot, pool, w_out, w_up, w_down, vecs, b_up):
    total, width = x.shape
    count = lengths.shape[0]
    full = total // count
    hidden = w_up.shape[1]
    wide = hidden // width
    blocks = full // ROWS
    narrow = pl.BlockSpec((ROWS, width), lambda i, *_: (i, 0))
    broad = pl.BlockSpec((ROWS, hidden), lambda i, *_: (i, 0))
    single = pl.BlockSpec((1, 1, width), lambda i, *_: (i // blocks, 0, 0))
    thin = jax.ShapeDtypeStruct((total, width), bf16)
    thick = jax.ShapeDtypeStruct((total, hidden), bf16)
    return pl.pallas_call(
        functools.partial(rows_kernel, blocks),
        grid_spec=pltpu.PrefetchScalarGridSpec(
            num_scalar_prefetch=1,
            grid=(total // ROWS,),
            in_specs=[
                narrow,
                narrow,
                narrow,
                single,
                fixed((width, width)),
                fixed((width, hidden)),
                fixed((hidden, width)),
                fixed(vecs.shape),
                fixed((wide, width)),
            ],
            out_specs=[
                narrow,
                single,
                narrow,
                broad,
                narrow,
                broad,
                narrow,
                narrow,
                pl.BlockSpec((16, width), lambda i, *_: (0, 0)),
            ],
            scratch_shapes=[pltpu.VMEM((ROWS, hidden), f32)],
        ),
        out_shape=[
            thin,
            jax.ShapeDtypeStruct((count, 1, width), f32),
            thin,
            thick,
            thin,
            thick,
            jax.ShapeDtypeStruct((total, width), f32),
            thin,
            jax.ShapeDtypeStruct((16, width), f32),
        ],
        compiler_params=params(56),
        cost_estimate=cost(
            4 * total * width * (width + 2 * hidden),
            2 * total * (8 * width + 2 * hidden) + 2 * width * (width + 2 * hidden),
        ),
    )(lengths, x, mixed, cot, pool, w_out, w_up, w_down, vecs, b_up)


def dense_outer_kernel(side_ref, act_ref, second_ref, low_ref, inner_ref, out_ref):
    step = pl.program_id(0)
    half = pl.num_programs(0) // 2

    @pl.when(step < half)
    def _():
        out_ref[0] = mul(act_ref[...], second_ref[...], TN).astype(bf16)

    @pl.when(step >= half)
    def _():
        out_ref[0] = mul(low_ref[...], inner_ref[...], TN).astype(bf16)


def dense_outer(side, act, second, low, inner):
    total, width = second.shape
    wide = act.shape[1] // width
    half = wide // 2
    return pl.pallas_call(
        dense_outer_kernel,
        grid_spec=pltpu.PrefetchScalarGridSpec(
            num_scalar_prefetch=1,
            grid=(wide,),
            in_specs=[
                pl.BlockSpec(
                    (total, width), lambda i, s: (0, s[0] * half + jnp.minimum(i, half - 1))
                ),
                fixed((total, width)),
                fixed((total, width)),
                pl.BlockSpec(
                    (total, width), lambda i, s: (0, s[0] * half + jnp.maximum(i - half, 0))
                ),
            ],
            out_specs=pl.BlockSpec((1, width, width), lambda i, s: (i, 0, 0)),
        ),
        out_shape=jax.ShapeDtypeStruct((wide, width, width), bf16),
        compiler_params=params(48),
        cost_estimate=cost(
            2 * total * width * width * wide, 2 * (wide + 2) * total * width + 2 * wide * width * width
        ),
    )(side, act, second, low, inner).reshape(wide * width, width)


def attend_outer_kernel(side_ref, x_ref, dq_ref, dk_ref, dv_ref, mix_ref, branch_ref, out_ref):
    block = side_ref[0] * 2 + pl.program_id(0)
    for at, grad_ref in enumerate((dq_ref, dk_ref, dv_ref)):

        @pl.when(block == at)
        def _(grad_ref=grad_ref):
            out_ref[0] = mul(x_ref[...], grad_ref[...], TN).astype(bf16)

    @pl.when(block == 3)
    def _():
        out_ref[0] = mul(mix_ref[...], branch_ref[...].astype(bf16), TN).astype(bf16)


def attend_outer(side, x, dq, dk, dv, mixed, branch_in):
    total, width = x.shape
    whole = fixed((total, width))
    return pl.pallas_call(
        attend_outer_kernel,
        grid_spec=pltpu.PrefetchScalarGridSpec(
            num_scalar_prefetch=1,
            grid=(2,),
            in_specs=[whole] * 6,
            out_specs=pl.BlockSpec((1, width, width), lambda i, s: (i, 0, 0)),
        ),
        out_shape=jax.ShapeDtypeStruct((2, width, width), bf16),
        compiler_params=params(48),
        cost_estimate=cost(4 * total * width * width, 14 * total * width + 4 * width * width),
    )(side, x, dq, dk, dv, mixed, branch_in).reshape(2 * width, width)


def input_kernel(branch_ref, dq_ref, dk_ref, dv_ref, wq_ref, wk_ref, wv_ref, out_ref):
    total = branch_ref[...] + mul(dq_ref[...], wq_ref[...], NT)
    total += mul(dk_ref[...], wk_ref[...], NT)
    total += mul(dv_ref[...], wv_ref[...], NT)
    out_ref[...] = total.astype(bf16)


def input_grad(branch_in, dq, dk, dv, w_query, w_key, w_value):
    total, width = branch_in.shape
    rows = pl.BlockSpec((ROWS, width), lambda i: (i, 0))
    return pl.pallas_call(
        input_kernel,
        grid=(total // ROWS,),
        in_specs=[rows] * 4 + [fixed((width, width))] * 3,
        out_specs=rows,
        out_shape=jax.ShapeDtypeStruct((total, width), bf16),
        compiler_params=params(48),
        cost_estimate=cost(6 * total * width * width, 12 * total * width + 6 * width * width),
    )(branch_in, dq, dk, dv, w_query, w_key, w_value)


def exchange(value, axis, mask):
    count = lax.axis_size(axis)
    return lax.ppermute(value, axis, [(i, i ^ mask) for i in range(count)])


def to_passages(value):
    count = lax.axis_size("seq")
    mine = lax.axis_index("seq")
    held, piece, width = value.shape
    own = held // count
    whole = jnp.zeros((own, piece * count, width), value.dtype)
    for mask in range(count):
        peer = mine ^ mask
        part = lax.dynamic_slice_in_dim(value, peer * own, own, 0)
        if mask:
            part = exchange(part, "seq", mask)
        whole = lax.dynamic_update_slice_in_dim(whole, part, peer * piece, 1)
    return whole


def position_pieces(value):
    count = lax.axis_size("seq")
    piece = value.shape[1] // count
    mine = lax.axis_index("seq")
    return [
        lax.dynamic_slice_in_dim(value, (mine ^ mask) * piece, piece, 1) for mask in range(count)
    ]


def to_positions(pieces):
    mine = lax.axis_index("seq")
    own, piece, width = pieces[0].shape
    result = jnp.zeros((own * len(pieces), piece, width), pieces[0].dtype)
    for mask, part in enumerate(pieces):
        if mask:
            part = exchange(part, "seq", mask)
        result = lax.dynamic_update_slice_in_dim(result, part, (mine ^ mask) * own, 0)
    return result


def axis_bits(axis):
    return [(axis, 1 << i) for i in range(lax.axis_size(axis).bit_length() - 1)]


def upper(dim):
    axis, mask = dim
    return (lax.axis_index(axis) & mask) // mask


def swap(value, dim):
    return exchange(value, dim[0], dim[1])


def total_of(parts):
    total = parts[0].astype(f32)
    for part in parts[1:]:
        total += part.astype(f32)
    return total.astype(bf16)


PARTS = 3
SHARD_STEP = 16


class Plan:
    def __init__(self, rows):
        dims = axis_bits("seq") + axis_bits("dp")
        self.first = dims[0]
        rest = dims[1:]
        self.rows = rows // PARTS
        halved = 0
        while halved < len(rest) and (self.rows >> (halved + 1)) % SHARD_STEP == 0:
            halved += 1
        self.last = rest[halved - 1]
        self.plain = rest[halved:]
        split = rest[: halved - 1]
        self.orders = [split[i % len(split) :] + split[: i % len(split)] for i in range(PARTS)]
        self.shards = 1 << halved
        self.shard = self.rows >> halved

    def codes(self):
        found = []
        for order in self.orders:
            code = upper(self.last)
            for at, dim in enumerate(reversed(order)):
                code += upper(dim) << (at + 1)
            found.append(code)
        return jnp.stack(found).astype(jnp.int32)


class Chain:
    def __init__(self):
        self.token = None

    def tie(self, values):
        if self.token is None:
            return values
        return lax.optimization_barrier((values, self.token))[0]

    def mark(self, values):
        self.token = values
        return values


def sum_steps(plan, chain, keep, got, found):
    pairs = [[keep, got]] * PARTS
    bases = [i * plan.rows for i in range(PARTS)]
    size = plan.rows
    for step in range(len(plan.orders[0])):
        pairs = chain.tie(pairs)
        size //= 2
        dims = [order[step] for order in plan.orders]

        def halves(pair, base, at):
            return total_of([lax.dynamic_slice_in_dim(p, base + at * size, size, 0) for p in pair])

        sends = [halves(p, base, 1 - upper(d)) for p, base, d in zip(pairs, bases, dims)]
        chain.mark(sends)
        mine = [halves(p, base, upper(d)) for p, base, d in zip(pairs, bases, dims)]
        pairs = [[m, swap(s, d)] for m, s, d in zip(mine, sends, dims)]
        bases = [0] * PARTS
        yield
    size = plan.shard
    bit = upper(plan.last)
    pairs = chain.tie(pairs)

    def side(at):
        return jnp.concatenate(
            [total_of([lax.dynamic_slice_in_dim(p, at * size, size, 0) for p in pair]) for pair in pairs],
            axis=0,
        )

    send = chain.mark(side(1 - bit))
    shard = side(bit)
    got = swap(send, plan.last)
    yield
    shard, got = chain.tie((shard, got))
    shard = total_of([shard, got])
    for dim in plan.plain:
        shard = total_of([shard, swap(shard, dim)])
    chain.mark(shard)
    got = swap(shard, plan.last)
    yield
    values = [(shard[i * size : (i + 1) * size], got[i * size : (i + 1) * size]) for i in range(PARTS)]
    for step in reversed(range(len(plan.orders[0]))):
        values = chain.tie(values)
        values = [jnp.concatenate(pair, axis=0) for pair in values]
        chain.mark(values)
        values = [(v, swap(v, order[step])) for v, order in zip(values, plan.orders)]
        yield
    values = chain.tie(values)
    found += [v for pair in values for v in pair]
    found += [swap(v, plan.first) for v in found]
    chain.mark(values)
    yield


def place(plan, refs, code_ref, row, store):
    part = row // plan.rows
    shard = ((row % plan.rows) // plan.shard) ^ code_ref[part]
    half = plan.shards // 2
    at = pl.ds(pl.multiple_of((shard & (half - 1)) * plan.shard, plan.shard), plan.shard)
    low, high = refs[2 * part][at, :], refs[2 * part + 1][at, :]
    store(jnp.where(shard >= half, high.astype(f32), low.astype(f32)))


def dense_place_kernel(plan, half, code_ref, *refs):
    sources, (down_ref, up_ref) = refs[: 4 * PARTS], refs[4 * PARTS :]
    width = down_ref.shape[1]
    for step in range(4 * half):

        @pl.when(pl.program_id(0) == step)
        def _(step=step):
            side, block = step // (2 * half), step % (2 * half)
            own = sources[2 * PARTS * side : 2 * PARTS * (side + 1)]
            out_ref = down_ref if block < half else up_ref
            for row in range(0, width, plan.shard):

                def store(value, row=row):
                    out_ref[row : row + plan.shard, :] = value

                place(plan, own, code_ref, block * width + row, store)


def dense_place(plan, info, sources, width, wide):
    half = wide // 2

    def spot(i, info, shift):
        step = jnp.clip(i - shift, 0, 4 * half - 1)
        turn = step // (2 * half)
        side = jnp.where(turn == 0, info[PARTS], 1 - info[PARTS])
        return side * half + jnp.minimum(step % (2 * half), half - 1)

    return pl.pallas_call(
        functools.partial(dense_place_kernel, plan, half),
        grid_spec=pltpu.PrefetchScalarGridSpec(
            num_scalar_prefetch=1,
            grid=(4 * half,),
            in_specs=[fixed(x.shape) for x in sources],
            out_specs=[
                pl.BlockSpec((width, width), lambda i, s: (spot(i, s, 0), 0)),
                pl.BlockSpec((width, width), lambda i, s: (0, spot(i, s, half))),
            ],
        ),
        out_shape=[
            jax.ShapeDtypeStruct((wide * width, width), f32),
            jax.ShapeDtypeStruct((width, wide * width), f32),
        ],
        compiler_params=params(48),
        cost_estimate=cost(0, 12 * wide * width * width),
    )(info, *sources)


def attend_place_kernel(plan, code_ref, *refs):
    sources, outs = refs[: 4 * PARTS], refs[4 * PARTS :]
    width = outs[0].shape[1]
    for step in range(4):

        @pl.when(pl.program_id(0) == step)
        def _(step=step):
            turn, block = step // 2, step % 2
            own = sources[2 * PARTS * turn : 2 * PARTS * (turn + 1)]
            for row in range(0, width, plan.shard):

                def store(value, row=row):
                    for side in range(2):

                        @pl.when(code_ref[PARTS] == (side if turn == 0 else 1 - side))
                        def _():
                            outs[2 * side + block][row : row + plan.shard, :] = value

                place(plan, own, code_ref, block * width + row, store)


def attend_place(plan, info, sources, width):
    return pl.pallas_call(
        functools.partial(attend_place_kernel, plan),
        grid_spec=pltpu.PrefetchScalarGridSpec(
            num_scalar_prefetch=1,
            grid=(4,),
            in_specs=[fixed(x.shape) for x in sources],
            out_specs=[pl.BlockSpec((width, width), lambda i, s: (0, 0))] * 4,
        ),
        out_shape=[jax.ShapeDtypeStruct((width, width), f32)] * 4,
        compiler_params=params(48),
        cost_estimate=cost(0, 24 * width * width),
    )(info, *sources)


def shards(
    tokens,
    lengths,
    w_query,
    b_query,
    w_key,
    w_value,
    b_value,
    w_out,
    b_out,
    gain_one,
    shift_one,
    w_up,
    b_up,
    w_down,
    b_down,
    gain_two,
    shift_two,
    out_grad,
    pooled_grad,
):
    seq_count = lax.axis_size("seq")
    held, piece, width = tokens.shape
    full = piece * seq_count
    count = held // seq_count
    mine = lax.axis_index("seq")
    wide = w_up.shape[1] // width
    total = count * full

    def flat(value):
        return value.reshape(total, width)

    def split(value):
        return value.reshape(count, full, width)

    x = to_passages(tokens)
    cot = to_passages(lax.optimization_barrier((out_grad, x))[0])
    local_len = lax.dynamic_slice_in_dim(lengths, mine * count, count, 0)
    len_float = local_len.astype(f32)[:, None, None]
    pool = lax.dynamic_slice_in_dim(pooled_grad, mine * count, count, 0)[:, None, :] / len_float

    q, k, v, mixed, stat = attend(
        local_len, x, w_query, b_query.astype(f32)[None], w_key, w_value, b_value.astype(f32)[None]
    )
    vecs = jnp.stack([b_out, gain_one, shift_one, b_down, gain_two, shift_two]).astype(f32)
    vecs = jnp.pad(vecs, ((0, 2), (0, 0)))
    result, pooled_sum, first_low, act, second, inner, branch_in, mixed_grad, sums = row_work(
        local_len,
        flat(x),
        flat(mixed),
        flat(cot),
        pool,
        w_out,
        w_up,
        w_down,
        vecs,
        b_up.astype(f32).reshape(wide, width),
    )
    first = axis_bits("seq")[0]
    own = upper(first).astype(jnp.int32)[None]
    dense_plan = Plan(wide * width)
    outer_plan = Plan(2 * width)
    chain = Chain()
    pooled_mine = pooled_sum[:, 0] / len_float[:, 0]
    pooled = lax.all_gather(pooled_mine, "seq", axis=0, tiled=True)

    pieces = chain.mark(position_pieces(split(result)))
    block_out = to_positions(pieces)
    send = dense_outer(1 - own, *chain.tie((act, second, first_low, inner)))
    chain.mark(send)
    got = swap(send, first)
    keep = chain.mark(dense_outer(own, *chain.tie((act, second, first_low, inner))))
    dense, outer = [], []
    dense_steps = sum_steps(dense_plan, chain, keep, got, dense)
    next(dense_steps)
    dq, dk, dv, bias_sums = attend_back(local_len, q, k, v, chain.tie(split(mixed_grad)), stat)
    chain.mark(bias_sums)
    dq, dk, dv = flat(dq), flat(dk), flat(dv)
    vectors = sums + jnp.pad(bias_sums, ((0, 8), (0, 0)))
    vectors = lax.all_gather(vectors, ("dp", "seq"), axis=0, tiled=True)
    vectors = jnp.sum(vectors.reshape(-1, *sums.shape), axis=0)
    next(dense_steps)
    send = attend_outer(1 - own, flat(x), *chain.tie((dq, dk, dv)), flat(mixed), branch_in)
    chain.mark(send)
    got = swap(send, first)
    keep = attend_outer(own, flat(x), *chain.tie((dq, dk, dv)), flat(mixed), branch_in)
    chain.mark(keep)
    next(dense_steps)
    outer_steps = sum_steps(outer_plan, chain, keep, got, outer)
    next(outer_steps)
    input_low = input_grad(branch_in, *chain.tie((dq, dk, dv)), w_query, w_key, w_value)
    chain.mark(input_low)
    next(dense_steps)
    next(outer_steps)
    pieces = chain.mark(position_pieces(split(chain.tie(input_low))))
    tokens_grad = to_positions(pieces)
    running = [outer_steps, dense_steps]
    while running:
        for steps in list(running):
            if next(steps, chain) is chain:
                running.remove(steps)
    down_sum, up_sum = dense_place(
        dense_plan, jnp.concatenate([dense_plan.codes(), own]), dense, width, wide
    )
    outer = attend_place(outer_plan, jnp.concatenate([outer_plan.codes(), own]), outer, width)
    return (
        block_out,
        pooled,
        tokens_grad,
        outer[0],
        vectors[0],
        outer[1],
        outer[2],
        vectors[1],
        outer[3],
        vectors[2],
        vectors[3],
        vectors[4],
        up_sum,
        vectors[8 : 8 + wide].reshape(-1),
        down_sum,
        vectors[5],
        vectors[6],
        vectors[7],
    )


def solution(mesh):
    in_specs = (
        (P("dp", "seq", None), P("dp"))
        + (P(),) * 15
        + (P("dp", "seq", None), P("dp", None))
    )
    out_specs = (P("dp", "seq", None), P("dp", None), P("dp", "seq", None)) + (P(),) * 15
    return jax.shard_map(shards, mesh=mesh, in_specs=in_specs, out_specs=out_specs, check_vma=False)
```

```python
import functools

import jax
import jax.numpy as jnp
from jax import lax
from jax.experimental import pallas as pl
from jax.experimental.pallas import tpu as pltpu
from jax.sharding import PartitionSpec as P

HEADS = 12
HEAD_DIM = 64
PAIR = 2 * HEAD_DIM
PAIRS = HEADS // 2
SCALE = HEAD_DIM ** (-0.5)
ROWS = 256
KEY_STEP = 128
MIB = 1024 * 1024

eps = 1e-06
root_half = 0.7071067811865476
inv_root_two_pi = 0.3989422804014327

f32 = jnp.float32
bf16 = jnp.bfloat16

NN = (((1,), (0,)), ((), ()))
NT = (((1,), (1,)), ((), ()))
TN = (((0,), (0,)), ((), ()))


def mul(left, right, dims=NN):
    return lax.dot_general(left, right, dims, preferred_element_type=f32)


def fixed(shape):
    return pl.BlockSpec(shape, lambda *_: (0,) * len(shape), pipeline_mode=pl.Buffered(1))


def params(mib):
    return pltpu.CompilerParams(
        dimension_semantics=("arbitrary",), vmem_limit_bytes=mib * MIB
    )


def cost(flops, moved, exps=0):
    return pl.CostEstimate(flops=int(flops), bytes_accessed=int(moved), transcendentals=int(exps))


def over_extents(length, full, body):
    for extent in range(KEY_STEP, full + 1, KEY_STEP):
        pl.when((length > extent - KEY_STEP) & (length <= extent))(functools.partial(body, extent))


def attend_kernel(pieces, info_ref, *refs):
    part_refs, refs = refs[:pieces], refs[pieces:]
    wq_ref, bq_ref, wk_ref, wv_ref, bv_ref = refs[:5]
    xm_ref, q_ref, k_ref, v_ref, stat_ref = refs[-5:]
    x_ref, mix_ref = xm_ref.at[0], xm_ref.at[1]
    length, mine = info_ref[0], info_ref[1]
    size = part_refs[0].shape[1]
    for mask, part_ref in enumerate(part_refs):
        x_ref[0, pl.ds(pl.multiple_of((mine ^ mask) * size, size), size)] = part_ref[0]
    q_ref[0] = (mul(x_ref[0], wq_ref[...]) + bq_ref[...]).astype(bf16)
    stat_ref[0] = jnp.zeros(stat_ref.shape[1:], f32)
    lane = lax.broadcasted_iota(jnp.int32, (1, PAIR), 1)
    full = size * pieces

    def run(extent):
        x = x_ref[0, :extent]
        k_ref[0, :extent] = mul(x, wk_ref[...]).astype(bf16)
        v_ref[0, :extent] = (mul(x, wv_ref[...]) + bv_ref[...]).astype(bf16)
        key_at = lax.broadcasted_iota(jnp.int32, (1, extent), 1)
        dead = jnp.where(key_at < length, 0.0, -1e30)

        def pair_step(pair, carry):
            at = pl.ds(pl.multiple_of(pair * PAIR, PAIR), PAIR)
            q, k, v = q_ref[0, :, at], k_ref[0, :extent, at], v_ref[0, :extent, at]
            mixed = []
            stat = stat_ref[0]
            for half in range(2):
                own = (lane >= half * HEAD_DIM) & (lane < (half + 1) * HEAD_DIM)
                q_own = jnp.where(own, q * SCALE, 0).astype(bf16)
                scores = mul(q_own, k, NT) + dead
                top = jnp.max(scores, axis=1, keepdims=True)
                expo = jnp.exp(scores - top)
                total = jnp.sum(expo, axis=1, keepdims=True)
                probs = (expo * (1.0 / total)).astype(bf16)
                mixed.append(mul(probs, v))
                stat = jnp.where(lane == pair * 2 + half, top + jnp.log(total), stat)
            stat_ref[0] = stat
            mix_ref[0, :, at] = jnp.where(lane < HEAD_DIM, mixed[0], mixed[1]).astype(bf16)
            return carry

        lax.fori_loop(0, PAIRS, pair_step, 0)

    over_extents(length, full, run)


def attend(passage, count, length, mine, tokens, parts, weights, before):
    piece, width = tokens.shape[1:]
    pieces = len(parts) + 1
    full = piece * pieces
    rows = pl.BlockSpec((1, full, width), lambda i, s: (passage, 0, 0))
    act = jax.ShapeDtypeStruct((count, full, width), bf16)
    got = pl.BlockSpec((1, piece, width), lambda i, s: (0, 0, 0))
    kept = [] if before is None else list(before)
    first_kept = 1 + pieces + len(weights)
    return pl.pallas_call(
        functools.partial(attend_kernel, pieces),
        grid_spec=pltpu.PrefetchScalarGridSpec(
            num_scalar_prefetch=1,
            grid=(1,),
            in_specs=[pl.BlockSpec((1, piece, width), lambda i, s: (s[1] * count + passage, 0, 0))]
            + [got] * len(parts)
            + [fixed(w.shape) for w in weights]
            + [pl.BlockSpec(memory_space=pl.ANY)] * len(kept),
            out_specs=[pl.BlockSpec((2, 1, full, width), lambda i, s: (0, passage, 0, 0))]
            + [rows] * 3
            + [pl.BlockSpec((1, full, PAIR), lambda i, s: (passage, 0, 0))],
        ),
        out_shape=[jax.ShapeDtypeStruct((2, count, full, width), bf16)]
        + [act] * 3
        + [jax.ShapeDtypeStruct((count, full, PAIR), f32)],
        input_output_aliases={first_kept + i: i for i in range(len(kept))},
        compiler_params=params(40),
        cost_estimate=cost(
            2 * full * (3 * width * width + 4 * 2 * full * width),
            12 * full * width + 6 * width * width,
        ),
    )(jnp.stack([length, mine]), tokens, *parts, *weights, *kept)


def attend_back_kernel(
    len_ref, q_ref, k_ref, v_ref, mg_ref, branch_ref, stat_ref, grads_ref, bias_ref, log_ref
):
    dq_ref, dk_ref, dv_ref = (grads_ref.at[i] for i in range(3))
    grads_ref[3] = branch_ref[...].astype(bf16)
    full = q_ref.shape[1]
    length = len_ref[pl.program_id(0)]
    lane = lax.broadcasted_iota(jnp.int32, (1, PAIR), 1)
    log_ref[...] = stat_ref[0].T
    row = lax.broadcasted_iota(jnp.int32, (8, 1), 0)

    @pl.when(pl.program_id(0) == 0)
    def _():
        bias_ref[...] = jnp.zeros(bias_ref.shape, f32)

    def run(extent):
        key_at = lax.broadcasted_iota(jnp.int32, (extent, 1), 0)
        dead = jnp.where(key_at < length, 0.0, -1e30)
        if extent < full:
            dk_ref[0, extent:] = jnp.zeros((full - extent, dk_ref.shape[2]), bf16)
            dv_ref[0, extent:] = jnp.zeros((full - extent, dv_ref.shape[2]), bf16)

        def pair_step(pair, carry):
            at = pl.ds(pl.multiple_of(pair * PAIR, PAIR), PAIR)
            q, mg = q_ref[0, :, at], mg_ref[0, :, at]
            k, v = k_ref[0, :extent, at], v_ref[0, :extent, at]
            dq, dk, dv = [], [], []
            for half in range(2):
                own = (lane >= half * HEAD_DIM) & (lane < (half + 1) * HEAD_DIM)
                k_own = jnp.where(own, k * SCALE, 0).astype(bf16)
                v_own = jnp.where(own, v, 0).astype(bf16)
                log_row = log_ref[pl.ds(pair * 2 + half, 1), :]
                probs = jnp.exp(mul(k_own, q, NT) + dead - log_row)
                prob_grad = mul(v_own, mg, NT)
                along = jnp.sum(probs * prob_grad, axis=0, keepdims=True)
                score_grad = (probs * (prob_grad - along)).astype(bf16)
                dv.append(mul(probs.astype(bf16), mg))
                dk.append(mul(score_grad, q))
                dq.append(mul(score_grad, k, TN))
            first = lane < HEAD_DIM
            dq_pair = jnp.where(first, dq[0], dq[1]) * SCALE
            dk_pair = jnp.where(first, dk[0], dk[1]) * SCALE
            dv_pair = jnp.where(first, dv[0], dv[1])
            dq_ref[0, :, at] = dq_pair.astype(bf16)
            dk_ref[0, :extent, at] = dk_pair.astype(bf16)
            dv_ref[0, :extent, at] = dv_pair.astype(bf16)
            sums = jnp.where(
                row == 0,
                jnp.sum(dq_pair, axis=0, keepdims=True),
                jnp.where(row == 1, jnp.sum(dv_pair, axis=0, keepdims=True), 0.0),
            )
            bias_ref[:, at] += sums
            return carry

        lax.fori_loop(0, PAIRS, pair_step, 0)

    over_extents(length, full, run)


def attend_back(lengths, q, k, v, mixed_grad, branch_in, stat):
    count, full, width = q.shape
    rows = pl.BlockSpec((1, full, width), lambda i, *_: (i, 0, 0))
    return pl.pallas_call(
        attend_back_kernel,
        grid_spec=pltpu.PrefetchScalarGridSpec(
            num_scalar_prefetch=1,
            grid=(count,),
            in_specs=[rows] * 5 + [pl.BlockSpec((1, full, PAIR), lambda i, *_: (i, 0, 0))],
            out_specs=[
                pl.BlockSpec((4, 1, full, width), lambda i, *_: (0, i, 0, 0)),
                pl.BlockSpec((8, width), lambda i, *_: (0, 0)),
            ],
            scratch_shapes=[pltpu.VMEM((PAIR, full), f32)],
        ),
        out_shape=[
            jax.ShapeDtypeStruct((4, count, full, width), bf16),
            jax.ShapeDtypeStruct((8, width), f32),
        ],
        compiler_params=params(48),
        cost_estimate=cost(
            2 * count * full * 10 * 2 * full * width, 14 * count * full * width
        ),
    )(lengths, q, k, v, mixed_grad, branch_in, stat)


def norm_parts(hidden):
    centred = hidden - jnp.mean(hidden, axis=1, keepdims=True)
    inv_scale = lax.rsqrt(jnp.mean(centred * centred, axis=1, keepdims=True) + eps)
    return centred * inv_scale, inv_scale


def norm_back(scaled, normed, inv_scale):
    mean = jnp.mean(scaled, axis=1, keepdims=True)
    along = jnp.mean(scaled * normed, axis=1, keepdims=True)
    return (scaled - mean - normed * along) * inv_scale


def gelu_parts(u):
    expo = jnp.exp(u * u * -0.5)
    base = 1.0 + jnp.abs(u) * (0.3275911 * root_half)
    t = pl.reciprocal(base, approx=True)
    t = t * (2.0 - base * t)
    poly = t * (
        0.5 * 0.254829592
        + t
        * (
            0.5 * -0.284496736
            + t * (0.5 * 1.421413741 + t * (0.5 * -1.453152027 + t * (0.5 * 1.061405429)))
        )
    )
    tail = poly * expo
    return jnp.where(u >= 0, 1.0 - tail, tail), expo


def rows_kernel(
    blocks,
    len_ref,
    x_ref,
    mix_ref,
    cot_ref,
    pool_ref,
    wo_ref,
    wu_ref,
    wd_ref,
    vec_ref,
    bu_ref,
    out_ref,
    pooled_ref,
    low_ref,
    act_ref,
    second_ref,
    inner_ref,
    branch_ref,
    mg_ref,
    sum_ref,
    slope_ref,
):
    step = pl.program_id(0)
    rows, width = cot_ref.shape
    wide = bu_ref.shape[0]
    b_out, gain_one, shift_one, b_down, gain_two, shift_two = (vec_ref[i : i + 1] for i in range(6))
    length = len_ref[step // blocks]
    row_at = lax.broadcasted_iota(jnp.int32, (rows, 1), 0) + (step % blocks) * rows
    live = jnp.where(row_at < length, 1.0, 0.0)

    @pl.when(step == 0)
    def _():
        sum_ref[...] = jnp.zeros(sum_ref.shape, f32)

    @pl.when(step % blocks == 0)
    def _():
        pooled_ref[...] = jnp.zeros(pooled_ref.shape, f32)

    def tally(at, value):
        sum_ref[at : at + 1] += jnp.sum(value, axis=0, keepdims=True)

    part = [slice(i * width, (i + 1) * width) for i in range(wide)]
    hidden = x_ref[0].astype(f32) + mul(mix_ref[0], wo_ref[...]) + b_out
    normed_one, scale_one = norm_parts(hidden)
    first = normed_one * gain_one + shift_one
    first_low = first.astype(bf16)
    low_ref[...] = first_low
    hidden = first + b_down
    for i in range(wide):
        pre = mul(first_low, wu_ref[:, part[i]]) + bu_ref[i : i + 1]
        phi, expo = gelu_parts(pre)
        act = (pre * phi).astype(bf16)
        act_ref[:, part[i]] = act
        slope_ref[:, part[i]] = phi + pre * expo * inv_root_two_pi
        hidden += mul(act, wd_ref[part[i], :])
    normed_two, scale_two = norm_parts(hidden)
    result = normed_two * gain_two + shift_two
    out_ref[...] = result.astype(bf16)
    pooled_ref[0] += jnp.sum(result * live, axis=0, keepdims=True)
    upstream = cot_ref[...].astype(f32) + live * pool_ref[0]
    tally(6, upstream * normed_two)
    tally(7, upstream)
    second_in = norm_back(upstream * gain_two, normed_two, scale_two)
    tally(5, second_in)
    second = second_in.astype(bf16)
    second_ref[...] = second
    first_up = second_in
    for i in range(wide):
        inner = mul(second, wd_ref[part[i], :], NT) * slope_ref[:, part[i]]
        tally(8 + i, inner)
        inner = inner.astype(bf16)
        inner_ref[:, part[i]] = inner
        first_up += mul(inner, wu_ref[:, part[i]], NT)
    tally(3, first_up * normed_one)
    tally(4, first_up)
    branch_in = norm_back(first_up * gain_one, normed_one, scale_one)
    tally(2, branch_in)
    branch_ref[...] = branch_in
    mg_ref[...] = mul(branch_in.astype(bf16), wo_ref[...], NT).astype(bf16)


def row_work(lengths, stacked, cot, pool, w_out, w_up, w_down, vecs, b_up):
    total, width = cot.shape
    count = lengths.shape[0]
    full = total // count
    hidden = w_up.shape[1]
    wide = hidden // width
    blocks = full // ROWS
    narrow = pl.BlockSpec((ROWS, width), lambda i, *_: (i, 0))
    broad = pl.BlockSpec((ROWS, hidden), lambda i, *_: (i, 0))
    single = pl.BlockSpec((1, 1, width), lambda i, *_: (i // blocks, 0, 0))
    thin = jax.ShapeDtypeStruct((total, width), bf16)
    thick = jax.ShapeDtypeStruct((total, hidden), bf16)
    return pl.pallas_call(
        functools.partial(rows_kernel, blocks),
        grid_spec=pltpu.PrefetchScalarGridSpec(
            num_scalar_prefetch=1,
            grid=(total // ROWS,),
            in_specs=[
                pl.BlockSpec((1, ROWS, width), lambda i, *_: (0, i, 0)),
                pl.BlockSpec((1, ROWS, width), lambda i, *_: (1, i, 0)),
                narrow,
                single,
                fixed((width, width)),
                fixed((width, hidden)),
                fixed((hidden, width)),
                fixed(vecs.shape),
                fixed((wide, width)),
            ],
            out_specs=[
                narrow,
                single,
                narrow,
                broad,
                narrow,
                broad,
                narrow,
                narrow,
                pl.BlockSpec((16, width), lambda i, *_: (0, 0)),
            ],
            scratch_shapes=[pltpu.VMEM((ROWS, hidden), f32)],
        ),
        out_shape=[
            thin,
            jax.ShapeDtypeStruct((count, 1, width), f32),
            thin,
            thick,
            thin,
            thick,
            jax.ShapeDtypeStruct((total, width), f32),
            thin,
            jax.ShapeDtypeStruct((16, width), f32),
        ],
        compiler_params=params(56),
        cost_estimate=cost(
            4 * total * width * (width + 2 * hidden),
            2 * total * (8 * width + 2 * hidden) + 2 * width * (width + 2 * hidden),
        ),
    )(lengths, stacked, stacked, cot, pool, w_out, w_up, w_down, vecs, b_up)


def dense_outer_kernel(side_ref, act_ref, second_ref, low_ref, inner_ref, out_ref):
    step = pl.program_id(0)
    half = pl.num_programs(0) // 2

    @pl.when(step < half)
    def _():
        out_ref[0] = mul(act_ref[...], second_ref[...], TN).astype(bf16)

    @pl.when(step >= half)
    def _():
        out_ref[0] = mul(low_ref[...], inner_ref[...], TN).astype(bf16)


def dense_outer(side, act, second, low, inner):
    total, width = second.shape
    wide = act.shape[1] // width
    half = wide // 2
    return pl.pallas_call(
        dense_outer_kernel,
        grid_spec=pltpu.PrefetchScalarGridSpec(
            num_scalar_prefetch=1,
            grid=(wide,),
            in_specs=[
                pl.BlockSpec(
                    (total, width), lambda i, s: (0, s[0] * half + jnp.minimum(i, half - 1))
                ),
                fixed((total, width)),
                fixed((total, width)),
                pl.BlockSpec(
                    (total, width), lambda i, s: (0, s[0] * half + jnp.maximum(i - half, 0))
                ),
            ],
            out_specs=pl.BlockSpec((1, width, width), lambda i, s: (i, 0, 0)),
        ),
        out_shape=jax.ShapeDtypeStruct((wide, width, width), bf16),
        compiler_params=params(48),
        cost_estimate=cost(
            2 * total * width * width * wide, 2 * (wide + 2) * total * width + 2 * wide * width * width
        ),
    )(side, act, second, low, inner).reshape(wide * width, width)


def attend_outer_kernel(side_ref, left_ref, right_ref, out_ref):
    out_ref[0] = mul(left_ref[0], right_ref[0], TN).astype(bf16)


def attend_outer(side, stacked, grads):
    total, width = stacked.shape[1:]
    return pl.pallas_call(
        attend_outer_kernel,
        grid_spec=pltpu.PrefetchScalarGridSpec(
            num_scalar_prefetch=1,
            grid=(2,),
            in_specs=[
                pl.BlockSpec((1, total, width), lambda i, s: ((s[0] * 2 + i) // 3, 0, 0)),
                pl.BlockSpec((1, total, width), lambda i, s: (s[0] * 2 + i, 0, 0)),
            ],
            out_specs=pl.BlockSpec((1, width, width), lambda i, s: (i, 0, 0)),
        ),
        out_shape=jax.ShapeDtypeStruct((2, width, width), bf16),
        compiler_params=params(40),
        cost_estimate=cost(4 * total * width * width, 8 * total * width + 4 * width * width),
    )(side, stacked, grads).reshape(2 * width, width)


def input_kernel(branch_ref, dq_ref, dk_ref, dv_ref, wq_ref, wk_ref, wv_ref, out_ref):
    total = branch_ref[...] + mul(dq_ref[0], wq_ref[...], NT)
    total += mul(dk_ref[0], wk_ref[...], NT)
    total += mul(dv_ref[0], wv_ref[...], NT)
    out_ref[...] = total.astype(bf16)


def input_grad(branch_in, grads, w_query, w_key, w_value):
    total, width = branch_in.shape
    rows = pl.BlockSpec((ROWS, width), lambda i: (i, 0))
    return pl.pallas_call(
        input_kernel,
        grid=(total // ROWS,),
        in_specs=[rows]
        + [pl.BlockSpec((1, ROWS, width), lambda i, at=at: (at, i, 0)) for at in range(3)]
        + [fixed((width, width))] * 3,
        out_specs=rows,
        out_shape=jax.ShapeDtypeStruct((total, width), bf16),
        compiler_params=params(48),
        cost_estimate=cost(6 * total * width * width, 12 * total * width + 6 * width * width),
    )(branch_in, grads, grads, grads, w_query, w_key, w_value)


def exchange(value, axis, mask):
    count = lax.axis_size(axis)
    return lax.ppermute(value, axis, [(i, i ^ mask) for i in range(count)])


def to_passages(value):
    count = lax.axis_size("seq")
    mine = lax.axis_index("seq")
    held, piece, width = value.shape
    own = held // count
    whole = jnp.zeros((own, piece * count, width), value.dtype)
    for mask in range(count):
        peer = mine ^ mask
        part = lax.dynamic_slice_in_dim(value, peer * own, own, 0)
        if mask:
            part = exchange(part, "seq", mask)
        whole = lax.dynamic_update_slice_in_dim(whole, part, peer * piece, 1)
    return whole


def position_pieces(value):
    count = lax.axis_size("seq")
    piece = value.shape[1] // count
    mine = lax.axis_index("seq")
    return [
        lax.dynamic_slice_in_dim(value, (mine ^ mask) * piece, piece, 1) for mask in range(count)
    ]


def traded(pieces):
    return [exchange(part, "seq", mask) if mask else part for mask, part in enumerate(pieces)]


def to_positions(pieces):
    mine = lax.axis_index("seq")
    own, piece, width = pieces[0].shape
    result = jnp.zeros((own * len(pieces), piece, width), pieces[0].dtype)
    for mask, part in enumerate(pieces):
        result = lax.dynamic_update_slice_in_dim(result, part, (mine ^ mask) * own, 0)
    return result


def axis_bits(axis):
    return [(axis, 1 << i) for i in range(lax.axis_size(axis).bit_length() - 1)]


def upper(dim):
    axis, mask = dim
    return (lax.axis_index(axis) & mask) // mask


def swap(value, dim):
    return exchange(value, dim[0], dim[1])


def total_of(parts):
    total = parts[0].astype(f32)
    for part in parts[1:]:
        total += part.astype(f32)
    return total.astype(bf16)


PARTS = 3
SHARD_STEP = 16


class Plan:
    def __init__(self, rows):
        dims = axis_bits("seq") + axis_bits("dp")
        self.first = dims[0]
        rest = dims[1:]
        self.rows = rows // PARTS
        halved = 0
        while halved < len(rest) and (self.rows >> (halved + 1)) % SHARD_STEP == 0:
            halved += 1
        self.last = rest[halved - 1]
        self.plain = rest[halved:]
        split = rest[: halved - 1]
        self.orders = [split[i % len(split) :] + split[: i % len(split)] for i in range(PARTS)]
        self.shards = 1 << halved
        self.shard = self.rows >> halved

    def codes(self):
        found = []
        for order in self.orders:
            code = upper(self.last)
            for at, dim in enumerate(reversed(order)):
                code += upper(dim) << (at + 1)
            found.append(code)
        return jnp.stack(found).astype(jnp.int32)


class Chain:
    def __init__(self):
        self.token = None

    def tie(self, values):
        if self.token is None:
            return values
        return lax.optimization_barrier((values, self.token))[0]

    def mark(self, values):
        self.token = values
        return values


def sum_steps(plan, chain, keep, got, found):
    pairs = [[keep, got]] * PARTS
    bases = [i * plan.rows for i in range(PARTS)]
    size = plan.rows
    for step in range(len(plan.orders[0])):
        pairs = chain.tie(pairs)
        size //= 2
        dims = [order[step] for order in plan.orders]

        def halves(pair, base, at):
            return total_of([lax.dynamic_slice_in_dim(p, base + at * size, size, 0) for p in pair])

        sends = [halves(p, base, 1 - upper(d)) for p, base, d in zip(pairs, bases, dims)]
        chain.mark(sends)
        mine = [halves(p, base, upper(d)) for p, base, d in zip(pairs, bases, dims)]
        pairs = [[m, swap(s, d)] for m, s, d in zip(mine, sends, dims)]
        bases = [0] * PARTS
        yield
    size = plan.shard
    bit = upper(plan.last)
    pairs = chain.tie(pairs)

    def side(at):
        return jnp.concatenate(
            [total_of([lax.dynamic_slice_in_dim(p, at * size, size, 0) for p in pair]) for pair in pairs],
            axis=0,
        )

    send = chain.mark(side(1 - bit))
    shard = side(bit)
    got = swap(send, plan.last)
    yield
    shard, got = chain.tie((shard, got))
    shard = total_of([shard, got])
    for dim in plan.plain:
        shard = total_of([shard, swap(shard, dim)])
    chain.mark(shard)
    got = swap(shard, plan.last)
    yield
    values = [(shard[i * size : (i + 1) * size], got[i * size : (i + 1) * size]) for i in range(PARTS)]
    for step in reversed(range(len(plan.orders[0]))):
        values = chain.tie(values)
        values = [jnp.concatenate(pair, axis=0) for pair in values]
        chain.mark(values)
        if step == 0:
            lower = [swap(v, plan.first) for v in values]
        values = [(v, swap(v, order[step])) for v, order in zip(values, plan.orders)]
        yield
    values = chain.tie(values)
    chain.mark(values)
    found += [v for pair in values for v in pair]
    found += [v for low, pair in zip(lower, values) for v in (low, swap(pair[1], plan.first))]
    yield


def place(plan, refs, code_ref, row, store):
    part = row // plan.rows
    shard = ((row % plan.rows) // plan.shard) ^ code_ref[part]
    half = plan.shards // 2
    at = pl.ds(pl.multiple_of((shard & (half - 1)) * plan.shard, plan.shard), plan.shard)
    low, high = refs[2 * part][at, :], refs[2 * part + 1][at, :]
    store(jnp.where(shard >= half, high.astype(f32), low.astype(f32)))


def dense_place_kernel(plan, half, code_ref, *refs):
    sources, (down_ref, up_ref) = refs[: 4 * PARTS], refs[4 * PARTS :]
    width = down_ref.shape[1]
    for step in range(4 * half):

        @pl.when(pl.program_id(0) == step)
        def _(step=step):
            side, block = step // (2 * half), step % (2 * half)
            own = sources[2 * PARTS * side : 2 * PARTS * (side + 1)]
            out_ref = down_ref if block < half else up_ref
            for row in range(0, width, plan.shard):

                def store(value, row=row):
                    out_ref[row : row + plan.shard, :] = value

                place(plan, own, code_ref, block * width + row, store)


def dense_place(plan, info, sources, width, wide):
    half = wide // 2

    def spot(i, info, shift):
        step = jnp.clip(i - shift, 0, 4 * half - 1)
        turn = step // (2 * half)
        side = jnp.where(turn == 0, info[PARTS], 1 - info[PARTS])
        return side * half + jnp.minimum(step % (2 * half), half - 1)

    return pl.pallas_call(
        functools.partial(dense_place_kernel, plan, half),
        grid_spec=pltpu.PrefetchScalarGridSpec(
            num_scalar_prefetch=1,
            grid=(4 * half,),
            in_specs=[fixed(x.shape) for x in sources],
            out_specs=[
                pl.BlockSpec((width, width), lambda i, s: (spot(i, s, 0), 0)),
                pl.BlockSpec((width, width), lambda i, s: (0, spot(i, s, half))),
            ],
        ),
        out_shape=[
            jax.ShapeDtypeStruct((wide * width, width), f32),
            jax.ShapeDtypeStruct((width, wide * width), f32),
        ],
        compiler_params=params(48),
        cost_estimate=cost(0, 12 * wide * width * width),
    )(info, *sources)


PLACE_ROWS = 256


def attend_place_kernel(plan, code_ref, *refs):
    sources, outs = refs[: 4 * PARTS], refs[4 * PARTS :]
    width = outs[0].shape[1]
    steps = width // PLACE_ROWS
    for step in range(4 * steps):

        @pl.when(pl.program_id(0) == step)
        def _(step=step):
            turn, block, base = step // (2 * steps), step // steps % 2, step % steps * PLACE_ROWS
            own = sources[2 * PARTS * turn : 2 * PARTS * (turn + 1)]
            for row in range(0, PLACE_ROWS, plan.shard):

                def store(value, row=row):
                    for side in range(2):

                        @pl.when(code_ref[PARTS] == (side if turn == 0 else 1 - side))
                        def _():
                            outs[2 * side + block][row : row + plan.shard, :] = value

                place(plan, own, code_ref, block * width + base + row, store)


def attend_place(plan, info, sources, width):
    steps = width // PLACE_ROWS

    def out_spec(at):
        def index(i, s):
            begin = ((at // 2) ^ s[PARTS]) * 2 + at % 2
            return (jnp.clip(i - begin * steps, 0, steps - 1), 0)

        return pl.BlockSpec((PLACE_ROWS, width), index)

    return pl.pallas_call(
        functools.partial(attend_place_kernel, plan),
        grid_spec=pltpu.PrefetchScalarGridSpec(
            num_scalar_prefetch=1,
            grid=(4 * steps,),
            in_specs=[fixed(x.shape) for x in sources],
            out_specs=[out_spec(at) for at in range(4)],
        ),
        out_shape=[jax.ShapeDtypeStruct((width, width), f32)] * 4,
        compiler_params=params(40),
        cost_estimate=cost(0, 24 * width * width),
    )(info, *sources)


def shards(
    tokens,
    lengths,
    w_query,
    b_query,
    w_key,
    w_value,
    b_value,
    w_out,
    b_out,
    gain_one,
    shift_one,
    w_up,
    b_up,
    w_down,
    b_down,
    gain_two,
    shift_two,
    out_grad,
    pooled_grad,
):
    seq_count = lax.axis_size("seq")
    held, piece, width = tokens.shape
    full = piece * seq_count
    count = held // seq_count
    mine = lax.axis_index("seq")
    wide = w_up.shape[1] // width
    total = count * full

    def flat(value):
        return value.reshape(total, width)

    def split(value):
        return value.reshape(count, full, width)

    local_len = lax.dynamic_slice_in_dim(lengths, mine * count, count, 0)
    len_float = local_len.astype(f32)[:, None, None]
    pool = lax.dynamic_slice_in_dim(pooled_grad, mine * count, count, 0)[:, None, :] / len_float
    vecs = jnp.stack([b_out, gain_one, shift_one, b_down, gain_two, shift_two]).astype(f32)
    vecs = jnp.pad(vecs, ((0, 2), (0, 0)))
    first = axis_bits("seq")[0]
    own = upper(first).astype(jnp.int32)[None]
    dense_plan = Plan(wide * width)
    outer_plan = Plan(2 * width)
    dense_info = jnp.concatenate([dense_plan.codes(), own])
    outer_info = jnp.concatenate([outer_plan.codes(), own])

    weights = [w_query, b_query.astype(f32)[None], w_key, w_value, b_value.astype(f32)[None]]
    done = None
    source = tokens
    parts = []
    for passage in range(count):
        if parts:
            source = lax.optimization_barrier((tokens, parts))[0]
        parts = [
            exchange(
                lax.dynamic_slice_in_dim(source, (mine ^ mask) * count + passage, 1, 0), "seq", mask
            )
            for mask in range(1, seq_count)
        ]
        done = attend(passage, count, local_len[passage], mine, tokens, parts, weights, done)
    stacked, q, k, v, stat = done
    cot = to_passages(lax.optimization_barrier((out_grad, parts))[0])
    stacked = stacked.reshape(2, total, width)
    result, pooled_sum, first_low, act, second, inner, branch_in, mixed_grad, sums = row_work(
        local_len,
        stacked,
        flat(cot),
        pool,
        w_out,
        w_up,
        w_down,
        vecs,
        b_up.astype(f32).reshape(wide, width),
    )
    chain = Chain()
    pooled_mine = pooled_sum[:, 0] / len_float[:, 0]
    pooled = lax.all_gather(pooled_mine, "seq", axis=0, tiled=True)

    pieces = chain.mark(position_pieces(split(result)))
    out_pieces = traded(pieces)
    send = dense_outer(1 - own, *chain.tie((act, second, first_low, inner)))
    chain.mark(send)
    got = swap(send, first)
    keep = chain.mark(dense_outer(own, *chain.tie((act, second, first_low, inner))))
    dense, outer = [], []
    dense_steps = sum_steps(dense_plan, chain, keep, got, dense)
    next(dense_steps)
    chain.mark((chain.token, out_pieces))
    block_out = to_positions(out_pieces)
    grads, bias_sums = attend_back(
        local_len, q, k, v, chain.tie(split(mixed_grad)), split(branch_in), stat
    )
    chain.mark(bias_sums)
    grads = grads.reshape(4, total, width)
    vectors = sums + jnp.pad(bias_sums, ((0, 8), (0, 0)))
    vectors = lax.all_gather(vectors, ("dp", "seq"), axis=0, tiled=True)
    vectors = jnp.sum(vectors.reshape(-1, *sums.shape), axis=0)
    next(dense_steps)
    send = attend_outer(1 - own, stacked, chain.tie(grads))
    chain.mark(send)
    got = swap(send, first)
    keep = attend_outer(own, stacked, chain.tie(grads))
    chain.mark(keep)
    next(dense_steps)
    outer_steps = sum_steps(outer_plan, chain, keep, got, outer)
    next(outer_steps)
    input_low = input_grad(branch_in, chain.tie(grads), w_query, w_key, w_value)
    chain.mark(input_low)
    next(dense_steps)
    next(outer_steps)
    pieces = chain.mark(position_pieces(split(chain.tie(input_low))))
    in_pieces = traded(pieces)
    next(outer_steps)
    next(dense_steps)
    next(outer_steps)
    next(dense_steps)
    next(outer_steps)
    chain.mark((chain.token, in_pieces))
    tokens_grad = to_positions(in_pieces)
    for steps in [dense_steps, outer_steps] * 2:
        next(steps)
    for _ in dense_steps:
        pass
    next(outer_steps)
    down_sum, up_sum = dense_place(dense_plan, dense_info, chain.tie(dense), width, wide)
    chain.mark((down_sum, up_sum))
    for _ in outer_steps:
        pass
    outer = attend_place(outer_plan, outer_info, outer, width)
    return (
        block_out,
        pooled,
        tokens_grad,
        outer[0],
        vectors[0],
        outer[1],
        outer[2],
        vectors[1],
        outer[3],
        vectors[2],
        vectors[3],
        vectors[4],
        up_sum,
        vectors[8 : 8 + wide].reshape(-1),
        down_sum,
        vectors[5],
        vectors[6],
        vectors[7],
    )


def solution(mesh):
    in_specs = (
        (P("dp", "seq", None), P("dp"))
        + (P(),) * 15
        + (P("dp", "seq", None), P("dp", None))
    )
    out_specs = (P("dp", "seq", None), P("dp", None), P("dp", "seq", None)) + (P(),) * 15
    return jax.shard_map(shards, mesh=mesh, in_specs=in_specs, out_specs=out_specs, check_vma=False)
```

```python
import functools

import jax
import jax.numpy as jnp
from jax import lax
from jax.experimental import pallas as pl
from jax.experimental.pallas import tpu as pltpu
from jax.sharding import PartitionSpec as P

HEADS = 12
HEAD_DIM = 64
PAIR = 2 * HEAD_DIM
PAIRS = HEADS // 2
SCALE = HEAD_DIM ** (-0.5)
ROWS = 256
CHUNK = 256
KEY_STEP = 128
VMEM_BYTES = 62 * 1024 * 1024

eps = 1e-06
root_half = 0.7071067811865476
inv_root_two_pi = 0.3989422804014327

f32 = jnp.float32
bf16 = jnp.bfloat16

NN = (((1,), (0,)), ((), ()))
NT = (((1,), (1,)), ((), ()))
TN = (((0,), (0,)), ((), ()))


def mul(left, right, dims=NN):
    return lax.dot_general(left, right, dims, preferred_element_type=f32)


def fixed(shape):
    return pl.BlockSpec(shape, lambda *_: (0,) * len(shape), pipeline_mode=pl.Buffered(1))


PARAMS = pltpu.CompilerParams(dimension_semantics=("arbitrary",), vmem_limit_bytes=VMEM_BYTES)


def cost(flops, moved, exps=0):
    return pl.CostEstimate(flops=int(flops), bytes_accessed=int(moved), transcendentals=int(exps))


def over_extents(length, full, body):
    for extent in range(KEY_STEP, full + 1, KEY_STEP):
        pl.when((length > extent - KEY_STEP) & (length <= extent))(functools.partial(body, extent))


def attend_kernel(pieces, passage, count, held, info_ref, *refs):
    part_refs, refs = refs[:pieces], refs[pieces:]
    wq_ref, wk_ref, wv_ref, vec_ref = refs[:4]
    xm_ref, q_ref, k_ref, v_ref, stat_ref = refs[-5:]
    x_ref, mix_ref = xm_ref.at[0], xm_ref.at[1]
    mine = info_ref[held]
    length = info_ref[mine * count + passage]
    size = part_refs[0].shape[1]
    for mask, part_ref in enumerate(part_refs):
        x_ref[0, pl.ds(pl.multiple_of((mine ^ mask) * size, size), size)] = part_ref[0]
    q_ref[0] = (mul(x_ref[0], wq_ref[...]) + vec_ref[0:1]).astype(bf16)
    stat_ref[0] = jnp.zeros(stat_ref.shape[1:], f32)
    lane = lax.broadcasted_iota(jnp.int32, (1, PAIR), 1)
    full = size * pieces

    def run(extent):
        x = x_ref[0, :extent]
        k_ref[0, :extent] = mul(x, wk_ref[...]).astype(bf16)
        v_ref[0, :extent] = (mul(x, wv_ref[...]) + vec_ref[1:2]).astype(bf16)
        key_at = lax.broadcasted_iota(jnp.int32, (1, extent), 1)
        dead = jnp.where(key_at < length, 0.0, -1e30)

        def pair_step(pair, carry):
            at = pl.ds(pl.multiple_of(pair * PAIR, PAIR), PAIR)
            q, k, v = q_ref[0, :, at], k_ref[0, :extent, at], v_ref[0, :extent, at]
            mixed = []
            stat = stat_ref[0]
            for half in range(2):
                own = (lane >= half * HEAD_DIM) & (lane < (half + 1) * HEAD_DIM)
                q_own = jnp.where(own, q * SCALE, 0).astype(bf16)
                scores = mul(q_own, k, NT) + dead
                top = jnp.max(scores, axis=1, keepdims=True)
                expo = jnp.exp(scores - top)
                total = jnp.sum(expo, axis=1, keepdims=True)
                probs = (expo * (1.0 / total)).astype(bf16)
                mixed.append(mul(probs, v))
                stat = jnp.where(lane == pair * 2 + half, top + jnp.log(total), stat)
            stat_ref[0] = stat
            mix_ref[0, :, at] = jnp.where(lane < HEAD_DIM, mixed[0], mixed[1]).astype(bf16)
            return carry

        lax.fori_loop(0, PAIRS, pair_step, 0)

    over_extents(length, full, run)


def attend(passage, count, info, tokens, parts, weights, before):
    held, piece, width = tokens.shape
    pieces = len(parts) + 1
    full = piece * pieces
    rows = pl.BlockSpec((1, full, width), lambda i, s: (passage, 0, 0))
    act = jax.ShapeDtypeStruct((count, full, width), bf16)
    got = pl.BlockSpec((1, piece, width), lambda i, s: (0, 0, 0))
    kept = [] if before is None else list(before)
    first_kept = 1 + pieces + len(weights)
    return pl.pallas_call(
        functools.partial(attend_kernel, pieces, passage, count, held),
        grid_spec=pltpu.PrefetchScalarGridSpec(
            num_scalar_prefetch=1,
            grid=(1,),
            in_specs=[pl.BlockSpec((1, piece, width), lambda i, s: (s[held] * count + passage, 0, 0))]
            + [got] * len(parts)
            + [fixed(w.shape) for w in weights]
            + [pl.BlockSpec(memory_space=pl.ANY)] * len(kept),
            out_specs=[pl.BlockSpec((2, 1, full, width), lambda i, s: (0, passage, 0, 0))]
            + [rows] * 3
            + [pl.BlockSpec((1, full, PAIR), lambda i, s: (passage, 0, 0))],
        ),
        out_shape=[jax.ShapeDtypeStruct((2, count, full, width), bf16)]
        + [act] * 3
        + [jax.ShapeDtypeStruct((count, full, PAIR), f32)],
        input_output_aliases={first_kept + i: i for i in range(len(kept))},
        compiler_params=PARAMS,
        cost_estimate=cost(
            2 * full * (3 * width * width + 4 * 2 * full * width),
            12 * full * width + 6 * width * width,
        ),
    )(info, tokens, *parts, *weights, *kept)


def attend_back_kernel(
    held, info_ref, q_ref, k_ref, v_ref, mg_ref, branch_ref, stat_ref, sum_ref, grads_ref, bias_ref, log_ref
):
    dq_ref, dk_ref, dv_ref = (grads_ref.at[i] for i in range(3))
    grads_ref[3] = branch_ref[...].astype(bf16)
    full = q_ref.shape[1]
    length = info_ref[info_ref[held] * pl.num_programs(0) + pl.program_id(0)]
    lane = lax.broadcasted_iota(jnp.int32, (1, PAIR), 1)
    log_ref[...] = stat_ref[0].T
    row = lax.broadcasted_iota(jnp.int32, (8, 1), 0)

    @pl.when(pl.program_id(0) == 0)
    def _():
        bias_ref[...] = sum_ref[...]

    def run(extent):
        key_at = lax.broadcasted_iota(jnp.int32, (extent, 1), 0)
        dead = jnp.where(key_at < length, 0.0, -1e30)
        if extent < full:
            dk_ref[0, extent:] = jnp.zeros((full - extent, dk_ref.shape[2]), bf16)
            dv_ref[0, extent:] = jnp.zeros((full - extent, dv_ref.shape[2]), bf16)

        def pair_step(pair, carry):
            at = pl.ds(pl.multiple_of(pair * PAIR, PAIR), PAIR)
            q, mg = q_ref[0, :, at], mg_ref[0, :, at]
            k, v = k_ref[0, :extent, at], v_ref[0, :extent, at]
            dq, dk, dv = [], [], []
            for half in range(2):
                own = (lane >= half * HEAD_DIM) & (lane < (half + 1) * HEAD_DIM)
                k_own = jnp.where(own, k * SCALE, 0).astype(bf16)
                v_own = jnp.where(own, v, 0).astype(bf16)
                log_row = log_ref[pl.ds(pair * 2 + half, 1), :]
                probs = jnp.exp(mul(k_own, q, NT) + dead - log_row)
                prob_grad = mul(v_own, mg, NT)
                along = jnp.sum(probs * prob_grad, axis=0, keepdims=True)
                score_grad = (probs * (prob_grad - along)).astype(bf16)
                dv.append(mul(probs.astype(bf16), mg))
                dk.append(mul(score_grad, q))
                dq.append(mul(score_grad, k, TN))
            first = lane < HEAD_DIM
            dq_pair = jnp.where(first, dq[0], dq[1]) * SCALE
            dk_pair = jnp.where(first, dk[0], dk[1]) * SCALE
            dv_pair = jnp.where(first, dv[0], dv[1])
            dq_ref[0, :, at] = dq_pair.astype(bf16)
            dk_ref[0, :extent, at] = dk_pair.astype(bf16)
            dv_ref[0, :extent, at] = dv_pair.astype(bf16)
            sums = jnp.where(
                row == 0,
                jnp.sum(dq_pair, axis=0, keepdims=True),
                jnp.where(row == 1, jnp.sum(dv_pair, axis=0, keepdims=True), 0.0),
            )
            bias_ref[0:8, at] += sums
            return carry

        lax.fori_loop(0, PAIRS, pair_step, 0)

    over_extents(length, full, run)


def attend_back(held, info, q, k, v, mixed_grad, branch_in, stat, sums):
    count, full, width = q.shape
    rows = pl.BlockSpec((1, full, width), lambda i, *_: (i, 0, 0))
    return pl.pallas_call(
        functools.partial(attend_back_kernel, held),
        grid_spec=pltpu.PrefetchScalarGridSpec(
            num_scalar_prefetch=1,
            grid=(count,),
            in_specs=[rows] * 5
            + [pl.BlockSpec((1, full, PAIR), lambda i, *_: (i, 0, 0)), fixed(sums.shape)],
            out_specs=[
                pl.BlockSpec((4, 1, full, width), lambda i, *_: (0, i, 0, 0)),
                pl.BlockSpec(sums.shape, lambda i, *_: (0, 0)),
            ],
            scratch_shapes=[pltpu.VMEM((PAIR, full), f32)],
        ),
        out_shape=[
            jax.ShapeDtypeStruct((4, count, full, width), bf16),
            jax.ShapeDtypeStruct(sums.shape, f32),
        ],
        compiler_params=PARAMS,
        cost_estimate=cost(
            2 * count * full * 10 * 2 * full * width, 14 * count * full * width
        ),
    )(info, q, k, v, mixed_grad, branch_in, stat, sums)


def norm_parts(hidden):
    centred = hidden - jnp.mean(hidden, axis=1, keepdims=True)
    inv_scale = lax.rsqrt(jnp.mean(centred * centred, axis=1, keepdims=True) + eps)
    return centred * inv_scale, inv_scale


def norm_back(scaled, normed, inv_scale):
    mean = jnp.mean(scaled, axis=1, keepdims=True)
    along = jnp.mean(scaled * normed, axis=1, keepdims=True)
    return (scaled - mean - normed * along) * inv_scale


def gelu_parts(u):
    expo = jnp.exp(u * u * -0.5)
    base = 1.0 + jnp.abs(u) * (0.3275911 * root_half)
    t = pl.reciprocal(base, approx=True)
    t = t * (2.0 - base * t)
    poly = t * (
        0.5 * 0.254829592
        + t
        * (
            0.5 * -0.284496736
            + t * (0.5 * 1.421413741 + t * (0.5 * -1.453152027 + t * (0.5 * 1.061405429)))
        )
    )
    tail = poly * expo
    return jnp.where(u >= 0, 1.0 - tail, tail), expo


def rows_kernel(
    blocks,
    count,
    held,
    info_ref,
    x_ref,
    mix_ref,
    cot_ref,
    pool_ref,
    wo_ref,
    wu_ref,
    wd_ref,
    vec_ref,
    out_ref,
    pooled_ref,
    low_ref,
    act_ref,
    second_ref,
    inner_ref,
    branch_ref,
    mg_ref,
    sum_ref,
    slope_ref,
):
    step = pl.program_id(0)
    rows, width = cot_ref.shape
    hidden_width = wu_ref.shape[1]
    b_out, gain_one, shift_one, b_down, gain_two, shift_two = (
        vec_ref[i : i + 1] for i in range(2, 8)
    )
    passage = info_ref[held] * count + step // blocks
    length = info_ref[passage]
    inv_length = 1.0 / jnp.full((1, width), length, jnp.int32).astype(f32)
    row_at = lax.broadcasted_iota(jnp.int32, (rows, 1), 0) + (step % blocks) * rows
    live = jnp.where(row_at < length, 1.0, 0.0)

    @pl.when(step == 0)
    def _():
        sum_ref[...] = jnp.zeros(sum_ref.shape, f32)

    @pl.when(step % blocks == 0)
    def _():
        pooled_ref[...] = jnp.zeros(pooled_ref.shape, f32)

    def tally(at, value, columns=slice(None)):
        sum_ref[at : at + 1, columns] += jnp.sum(value, axis=0, keepdims=True)

    groups = width // CHUNK
    chunks = hidden_width // CHUNK
    part = [slice(i * CHUNK, (i + 1) * CHUNK) for i in range(chunks)]
    whole = [slice(i * width, (i + 1) * width) for i in range(hidden_width // width)]

    hidden = x_ref[0].astype(f32) + mul(mix_ref[0], wo_ref[...]) + b_out
    normed_one, scale_one = norm_parts(hidden)
    first = normed_one * gain_one + shift_one
    first_low = first.astype(bf16)
    low_ref[...] = first_low
    hidden = first + b_down

    def up(i):
        return mul(first_low, wu_ref[:, part[i]]) + vec_ref[8 + i // groups : 9 + i // groups, part[i % groups]]

    def activate(i, pre):
        phi, expo = gelu_parts(pre)
        act_ref[:, part[i]] = (pre * phi).astype(bf16)
        slope_ref[:, part[i]] = phi + pre * expo * inv_root_two_pi

    pre = up(0)
    for i in range(chunks):
        ahead = up(i + 1) if i + 1 < chunks else None
        activate(i, pre)
        if i % groups == 0 and i:
            done = whole[i // groups - 1]
            hidden += mul(act_ref[:, done], wd_ref[done, :])
        pre = ahead
    hidden += mul(act_ref[:, whole[-1]], wd_ref[whole[-1], :])

    normed_two, scale_two = norm_parts(hidden)
    result = normed_two * gain_two + shift_two
    out_ref[...] = result.astype(bf16)
    pooled_ref[0] += jnp.sum(result * live, axis=0, keepdims=True)

    @pl.when(step % blocks == blocks - 1)
    def _():
        pooled_ref[0] = pooled_ref[0] * inv_length

    upstream = cot_ref[...].astype(f32) + live * (pool_ref[pl.ds(passage, 1), :] * inv_length)
    tally(6, upstream * normed_two)
    tally(7, upstream)
    second_in = norm_back(upstream * gain_two, normed_two, scale_two)
    tally(5, second_in)
    second = second_in.astype(bf16)
    second_ref[...] = second
    first_up = second_in

    def back(i):
        return mul(second, wd_ref[part[i], :], NT)

    grad = back(0)
    for i in range(chunks):
        ahead = back(i + 1) if i + 1 < chunks else None
        inner = grad * slope_ref[:, part[i]]
        tally(8 + i // groups, inner, part[i % groups])
        inner_ref[:, part[i]] = inner.astype(bf16)
        if i % groups == 0 and i:
            done = whole[i // groups - 1]
            first_up += mul(inner_ref[:, done], wu_ref[:, done], NT)
        grad = ahead
    first_up += mul(inner_ref[:, whole[-1]], wu_ref[:, whole[-1]], NT)

    tally(3, first_up * normed_one)
    tally(4, first_up)
    branch_in = norm_back(first_up * gain_one, normed_one, scale_one)
    tally(2, branch_in)
    branch_ref[...] = branch_in
    mg_ref[...] = mul(branch_in.astype(bf16), wo_ref[...], NT).astype(bf16)


def row_work(held, info, stacked, cot, pool, w_out, w_up, w_down, vecs, count):
    total, width = cot.shape
    full = total // count
    hidden = w_up.shape[1]
    blocks = full // ROWS
    narrow = pl.BlockSpec((ROWS, width), lambda i, *_: (i, 0))
    broad = pl.BlockSpec((ROWS, hidden), lambda i, *_: (i, 0))
    thin = jax.ShapeDtypeStruct((total, width), bf16)
    thick = jax.ShapeDtypeStruct((total, hidden), bf16)
    return pl.pallas_call(
        functools.partial(rows_kernel, blocks, count, held),
        grid_spec=pltpu.PrefetchScalarGridSpec(
            num_scalar_prefetch=1,
            grid=(total // ROWS,),
            in_specs=[
                pl.BlockSpec((1, ROWS, width), lambda i, *_: (0, i, 0)),
                pl.BlockSpec((1, ROWS, width), lambda i, *_: (1, i, 0)),
                narrow,
                fixed(pool.shape),
                fixed((width, width)),
                fixed((width, hidden)),
                fixed((hidden, width)),
                fixed(vecs.shape),
            ],
            out_specs=[
                narrow,
                pl.BlockSpec((1, 1, width), lambda i, *_: (i // blocks, 0, 0)),
                narrow,
                broad,
                narrow,
                broad,
                narrow,
                narrow,
                pl.BlockSpec((16, width), lambda i, *_: (0, 0)),
            ],
            scratch_shapes=[pltpu.VMEM((ROWS, hidden), f32)],
        ),
        out_shape=[
            thin,
            jax.ShapeDtypeStruct((count, 1, width), f32),
            thin,
            thick,
            thin,
            thick,
            jax.ShapeDtypeStruct((total, width), f32),
            thin,
            jax.ShapeDtypeStruct((16, width), f32),
        ],
        compiler_params=PARAMS,
        cost_estimate=cost(
            4 * total * width * (width + 2 * hidden),
            2 * total * (8 * width + 2 * hidden) + 2 * width * (width + 2 * hidden),
        ),
    )(info, stacked, stacked, cot, pool, w_out, w_up, w_down, vecs)


def dense_outer_kernel(side_ref, act_ref, second_ref, low_ref, inner_ref, out_ref):
    step = pl.program_id(0)
    half = pl.num_programs(0) // 2

    @pl.when(step < half)
    def _():
        out_ref[0] = mul(act_ref[...], second_ref[...], TN).astype(bf16)

    @pl.when(step >= half)
    def _():
        out_ref[0] = mul(low_ref[...], inner_ref[...], TN).astype(bf16)


def dense_outer(at, flip, info, act, second, low, inner):
    total, width = second.shape
    wide = act.shape[1] // width
    half = wide // 2
    return pl.pallas_call(
        dense_outer_kernel,
        grid_spec=pltpu.PrefetchScalarGridSpec(
            num_scalar_prefetch=1,
            grid=(wide,),
            in_specs=[
                pl.BlockSpec(
                    (total, width), lambda i, s: (0, (s[at] ^ flip) * half + jnp.minimum(i, half - 1))
                ),
                fixed((total, width)),
                fixed((total, width)),
                pl.BlockSpec(
                    (total, width), lambda i, s: (0, (s[at] ^ flip) * half + jnp.maximum(i - half, 0))
                ),
            ],
            out_specs=pl.BlockSpec((1, width, width), lambda i, s: (i, 0, 0)),
        ),
        out_shape=jax.ShapeDtypeStruct((wide, width, width), bf16),
        compiler_params=PARAMS,
        cost_estimate=cost(
            2 * total * width * width * wide, 2 * (wide + 2) * total * width + 2 * wide * width * width
        ),
    )(info, act, second, low, inner).reshape(wide * width, width)


def attend_outer_kernel(side_ref, left_ref, right_ref, out_ref):
    out_ref[0] = mul(left_ref[0], right_ref[0], TN).astype(bf16)


def attend_outer(at, flip, info, stacked, grads):
    total, width = stacked.shape[1:]
    return pl.pallas_call(
        attend_outer_kernel,
        grid_spec=pltpu.PrefetchScalarGridSpec(
            num_scalar_prefetch=1,
            grid=(2,),
            in_specs=[
                pl.BlockSpec((1, total, width), lambda i, s: (((s[at] ^ flip) * 2 + i) // 3, 0, 0)),
                pl.BlockSpec((1, total, width), lambda i, s: ((s[at] ^ flip) * 2 + i, 0, 0)),
            ],
            out_specs=pl.BlockSpec((1, width, width), lambda i, s: (i, 0, 0)),
        ),
        out_shape=jax.ShapeDtypeStruct((2, width, width), bf16),
        compiler_params=PARAMS,
        cost_estimate=cost(4 * total * width * width, 8 * total * width + 4 * width * width),
    )(info, stacked, grads).reshape(2 * width, width)


def input_kernel(branch_ref, dq_ref, dk_ref, dv_ref, wq_ref, wk_ref, wv_ref, out_ref):
    total = branch_ref[...] + mul(dq_ref[0], wq_ref[...], NT)
    total += mul(dk_ref[0], wk_ref[...], NT)
    total += mul(dv_ref[0], wv_ref[...], NT)
    out_ref[...] = total.astype(bf16)


def input_grad(branch_in, grads, w_query, w_key, w_value):
    total, width = branch_in.shape
    rows = pl.BlockSpec((ROWS, width), lambda i: (i, 0))
    return pl.pallas_call(
        input_kernel,
        grid=(total // ROWS,),
        in_specs=[rows]
        + [pl.BlockSpec((1, ROWS, width), lambda i, at=at: (at, i, 0)) for at in range(3)]
        + [fixed((width, width))] * 3,
        out_specs=rows,
        out_shape=jax.ShapeDtypeStruct((total, width), bf16),
        compiler_params=PARAMS,
        cost_estimate=cost(6 * total * width * width, 12 * total * width + 6 * width * width),
    )(branch_in, grads, grads, grads, w_query, w_key, w_value)


def exchange(value, axis, mask):
    count = lax.axis_size(axis)
    return lax.ppermute(value, axis, [(i, i ^ mask) for i in range(count)])


def to_passages(value):
    count = lax.axis_size("seq")
    mine = lax.axis_index("seq")
    held, piece, width = value.shape
    own = held // count
    whole = jnp.zeros((own, piece * count, width), value.dtype)
    for mask in range(count):
        peer = mine ^ mask
        part = lax.dynamic_slice_in_dim(value, peer * own, own, 0)
        if mask:
            part = exchange(part, "seq", mask)
        whole = lax.dynamic_update_slice_in_dim(whole, part, peer * piece, 1)
    return whole


def position_pieces(value):
    count = lax.axis_size("seq")
    piece = value.shape[1] // count
    mine = lax.axis_index("seq")
    return [
        lax.dynamic_slice_in_dim(value, (mine ^ mask) * piece, piece, 1) for mask in range(count)
    ]


def traded(pieces):
    return [exchange(part, "seq", mask) if mask else part for mask, part in enumerate(pieces)]


def to_positions(pieces):
    mine = lax.axis_index("seq")
    own, piece, width = pieces[0].shape
    result = jnp.zeros((own * len(pieces), piece, width), pieces[0].dtype)
    for mask, part in enumerate(pieces):
        result = lax.dynamic_update_slice_in_dim(result, part, (mine ^ mask) * own, 0)
    return result


def axis_bits(axis):
    return [(axis, 1 << i) for i in range(lax.axis_size(axis).bit_length() - 1)]


def upper(dim):
    axis, mask = dim
    return (lax.axis_index(axis) & mask) // mask


def swap(value, dim):
    return exchange(value, dim[0], dim[1])


def total_of(parts):
    total = parts[0].astype(f32)
    for part in parts[1:]:
        total += part.astype(f32)
    return total.astype(bf16)


PARTS = 3
SHARD_STEP = 16


class Plan:
    def __init__(self, rows):
        dims = axis_bits("seq") + axis_bits("dp")
        self.first = dims[0]
        rest = dims[1:]
        self.rows = rows // PARTS
        halved = 0
        while halved < len(rest) and (self.rows >> (halved + 1)) % SHARD_STEP == 0:
            halved += 1
        self.last = rest[halved - 1]
        self.plain = rest[halved:]
        split = rest[: halved - 1]
        self.orders = [split[i % len(split) :] + split[: i % len(split)] for i in range(PARTS)]
        self.shards = 1 << halved
        self.shard = self.rows >> halved

    def codes(self):
        found = []
        for order in self.orders:
            code = upper(self.last)
            for at, dim in enumerate(reversed(order)):
                code += upper(dim) << (at + 1)
            found.append(code)
        return [code.astype(jnp.int32) for code in found]


class Chain:
    def __init__(self):
        self.token = None

    def tie(self, values):
        if self.token is None:
            return values
        return lax.optimization_barrier((values, self.token))[0]

    def mark(self, values):
        self.token = values
        return values


def sum_steps(plan, chain, keep, got, found):
    pairs = [[keep, got]] * PARTS
    bases = [i * plan.rows for i in range(PARTS)]
    size = plan.rows
    for step in range(len(plan.orders[0])):
        pairs = chain.tie(pairs)
        size //= 2
        dims = [order[step] for order in plan.orders]

        def halves(pair, base, at):
            return total_of([lax.dynamic_slice_in_dim(p, base + at * size, size, 0) for p in pair])

        sends = [halves(p, base, 1 - upper(d)) for p, base, d in zip(pairs, bases, dims)]
        chain.mark(sends)
        mine = [halves(p, base, upper(d)) for p, base, d in zip(pairs, bases, dims)]
        pairs = [[m, swap(s, d)] for m, s, d in zip(mine, sends, dims)]
        bases = [0] * PARTS
        yield
    size = plan.shard
    bit = upper(plan.last)
    pairs = chain.tie(pairs)

    def side(at):
        return jnp.concatenate(
            [total_of([lax.dynamic_slice_in_dim(p, at * size, size, 0) for p in pair]) for pair in pairs],
            axis=0,
        )

    send = chain.mark(side(1 - bit))
    shard = side(bit)
    got = swap(send, plan.last)
    yield
    shard, got = chain.tie((shard, got))
    shard = total_of([shard, got])
    for dim in plan.plain:
        shard = total_of([shard, swap(shard, dim)])
    chain.mark(shard)
    got = swap(shard, plan.last)
    yield
    values = [(shard[i * size : (i + 1) * size], got[i * size : (i + 1) * size]) for i in range(PARTS)]
    for step in reversed(range(len(plan.orders[0]))):
        values = chain.tie(values)
        values = [jnp.concatenate(pair, axis=0) for pair in values]
        chain.mark(values)
        values = [(v, swap(v, order[step])) for v, order in zip(values, plan.orders)]
        yield
    values = chain.tie(values)
    chain.mark(values)
    found += [v for pair in values for v in pair]
    found += [swap(v, plan.first) for v in found]
    yield


def vector_steps(chain, value, found):
    dims = axis_bits("seq") + axis_bits("dp")
    got = swap(value, dims[0])
    yield
    for dim in dims[1:]:
        value, got = chain.tie((value, got))
        value = value + got
        chain.mark((chain.token, value))
        got = swap(value, dim)
        yield
    found.append(value + got)
    yield


def place(plan, refs, codes, row, store):
    part = row // plan.rows
    shard = ((row % plan.rows) // plan.shard) ^ codes[part]
    half = plan.shards // 2
    at = pl.ds(pl.multiple_of((shard & (half - 1)) * plan.shard, plan.shard), plan.shard)
    low, high = refs[2 * part][at, :], refs[2 * part + 1][at, :]
    store(jnp.where(shard >= half, high.astype(f32), low.astype(f32)))


def dense_place_kernel(plan, half, first_code, info_ref, *refs):
    sources, (down_ref, up_ref) = refs[: 2 * PARTS], refs[-2:]
    codes = [info_ref[first_code + i] for i in range(PARTS)]
    width = down_ref.shape[1]
    for block in range(2 * half):

        @pl.when(pl.program_id(0) == block)
        def _(block=block):
            out_ref = down_ref if block < half else up_ref
            for row in range(0, width, plan.shard):

                def store(value, row=row):
                    out_ref[row : row + plan.shard, :] = value

                place(plan, sources, codes, block * width + row, store)


def dense_place(plan, first_code, at, flip, info, sources, width, wide, before):
    half = wide // 2
    kept = list(before)

    def spot(step, s):
        return (s[at] ^ flip) * half + jnp.clip(step, 0, half - 1)

    return pl.pallas_call(
        functools.partial(dense_place_kernel, plan, half, first_code),
        grid_spec=pltpu.PrefetchScalarGridSpec(
            num_scalar_prefetch=1,
            grid=(2 * half,),
            in_specs=[fixed(x.shape) for x in sources]
            + [pl.BlockSpec(memory_space=pl.ANY)] * len(kept),
            out_specs=[
                pl.BlockSpec((width, width), lambda i, s: (spot(i, s), 0)),
                pl.BlockSpec((width, width), lambda i, s: (0, spot(i - half, s))),
            ],
        ),
        out_shape=[
            jax.ShapeDtypeStruct((wide * width, width), f32),
            jax.ShapeDtypeStruct((width, wide * width), f32),
        ],
        input_output_aliases={1 + len(sources) + i: i for i in range(len(kept))},
        compiler_params=PARAMS,
        cost_estimate=cost(0, 6 * wide * width * width),
    )(info, *sources, *kept)


def attend_place_kernel(plan, first_code, at, flip, info_ref, *refs):
    sources, (hold_ref, sems) = refs[: 2 * PARTS], refs[-2:]
    outs = refs[-6:-2]
    codes = [info_ref[first_code + i] for i in range(PARTS)]
    own = info_ref[at] ^ flip
    width = hold_ref.shape[2]

    def move(block, act):
        for side in range(2):

            @pl.when(own == side)
            def _():
                act(pltpu.make_async_copy(hold_ref.at[block], outs[2 * side + block], sems.at[block]))

    for block in range(2):
        for row in range(0, width, plan.shard):

            def store(value, row=row):
                hold_ref[block, row : row + plan.shard, :] = value

            place(plan, sources, codes, block * width + row, store)
        move(block, lambda copy: copy.start())
    for block in range(2):
        move(block, lambda copy: copy.wait())


def attend_place(plan, first_code, at, flip, info, sources, width, before):
    kept = list(before)
    return pl.pallas_call(
        functools.partial(attend_place_kernel, plan, first_code, at, flip),
        grid_spec=pltpu.PrefetchScalarGridSpec(
            num_scalar_prefetch=1,
            grid=(1,),
            in_specs=[fixed(x.shape) for x in sources]
            + [pl.BlockSpec(memory_space=pl.ANY)] * len(kept),
            out_specs=[pl.BlockSpec(memory_space=pl.ANY)] * 4,
            scratch_shapes=[pltpu.VMEM((2, width, width), f32), pltpu.SemaphoreType.DMA((2,))],
        ),
        out_shape=[jax.ShapeDtypeStruct((width, width), f32)] * 4,
        input_output_aliases={1 + len(sources) + i: i for i in range(len(kept))},
        compiler_params=PARAMS,
        cost_estimate=cost(0, 12 * width * width),
    )(info, *sources, *kept)


def shards(
    tokens,
    lengths,
    w_query,
    b_query,
    w_key,
    w_value,
    b_value,
    w_out,
    b_out,
    gain_one,
    shift_one,
    w_up,
    b_up,
    w_down,
    b_down,
    gain_two,
    shift_two,
    out_grad,
    pooled_grad,
):
    seq_count = lax.axis_size("seq")
    held, piece, width = tokens.shape
    full = piece * seq_count
    count = held // seq_count
    mine = lax.axis_index("seq")
    wide = w_up.shape[1] // width
    total = count * full

    def flat(value):
        return value.reshape(total, width)

    def split(value):
        return value.reshape(count, full, width)

    dense_plan = Plan(wide * width)
    outer_plan = Plan(2 * width)
    first = axis_bits("seq")[0]
    scalars = [mine, upper(first)] + dense_plan.codes() + outer_plan.codes()
    own_at, dense_at, outer_at = held + 1, held + 2, held + 2 + PARTS
    info = jnp.concatenate([lengths, jnp.stack([v.astype(jnp.int32) for v in scalars])])
    vecs = jnp.concatenate(
        [b_query, b_value, b_out, gain_one, shift_one, b_down, gain_two, shift_two, b_up]
    )
    vecs = vecs.astype(f32).reshape(-1, width)

    weights = [w_query, w_key, w_value, vecs]
    done = None
    source = tokens
    parts = []
    for passage in range(count):
        if parts:
            source = lax.optimization_barrier((tokens, parts))[0]
        parts = [
            exchange(
                lax.dynamic_slice_in_dim(source, (mine ^ mask) * count + passage, 1, 0), "seq", mask
            )
            for mask in range(1, seq_count)
        ]
        done = attend(passage, count, info, tokens, parts, weights, done)
    stacked, q, k, v, stat = done
    cot = to_passages(lax.optimization_barrier((out_grad, parts))[0])
    stacked = stacked.reshape(2, total, width)
    result, pooled_mine, first_low, act, second, inner, branch_in, mixed_grad, sums = row_work(
        held, info, stacked, flat(cot), pooled_grad, w_out, w_up, w_down, vecs, count
    )
    chain = Chain()
    pooled = lax.all_gather(pooled_mine[:, 0], "seq", axis=0, tiled=True)

    pieces = chain.mark(position_pieces(split(result)))
    out_pieces = traded(pieces)
    send = dense_outer(own_at, 1, info, *chain.tie((act, second, first_low, inner)))
    chain.mark(send)
    got = swap(send, first)
    keep = chain.mark(dense_outer(own_at, 0, info, *chain.tie((act, second, first_low, inner))))
    dense, outer, vectors = [], [], []
    dense_steps = sum_steps(dense_plan, chain, keep, got, dense)
    next(dense_steps)
    chain.mark((chain.token, out_pieces))
    block_out = to_positions(out_pieces)
    grads, sums = attend_back(
        held, info, q, k, v, chain.tie(split(mixed_grad)), split(branch_in), stat, sums
    )
    chain.mark(sums)
    grads = grads.reshape(4, total, width)
    sums_steps = vector_steps(chain, sums, vectors)
    next(dense_steps)
    next(sums_steps)
    send = attend_outer(own_at, 1, info, stacked, chain.tie(grads))
    chain.mark(send)
    got = swap(send, first)
    keep = attend_outer(own_at, 0, info, stacked, chain.tie(grads))
    chain.mark(keep)
    next(dense_steps)
    outer_steps = sum_steps(outer_plan, chain, keep, got, outer)
    next(outer_steps)
    next(sums_steps)
    input_low = input_grad(branch_in, chain.tie(grads), w_query, w_key, w_value)
    chain.mark(input_low)
    next(dense_steps)
    next(outer_steps)
    pieces = chain.mark(position_pieces(split(chain.tie(input_low))))
    in_pieces = traded(pieces)
    next(outer_steps)
    next(sums_steps)
    next(dense_steps)
    next(outer_steps)
    next(dense_steps)
    next(outer_steps)
    next(sums_steps)
    chain.mark((chain.token, in_pieces))
    tokens_grad = to_positions(in_pieces)
    for steps in [dense_steps, outer_steps, sums_steps] * 2:
        next(steps)
    for _ in sums_steps:
        pass
    next(outer_steps)
    for _ in dense_steps:
        pass
    vectors = vectors[0]

    def place_dense(flip, before):
        pick = dense[2 * PARTS :] if flip else dense[: 2 * PARTS]
        return chain.mark(
            dense_place(
                dense_plan, dense_at, own_at, flip, info, chain.tie(pick), width, wide, before
            )
        )

    def place_outer(flip, before):
        pick = outer[2 * PARTS :] if flip else outer[: 2 * PARTS]
        return chain.mark(
            attend_place(outer_plan, outer_at, own_at, flip, info, chain.tie(pick), width, before)
        )

    placed = place_dense(0, [])
    for _ in outer_steps:
        pass
    down_sum, up_sum = place_dense(1, placed)
    placed = place_outer(0, [])
    outer = place_outer(1, placed)
    return (
        block_out,
        pooled,
        tokens_grad,
        outer[0],
        vectors[0],
        outer[1],
        outer[2],
        vectors[1],
        outer[3],
        vectors[2],
        vectors[3],
        vectors[4],
        up_sum,
        vectors[8 : 8 + wide].reshape(-1),
        down_sum,
        vectors[5],
        vectors[6],
        vectors[7],
    )


def solution(mesh):
    in_specs = (
        (P("dp", "seq", None), P("dp"))
        + (P(),) * 15
        + (P("dp", "seq", None), P("dp", None))
    )
    out_specs = (P("dp", "seq", None), P("dp", None), P("dp", "seq", None)) + (P(),) * 15
    return jax.shard_map(shards, mesh=mesh, in_specs=in_specs, out_specs=out_specs, check_vma=False)
```

```python
import functools

import jax
import jax.numpy as jnp
from jax import lax
from jax.experimental import pallas as pl
from jax.experimental.pallas import tpu as pltpu
from jax.sharding import PartitionSpec as P

HEADS = 12
HEAD_DIM = 64
PAIR = 2 * HEAD_DIM
PAIRS = HEADS // 2
SCALE = HEAD_DIM ** (-0.5)
ROWS = 256
CHUNK = 256
KEY_STEP = 128
VMEM_BYTES = 62 * 1024 * 1024
SMALL_BYTES = 40 * 1024 * 1024
SUM_ROWS = 16
POOL_ROW = 12

eps = 1e-06
root_half = 0.7071067811865476
inv_root_two_pi = 0.3989422804014327

f32 = jnp.float32
bf16 = jnp.bfloat16

NN = (((1,), (0,)), ((), ()))
NT = (((1,), (1,)), ((), ()))
TN = (((0,), (0,)), ((), ()))


def mul(left, right, dims=NN):
    return lax.dot_general(left, right, dims, preferred_element_type=f32)


def fixed(shape):
    return pl.BlockSpec(shape, lambda *_: (0,) * len(shape), pipeline_mode=pl.Buffered(1))


PARAMS = pltpu.CompilerParams(dimension_semantics=("arbitrary",), vmem_limit_bytes=VMEM_BYTES)
SMALL = pltpu.CompilerParams(dimension_semantics=("arbitrary",), vmem_limit_bytes=SMALL_BYTES)


def cost(flops, moved, exps=0):
    return pl.CostEstimate(flops=int(flops), bytes_accessed=int(moved), transcendentals=int(exps))


def over_extents(length, full, body):
    for extent in range(KEY_STEP, full + 1, KEY_STEP):
        pl.when((length > extent - KEY_STEP) & (length <= extent))(functools.partial(body, extent))


def attend_kernel(pieces, passage, count, held, info_ref, *refs):
    part_refs, refs = refs[:pieces], refs[pieces:]
    wq_ref, wk_ref, wv_ref, vec_ref = refs[:4]
    xm_ref, q_ref, k_ref, v_ref, stat_ref = refs[-5:]
    x_ref, mix_ref = xm_ref.at[0], xm_ref.at[1]
    mine = info_ref[held]
    length = info_ref[mine * count + passage]
    size = part_refs[0].shape[1]
    for mask, part_ref in enumerate(part_refs):
        x_ref[0, pl.ds(pl.multiple_of((mine ^ mask) * size, size), size)] = part_ref[0]
    q_ref[0] = (mul(x_ref[0], wq_ref[...]) + vec_ref[0:1]).astype(bf16)
    stat_ref[0] = jnp.zeros(stat_ref.shape[1:], f32)
    lane = lax.broadcasted_iota(jnp.int32, (1, PAIR), 1)
    full = size * pieces

    def run(extent):
        x = x_ref[0, :extent]
        k_ref[0, :extent] = mul(x, wk_ref[...]).astype(bf16)
        v_ref[0, :extent] = (mul(x, wv_ref[...]) + vec_ref[1:2]).astype(bf16)
        key_at = lax.broadcasted_iota(jnp.int32, (1, extent), 1)
        dead = jnp.where(key_at < length, 0.0, -1e30)

        def pair_step(pair, carry):
            at = pl.ds(pl.multiple_of(pair * PAIR, PAIR), PAIR)
            q, k, v = q_ref[0, :, at], k_ref[0, :extent, at], v_ref[0, :extent, at]
            mixed = []
            stat = stat_ref[0]
            for half in range(2):
                own = (lane >= half * HEAD_DIM) & (lane < (half + 1) * HEAD_DIM)
                q_own = jnp.where(own, q * SCALE, 0).astype(bf16)
                scores = mul(q_own, k, NT) + dead
                top = jnp.max(scores, axis=1, keepdims=True)
                expo = jnp.exp(scores - top)
                total = jnp.sum(expo, axis=1, keepdims=True)
                probs = (expo * (1.0 / total)).astype(bf16)
                mixed.append(mul(probs, v))
                stat = jnp.where(lane == pair * 2 + half, top + jnp.log(total), stat)
            stat_ref[0] = stat
            mix_ref[0, :, at] = jnp.where(lane < HEAD_DIM, mixed[0], mixed[1]).astype(bf16)
            return carry

        lax.fori_loop(0, PAIRS, pair_step, 0)

    over_extents(length, full, run)


def attend(passage, count, info, tokens, parts, weights, before):
    held, piece, width = tokens.shape
    pieces = len(parts) + 1
    full = piece * pieces
    rows = pl.BlockSpec((1, full, width), lambda i, s: (passage, 0, 0))
    act = jax.ShapeDtypeStruct((count, full, width), bf16)
    got = pl.BlockSpec((1, piece, width), lambda i, s: (0, 0, 0))
    kept = [] if before is None else list(before)
    first_kept = 1 + pieces + len(weights)
    return pl.pallas_call(
        functools.partial(attend_kernel, pieces, passage, count, held),
        grid_spec=pltpu.PrefetchScalarGridSpec(
            num_scalar_prefetch=1,
            grid=(1,),
            in_specs=[pl.BlockSpec((1, piece, width), lambda i, s: (s[held] * count + passage, 0, 0))]
            + [got] * len(parts)
            + [fixed(w.shape) for w in weights]
            + [pl.BlockSpec(memory_space=pl.ANY)] * len(kept),
            out_specs=[pl.BlockSpec((2, 1, full, width), lambda i, s: (0, passage, 0, 0))]
            + [rows] * 3
            + [pl.BlockSpec((1, full, PAIR), lambda i, s: (passage, 0, 0))],
        ),
        out_shape=[jax.ShapeDtypeStruct((2, count, full, width), bf16)]
        + [act] * 3
        + [jax.ShapeDtypeStruct((count, full, PAIR), f32)],
        input_output_aliases={first_kept + i: i for i in range(len(kept))},
        compiler_params=PARAMS,
        cost_estimate=cost(
            2 * full * (3 * width * width + 4 * 2 * full * width),
            12 * full * width + 6 * width * width,
        ),
    )(info, tokens, *parts, *weights, *kept)


def attend_back_kernel(
    held, info_ref, q_ref, k_ref, v_ref, mg_ref, branch_ref, stat_ref, sum_ref, grads_ref, word_ref, log_ref, bias_ref
):
    dq_ref, dk_ref, dv_ref = (grads_ref.at[i] for i in range(3))
    grads_ref[3] = branch_ref[...].astype(bf16)
    full = q_ref.shape[1]
    length = info_ref[info_ref[held] * pl.num_programs(0) + pl.program_id(0)]
    lane = lax.broadcasted_iota(jnp.int32, (1, PAIR), 1)
    log_ref[...] = stat_ref[0].T
    row = lax.broadcasted_iota(jnp.int32, (8, 1), 0)

    @pl.when(pl.program_id(0) == 0)
    def _():
        bias_ref[...] = sum_ref[...]

    def run(extent):
        key_at = lax.broadcasted_iota(jnp.int32, (extent, 1), 0)
        dead = jnp.where(key_at < length, 0.0, -1e30)
        if extent < full:
            dk_ref[0, extent:] = jnp.zeros((full - extent, dk_ref.shape[2]), bf16)
            dv_ref[0, extent:] = jnp.zeros((full - extent, dv_ref.shape[2]), bf16)

        def pair_step(pair, carry):
            at = pl.ds(pl.multiple_of(pair * PAIR, PAIR), PAIR)
            q, mg = q_ref[0, :, at], mg_ref[0, :, at]
            k, v = k_ref[0, :extent, at], v_ref[0, :extent, at]
            dq, dk, dv = [], [], []
            for half in range(2):
                own = (lane >= half * HEAD_DIM) & (lane < (half + 1) * HEAD_DIM)
                k_own = jnp.where(own, k * SCALE, 0).astype(bf16)
                v_own = jnp.where(own, v, 0).astype(bf16)
                log_row = log_ref[pl.ds(pair * 2 + half, 1), :]
                probs = jnp.exp(mul(k_own, q, NT) + dead - log_row)
                prob_grad = mul(v_own, mg, NT)
                along = jnp.sum(probs * prob_grad, axis=0, keepdims=True)
                score_grad = (probs * (prob_grad - along)).astype(bf16)
                dv.append(mul(probs.astype(bf16), mg))
                dk.append(mul(score_grad, q))
                dq.append(mul(score_grad, k, TN))
            first = lane < HEAD_DIM
            dq_pair = jnp.where(first, dq[0], dq[1]) * SCALE
            dk_pair = jnp.where(first, dk[0], dk[1]) * SCALE
            dv_pair = jnp.where(first, dv[0], dv[1])
            dq_ref[0, :, at] = dq_pair.astype(bf16)
            dk_ref[0, :extent, at] = dk_pair.astype(bf16)
            dv_ref[0, :extent, at] = dv_pair.astype(bf16)
            sums = jnp.where(
                row == 0,
                jnp.sum(dq_pair, axis=0, keepdims=True),
                jnp.where(row == 1, jnp.sum(dv_pair, axis=0, keepdims=True), 0.0),
            )
            bias_ref[0:8, at] += sums
            return carry

        lax.fori_loop(0, PAIRS, pair_step, 0)

    over_extents(length, full, run)

    @pl.when(pl.program_id(0) == pl.num_programs(0) - 1)
    def _():
        high = bias_ref[...].astype(bf16)
        word_ref[:SUM_ROWS] = high
        word_ref[SUM_ROWS:] = (bias_ref[...] - high.astype(f32)).astype(bf16)


def attend_back(held, info, q, k, v, mixed_grad, branch_in, stat, sums):
    count, full, width = q.shape
    rows = pl.BlockSpec((1, full, width), lambda i, *_: (i, 0, 0))
    return pl.pallas_call(
        functools.partial(attend_back_kernel, held),
        grid_spec=pltpu.PrefetchScalarGridSpec(
            num_scalar_prefetch=1,
            grid=(count,),
            in_specs=[rows] * 5
            + [pl.BlockSpec((1, full, PAIR), lambda i, *_: (i, 0, 0)), fixed(sums.shape)],
            out_specs=[
                pl.BlockSpec((4, 1, full, width), lambda i, *_: (0, i, 0, 0)),
                pl.BlockSpec((2 * SUM_ROWS, width), lambda i, *_: (0, 0)),
            ],
            scratch_shapes=[pltpu.VMEM((PAIR, full), f32), pltpu.VMEM(sums.shape, f32)],
        ),
        out_shape=[
            jax.ShapeDtypeStruct((4, count, full, width), bf16),
            jax.ShapeDtypeStruct((2 * SUM_ROWS, width), bf16),
        ],
        compiler_params=PARAMS,
        cost_estimate=cost(
            2 * count * full * 10 * 2 * full * width, 14 * count * full * width
        ),
    )(info, q, k, v, mixed_grad, branch_in, stat, sums)


def norm_parts(hidden):
    centred = hidden - jnp.mean(hidden, axis=1, keepdims=True)
    inv_scale = lax.rsqrt(jnp.mean(centred * centred, axis=1, keepdims=True) + eps)
    return centred * inv_scale, inv_scale


def norm_back(scaled, normed, inv_scale):
    mean = jnp.mean(scaled, axis=1, keepdims=True)
    along = jnp.mean(scaled * normed, axis=1, keepdims=True)
    return (scaled - mean - normed * along) * inv_scale


def gelu_parts(u):
    expo = jnp.exp(u * u * -0.5)
    base = 1.0 + jnp.abs(u) * (0.3275911 * root_half)
    t = pl.reciprocal(base, approx=True)
    t = t * (2.0 - base * t)
    poly = t * (
        0.5 * 0.254829592
        + t
        * (
            0.5 * -0.284496736
            + t * (0.5 * 1.421413741 + t * (0.5 * -1.453152027 + t * (0.5 * 1.061405429)))
        )
    )
    tail = poly * expo
    return jnp.where(u >= 0, 1.0 - tail, tail), expo


def rows_kernel(
    blocks,
    count,
    held,
    info_ref,
    x_ref,
    mix_ref,
    cot_ref,
    pool_ref,
    wo_ref,
    wu_ref,
    wd_ref,
    vec_ref,
    out_ref,
    low_ref,
    act_ref,
    second_ref,
    inner_ref,
    branch_ref,
    mg_ref,
    sum_ref,
    slope_ref,
):
    step = pl.program_id(0)
    rows, width = cot_ref.shape
    hidden_width = wu_ref.shape[1]
    b_out, gain_one, shift_one, b_down, gain_two, shift_two = (
        vec_ref[i : i + 1] for i in range(2, 8)
    )
    passage = info_ref[held] * count + step // blocks
    length = info_ref[passage]
    inv_length = 1.0 / jnp.full((1, width), length, jnp.int32).astype(f32)
    row_at = lax.broadcasted_iota(jnp.int32, (rows, 1), 0) + (step % blocks) * rows
    live = jnp.where(row_at < length, 1.0, 0.0)

    @pl.when(step == 0)
    def _():
        sum_ref[...] = jnp.zeros(sum_ref.shape, f32)

    def tally(at, value, columns=slice(None)):
        sum_ref[at : at + 1, columns] += jnp.sum(value, axis=0, keepdims=True)

    groups = width // CHUNK
    chunks = hidden_width // CHUNK
    part = [slice(i * CHUNK, (i + 1) * CHUNK) for i in range(chunks)]
    whole = [slice(i * width, (i + 1) * width) for i in range(hidden_width // width)]

    hidden = x_ref[0].astype(f32) + mul(mix_ref[0], wo_ref[...]) + b_out
    normed_one, scale_one = norm_parts(hidden)
    first = normed_one * gain_one + shift_one
    first_low = first.astype(bf16)
    low_ref[...] = first_low
    hidden = first + b_down

    def up(i):
        return mul(first_low, wu_ref[:, part[i]]) + vec_ref[8 + i // groups : 9 + i // groups, part[i % groups]]

    def activate(i, pre):
        phi, expo = gelu_parts(pre)
        act_ref[:, part[i]] = (pre * phi).astype(bf16)
        slope_ref[:, part[i]] = phi + pre * expo * inv_root_two_pi

    pre = up(0)
    for i in range(chunks):
        ahead = up(i + 1) if i + 1 < chunks else None
        activate(i, pre)
        if i % groups == 0 and i:
            done = whole[i // groups - 1]
            hidden += mul(act_ref[:, done], wd_ref[done, :])
        pre = ahead
    hidden += mul(act_ref[:, whole[-1]], wd_ref[whole[-1], :])

    normed_two, scale_two = norm_parts(hidden)
    result = normed_two * gain_two + shift_two
    out_ref[...] = result.astype(bf16)
    sum_ref[pl.ds(POOL_ROW + step // blocks, 1), :] += (
        jnp.sum(result * live, axis=0, keepdims=True) * inv_length
    )

    upstream = cot_ref[...].astype(f32) + live * (pool_ref[pl.ds(passage, 1), :] * inv_length)
    tally(6, upstream * normed_two)
    tally(7, upstream)
    second_in = norm_back(upstream * gain_two, normed_two, scale_two)
    tally(5, second_in)
    second = second_in.astype(bf16)
    second_ref[...] = second
    first_up = second_in

    def back(i):
        return mul(second, wd_ref[part[i], :], NT)

    grad = back(0)
    for i in range(chunks):
        ahead = back(i + 1) if i + 1 < chunks else None
        inner = grad * slope_ref[:, part[i]]
        tally(8 + i // groups, inner, part[i % groups])
        inner_ref[:, part[i]] = inner.astype(bf16)
        if i % groups == 0 and i:
            done = whole[i // groups - 1]
            first_up += mul(inner_ref[:, done], wu_ref[:, done], NT)
        grad = ahead
    first_up += mul(inner_ref[:, whole[-1]], wu_ref[:, whole[-1]], NT)

    tally(3, first_up * normed_one)
    tally(4, first_up)
    branch_in = norm_back(first_up * gain_one, normed_one, scale_one)
    tally(2, branch_in)
    branch_ref[...] = branch_in
    mg_ref[...] = mul(branch_in.astype(bf16), wo_ref[...], NT).astype(bf16)


def row_work(held, info, stacked, cot, pool, w_out, w_up, w_down, vecs, count):
    total, width = cot.shape
    full = total // count
    assert POOL_ROW + count <= SUM_ROWS
    hidden = w_up.shape[1]
    blocks = full // ROWS
    narrow = pl.BlockSpec((ROWS, width), lambda i, *_: (i, 0))
    broad = pl.BlockSpec((ROWS, hidden), lambda i, *_: (i, 0))
    thin = jax.ShapeDtypeStruct((total, width), bf16)
    thick = jax.ShapeDtypeStruct((total, hidden), bf16)
    return pl.pallas_call(
        functools.partial(rows_kernel, blocks, count, held),
        grid_spec=pltpu.PrefetchScalarGridSpec(
            num_scalar_prefetch=1,
            grid=(total // ROWS,),
            in_specs=[
                pl.BlockSpec((1, ROWS, width), lambda i, *_: (0, i, 0)),
                pl.BlockSpec((1, ROWS, width), lambda i, *_: (1, i, 0)),
                narrow,
                fixed(pool.shape),
                fixed((width, width)),
                fixed((width, hidden)),
                fixed((hidden, width)),
                fixed(vecs.shape),
            ],
            out_specs=[
                narrow,
                narrow,
                broad,
                narrow,
                broad,
                narrow,
                narrow,
                pl.BlockSpec((SUM_ROWS, width), lambda i, *_: (0, 0)),
            ],
            scratch_shapes=[pltpu.VMEM((ROWS, hidden), f32)],
        ),
        out_shape=[
            thin,
            thin,
            thick,
            thin,
            thick,
            jax.ShapeDtypeStruct((total, width), f32),
            thin,
            jax.ShapeDtypeStruct((SUM_ROWS, width), f32),
        ],
        compiler_params=PARAMS,
        cost_estimate=cost(
            4 * total * width * (width + 2 * hidden),
            2 * total * (8 * width + 2 * hidden) + 2 * width * (width + 2 * hidden),
        ),
    )(info, stacked, stacked, cot, pool, w_out, w_up, w_down, vecs)


def dense_outer_kernel(side_ref, act_ref, second_ref, low_ref, inner_ref, out_ref):
    step = pl.program_id(0)
    half = pl.num_programs(0) // 2

    @pl.when(step < half)
    def _():
        out_ref[0] = mul(act_ref[...], second_ref[...], TN).astype(bf16)

    @pl.when(step >= half)
    def _():
        out_ref[0] = mul(low_ref[...], inner_ref[...], TN).astype(bf16)


def dense_outer(at, flip, info, act, second, low, inner):
    total, width = second.shape
    wide = act.shape[1] // width
    half = wide // 2
    return pl.pallas_call(
        dense_outer_kernel,
        grid_spec=pltpu.PrefetchScalarGridSpec(
            num_scalar_prefetch=1,
            grid=(wide,),
            in_specs=[
                pl.BlockSpec(
                    (total, width), lambda i, s: (0, (s[at] ^ flip) * half + jnp.minimum(i, half - 1))
                ),
                fixed((total, width)),
                fixed((total, width)),
                pl.BlockSpec(
                    (total, width), lambda i, s: (0, (s[at] ^ flip) * half + jnp.maximum(i - half, 0))
                ),
            ],
            out_specs=pl.BlockSpec((1, width, width), lambda i, s: (i, 0, 0)),
        ),
        out_shape=jax.ShapeDtypeStruct((wide, width, width), bf16),
        compiler_params=SMALL,
        cost_estimate=cost(
            2 * total * width * width * wide, 2 * (wide + 2) * total * width + 2 * wide * width * width
        ),
    )(info, act, second, low, inner).reshape(wide * width, width)


def attend_outer_kernel(side_ref, left_ref, right_ref, out_ref):
    out_ref[0] = mul(left_ref[0], right_ref[0], TN).astype(bf16)


def attend_outer(at, flip, info, stacked, grads):
    total, width = stacked.shape[1:]
    return pl.pallas_call(
        attend_outer_kernel,
        grid_spec=pltpu.PrefetchScalarGridSpec(
            num_scalar_prefetch=1,
            grid=(2,),
            in_specs=[
                pl.BlockSpec((1, total, width), lambda i, s: (((s[at] ^ flip) * 2 + i) // 3, 0, 0)),
                pl.BlockSpec((1, total, width), lambda i, s: ((s[at] ^ flip) * 2 + i, 0, 0)),
            ],
            out_specs=pl.BlockSpec((1, width, width), lambda i, s: (i, 0, 0)),
        ),
        out_shape=jax.ShapeDtypeStruct((2, width, width), bf16),
        compiler_params=SMALL,
        cost_estimate=cost(4 * total * width * width, 8 * total * width + 4 * width * width),
    )(info, stacked, grads).reshape(2 * width, width)


def input_kernel(branch_ref, dq_ref, dk_ref, dv_ref, wq_ref, wk_ref, wv_ref, out_ref):
    total = branch_ref[...] + mul(dq_ref[0], wq_ref[...], NT)
    total += mul(dk_ref[0], wk_ref[...], NT)
    total += mul(dv_ref[0], wv_ref[...], NT)
    out_ref[...] = total.astype(bf16)


def input_grad(branch_in, grads, w_query, w_key, w_value):
    total, width = branch_in.shape
    rows = pl.BlockSpec((ROWS, width), lambda i: (i, 0))
    return pl.pallas_call(
        input_kernel,
        grid=(total // ROWS,),
        in_specs=[rows]
        + [pl.BlockSpec((1, ROWS, width), lambda i, at=at: (at, i, 0)) for at in range(3)]
        + [fixed((width, width))] * 3,
        out_specs=rows,
        out_shape=jax.ShapeDtypeStruct((total, width), bf16),
        compiler_params=SMALL,
        cost_estimate=cost(6 * total * width * width, 12 * total * width + 6 * width * width),
    )(branch_in, grads, grads, grads, w_query, w_key, w_value)


def exchange(value, axis, mask):
    count = lax.axis_size(axis)
    return lax.ppermute(value, axis, [(i, i ^ mask) for i in range(count)])


def to_passages(value):
    count = lax.axis_size("seq")
    mine = lax.axis_index("seq")
    held, piece, width = value.shape
    own = held // count
    whole = jnp.zeros((own, piece * count, width), value.dtype)
    for mask in range(count):
        peer = mine ^ mask
        part = lax.dynamic_slice_in_dim(value, peer * own, own, 0)
        if mask:
            part = exchange(part, "seq", mask)
        whole = lax.dynamic_update_slice_in_dim(whole, part, peer * piece, 1)
    return whole


def position_pieces(value):
    count = lax.axis_size("seq")
    piece = value.shape[1] // count
    mine = lax.axis_index("seq")
    return [
        lax.dynamic_slice_in_dim(value, (mine ^ mask) * piece, piece, 1) for mask in range(count)
    ]


def traded(pieces):
    return [exchange(part, "seq", mask) if mask else part for mask, part in enumerate(pieces)]


def to_positions(pieces):
    mine = lax.axis_index("seq")
    own, piece, width = pieces[0].shape
    result = jnp.zeros((own * len(pieces), piece, width), pieces[0].dtype)
    for mask, part in enumerate(pieces):
        result = lax.dynamic_update_slice_in_dim(result, part, (mine ^ mask) * own, 0)
    return result


def axis_bits(axis):
    return [(axis, 1 << i) for i in range(lax.axis_size(axis).bit_length() - 1)]


def upper(dim):
    axis, mask = dim
    return (lax.axis_index(axis) & mask) // mask


def swap(value, dim):
    return exchange(value, dim[0], dim[1])


def total_of(parts):
    total = parts[0].astype(f32)
    for part in parts[1:]:
        total += part.astype(f32)
    return total.astype(bf16)


PARTS = 3
SHARD_STEP = 16


class Plan:
    def __init__(self, rows):
        dims = axis_bits("seq") + axis_bits("dp")
        self.first = dims[0]
        rest = dims[1:]
        self.rows = rows // PARTS
        halved = 0
        while halved < len(rest) and (self.rows >> (halved + 1)) % SHARD_STEP == 0:
            halved += 1
        self.last = rest[halved - 1]
        self.plain = rest[halved:]
        split = rest[: halved - 1]
        self.orders = [split[i % len(split) :] + split[: i % len(split)] for i in range(PARTS)]
        self.shards = 1 << halved
        self.shard = self.rows >> halved

    def table(self, blocks, width, each):
        places = {}
        devices = 1
        weight = {}
        for axis in ("seq", "dp"):
            for _, mask in axis_bits(axis):
                weight[(axis, mask)] = devices
                devices *= 2
        for side in range(2):
            for part, order in enumerate(self.orders):
                dims = [self.last] + order[::-1]
                for code in range(self.shards):
                    device = side * weight[self.first]
                    device += sum(weight[d] for i, d in enumerate(dims) if (code >> i) & 1)
                    row = part * self.rows + code * self.shard
                    places[side, row] = device * each + part * self.shard
        half = blocks // 4
        found = []
        for block in range(blocks):
            side = block % (2 * half) // half
            local = block // (2 * half) * half + block % half
            for row in range(0, width, self.shard):
                found.append(places[side, local * width + row])
        return found

    def codes(self):
        found = []
        for order in self.orders:
            code = upper(self.last)
            for at, dim in enumerate(reversed(order)):
                code += upper(dim) << (at + 1)
            found.append(code)
        return [code.astype(jnp.int32) for code in found]


class Chain:
    def __init__(self):
        self.token = None

    def tie(self, values):
        if self.token is None:
            return values
        return lax.optimization_barrier((values, self.token))[0]

    def mark(self, values):
        self.token = values
        return values


def scatter_steps(plan, chain, keep, got, found):
    pairs = [[keep, got]] * PARTS
    bases = [i * plan.rows for i in range(PARTS)]
    size = plan.rows
    for step in range(len(plan.orders[0])):
        pairs = chain.tie(pairs)
        size //= 2
        dims = [order[step] for order in plan.orders]

        def halves(pair, base, at):
            return total_of([lax.dynamic_slice_in_dim(p, base + at * size, size, 0) for p in pair])

        sends = [halves(p, base, 1 - upper(d)) for p, base, d in zip(pairs, bases, dims)]
        chain.mark(sends)
        mine = [halves(p, base, upper(d)) for p, base, d in zip(pairs, bases, dims)]
        pairs = [[m, swap(s, d)] for m, s, d in zip(mine, sends, dims)]
        bases = [0] * PARTS
        yield
    size = plan.shard
    bit = upper(plan.last)
    pairs = chain.tie(pairs)

    def side(at):
        return jnp.concatenate(
            [total_of([lax.dynamic_slice_in_dim(p, at * size, size, 0) for p in pair]) for pair in pairs],
            axis=0,
        )

    send = chain.mark(side(1 - bit))
    shard = side(bit)
    got = swap(send, plan.last)
    yield
    shard, got = chain.tie((shard, got))
    shard = total_of([shard, got])
    for dim in plan.plain:
        shard = total_of([shard, swap(shard, dim)])
    found.append(chain.mark(shard))
    yield


def gather_steps(plan, chain, shard, found):
    size = plan.shard
    got = swap(shard, plan.last)
    yield
    values = [(shard[i * size : (i + 1) * size], got[i * size : (i + 1) * size]) for i in range(PARTS)]
    for step in reversed(range(len(plan.orders[0]))):
        values = chain.tie(values)
        values = [jnp.concatenate(pair, axis=0) for pair in values]
        chain.mark(values)
        values = [(v, swap(v, order[step])) for v, order in zip(values, plan.orders)]
        yield
    values = chain.tie(values)
    chain.mark(values)
    found += [v for pair in values for v in pair]
    found += [swap(v, plan.first) for v in found]
    yield


def place(plan, refs, codes, row, store):
    part = row // plan.rows
    shard = ((row % plan.rows) // plan.shard) ^ codes[part]
    half = plan.shards // 2
    at = pl.ds(pl.multiple_of((shard & (half - 1)) * plan.shard, plan.shard), plan.shard)
    low, high = refs[2 * part][at, :], refs[2 * part + 1][at, :]
    store(jnp.where(shard >= half, high.astype(f32), low.astype(f32)))


def dense_place_kernel(
    shard, each, held, table_ref, info_ref, all_ref, down_ref, up_ref, vec_ref, pool_ref, hold_ref, word_ref, sems, word_sem
):
    step, steps = pl.program_id(0), pl.num_programs(0)
    width = down_ref.shape[1]
    parts = width // shard

    def fetch(block, slot):
        for i in range(parts):
            at = pl.multiple_of(table_ref[block * parts + i], SHARD_STEP)
            pltpu.make_async_copy(
                all_ref.at[pl.ds(at, shard)],
                hold_ref.at[slot, pl.ds(i * shard, shard)],
                sems.at[slot],
            ).start()

    def words(device):
        return pltpu.make_async_copy(
            all_ref.at[pl.ds(device * each + each - 2 * SUM_ROWS, 2 * SUM_ROWS)],
            word_ref.at[device],
            word_sem,
        )

    devices = word_ref.shape[0]

    @pl.when(step == 0)
    def _():
        fetch(0, 0)
        for device in range(devices):
            words(device).start()

    @pl.when(step + 1 < steps)
    def _():
        fetch(step + 1, (step + 1) % 2)

    slot = step % 2
    pltpu.make_async_copy(all_ref.at[pl.ds(0, width)], hold_ref.at[slot], sems.at[slot]).wait()

    @pl.when(step < steps // 2)
    def _():
        down_ref[...] = hold_ref[slot].astype(f32)

    @pl.when(step >= steps // 2)
    def _():
        up_ref[...] = hold_ref[slot].astype(f32)

    @pl.when(step == steps - 1)
    def _():
        pltpu.make_async_copy(word_ref, word_ref, word_sem).wait()

        def both(device):
            return word_ref[device, :SUM_ROWS].astype(f32) + word_ref[device, SUM_ROWS:].astype(f32)

        vec_ref[...] = lax.fori_loop(
            0, devices, lambda i, total: total + both(i), jnp.zeros(vec_ref.shape, f32)
        )
        group = pool_ref.shape[0]
        for i in range(group):
            pool_ref[i] = both(info_ref[held] + i)[POOL_ROW:]


def dense_place(plan, gathered, each, width, wide, devices, seq_count, group):
    table = jnp.array(plan.table(2 * wide, width, each), jnp.int32)
    return pl.pallas_call(
        functools.partial(dense_place_kernel, plan.shard, each, 0),
        grid_spec=pltpu.PrefetchScalarGridSpec(
            num_scalar_prefetch=2,
            grid=(2 * wide,),
            in_specs=[pl.BlockSpec(memory_space=pl.ANY)],
            out_specs=[
                pl.BlockSpec((width, width), lambda i, *_: (jnp.minimum(i, wide - 1), 0)),
                pl.BlockSpec((width, width), lambda i, *_: (0, jnp.maximum(i - wide, 0))),
                pl.BlockSpec((SUM_ROWS, width), lambda i, *_: (0, 0)),
                pl.BlockSpec((seq_count, SUM_ROWS - POOL_ROW, width), lambda i, *_: (0, 0, 0)),
            ],
            scratch_shapes=[
                pltpu.VMEM((2, width, width), bf16),
                pltpu.VMEM((devices, 2 * SUM_ROWS, width), bf16),
                pltpu.SemaphoreType.DMA((2,)),
                pltpu.SemaphoreType.DMA(()),
            ],
        ),
        out_shape=[
            jax.ShapeDtypeStruct((wide * width, width), f32),
            jax.ShapeDtypeStruct((width, wide * width), f32),
            jax.ShapeDtypeStruct((SUM_ROWS, width), f32),
            jax.ShapeDtypeStruct((seq_count, SUM_ROWS - POOL_ROW, width), f32),
        ],
        compiler_params=SMALL,
        cost_estimate=cost(0, 12 * wide * width * width),
    )(table, group, gathered)


def attend_place_kernel(plan, first_code, at, flip, info_ref, *refs):
    sources, (hold_ref, sems) = refs[: 2 * PARTS], refs[-2:]
    outs = refs[-6:-2]
    codes = [info_ref[first_code + i] for i in range(PARTS)]
    own = info_ref[at] ^ flip
    width = hold_ref.shape[2]

    def move(block, act):
        for side in range(2):

            @pl.when(own == side)
            def _():
                act(pltpu.make_async_copy(hold_ref.at[block], outs[2 * side + block], sems.at[block]))

    for block in range(2):
        for row in range(0, width, plan.shard):

            def store(value, row=row):
                hold_ref[block, row : row + plan.shard, :] = value

            place(plan, sources, codes, block * width + row, store)
        move(block, lambda copy: copy.start())
    for block in range(2):
        move(block, lambda copy: copy.wait())


def attend_place(plan, first_code, at, flip, info, sources, width, before):
    kept = list(before)
    return pl.pallas_call(
        functools.partial(attend_place_kernel, plan, first_code, at, flip),
        grid_spec=pltpu.PrefetchScalarGridSpec(
            num_scalar_prefetch=1,
            grid=(1,),
            in_specs=[fixed(x.shape) for x in sources]
            + [pl.BlockSpec(memory_space=pl.ANY)] * len(kept),
            out_specs=[pl.BlockSpec(memory_space=pl.ANY)] * 4,
            scratch_shapes=[pltpu.VMEM((2, width, width), f32), pltpu.SemaphoreType.DMA((2,))],
        ),
        out_shape=[jax.ShapeDtypeStruct((width, width), f32)] * 4,
        input_output_aliases={1 + len(sources) + i: i for i in range(len(kept))},
        compiler_params=SMALL,
        cost_estimate=cost(0, 12 * width * width),
    )(info, *sources, *kept)


def shards(
    tokens,
    lengths,
    w_query,
    b_query,
    w_key,
    w_value,
    b_value,
    w_out,
    b_out,
    gain_one,
    shift_one,
    w_up,
    b_up,
    w_down,
    b_down,
    gain_two,
    shift_two,
    out_grad,
    pooled_grad,
):
    seq_count = lax.axis_size("seq")
    held, piece, width = tokens.shape
    full = piece * seq_count
    count = held // seq_count
    mine = lax.axis_index("seq")
    wide = w_up.shape[1] // width
    total = count * full

    def flat(value):
        return value.reshape(total, width)

    def split(value):
        return value.reshape(count, full, width)

    dense_plan = Plan(wide * width)
    outer_plan = Plan(2 * width)
    first = axis_bits("seq")[0]
    scalars = [mine, upper(first)] + dense_plan.codes() + outer_plan.codes()
    own_at, dense_at, outer_at = held + 1, held + 2, held + 2 + PARTS
    info = jnp.concatenate([lengths, jnp.stack([v.astype(jnp.int32) for v in scalars])])
    vecs = jnp.concatenate(
        [b_query, b_value, b_out, gain_one, shift_one, b_down, gain_two, shift_two, b_up]
    )
    vecs = vecs.astype(f32).reshape(-1, width)

    weights = [w_query, w_key, w_value, vecs]
    done = None
    source = tokens
    parts = []
    for passage in range(count):
        if parts:
            source = lax.optimization_barrier((tokens, parts))[0]
        parts = [
            exchange(
                lax.dynamic_slice_in_dim(source, (mine ^ mask) * count + passage, 1, 0), "seq", mask
            )
            for mask in range(1, seq_count)
        ]
        done = attend(passage, count, info, tokens, parts, weights, done)
    stacked, q, k, v, stat = done
    cot = to_passages(lax.optimization_barrier((out_grad, parts))[0])
    stacked = stacked.reshape(2, total, width)
    result, first_low, act, second, inner, branch_in, mixed_grad, sums = row_work(
        held, info, stacked, flat(cot), pooled_grad, w_out, w_up, w_down, vecs, count
    )
    chain = Chain()
    pieces = chain.mark(position_pieces(split(result)))
    out_pieces = traded(pieces)
    send = dense_outer(own_at, 1, info, *chain.tie((act, second, first_low, inner)))
    chain.mark(send)
    got = swap(send, first)
    keep = chain.mark(dense_outer(own_at, 0, info, *chain.tie((act, second, first_low, inner))))
    dense, shard, outer = [], [], []
    dense_steps = scatter_steps(dense_plan, chain, keep, got, dense)
    next(dense_steps)
    chain.mark((chain.token, out_pieces))
    block_out = to_positions(out_pieces)
    grads, words = attend_back(
        held, info, q, k, v, chain.tie(split(mixed_grad)), split(branch_in), stat, sums
    )
    chain.mark(words)
    grads = grads.reshape(4, total, width)
    next(dense_steps)
    send = attend_outer(own_at, 1, info, stacked, chain.tie(grads))
    chain.mark(send)
    got = swap(send, first)
    keep = attend_outer(own_at, 0, info, stacked, chain.tie(grads))
    chain.mark(keep)
    next(dense_steps)
    outer_steps = scatter_steps(outer_plan, chain, keep, got, shard)
    next(outer_steps)
    input_low = input_grad(branch_in, chain.tie(grads), w_query, w_key, w_value)
    chain.mark(input_low)
    next(dense_steps)
    next(outer_steps)
    for _ in dense_steps:
        pass
    gathered = jnp.concatenate([dense[0], words], axis=0)
    each = gathered.shape[0]
    gathered = chain.mark(gathered)
    gathered = lax.all_gather(gathered, ("dp", "seq"), axis=0, tiled=True)
    next(outer_steps)
    next(outer_steps)
    pieces = chain.mark(position_pieces(split(chain.tie(input_low))))
    in_pieces = traded(pieces)
    for _ in outer_steps:
        pass
    outer_steps = gather_steps(outer_plan, chain, shard[0], outer)
    next(outer_steps)
    next(outer_steps)
    next(outer_steps)
    chain.mark((chain.token, in_pieces))
    tokens_grad = to_positions(in_pieces)
    for _ in outer_steps:
        pass
    group = (lax.axis_index("dp") * seq_count).astype(jnp.int32)[None]
    down_sum, up_sum, vectors, pooled = dense_place(
        dense_plan, chain.tie(gathered), each, width, wide, gathered.shape[0] // each, seq_count, group
    )
    pooled = pooled[:, :count].reshape(held, width)

    def place_outer(flip, before):
        pick = outer[2 * PARTS :] if flip else outer[: 2 * PARTS]
        return chain.mark(
            attend_place(outer_plan, outer_at, own_at, flip, info, chain.tie(pick), width, before)
        )

    placed = place_outer(0, [])
    outer = place_outer(1, placed)
    return (
        block_out,
        pooled,
        tokens_grad,
        outer[0],
        vectors[0],
        outer[1],
        outer[2],
        vectors[1],
        outer[3],
        vectors[2],
        vectors[3],
        vectors[4],
        up_sum,
        vectors[8 : 8 + wide].reshape(-1),
        down_sum,
        vectors[5],
        vectors[6],
        vectors[7],
    )


def solution(mesh):
    in_specs = (
        (P("dp", "seq", None), P("dp"))
        + (P(),) * 15
        + (P("dp", "seq", None), P("dp", None))
    )
    out_specs = (P("dp", "seq", None), P("dp", None), P("dp", "seq", None)) + (P(),) * 15
    return jax.shard_map(shards, mesh=mesh, in_specs=in_specs, out_specs=out_specs, check_vma=False)
```

```python
import functools

import jax
import jax.numpy as jnp
from jax import lax
from jax.experimental import pallas as pl
from jax.experimental.pallas import tpu as pltpu
from jax.sharding import PartitionSpec as P

HEADS = 12
HEAD_DIM = 64
PAIR = 2 * HEAD_DIM
PAIRS = HEADS // 2
SCALE = HEAD_DIM ** (-0.5)
ROWS = 512
BACK_ROWS = 256
STRIP = 32
TOGETHER = 3
STAT_ROWS = 16
CHUNK = 256
KEY_STEP = 128
VMEM_BYTES = 62 * 1024 * 1024
SMALL_BYTES = 40 * 1024 * 1024
SUM_ROWS = 16
POOL_ROW = 12

eps = 1e-06
root_half = 0.7071067811865476
inv_root_two_pi = 0.3989422804014327

f32 = jnp.float32
bf16 = jnp.bfloat16

NN = (((1,), (0,)), ((), ()))
NT = (((1,), (1,)), ((), ()))
TN = (((0,), (0,)), ((), ()))


def mul(left, right, dims=NN):
    return lax.dot_general(left, right, dims, preferred_element_type=f32)


def fixed(shape):
    return pl.BlockSpec(shape, lambda *_: (0,) * len(shape), pipeline_mode=pl.Buffered(1))


PARAMS = pltpu.CompilerParams(dimension_semantics=("arbitrary",), vmem_limit_bytes=VMEM_BYTES)
SMALL = pltpu.CompilerParams(dimension_semantics=("arbitrary",), vmem_limit_bytes=SMALL_BYTES)


def cost(flops, moved, exps=0):
    return pl.CostEstimate(flops=int(flops), bytes_accessed=int(moved), transcendentals=int(exps))


def over_extents(length, full, body):
    for extent in range(KEY_STEP, full + 1, KEY_STEP):
        pl.when((length > extent - KEY_STEP) & (length <= extent))(functools.partial(body, extent))


def by_eight(value):
    return value.reshape(value.shape[0] // 8, 8, value.shape[1])


def fill_dead(dead_ref, extent, length):
    key_at = lax.broadcasted_iota(jnp.int32, dead_ref.shape, 0) + (extent - KEY_STEP)
    dead_ref[...] = jnp.where(key_at < length, 0.0, -1e30)


def live_strip(scores, dead_ref, extent, row):
    strip = scores[row : row + STRIP]
    last = row - (extent - KEY_STEP)
    return strip + dead_ref[last : last + STRIP] if last >= 0 else strip


def attend_kernel(pieces, passage, count, held, info_ref, *refs):
    part_refs, refs = refs[:pieces], refs[pieces:]
    wq_ref, wk_ref, wv_ref, vec_ref = refs[:4]
    xm_ref, q_ref, k_ref, v_ref, stat_ref, prob_ref, dead_ref = refs[-7:]
    x_ref, mix_ref = xm_ref.at[0], xm_ref.at[1]
    mine = info_ref[held]
    length = info_ref[mine * count + passage]
    size = part_refs[0].shape[1]
    for mask, part_ref in enumerate(part_refs):
        x_ref[0, pl.ds(pl.multiple_of((mine ^ mask) * size, size), size)] = part_ref[0]
    q_ref[0] = (mul(x_ref[0], wq_ref[...]) + vec_ref[0:1]).astype(bf16)
    stat_ref[0] = jnp.zeros(stat_ref.shape[1:], f32)
    full = size * pieces
    lane = lax.broadcasted_iota(jnp.int32, (1, PAIR), 1)

    def run(extent):
        x = x_ref[0, :extent]
        k_ref[0, :extent] = mul(x, wk_ref[...]).astype(bf16)
        v_ref[0, :extent] = (mul(x, wv_ref[...]) + vec_ref[1:2]).astype(bf16)
        fill_dead(dead_ref, extent, length)

        def head(at, number, half, slot):
            q, k = q_ref[0, :, at], k_ref[0, :extent, at]
            own = (lane >= half * HEAD_DIM) & (lane < (half + 1) * HEAD_DIM)
            scores = mul(jnp.where(own, k * SCALE, 0).astype(bf16), q, NT)
            top = jnp.full((8, full), -jnp.inf, f32)
            for row in range(0, extent, STRIP):
                top = jnp.maximum(top, by_eight(live_strip(scores, dead_ref, extent, row)).max(axis=0))
            top = jnp.max(top, axis=0, keepdims=True)
            total = jnp.zeros((8, full), f32)
            for row in range(0, extent, STRIP):
                expo = jnp.exp(live_strip(scores, dead_ref, extent, row) - top)
                total += by_eight(expo).sum(axis=0)
                prob_ref[slot, row : row + STRIP] = expo.astype(bf16)
            total = jnp.sum(total, axis=0, keepdims=True)
            stat_ref[0, pl.ds(number, 1), :] = top + jnp.log(total)
            return 1.0 / total

        def group(index, carry):
            for i in range(TOGETHER):
                pair = index * TOGETHER + i
                at = pl.ds(pl.multiple_of(pair * PAIR, PAIR), PAIR)
                values = v_ref[0, :extent, at].T
                mixed = []
                for half in range(2):
                    slot = 2 * i + half
                    scale = head(at, pair * 2 + half, half, slot)
                    own = values[half * HEAD_DIM : (half + 1) * HEAD_DIM]
                    mixed.append(mul(own, prob_ref[slot, :extent]) * scale)
                mix_ref[0, :, at] = jnp.concatenate(mixed, axis=0).T.astype(bf16)
            return carry

        lax.fori_loop(0, PAIRS // TOGETHER, group, 0)

    over_extents(length, full, run)


def attend(passage, count, info, tokens, parts, weights, before):
    held, piece, width = tokens.shape
    pieces = len(parts) + 1
    full = piece * pieces
    rows = pl.BlockSpec((1, full, width), lambda i, s: (passage, 0, 0))
    act = jax.ShapeDtypeStruct((count, full, width), bf16)
    got = pl.BlockSpec((1, piece, width), lambda i, s: (0, 0, 0))
    kept = [] if before is None else list(before)
    first_kept = 1 + pieces + len(weights)
    return pl.pallas_call(
        functools.partial(attend_kernel, pieces, passage, count, held),
        grid_spec=pltpu.PrefetchScalarGridSpec(
            num_scalar_prefetch=1,
            grid=(1,),
            in_specs=[pl.BlockSpec((1, piece, width), lambda i, s: (s[held] * count + passage, 0, 0))]
            + [got] * len(parts)
            + [fixed(w.shape) for w in weights]
            + [pl.BlockSpec(memory_space=pl.ANY)] * len(kept),
            out_specs=[pl.BlockSpec((2, 1, full, width), lambda i, s: (0, passage, 0, 0))]
            + [rows] * 3
            + [pl.BlockSpec((1, STAT_ROWS, full), lambda i, s: (passage, 0, 0))],
            scratch_shapes=[
                pltpu.VMEM((2 * TOGETHER, full, full), bf16),
                pltpu.VMEM((KEY_STEP, full), f32),
            ],
        ),
        out_shape=[jax.ShapeDtypeStruct((2, count, full, width), bf16)]
        + [act] * 3
        + [jax.ShapeDtypeStruct((count, STAT_ROWS, full), f32)],
        input_output_aliases={first_kept + i: i for i in range(len(kept))},
        compiler_params=PARAMS,
        cost_estimate=cost(
            2 * full * (3 * width * width + 4 * 2 * full * width),
            12 * full * width + 6 * width * width,
        ),
    )(info, tokens, *parts, *weights, *kept)


def attend_back_kernel(
    held,
    info_ref,
    q_ref,
    k_ref,
    v_ref,
    mg_ref,
    mix_ref,
    branch_ref,
    stat_ref,
    sum_ref,
    grads_ref,
    word_ref,
    bias_ref,
    along_ref,
    prob_ref,
    score_ref,
    dead_ref,
):
    dq_ref, dk_ref, dv_ref = (grads_ref.at[i] for i in range(3))
    grads_ref[3] = branch_ref[...].astype(bf16)
    full, width = q_ref.shape[1:]
    length = info_ref[info_ref[held] * pl.num_programs(0) + pl.program_id(0)]
    lane = lax.broadcasted_iota(jnp.int32, (1, PAIR), 1)
    row = lax.broadcasted_iota(jnp.int32, (8, 1), 0)

    @pl.when(pl.program_id(0) == 0)
    def _():
        bias_ref[...] = sum_ref[...]

    feature = lax.broadcasted_iota(jnp.int32, (STAT_ROWS, width), 1)
    number = lax.broadcasted_iota(jnp.int32, (STAT_ROWS, width), 0)
    ours = jnp.where(
        (feature >= number * HEAD_DIM) & (feature < (number + 1) * HEAD_DIM), 1.0, 0.0
    ).astype(bf16)
    product = mg_ref[0].astype(f32) * mix_ref[0, 0].astype(f32)
    high = product.astype(bf16)
    low = (product - high.astype(f32)).astype(bf16)
    along_ref[...] = mul(ours, high, NT) + mul(ours, low, NT)

    def run(extent):
        fill_dead(dead_ref, extent, length)
        if extent < full:
            dk_ref[0, extent:] = jnp.zeros((full - extent, width), bf16)
            dv_ref[0, extent:] = jnp.zeros((full - extent, width), bf16)

        def group(index, carry):
            for i in range(TOGETHER):
                pair = index * TOGETHER + i
                at = pl.ds(pl.multiple_of(pair * PAIR, PAIR), PAIR)
                q, mg = q_ref[0, :, at], mg_ref[0, :, at]
                k, v = k_ref[0, :extent, at], v_ref[0, :extent, at]
                keys = k.T
                dq, dk, dv = [], [], []
                for half in range(2):
                    slot = 2 * i + half
                    own = (lane >= half * HEAD_DIM) & (lane < (half + 1) * HEAD_DIM)
                    scores = mul(jnp.where(own, k * SCALE, 0).astype(bf16), q, NT)
                    prob_grad = mul(jnp.where(own, v, 0).astype(bf16), mg, NT)
                    log_row = stat_ref[0, pl.ds(pair * 2 + half, 1), :]
                    along = along_ref[pl.ds(pair * 2 + half, 1), :]
                    for at_row in range(0, extent, STRIP):
                        rows = slice(at_row, at_row + STRIP)
                        probs = jnp.exp(live_strip(scores, dead_ref, extent, at_row) - log_row)
                        prob_ref[slot, rows] = probs.astype(bf16)
                        score_ref[slot, rows] = (probs * (prob_grad[rows] - along)).astype(bf16)
                    score_grad = score_ref[slot, :extent]
                    dv.append(mul(prob_ref[slot, :extent], mg))
                    dk.append(mul(score_grad, q))
                    dq.append(mul(keys[half * HEAD_DIM : (half + 1) * HEAD_DIM], score_grad))
                first = lane < HEAD_DIM
                dq_pair = jnp.concatenate(dq, axis=0).T * SCALE
                dk_pair = jnp.where(first, dk[0], dk[1]) * SCALE
                dv_pair = jnp.where(first, dv[0], dv[1])
                dq_ref[0, :, at] = dq_pair.astype(bf16)
                dk_ref[0, :extent, at] = dk_pair.astype(bf16)
                dv_ref[0, :extent, at] = dv_pair.astype(bf16)
                sums = jnp.where(
                    row == 0,
                    jnp.sum(dq_pair, axis=0, keepdims=True),
                    jnp.where(row == 1, jnp.sum(dv_pair, axis=0, keepdims=True), 0.0),
                )
                bias_ref[0:8, at] += sums
            return carry

        lax.fori_loop(0, PAIRS // TOGETHER, group, 0)

    over_extents(length, full, run)

    @pl.when(pl.program_id(0) == pl.num_programs(0) - 1)
    def _():
        high = bias_ref[...].astype(bf16)
        word_ref[:SUM_ROWS] = high
        word_ref[SUM_ROWS:] = (bias_ref[...] - high.astype(f32)).astype(bf16)


def attend_back(held, info, q, k, v, mixed_grad, stacked, branch_in, stat, sums):
    count, full, width = q.shape
    rows = pl.BlockSpec((1, full, width), lambda i, *_: (i, 0, 0))
    return pl.pallas_call(
        functools.partial(attend_back_kernel, held),
        grid_spec=pltpu.PrefetchScalarGridSpec(
            num_scalar_prefetch=1,
            grid=(count,),
            in_specs=[rows] * 4
            + [
                pl.BlockSpec((1, 1, full, width), lambda i, *_: (1, i, 0, 0)),
                rows,
                pl.BlockSpec((1, STAT_ROWS, full), lambda i, *_: (i, 0, 0)),
                fixed(sums.shape),
            ],
            out_specs=[
                pl.BlockSpec((4, 1, full, width), lambda i, *_: (0, i, 0, 0)),
                pl.BlockSpec((2 * SUM_ROWS, width), lambda i, *_: (0, 0)),
            ],
            scratch_shapes=[
                pltpu.VMEM(sums.shape, f32),
                pltpu.VMEM((STAT_ROWS, full), f32),
                pltpu.VMEM((2 * TOGETHER, full, full), bf16),
                pltpu.VMEM((2 * TOGETHER, full, full), bf16),
                pltpu.VMEM((KEY_STEP, full), f32),
            ],
        ),
        out_shape=[
            jax.ShapeDtypeStruct((4, count, full, width), bf16),
            jax.ShapeDtypeStruct((2 * SUM_ROWS, width), bf16),
        ],
        compiler_params=PARAMS,
        cost_estimate=cost(
            2 * count * full * 10 * 2 * full * width, 16 * count * full * width
        ),
    )(info, q, k, v, mixed_grad, stacked, branch_in, stat, sums)


def norm_parts(hidden):
    centred = hidden - jnp.mean(hidden, axis=1, keepdims=True)
    inv_scale = lax.rsqrt(jnp.mean(centred * centred, axis=1, keepdims=True) + eps)
    return centred * inv_scale, inv_scale


def norm_back(scaled, normed, inv_scale):
    mean = jnp.mean(scaled, axis=1, keepdims=True)
    along = jnp.mean(scaled * normed, axis=1, keepdims=True)
    return (scaled - mean - normed * along) * inv_scale


def gelu_parts(u):
    expo = jnp.exp(u * u * -0.5)
    base = 1.0 + jnp.abs(u) * (0.3275911 * root_half)
    t = pl.reciprocal(base, approx=True)
    t = t * (2.0 - base * t)
    poly = t * (
        0.5 * 0.254829592
        + t
        * (
            0.5 * -0.284496736
            + t * (0.5 * 1.421413741 + t * (0.5 * -1.453152027 + t * (0.5 * 1.061405429)))
        )
    )
    tail = poly * expo
    return jnp.where(u >= 0, 1.0 - tail, tail), expo


def rows_kernel(
    blocks,
    count,
    held,
    info_ref,
    x_ref,
    mix_ref,
    cot_ref,
    pool_ref,
    wo_ref,
    vec_ref,
    wu_all,
    wd_all,
    out_ref,
    low_ref,
    act_all,
    second_ref,
    inner_all,
    branch_ref,
    mg_ref,
    sum_ref,
    wu_ref,
    wd_ref,
    act_ref,
    inner_ref,
    slope_ref,
    first_ref,
    normed_ref,
    total_ref,
    scale_ref,
    sems,
):
    step, steps = pl.program_id(0), pl.num_programs(0)
    rows, width = cot_ref.shape
    hidden_width = wu_ref.shape[1]
    b_out, gain_one, shift_one, b_down, gain_two, shift_two = (
        vec_ref[i : i + 1] for i in range(2, 8)
    )
    passage = info_ref[held] * count + step // blocks
    length = info_ref[passage]
    inv_length = 1.0 / jnp.full((1, width), length, jnp.int32).astype(f32)
    pool = pool_ref[pl.ds(passage, 1), :] * inv_length
    first_row = (step % blocks) * rows
    load_up = pltpu.make_async_copy(wu_all, wu_ref, sems.at[0])
    load_down = pltpu.make_async_copy(wd_all, wd_ref, sems.at[1])

    def give(source_ref, all_ref, at):
        return pltpu.make_async_copy(
            source_ref, all_ref.at[pl.ds(pl.multiple_of(at * rows, rows), rows)], sems.at[2 if source_ref is act_ref else 3]
        )

    @pl.when(step == 0)
    def _():
        load_up.start()
        load_down.start()
        sum_ref[...] = jnp.zeros(sum_ref.shape, f32)

    def tally(at, value, columns=slice(None)):
        sum_ref[at : at + 1, columns] += jnp.sum(value, axis=0, keepdims=True)

    def strips(size):
        return [slice(i, i + size) for i in range(0, rows, size)]

    groups = width // CHUNK
    chunks = hidden_width // CHUNK
    part = [slice(i * CHUNK, (i + 1) * CHUNK) for i in range(chunks)]
    whole = [slice(i * width, (i + 1) * width) for i in range(hidden_width // width)]
    lanes = scale_ref.shape[1]

    branch = mul(mix_ref[0], wo_ref[...])
    for at in strips(STRIP):
        normed, scale = norm_parts(x_ref[0, at].astype(f32) + branch[at] + b_out)
        first = normed * gain_one + shift_one
        normed_ref[at] = normed
        scale_ref[at] = jnp.broadcast_to(scale, (STRIP, lanes))
        first_ref[at] = first + b_down
        low_ref[at] = first.astype(bf16)

    @pl.when(step == 0)
    def _():
        load_up.wait()
        load_down.wait()

    @pl.when(step > 0)
    def _():
        give(act_ref, act_all, step - 1).wait()

    def up(i):
        return mul(low_ref[...], wu_ref[:, part[i]])

    pre = up(0)
    for i in range(chunks):
        ahead = up(i + 1) if i + 1 < chunks else None
        bias = vec_ref[8 + i // groups : 9 + i // groups, part[i % groups]]
        for at in strips(2 * STRIP):
            u = pre[at] + bias
            phi, expo = gelu_parts(u)
            act_ref[at, part[i]] = (u * phi).astype(bf16)
            slope_ref[at, part[i]] = phi + u * expo * inv_root_two_pi
        if i % groups == 0 and i:
            done = whole[i // groups - 1]
            first_ref[...] += mul(act_ref[:, done], wd_ref[done, :])
        pre = ahead
    last = mul(act_ref[:, whole[-1]], wd_ref[whole[-1], :])
    give(act_ref, act_all, step).start()

    pooled, shift, gain, down = (jnp.zeros((8, width), f32) for _ in range(4))
    for at in strips(STRIP):
        normed, scale = norm_parts(first_ref[at] + last[at])
        result = normed * gain_two + shift_two
        out_ref[at] = result.astype(bf16)
        row_at = lax.broadcasted_iota(jnp.int32, (STRIP, 1), 0) + (first_row + at.start)
        live = jnp.where(row_at < length, 1.0, 0.0)
        pooled += by_eight(result * live).sum(axis=0)
        upstream = cot_ref[at].astype(f32) + live * pool
        gain += by_eight(upstream * normed).sum(axis=0)
        shift += by_eight(upstream).sum(axis=0)
        second_in = norm_back(upstream * gain_two, normed, scale)
        down += by_eight(second_in).sum(axis=0)
        total_ref[at] = second_in
        second_ref[at] = second_in.astype(bf16)
    tally(6, gain)
    tally(7, shift)
    tally(5, down)
    sum_ref[pl.ds(POOL_ROW + step // blocks, 1), :] += (
        jnp.sum(pooled, axis=0, keepdims=True) * inv_length
    )

    @pl.when(step > 0)
    def _():
        give(inner_ref, inner_all, step - 1).wait()

    def back(i):
        return mul(second_ref[...], wd_ref[part[i], :], NT)

    grad = back(0)
    for i in range(chunks):
        ahead = back(i + 1) if i + 1 < chunks else None
        bias = jnp.zeros((8, CHUNK), f32)
        for at in strips(2 * STRIP):
            inner = grad[at] * slope_ref[at, part[i]]
            bias += by_eight(inner).sum(axis=0)
            inner_ref[at, part[i]] = inner.astype(bf16)
        tally(8 + i // groups, bias, part[i % groups])
        if i % groups == 0 and i:
            done = whole[i // groups - 1]
            total_ref[...] += mul(inner_ref[:, done], wu_ref[:, done], NT)
        grad = ahead
    last = mul(inner_ref[:, whole[-1]], wu_ref[:, whole[-1]], NT)
    give(inner_ref, inner_all, step).start()

    gain, shift, out = (jnp.zeros((8, width), f32) for _ in range(3))
    for at in strips(STRIP):
        first_up = total_ref[at] + last[at]
        normed = normed_ref[at]
        gain += by_eight(first_up * normed).sum(axis=0)
        shift += by_eight(first_up).sum(axis=0)
        branch_in = norm_back(first_up * gain_one, normed, scale_ref[at, :1])
        out += by_eight(branch_in).sum(axis=0)
        branch_ref[at] = branch_in
    tally(3, gain)
    tally(4, shift)
    tally(2, out)
    mg_ref[...] = mul(branch_ref[...].astype(bf16), wo_ref[...], NT).astype(bf16)

    @pl.when(step == steps - 1)
    def _():
        give(act_ref, act_all, step).wait()
        give(inner_ref, inner_all, step).wait()


def row_work(held, info, stacked, cot, pool, w_out, w_up, w_down, vecs, count):
    total, width = cot.shape
    full = total // count
    assert POOL_ROW + count <= SUM_ROWS
    hidden = w_up.shape[1]
    blocks = full // ROWS
    narrow = pl.BlockSpec((ROWS, width), lambda i, *_: (i, 0))
    anywhere = pl.BlockSpec(memory_space=pl.ANY)
    thin = jax.ShapeDtypeStruct((total, width), bf16)
    thick = jax.ShapeDtypeStruct((total, hidden), bf16)
    return pl.pallas_call(
        functools.partial(rows_kernel, blocks, count, held),
        grid_spec=pltpu.PrefetchScalarGridSpec(
            num_scalar_prefetch=1,
            grid=(total // ROWS,),
            in_specs=[
                pl.BlockSpec((1, ROWS, width), lambda i, *_: (0, i, 0)),
                pl.BlockSpec((1, ROWS, width), lambda i, *_: (1, i, 0)),
                narrow,
                fixed(pool.shape),
                fixed((width, width)),
                fixed(vecs.shape),
                anywhere,
                anywhere,
            ],
            out_specs=[
                narrow,
                narrow,
                anywhere,
                narrow,
                anywhere,
                narrow,
                narrow,
                pl.BlockSpec((SUM_ROWS, width), lambda i, *_: (0, 0)),
            ],
            scratch_shapes=[
                pltpu.VMEM((width, hidden), bf16),
                pltpu.VMEM((hidden, width), bf16),
                pltpu.VMEM((ROWS, hidden), bf16),
                pltpu.VMEM((ROWS, hidden), bf16),
                pltpu.VMEM((ROWS, hidden), f32),
                pltpu.VMEM((ROWS, width), f32),
                pltpu.VMEM((ROWS, width), f32),
                pltpu.VMEM((ROWS, width), f32),
                pltpu.VMEM((ROWS, PAIR), f32),
                pltpu.SemaphoreType.DMA((4,)),
            ],
        ),
        out_shape=[
            thin,
            thin,
            thick,
            thin,
            thick,
            jax.ShapeDtypeStruct((total, width), f32),
            thin,
            jax.ShapeDtypeStruct((SUM_ROWS, width), f32),
        ],
        compiler_params=PARAMS,
        cost_estimate=cost(
            4 * total * width * (width + 2 * hidden),
            2 * total * (8 * width + 2 * hidden) + 2 * width * (width + 2 * hidden),
        ),
    )(info, stacked, stacked, cot, pool, w_out, vecs, w_up, w_down)


def dense_outer_kernel(side_ref, act_ref, second_ref, low_ref, inner_ref, out_ref):
    step = pl.program_id(0)
    half = pl.num_programs(0) // 2

    @pl.when(step < half)
    def _():
        out_ref[0] = mul(act_ref[...], second_ref[...], TN).astype(bf16)

    @pl.when(step >= half)
    def _():
        out_ref[0] = mul(low_ref[...], inner_ref[...], TN).astype(bf16)


def dense_outer(at, flip, info, act, second, low, inner):
    total, width = second.shape
    wide = act.shape[1] // width
    half = wide // 2
    return pl.pallas_call(
        dense_outer_kernel,
        grid_spec=pltpu.PrefetchScalarGridSpec(
            num_scalar_prefetch=1,
            grid=(wide,),
            in_specs=[
                pl.BlockSpec(
                    (total, width), lambda i, s: (0, (s[at] ^ flip) * half + jnp.minimum(i, half - 1))
                ),
                fixed((total, width)),
                fixed((total, width)),
                pl.BlockSpec(
                    (total, width), lambda i, s: (0, (s[at] ^ flip) * half + jnp.maximum(i - half, 0))
                ),
            ],
            out_specs=pl.BlockSpec((1, width, width), lambda i, s: (i, 0, 0)),
        ),
        out_shape=jax.ShapeDtypeStruct((wide, width, width), bf16),
        compiler_params=SMALL,
        cost_estimate=cost(
            2 * total * width * width * wide, 2 * (wide + 2) * total * width + 2 * wide * width * width
        ),
    )(info, act, second, low, inner).reshape(wide * width, width)


def attend_outer_kernel(side_ref, left_ref, right_ref, out_ref):
    out_ref[0] = mul(left_ref[0], right_ref[0], TN).astype(bf16)


def attend_outer(at, flip, info, stacked, grads):
    total, width = stacked.shape[1:]
    return pl.pallas_call(
        attend_outer_kernel,
        grid_spec=pltpu.PrefetchScalarGridSpec(
            num_scalar_prefetch=1,
            grid=(2,),
            in_specs=[
                pl.BlockSpec((1, total, width), lambda i, s: (((s[at] ^ flip) * 2 + i) // 3, 0, 0)),
                pl.BlockSpec((1, total, width), lambda i, s: ((s[at] ^ flip) * 2 + i, 0, 0)),
            ],
            out_specs=pl.BlockSpec((1, width, width), lambda i, s: (i, 0, 0)),
        ),
        out_shape=jax.ShapeDtypeStruct((2, width, width), bf16),
        compiler_params=SMALL,
        cost_estimate=cost(4 * total * width * width, 8 * total * width + 4 * width * width),
    )(info, stacked, grads).reshape(2 * width, width)


def input_kernel(branch_ref, dq_ref, dk_ref, dv_ref, wq_ref, wk_ref, wv_ref, out_ref):
    total = branch_ref[...] + mul(dq_ref[0], wq_ref[...], NT)
    total += mul(dk_ref[0], wk_ref[...], NT)
    total += mul(dv_ref[0], wv_ref[...], NT)
    out_ref[...] = total.astype(bf16)


def input_grad(branch_in, grads, w_query, w_key, w_value):
    total, width = branch_in.shape
    rows = pl.BlockSpec((BACK_ROWS, width), lambda i: (i, 0))
    return pl.pallas_call(
        input_kernel,
        grid=(total // BACK_ROWS,),
        in_specs=[rows]
        + [pl.BlockSpec((1, BACK_ROWS, width), lambda i, at=at: (at, i, 0)) for at in range(3)]
        + [fixed((width, width))] * 3,
        out_specs=rows,
        out_shape=jax.ShapeDtypeStruct((total, width), bf16),
        compiler_params=SMALL,
        cost_estimate=cost(6 * total * width * width, 12 * total * width + 6 * width * width),
    )(branch_in, grads, grads, grads, w_query, w_key, w_value)


def exchange(value, axis, mask):
    count = lax.axis_size(axis)
    return lax.ppermute(value, axis, [(i, i ^ mask) for i in range(count)])


def to_passages(value):
    count = lax.axis_size("seq")
    mine = lax.axis_index("seq")
    held, piece, width = value.shape
    own = held // count
    whole = jnp.zeros((own, piece * count, width), value.dtype)
    for mask in range(count):
        peer = mine ^ mask
        part = lax.dynamic_slice_in_dim(value, peer * own, own, 0)
        if mask:
            part = exchange(part, "seq", mask)
        whole = lax.dynamic_update_slice_in_dim(whole, part, peer * piece, 1)
    return whole


def position_pieces(value):
    count = lax.axis_size("seq")
    piece = value.shape[1] // count
    mine = lax.axis_index("seq")
    return [
        lax.dynamic_slice_in_dim(value, (mine ^ mask) * piece, piece, 1) for mask in range(count)
    ]


def traded(pieces):
    return [exchange(part, "seq", mask) if mask else part for mask, part in enumerate(pieces)]


def to_positions(pieces):
    mine = lax.axis_index("seq")
    own, piece, width = pieces[0].shape
    result = jnp.zeros((own * len(pieces), piece, width), pieces[0].dtype)
    for mask, part in enumerate(pieces):
        result = lax.dynamic_update_slice_in_dim(result, part, (mine ^ mask) * own, 0)
    return result


def axis_bits(axis):
    return [(axis, 1 << i) for i in range(lax.axis_size(axis).bit_length() - 1)]


def upper(dim):
    axis, mask = dim
    return (lax.axis_index(axis) & mask) // mask


def swap(value, dim):
    return exchange(value, dim[0], dim[1])


def total_of(parts):
    total = parts[0].astype(f32)
    for part in parts[1:]:
        total += part.astype(f32)
    return total.astype(bf16)


PARTS = 3
SHARD_STEP = 16


class Plan:
    def __init__(self, rows):
        dims = axis_bits("seq") + axis_bits("dp")
        self.first = dims[0]
        rest = dims[1:]
        self.rows = rows // PARTS
        halved = 0
        while halved < len(rest) and (self.rows >> (halved + 1)) % SHARD_STEP == 0:
            halved += 1
        self.last = rest[halved - 1]
        self.plain = rest[halved:]
        split = rest[: halved - 1]
        self.orders = [split[i % len(split) :] + split[: i % len(split)] for i in range(PARTS)]
        self.shards = 1 << halved
        self.shard = self.rows >> halved

    def table(self, blocks, width, each):
        places = {}
        devices = 1
        weight = {}
        for axis in ("seq", "dp"):
            for _, mask in axis_bits(axis):
                weight[(axis, mask)] = devices
                devices *= 2
        for side in range(2):
            for part, order in enumerate(self.orders):
                dims = [self.last] + order[::-1]
                for code in range(self.shards):
                    device = side * weight[self.first]
                    device += sum(weight[d] for i, d in enumerate(dims) if (code >> i) & 1)
                    row = part * self.rows + code * self.shard
                    places[side, row] = device * each + part * self.shard
        half = blocks // 4
        found = []
        for block in range(blocks):
            side = block % (2 * half) // half
            local = block // (2 * half) * half + block % half
            for row in range(0, width, self.shard):
                found.append(places[side, local * width + row])
        return found

    def codes(self):
        found = []
        for order in self.orders:
            code = upper(self.last)
            for at, dim in enumerate(reversed(order)):
                code += upper(dim) << (at + 1)
            found.append(code)
        return [code.astype(jnp.int32) for code in found]


class Chain:
    def __init__(self):
        self.token = None

    def tie(self, values):
        if self.token is None:
            return values
        return lax.optimization_barrier((values, self.token))[0]

    def mark(self, values):
        self.token = values
        return values


def scatter_steps(plan, chain, keep, got, found):
    pairs = [[keep, got]] * PARTS
    bases = [i * plan.rows for i in range(PARTS)]
    size = plan.rows
    for step in range(len(plan.orders[0])):
        pairs = chain.tie(pairs)
        size //= 2
        dims = [order[step] for order in plan.orders]

        def halves(pair, base, at):
            return total_of([lax.dynamic_slice_in_dim(p, base + at * size, size, 0) for p in pair])

        sends = [halves(p, base, 1 - upper(d)) for p, base, d in zip(pairs, bases, dims)]
        chain.mark(sends)
        mine = [halves(p, base, upper(d)) for p, base, d in zip(pairs, bases, dims)]
        pairs = [[m, swap(s, d)] for m, s, d in zip(mine, sends, dims)]
        bases = [0] * PARTS
        yield
    size = plan.shard
    bit = upper(plan.last)
    pairs = chain.tie(pairs)

    def side(at):
        return jnp.concatenate(
            [total_of([lax.dynamic_slice_in_dim(p, at * size, size, 0) for p in pair]) for pair in pairs],
            axis=0,
        )

    send = chain.mark(side(1 - bit))
    shard = side(bit)
    got = swap(send, plan.last)
    yield
    shard, got = chain.tie((shard, got))
    shard = total_of([shard, got])
    for dim in plan.plain:
        shard = total_of([shard, swap(shard, dim)])
    found.append(chain.mark(shard))
    yield


def gather_steps(plan, chain, shard, found):
    size = plan.shard
    got = swap(shard, plan.last)
    yield
    values = [(shard[i * size : (i + 1) * size], got[i * size : (i + 1) * size]) for i in range(PARTS)]
    for step in reversed(range(len(plan.orders[0]))):
        values = chain.tie(values)
        values = [jnp.concatenate(pair, axis=0) for pair in values]
        chain.mark(values)
        values = [(v, swap(v, order[step])) for v, order in zip(values, plan.orders)]
        yield
    values = chain.tie(values)
    chain.mark(values)
    found += [v for pair in values for v in pair]
    found += [swap(v, plan.first) for v in found]
    yield


def place(plan, refs, codes, row, store):
    part = row // plan.rows
    shard = ((row % plan.rows) // plan.shard) ^ codes[part]
    half = plan.shards // 2
    at = pl.ds(pl.multiple_of((shard & (half - 1)) * plan.shard, plan.shard), plan.shard)
    low, high = refs[2 * part][at, :], refs[2 * part + 1][at, :]
    store(jnp.where(shard >= half, high.astype(f32), low.astype(f32)))


def dense_place_kernel(
    shard, each, held, table_ref, info_ref, all_ref, down_ref, up_ref, vec_ref, pool_ref, hold_ref, word_ref, sems, word_sem
):
    step, steps = pl.program_id(0), pl.num_programs(0)
    width = down_ref.shape[1]
    parts = width // shard

    def fetch(block, slot):
        for i in range(parts):
            at = pl.multiple_of(table_ref[block * parts + i], SHARD_STEP)
            pltpu.make_async_copy(
                all_ref.at[pl.ds(at, shard)],
                hold_ref.at[slot, pl.ds(i * shard, shard)],
                sems.at[slot],
            ).start()

    def words(device):
        return pltpu.make_async_copy(
            all_ref.at[pl.ds(device * each + each - 2 * SUM_ROWS, 2 * SUM_ROWS)],
            word_ref.at[device],
            word_sem,
        )

    devices = word_ref.shape[0]

    @pl.when(step == 0)
    def _():
        fetch(0, 0)
        for device in range(devices):
            words(device).start()

    @pl.when(step + 1 < steps)
    def _():
        fetch(step + 1, (step + 1) % 2)

    slot = step % 2
    pltpu.make_async_copy(all_ref.at[pl.ds(0, width)], hold_ref.at[slot], sems.at[slot]).wait()

    @pl.when(step < steps // 2)
    def _():
        down_ref[...] = hold_ref[slot].astype(f32)

    @pl.when(step >= steps // 2)
    def _():
        up_ref[...] = hold_ref[slot].astype(f32)

    @pl.when(step == steps - 1)
    def _():
        pltpu.make_async_copy(word_ref, word_ref, word_sem).wait()

        def both(device):
            return word_ref[device, :SUM_ROWS].astype(f32) + word_ref[device, SUM_ROWS:].astype(f32)

        vec_ref[...] = lax.fori_loop(
            0, devices, lambda i, total: total + both(i), jnp.zeros(vec_ref.shape, f32)
        )
        group = pool_ref.shape[0]
        for i in range(group):
            pool_ref[i] = both(info_ref[held] + i)[POOL_ROW:]


def dense_place(plan, gathered, each, width, wide, devices, seq_count, group):
    table = jnp.array(plan.table(2 * wide, width, each), jnp.int32)
    return pl.pallas_call(
        functools.partial(dense_place_kernel, plan.shard, each, 0),
        grid_spec=pltpu.PrefetchScalarGridSpec(
            num_scalar_prefetch=2,
            grid=(2 * wide,),
            in_specs=[pl.BlockSpec(memory_space=pl.ANY)],
            out_specs=[
                pl.BlockSpec((width, width), lambda i, *_: (jnp.minimum(i, wide - 1), 0)),
                pl.BlockSpec((width, width), lambda i, *_: (0, jnp.maximum(i - wide, 0))),
                pl.BlockSpec((SUM_ROWS, width), lambda i, *_: (0, 0)),
                pl.BlockSpec((seq_count, SUM_ROWS - POOL_ROW, width), lambda i, *_: (0, 0, 0)),
            ],
            scratch_shapes=[
                pltpu.VMEM((2, width, width), bf16),
                pltpu.VMEM((devices, 2 * SUM_ROWS, width), bf16),
                pltpu.SemaphoreType.DMA((2,)),
                pltpu.SemaphoreType.DMA(()),
            ],
        ),
        out_shape=[
            jax.ShapeDtypeStruct((wide * width, width), f32),
            jax.ShapeDtypeStruct((width, wide * width), f32),
            jax.ShapeDtypeStruct((SUM_ROWS, width), f32),
            jax.ShapeDtypeStruct((seq_count, SUM_ROWS - POOL_ROW, width), f32),
        ],
        compiler_params=PARAMS,
        cost_estimate=cost(0, 12 * wide * width * width),
    )(table, group, gathered)


def attend_place_kernel(plan, first_code, at, flip, info_ref, *refs):
    sources, (hold_ref, sems) = refs[: 2 * PARTS], refs[-2:]
    outs = refs[-6:-2]
    codes = [info_ref[first_code + i] for i in range(PARTS)]
    own = info_ref[at] ^ flip
    width = hold_ref.shape[2]

    def move(block, act):
        for side in range(2):

            @pl.when(own == side)
            def _():
                act(pltpu.make_async_copy(hold_ref.at[block], outs[2 * side + block], sems.at[block]))

    for block in range(2):
        for row in range(0, width, plan.shard):

            def store(value, row=row):
                hold_ref[block, row : row + plan.shard, :] = value

            place(plan, sources, codes, block * width + row, store)
        move(block, lambda copy: copy.start())
    for block in range(2):
        move(block, lambda copy: copy.wait())


def attend_place(plan, first_code, at, flip, info, sources, width, before):
    kept = list(before)
    return pl.pallas_call(
        functools.partial(attend_place_kernel, plan, first_code, at, flip),
        grid_spec=pltpu.PrefetchScalarGridSpec(
            num_scalar_prefetch=1,
            grid=(1,),
            in_specs=[fixed(x.shape) for x in sources]
            + [pl.BlockSpec(memory_space=pl.ANY)] * len(kept),
            out_specs=[pl.BlockSpec(memory_space=pl.ANY)] * 4,
            scratch_shapes=[pltpu.VMEM((2, width, width), f32), pltpu.SemaphoreType.DMA((2,))],
        ),
        out_shape=[jax.ShapeDtypeStruct((width, width), f32)] * 4,
        input_output_aliases={1 + len(sources) + i: i for i in range(len(kept))},
        compiler_params=SMALL,
        cost_estimate=cost(0, 12 * width * width),
    )(info, *sources, *kept)


def shards(
    tokens,
    lengths,
    w_query,
    b_query,
    w_key,
    w_value,
    b_value,
    w_out,
    b_out,
    gain_one,
    shift_one,
    w_up,
    b_up,
    w_down,
    b_down,
    gain_two,
    shift_two,
    out_grad,
    pooled_grad,
):
    seq_count = lax.axis_size("seq")
    held, piece, width = tokens.shape
    full = piece * seq_count
    count = held // seq_count
    mine = lax.axis_index("seq")
    wide = w_up.shape[1] // width
    total = count * full

    def flat(value):
        return value.reshape(total, width)

    def split(value):
        return value.reshape(count, full, width)

    dense_plan = Plan(wide * width)
    outer_plan = Plan(2 * width)
    first = axis_bits("seq")[0]
    scalars = [mine, upper(first)] + dense_plan.codes() + outer_plan.codes()
    own_at, dense_at, outer_at = held + 1, held + 2, held + 2 + PARTS
    info = jnp.concatenate([lengths, jnp.stack([v.astype(jnp.int32) for v in scalars])])
    vecs = jnp.concatenate(
        [b_query, b_value, b_out, gain_one, shift_one, b_down, gain_two, shift_two, b_up]
    )
    vecs = vecs.astype(f32).reshape(-1, width)

    weights = [w_query, w_key, w_value, vecs]
    done = None
    source = tokens
    parts = []
    for passage in range(count):
        if parts:
            source = lax.optimization_barrier((tokens, parts))[0]
        parts = [
            exchange(
                lax.dynamic_slice_in_dim(source, (mine ^ mask) * count + passage, 1, 0), "seq", mask
            )
            for mask in range(1, seq_count)
        ]
        done = attend(passage, count, info, tokens, parts, weights, done)
    stacked, q, k, v, stat = done
    cot = to_passages(lax.optimization_barrier((out_grad, parts))[0])
    stacked = stacked.reshape(2, total, width)
    result, first_low, act, second, inner, branch_in, mixed_grad, sums = row_work(
        held, info, stacked, flat(cot), pooled_grad, w_out, w_up, w_down, vecs, count
    )
    chain = Chain()
    pieces = chain.mark(position_pieces(split(result)))
    out_pieces = traded(pieces)
    send = dense_outer(own_at, 1, info, *chain.tie((act, second, first_low, inner)))
    chain.mark(send)
    got = swap(send, first)
    keep = chain.mark(dense_outer(own_at, 0, info, *chain.tie((act, second, first_low, inner))))
    dense, shard, outer = [], [], []
    dense_steps = scatter_steps(dense_plan, chain, keep, got, dense)
    next(dense_steps)
    chain.mark((chain.token, out_pieces))
    block_out = to_positions(out_pieces)
    grads, words = attend_back(
        held,
        info,
        q,
        k,
        v,
        chain.tie(split(mixed_grad)),
        stacked.reshape(2, count, full, width),
        split(branch_in),
        stat,
        sums,
    )
    chain.mark(words)
    grads = grads.reshape(4, total, width)
    next(dense_steps)
    send = attend_outer(own_at, 1, info, stacked, chain.tie(grads))
    chain.mark(send)
    got = swap(send, first)
    keep = attend_outer(own_at, 0, info, stacked, chain.tie(grads))
    chain.mark(keep)
    next(dense_steps)
    outer_steps = scatter_steps(outer_plan, chain, keep, got, shard)
    next(outer_steps)
    input_low = input_grad(branch_in, chain.tie(grads), w_query, w_key, w_value)
    chain.mark(input_low)
    next(dense_steps)
    next(outer_steps)
    for _ in dense_steps:
        pass
    gathered = jnp.concatenate([dense[0], words], axis=0)
    each = gathered.shape[0]
    gathered = chain.mark(gathered)
    gathered = lax.all_gather(gathered, ("dp", "seq"), axis=0, tiled=True)
    next(outer_steps)
    next(outer_steps)
    pieces = chain.mark(position_pieces(split(chain.tie(input_low))))
    in_pieces = traded(pieces)
    for _ in outer_steps:
        pass
    outer_steps = gather_steps(outer_plan, chain, shard[0], outer)
    next(outer_steps)
    next(outer_steps)
    next(outer_steps)
    chain.mark((chain.token, in_pieces))
    tokens_grad = to_positions(in_pieces)
    for _ in outer_steps:
        pass
    group = (lax.axis_index("dp") * seq_count).astype(jnp.int32)[None]
    down_sum, up_sum, vectors, pooled = dense_place(
        dense_plan, chain.tie(gathered), each, width, wide, gathered.shape[0] // each, seq_count, group
    )
    pooled = pooled[:, :count].reshape(held, width)

    def place_outer(flip, before):
        pick = outer[2 * PARTS :] if flip else outer[: 2 * PARTS]
        return chain.mark(
            attend_place(outer_plan, outer_at, own_at, flip, info, chain.tie(pick), width, before)
        )

    placed = place_outer(0, [])
    outer = place_outer(1, placed)
    return (
        block_out,
        pooled,
        tokens_grad,
        outer[0],
        vectors[0],
        outer[1],
        outer[2],
        vectors[1],
        outer[3],
        vectors[2],
        vectors[3],
        vectors[4],
        up_sum,
        vectors[8 : 8 + wide].reshape(-1),
        down_sum,
        vectors[5],
        vectors[6],
        vectors[7],
    )


def solution(mesh):
    in_specs = (
        (P("dp", "seq", None), P("dp"))
        + (P(),) * 15
        + (P("dp", "seq", None), P("dp", None))
    )
    out_specs = (P("dp", "seq", None), P("dp", None), P("dp", "seq", None)) + (P(),) * 15
    return jax.shard_map(shards, mesh=mesh, in_specs=in_specs, out_specs=out_specs, check_vma=False)
```

```python
import functools

import jax
import jax.numpy as jnp
from jax import lax
from jax.experimental import pallas as pl
from jax.experimental.pallas import tpu as pltpu
from jax.sharding import PartitionSpec as P

HEADS = 12
HEAD_DIM = 64
PAIR = 2 * HEAD_DIM
PAIRS = HEADS // 2
SCALE = HEAD_DIM ** (-0.5)
ROWS = 512
BACK_ROWS = 256
STRIP = 32
UNROLL = 4
TOGETHER = 1
STAT_ROWS = 16
CHUNK = 256
KEY_STEP = 128
VMEM_BYTES = 62 * 1024 * 1024
SMALL_BYTES = 40 * 1024 * 1024
SUM_ROWS = 16
POOL_ROW = 12

eps = 1e-06
root_half = 0.7071067811865476
inv_root_two_pi = 0.3989422804014327

f32 = jnp.float32
bf16 = jnp.bfloat16

NN = (((1,), (0,)), ((), ()))
NT = (((1,), (1,)), ((), ()))
TN = (((0,), (0,)), ((), ()))


def mul(left, right, dims=NN):
    return lax.dot_general(left, right, dims, preferred_element_type=f32)


def fixed(shape):
    return pl.BlockSpec(shape, lambda *_: (0,) * len(shape), pipeline_mode=pl.Buffered(1))


PARAMS = pltpu.CompilerParams(dimension_semantics=("arbitrary",), vmem_limit_bytes=VMEM_BYTES)
SMALL = pltpu.CompilerParams(dimension_semantics=("arbitrary",), vmem_limit_bytes=SMALL_BYTES)


def cost(flops, moved, exps=0):
    return pl.CostEstimate(flops=int(flops), bytes_accessed=int(moved), transcendentals=int(exps))


def over_extents(length, full, body):
    for extent in range(KEY_STEP, full + 1, KEY_STEP):
        pl.when((length > extent - KEY_STEP) & (length <= extent))(functools.partial(body, extent))


def by_eight(value):
    return value.reshape(value.shape[0] // 8, 8, value.shape[1])


def fill_dead(dead_ref, extent, length):
    key_at = lax.broadcasted_iota(jnp.int32, dead_ref.shape, 0) + (extent - KEY_STEP)
    dead_ref[...] = jnp.where(key_at < length, 0.0, -1e30)


def live_strip(scores, dead_ref, extent, row):
    strip = scores[row : row + STRIP]
    last = row - (extent - KEY_STEP)
    return strip + dead_ref[last : last + STRIP] if last >= 0 else strip


def attend_kernel(pieces, passage, count, held, info_ref, *refs):
    part_refs, refs = refs[:pieces], refs[pieces:]
    wq_ref, wk_ref, wv_ref, vec_ref = refs[:4]
    xm_ref, q_ref, k_ref, v_ref, stat_ref, prob_ref, dead_ref = refs[-7:]
    x_ref, mix_ref = xm_ref.at[0], xm_ref.at[1]
    mine = info_ref[held]
    length = info_ref[mine * count + passage]
    size = part_refs[0].shape[1]
    for mask, part_ref in enumerate(part_refs):
        x_ref[0, pl.ds(pl.multiple_of((mine ^ mask) * size, size), size)] = part_ref[0]

    def project(index, carry):
        at = pl.ds(pl.multiple_of(index * CHUNK, CHUNK), CHUNK)
        x = x_ref[0]
        q_ref[0, :, at] = (mul(x, wq_ref[:, at]) + vec_ref[0:1, at]).astype(bf16)
        k_ref[0, :, at] = mul(x, wk_ref[:, at]).astype(bf16)
        v_ref[0, :, at] = (mul(x, wv_ref[:, at]) + vec_ref[1:2, at]).astype(bf16)
        return carry

    lax.fori_loop(0, wq_ref.shape[1] // CHUNK, project, 0)
    stat_ref[0] = jnp.zeros(stat_ref.shape[1:], f32)
    full = size * pieces
    lane = lax.broadcasted_iota(jnp.int32, (1, PAIR), 1)

    def run(extent):
        fill_dead(dead_ref, extent, length)

        def head(at, number, half, slot):
            q, k = q_ref[0, :, at], k_ref[0, :extent, at]
            own = (lane >= half * HEAD_DIM) & (lane < (half + 1) * HEAD_DIM)
            scores = mul(jnp.where(own, k * SCALE, 0).astype(bf16), q, NT)
            top = jnp.full((8, full), -jnp.inf, f32)
            for row in range(0, extent, STRIP):
                top = jnp.maximum(top, by_eight(live_strip(scores, dead_ref, extent, row)).max(axis=0))
            top = jnp.max(top, axis=0, keepdims=True)
            total = jnp.zeros((8, full), f32)
            for row in range(0, extent, STRIP):
                expo = jnp.exp(live_strip(scores, dead_ref, extent, row) - top)
                total += by_eight(expo).sum(axis=0)
                prob_ref[slot, row : row + STRIP] = expo.astype(bf16)
            total = jnp.sum(total, axis=0, keepdims=True)
            stat_ref[0, pl.ds(number, 1), :] = top + jnp.log(total)
            return 1.0 / total

        def group(index, carry):
            for i in range(TOGETHER):
                pair = index * TOGETHER + i
                at = pl.ds(pl.multiple_of(pair * PAIR, PAIR), PAIR)
                values = v_ref[0, :extent, at].T
                mixed = []
                for half in range(2):
                    slot = 2 * i + half
                    scale = head(at, pair * 2 + half, half, slot)
                    own = values[half * HEAD_DIM : (half + 1) * HEAD_DIM]
                    mixed.append(mul(own, prob_ref[slot, :extent]) * scale)
                mix_ref[0, :, at] = jnp.concatenate(mixed, axis=0).T.astype(bf16)
            return carry

        lax.fori_loop(0, PAIRS // TOGETHER, group, 0)

    over_extents(length, full, run)


def attend(passage, count, info, tokens, parts, weights, before):
    held, piece, width = tokens.shape
    pieces = len(parts) + 1
    full = piece * pieces
    rows = pl.BlockSpec((1, full, width), lambda i, s: (passage, 0, 0))
    act = jax.ShapeDtypeStruct((count, full, width), bf16)
    got = pl.BlockSpec((1, piece, width), lambda i, s: (0, 0, 0))
    kept = [] if before is None else list(before)
    first_kept = 1 + pieces + len(weights)
    return pl.pallas_call(
        functools.partial(attend_kernel, pieces, passage, count, held),
        grid_spec=pltpu.PrefetchScalarGridSpec(
            num_scalar_prefetch=1,
            grid=(1,),
            in_specs=[pl.BlockSpec((1, piece, width), lambda i, s: (s[held] * count + passage, 0, 0))]
            + [got] * len(parts)
            + [fixed(w.shape) for w in weights]
            + [pl.BlockSpec(memory_space=pl.ANY)] * len(kept),
            out_specs=[pl.BlockSpec((2, 1, full, width), lambda i, s: (0, passage, 0, 0))]
            + [rows] * 3
            + [pl.BlockSpec((1, STAT_ROWS, full), lambda i, s: (passage, 0, 0))],
            scratch_shapes=[
                pltpu.VMEM((2 * TOGETHER, full, full), bf16),
                pltpu.VMEM((KEY_STEP, full), f32),
            ],
        ),
        out_shape=[jax.ShapeDtypeStruct((2, count, full, width), bf16)]
        + [act] * 3
        + [jax.ShapeDtypeStruct((count, STAT_ROWS, full), f32)],
        input_output_aliases={first_kept + i: i for i in range(len(kept))},
        compiler_params=PARAMS,
        cost_estimate=cost(
            2 * full * (3 * width * width + 4 * 2 * full * width),
            12 * full * width + 6 * width * width,
        ),
    )(info, tokens, *parts, *weights, *kept)


def attend_back_kernel(
    held,
    info_ref,
    q_ref,
    k_ref,
    v_ref,
    mg_ref,
    mix_ref,
    branch_ref,
    stat_ref,
    sum_ref,
    grads_ref,
    word_ref,
    bias_ref,
    along_ref,
    prob_ref,
    score_ref,
    dead_ref,
):
    dq_ref, dk_ref, dv_ref = (grads_ref.at[i] for i in range(3))
    grads_ref[3] = branch_ref[...].astype(bf16)
    full, width = q_ref.shape[1:]
    length = info_ref[info_ref[held] * pl.num_programs(0) + pl.program_id(0)]
    lane = lax.broadcasted_iota(jnp.int32, (1, PAIR), 1)
    row = lax.broadcasted_iota(jnp.int32, (8, 1), 0)

    @pl.when(pl.program_id(0) == 0)
    def _():
        bias_ref[...] = sum_ref[...]

    feature = lax.broadcasted_iota(jnp.int32, (STAT_ROWS, width), 1)
    number = lax.broadcasted_iota(jnp.int32, (STAT_ROWS, width), 0)
    ours = jnp.where(
        (feature >= number * HEAD_DIM) & (feature < (number + 1) * HEAD_DIM), 1.0, 0.0
    ).astype(bf16)
    product = mg_ref[0].astype(f32) * mix_ref[0, 0].astype(f32)
    high = product.astype(bf16)
    low = (product - high.astype(f32)).astype(bf16)
    along_ref[...] = mul(ours, high, NT) + mul(ours, low, NT)

    def run(extent):
        fill_dead(dead_ref, extent, length)
        if extent < full:
            dk_ref[0, extent:] = jnp.zeros((full - extent, width), bf16)
            dv_ref[0, extent:] = jnp.zeros((full - extent, width), bf16)

        def group(index, carry):
            for i in range(TOGETHER):
                pair = index * TOGETHER + i
                at = pl.ds(pl.multiple_of(pair * PAIR, PAIR), PAIR)
                q, mg = q_ref[0, :, at], mg_ref[0, :, at]
                k, v = k_ref[0, :extent, at], v_ref[0, :extent, at]
                keys = k.T
                dq, dk, dv = [], [], []
                for half in range(2):
                    slot = 2 * i + half
                    own = (lane >= half * HEAD_DIM) & (lane < (half + 1) * HEAD_DIM)
                    scores = mul(jnp.where(own, k * SCALE, 0).astype(bf16), q, NT)
                    prob_grad = mul(jnp.where(own, v, 0).astype(bf16), mg, NT)
                    log_row = stat_ref[0, pl.ds(pair * 2 + half, 1), :]
                    along = along_ref[pl.ds(pair * 2 + half, 1), :]
                    for at_row in range(0, extent, STRIP):
                        rows = slice(at_row, at_row + STRIP)
                        probs = jnp.exp(live_strip(scores, dead_ref, extent, at_row) - log_row)
                        prob_ref[slot, rows] = probs.astype(bf16)
                        score_ref[slot, rows] = (probs * (prob_grad[rows] - along)).astype(bf16)
                    score_grad = score_ref[slot, :extent]
                    dv.append(mul(prob_ref[slot, :extent], mg))
                    dk.append(mul(score_grad, q))
                    dq.append(mul(keys[half * HEAD_DIM : (half + 1) * HEAD_DIM], score_grad))
                first = lane < HEAD_DIM
                dq_pair = jnp.concatenate(dq, axis=0).T * SCALE
                dk_pair = jnp.where(first, dk[0], dk[1]) * SCALE
                dv_pair = jnp.where(first, dv[0], dv[1])
                dq_ref[0, :, at] = dq_pair.astype(bf16)
                dk_ref[0, :extent, at] = dk_pair.astype(bf16)
                dv_ref[0, :extent, at] = dv_pair.astype(bf16)
                sums = jnp.where(
                    row == 0,
                    jnp.sum(dq_pair, axis=0, keepdims=True),
                    jnp.where(row == 1, jnp.sum(dv_pair, axis=0, keepdims=True), 0.0),
                )
                bias_ref[0:8, at] += sums
            return carry

        lax.fori_loop(0, PAIRS // TOGETHER, group, 0)

    over_extents(length, full, run)

    @pl.when(pl.program_id(0) == pl.num_programs(0) - 1)
    def _():
        high = bias_ref[...].astype(bf16)
        word_ref[:SUM_ROWS] = high
        word_ref[SUM_ROWS:] = (bias_ref[...] - high.astype(f32)).astype(bf16)


def attend_back(held, info, q, k, v, mixed_grad, stacked, branch_in, stat, sums):
    count, full, width = q.shape
    rows = pl.BlockSpec((1, full, width), lambda i, *_: (i, 0, 0))
    return pl.pallas_call(
        functools.partial(attend_back_kernel, held),
        grid_spec=pltpu.PrefetchScalarGridSpec(
            num_scalar_prefetch=1,
            grid=(count,),
            in_specs=[rows] * 4
            + [
                pl.BlockSpec((1, 1, full, width), lambda i, *_: (1, i, 0, 0)),
                rows,
                pl.BlockSpec((1, STAT_ROWS, full), lambda i, *_: (i, 0, 0)),
                fixed(sums.shape),
            ],
            out_specs=[
                pl.BlockSpec((4, 1, full, width), lambda i, *_: (0, i, 0, 0)),
                pl.BlockSpec((2 * SUM_ROWS, width), lambda i, *_: (0, 0)),
            ],
            scratch_shapes=[
                pltpu.VMEM(sums.shape, f32),
                pltpu.VMEM((STAT_ROWS, full), f32),
                pltpu.VMEM((2 * TOGETHER, full, full), bf16),
                pltpu.VMEM((2 * TOGETHER, full, full), bf16),
                pltpu.VMEM((KEY_STEP, full), f32),
            ],
        ),
        out_shape=[
            jax.ShapeDtypeStruct((4, count, full, width), bf16),
            jax.ShapeDtypeStruct((2 * SUM_ROWS, width), bf16),
        ],
        compiler_params=PARAMS,
        cost_estimate=cost(
            2 * count * full * 10 * 2 * full * width, 16 * count * full * width
        ),
    )(info, q, k, v, mixed_grad, stacked, branch_in, stat, sums)


def norm_parts(hidden):
    centred = hidden - jnp.mean(hidden, axis=1, keepdims=True)
    inv_scale = lax.rsqrt(jnp.mean(centred * centred, axis=1, keepdims=True) + eps)
    return centred * inv_scale, inv_scale


def norm_back(scaled, normed, inv_scale):
    mean = jnp.mean(scaled, axis=1, keepdims=True)
    along = jnp.mean(scaled * normed, axis=1, keepdims=True)
    return (scaled - mean - normed * along) * inv_scale


def gelu_parts(u):
    expo = jnp.exp(u * u * -0.5)
    base = 1.0 + jnp.abs(u) * (0.3275911 * root_half)
    t = pl.reciprocal(base, approx=True)
    t = t * (2.0 - base * t)
    poly = t * (
        0.5 * 0.254829592
        + t
        * (
            0.5 * -0.284496736
            + t * (0.5 * 1.421413741 + t * (0.5 * -1.453152027 + t * (0.5 * 1.061405429)))
        )
    )
    tail = poly * expo
    return jnp.where(u >= 0, 1.0 - tail, tail), expo


def rows_kernel(
    blocks,
    count,
    held,
    info_ref,
    x_ref,
    mix_ref,
    cot_ref,
    pool_ref,
    wo_ref,
    vec_ref,
    wu_all,
    wd_all,
    out_ref,
    low_ref,
    act_all,
    second_ref,
    inner_all,
    branch_ref,
    mg_ref,
    sum_ref,
    wu_ref,
    wd_ref,
    act_ref,
    inner_ref,
    slope_ref,
    first_ref,
    normed_ref,
    total_ref,
    scale_ref,
    sems,
):
    step, steps = pl.program_id(0), pl.num_programs(0)
    rows, width = cot_ref.shape
    hidden_width = wu_ref.shape[1]
    b_out, gain_one, shift_one, b_down, gain_two, shift_two = (
        vec_ref[i : i + 1] for i in range(2, 8)
    )
    passage = info_ref[held] * count + step // blocks
    length = info_ref[passage]
    inv_length = 1.0 / jnp.full((1, width), length, jnp.int32).astype(f32)
    pool = pool_ref[pl.ds(passage, 1), :] * inv_length
    first_row = (step % blocks) * rows
    load_up = pltpu.make_async_copy(wu_all, wu_ref, sems.at[0])
    load_down = pltpu.make_async_copy(wd_all, wd_ref, sems.at[1])

    def give(source_ref, all_ref, at):
        return pltpu.make_async_copy(
            source_ref, all_ref.at[pl.ds(pl.multiple_of(at * rows, rows), rows)], sems.at[2 if source_ref is act_ref else 3]
        )

    @pl.when(step == 0)
    def _():
        load_up.start()
        load_down.start()
        sum_ref[...] = jnp.zeros(sum_ref.shape, f32)

    def tally(at, value):
        sum_ref[at : at + 1] += jnp.sum(value, axis=0, keepdims=True)

    def strips(size):
        return [slice(i, i + size) for i in range(0, rows, size)]

    def over_strips(body, carry):
        def turn(index, carry):
            for i in range(UNROLL):
                at = pl.ds(pl.multiple_of((index * UNROLL + i) * STRIP, STRIP), STRIP)
                carry = body(at, carry)
            return carry

        return lax.fori_loop(0, rows // (STRIP * UNROLL), turn, carry)

    def columns(index):
        return pl.ds(pl.multiple_of(index * width, width), width)

    groups = hidden_width // width
    parts = [slice(i * CHUNK, (i + 1) * CHUNK) for i in range(width // CHUNK)]
    lanes = scale_ref.shape[1]

    total_ref[...] = mul(mix_ref[0], wo_ref[...])

    def first_norm(at, carry):
        normed, scale = norm_parts(x_ref[0, at, :].astype(f32) + total_ref[at, :] + b_out)
        first = normed * gain_one + shift_one
        normed_ref[at, :] = normed
        scale_ref[at, :] = jnp.broadcast_to(scale, (STRIP, lanes))
        first_ref[at, :] = first + b_down
        low_ref[at, :] = first.astype(bf16)
        return carry

    over_strips(first_norm, 0)

    @pl.when(step == 0)
    def _():
        load_up.wait()
        load_down.wait()

    @pl.when(step > 0)
    def _():
        give(act_ref, act_all, step - 1).wait()

    def forward(index, carry):
        start = index * width

        def chunk(i):
            return pl.ds(pl.multiple_of(start + i * CHUNK, CHUNK), CHUNK)

        def up(i):
            return mul(low_ref[...], wu_ref[:, chunk(i)])

        pre = up(0)
        for i in range(len(parts)):
            ahead = up(i + 1) if i + 1 < len(parts) else None
            bias = vec_ref[pl.ds(8 + index, 1), parts[i]]
            for at in strips(2 * STRIP):
                u = pre[at] + bias
                phi, expo = gelu_parts(u)
                act_ref[at, chunk(i)] = (u * phi).astype(bf16)
                slope_ref[at, chunk(i)] = phi + u * expo * inv_root_two_pi
            pre = ahead
        first_ref[...] += mul(act_ref[:, columns(index)], wd_ref[columns(index), :])
        return carry

    lax.fori_loop(0, groups, forward, 0)
    give(act_ref, act_all, step).start()

    def second_norm(at, carry):
        pooled, shift, gain, down = carry
        normed, scale = norm_parts(first_ref[at, :])
        result = normed * gain_two + shift_two
        out_ref[at, :] = result.astype(bf16)
        row_at = lax.broadcasted_iota(jnp.int32, (STRIP, 1), 0) + (first_row + at.start)
        live = jnp.where(row_at < length, 1.0, 0.0)
        pooled += by_eight(result * live).sum(axis=0)
        upstream = cot_ref[at, :].astype(f32) + live * pool
        gain += by_eight(upstream * normed).sum(axis=0)
        shift += by_eight(upstream).sum(axis=0)
        second_in = norm_back(upstream * gain_two, normed, scale)
        down += by_eight(second_in).sum(axis=0)
        total_ref[at, :] = second_in
        second_ref[at, :] = second_in.astype(bf16)
        return pooled, shift, gain, down

    zero = jnp.zeros((8, width), f32)
    pooled, shift, gain, down = over_strips(second_norm, (zero,) * 4)
    tally(6, gain)
    tally(7, shift)
    tally(5, down)
    sum_ref[pl.ds(POOL_ROW + step // blocks, 1), :] += (
        jnp.sum(pooled, axis=0, keepdims=True) * inv_length
    )

    @pl.when(step > 0)
    def _():
        give(inner_ref, inner_all, step - 1).wait()

    def backward(index, carry):
        start = index * width

        def chunk(i):
            return pl.ds(pl.multiple_of(start + i * CHUNK, CHUNK), CHUNK)

        def back(i):
            return mul(second_ref[...], wd_ref[chunk(i), :], NT)

        grad = back(0)
        for i in range(len(parts)):
            ahead = back(i + 1) if i + 1 < len(parts) else None
            bias = jnp.zeros((8, CHUNK), f32)
            for at in strips(2 * STRIP):
                inner = grad[at] * slope_ref[at, chunk(i)]
                bias += by_eight(inner).sum(axis=0)
                inner_ref[at, chunk(i)] = inner.astype(bf16)
            sum_ref[pl.ds(8 + index, 1), parts[i]] += jnp.sum(bias, axis=0, keepdims=True)
            grad = ahead
        total_ref[...] += mul(inner_ref[:, columns(index)], wu_ref[:, columns(index)], NT)
        return carry

    lax.fori_loop(0, groups, backward, 0)
    give(inner_ref, inner_all, step).start()

    def first_norm_back(at, carry):
        gain, shift, out = carry
        first_up = total_ref[at, :]
        normed = normed_ref[at, :]
        gain += by_eight(first_up * normed).sum(axis=0)
        shift += by_eight(first_up).sum(axis=0)
        branch_in = norm_back(first_up * gain_one, normed, scale_ref[at, :1])
        out += by_eight(branch_in).sum(axis=0)
        branch_ref[at, :] = branch_in
        return gain, shift, out

    gain, shift, out = over_strips(first_norm_back, (zero,) * 3)
    tally(3, gain)
    tally(4, shift)
    tally(2, out)
    mg_ref[...] = mul(branch_ref[...].astype(bf16), wo_ref[...], NT).astype(bf16)

    @pl.when(step == steps - 1)
    def _():
        give(act_ref, act_all, step).wait()
        give(inner_ref, inner_all, step).wait()


def row_work(held, info, stacked, cot, pool, w_out, w_up, w_down, vecs, count):
    total, width = cot.shape
    full = total // count
    assert POOL_ROW + count <= SUM_ROWS
    hidden = w_up.shape[1]
    blocks = full // ROWS
    narrow = pl.BlockSpec((ROWS, width), lambda i, *_: (i, 0))
    anywhere = pl.BlockSpec(memory_space=pl.ANY)
    thin = jax.ShapeDtypeStruct((total, width), bf16)
    thick = jax.ShapeDtypeStruct((total, hidden), bf16)
    return pl.pallas_call(
        functools.partial(rows_kernel, blocks, count, held),
        grid_spec=pltpu.PrefetchScalarGridSpec(
            num_scalar_prefetch=1,
            grid=(total // ROWS,),
            in_specs=[
                pl.BlockSpec((1, ROWS, width), lambda i, *_: (0, i, 0)),
                pl.BlockSpec((1, ROWS, width), lambda i, *_: (1, i, 0)),
                narrow,
                fixed(pool.shape),
                fixed((width, width)),
                fixed(vecs.shape),
                anywhere,
                anywhere,
            ],
            out_specs=[
                narrow,
                narrow,
                anywhere,
                narrow,
                anywhere,
                narrow,
                narrow,
                pl.BlockSpec((SUM_ROWS, width), lambda i, *_: (0, 0)),
            ],
            scratch_shapes=[
                pltpu.VMEM((width, hidden), bf16),
                pltpu.VMEM((hidden, width), bf16),
                pltpu.VMEM((ROWS, hidden), bf16),
                pltpu.VMEM((ROWS, hidden), bf16),
                pltpu.VMEM((ROWS, hidden), f32),
                pltpu.VMEM((ROWS, width), f32),
                pltpu.VMEM((ROWS, width), f32),
                pltpu.VMEM((ROWS, width), f32),
                pltpu.VMEM((ROWS, PAIR), f32),
                pltpu.SemaphoreType.DMA((4,)),
            ],
        ),
        out_shape=[
            thin,
            thin,
            thick,
            thin,
            thick,
            jax.ShapeDtypeStruct((total, width), f32),
            thin,
            jax.ShapeDtypeStruct((SUM_ROWS, width), f32),
        ],
        compiler_params=PARAMS,
        cost_estimate=cost(
            4 * total * width * (width + 2 * hidden),
            2 * total * (8 * width + 2 * hidden) + 2 * width * (width + 2 * hidden),
        ),
    )(info, stacked, stacked, cot, pool, w_out, vecs, w_up, w_down)


def dense_outer_kernel(side_ref, act_ref, second_ref, low_ref, inner_ref, out_ref):
    step = pl.program_id(0)
    half = pl.num_programs(0) // 2

    @pl.when(step < half)
    def _():
        out_ref[0] = mul(act_ref[...], second_ref[...], TN).astype(bf16)

    @pl.when(step >= half)
    def _():
        out_ref[0] = mul(low_ref[...], inner_ref[...], TN).astype(bf16)


def dense_outer(at, flip, info, act, second, low, inner):
    total, width = second.shape
    wide = act.shape[1] // width
    half = wide // 2
    return pl.pallas_call(
        dense_outer_kernel,
        grid_spec=pltpu.PrefetchScalarGridSpec(
            num_scalar_prefetch=1,
            grid=(wide,),
            in_specs=[
                pl.BlockSpec(
                    (total, width), lambda i, s: (0, (s[at] ^ flip) * half + jnp.minimum(i, half - 1))
                ),
                fixed((total, width)),
                fixed((total, width)),
                pl.BlockSpec(
                    (total, width), lambda i, s: (0, (s[at] ^ flip) * half + jnp.maximum(i - half, 0))
                ),
            ],
            out_specs=pl.BlockSpec((1, width, width), lambda i, s: (i, 0, 0)),
        ),
        out_shape=jax.ShapeDtypeStruct((wide, width, width), bf16),
        compiler_params=SMALL,
        cost_estimate=cost(
            2 * total * width * width * wide, 2 * (wide + 2) * total * width + 2 * wide * width * width
        ),
    )(info, act, second, low, inner).reshape(wide * width, width)


def attend_outer_kernel(side_ref, left_ref, right_ref, out_ref):
    out_ref[0] = mul(left_ref[0], right_ref[0], TN).astype(bf16)


def attend_outer(at, flip, info, stacked, grads):
    total, width = stacked.shape[1:]
    return pl.pallas_call(
        attend_outer_kernel,
        grid_spec=pltpu.PrefetchScalarGridSpec(
            num_scalar_prefetch=1,
            grid=(2,),
            in_specs=[
                pl.BlockSpec((1, total, width), lambda i, s: (((s[at] ^ flip) * 2 + i) // 3, 0, 0)),
                pl.BlockSpec((1, total, width), lambda i, s: ((s[at] ^ flip) * 2 + i, 0, 0)),
            ],
            out_specs=pl.BlockSpec((1, width, width), lambda i, s: (i, 0, 0)),
        ),
        out_shape=jax.ShapeDtypeStruct((2, width, width), bf16),
        compiler_params=SMALL,
        cost_estimate=cost(4 * total * width * width, 8 * total * width + 4 * width * width),
    )(info, stacked, grads).reshape(2 * width, width)


def input_kernel(branch_ref, dq_ref, dk_ref, dv_ref, wq_ref, wk_ref, wv_ref, out_ref):
    total = branch_ref[...] + mul(dq_ref[0], wq_ref[...], NT)
    total += mul(dk_ref[0], wk_ref[...], NT)
    total += mul(dv_ref[0], wv_ref[...], NT)
    out_ref[...] = total.astype(bf16)


def input_grad(branch_in, grads, w_query, w_key, w_value):
    total, width = branch_in.shape
    rows = pl.BlockSpec((BACK_ROWS, width), lambda i: (i, 0))
    return pl.pallas_call(
        input_kernel,
        grid=(total // BACK_ROWS,),
        in_specs=[rows]
        + [pl.BlockSpec((1, BACK_ROWS, width), lambda i, at=at: (at, i, 0)) for at in range(3)]
        + [fixed((width, width))] * 3,
        out_specs=rows,
        out_shape=jax.ShapeDtypeStruct((total, width), bf16),
        compiler_params=SMALL,
        cost_estimate=cost(6 * total * width * width, 12 * total * width + 6 * width * width),
    )(branch_in, grads, grads, grads, w_query, w_key, w_value)


def exchange(value, axis, mask):
    count = lax.axis_size(axis)
    return lax.ppermute(value, axis, [(i, i ^ mask) for i in range(count)])


def to_passages(value):
    count = lax.axis_size("seq")
    mine = lax.axis_index("seq")
    held, piece, width = value.shape
    own = held // count
    whole = jnp.zeros((own, piece * count, width), value.dtype)
    for mask in range(count):
        peer = mine ^ mask
        part = lax.dynamic_slice_in_dim(value, peer * own, own, 0)
        if mask:
            part = exchange(part, "seq", mask)
        whole = lax.dynamic_update_slice_in_dim(whole, part, peer * piece, 1)
    return whole


def position_pieces(value):
    count = lax.axis_size("seq")
    piece = value.shape[1] // count
    mine = lax.axis_index("seq")
    return [
        lax.dynamic_slice_in_dim(value, (mine ^ mask) * piece, piece, 1) for mask in range(count)
    ]


def traded(pieces):
    return [exchange(part, "seq", mask) if mask else part for mask, part in enumerate(pieces)]


def to_positions(pieces):
    mine = lax.axis_index("seq")
    own, piece, width = pieces[0].shape
    result = jnp.zeros((own * len(pieces), piece, width), pieces[0].dtype)
    for mask, part in enumerate(pieces):
        result = lax.dynamic_update_slice_in_dim(result, part, (mine ^ mask) * own, 0)
    return result


def axis_bits(axis):
    return [(axis, 1 << i) for i in range(lax.axis_size(axis).bit_length() - 1)]


def upper(dim):
    axis, mask = dim
    return (lax.axis_index(axis) & mask) // mask


def swap(value, dim):
    return exchange(value, dim[0], dim[1])


def total_of(parts):
    total = parts[0].astype(f32)
    for part in parts[1:]:
        total += part.astype(f32)
    return total.astype(bf16)


PARTS = 3
SHARD_STEP = 16


class Plan:
    def __init__(self, rows):
        dims = axis_bits("seq") + axis_bits("dp")
        self.first = dims[0]
        rest = dims[1:]
        self.rows = rows // PARTS
        halved = 0
        while halved < len(rest) and (self.rows >> (halved + 1)) % SHARD_STEP == 0:
            halved += 1
        self.last = rest[halved - 1]
        self.plain = rest[halved:]
        split = rest[: halved - 1]
        self.orders = [split[i % len(split) :] + split[: i % len(split)] for i in range(PARTS)]
        self.shards = 1 << halved
        self.shard = self.rows >> halved

    def table(self, blocks, width, each):
        places = {}
        devices = 1
        weight = {}
        for axis in ("seq", "dp"):
            for _, mask in axis_bits(axis):
                weight[(axis, mask)] = devices
                devices *= 2
        for side in range(2):
            for part, order in enumerate(self.orders):
                dims = [self.last] + order[::-1]
                for code in range(self.shards):
                    device = side * weight[self.first]
                    device += sum(weight[d] for i, d in enumerate(dims) if (code >> i) & 1)
                    row = part * self.rows + code * self.shard
                    places[side, row] = device * each + part * self.shard
        half = blocks // 4
        found = []
        for block in range(blocks):
            side = block % (2 * half) // half
            local = block // (2 * half) * half + block % half
            for row in range(0, width, self.shard):
                found.append(places[side, local * width + row])
        return found

    def codes(self):
        found = []
        for order in self.orders:
            code = upper(self.last)
            for at, dim in enumerate(reversed(order)):
                code += upper(dim) << (at + 1)
            found.append(code)
        return [code.astype(jnp.int32) for code in found]


class Chain:
    def __init__(self):
        self.token = None

    def tie(self, values):
        if self.token is None:
            return values
        return lax.optimization_barrier((values, self.token))[0]

    def mark(self, values):
        self.token = values
        return values


def scatter_steps(plan, chain, keep, got, found):
    pairs = [[keep, got]] * PARTS
    bases = [i * plan.rows for i in range(PARTS)]
    size = plan.rows
    for step in range(len(plan.orders[0])):
        pairs = chain.tie(pairs)
        size //= 2
        dims = [order[step] for order in plan.orders]

        def halves(pair, base, at):
            return total_of([lax.dynamic_slice_in_dim(p, base + at * size, size, 0) for p in pair])

        sends = [halves(p, base, 1 - upper(d)) for p, base, d in zip(pairs, bases, dims)]
        chain.mark(sends)
        mine = [halves(p, base, upper(d)) for p, base, d in zip(pairs, bases, dims)]
        pairs = [[m, swap(s, d)] for m, s, d in zip(mine, sends, dims)]
        bases = [0] * PARTS
        yield
    size = plan.shard
    bit = upper(plan.last)
    pairs = chain.tie(pairs)

    def side(at):
        return jnp.concatenate(
            [total_of([lax.dynamic_slice_in_dim(p, at * size, size, 0) for p in pair]) for pair in pairs],
            axis=0,
        )

    send = chain.mark(side(1 - bit))
    shard = side(bit)
    got = swap(send, plan.last)
    yield
    shard, got = chain.tie((shard, got))
    shard = total_of([shard, got])
    for dim in plan.plain:
        shard = total_of([shard, swap(shard, dim)])
    found.append(chain.mark(shard))
    yield


def gather_steps(plan, chain, shard, found):
    size = plan.shard
    got = swap(shard, plan.last)
    yield
    values = [(shard[i * size : (i + 1) * size], got[i * size : (i + 1) * size]) for i in range(PARTS)]
    for step in reversed(range(len(plan.orders[0]))):
        values = chain.tie(values)
        values = [jnp.concatenate(pair, axis=0) for pair in values]
        chain.mark(values)
        values = [(v, swap(v, order[step])) for v, order in zip(values, plan.orders)]
        yield
    values = chain.tie(values)
    chain.mark(values)
    found += [v for pair in values for v in pair]
    found += [swap(v, plan.first) for v in found]
    yield


def place(plan, refs, codes, row, store):
    part = row // plan.rows
    shard = ((row % plan.rows) // plan.shard) ^ codes[part]
    half = plan.shards // 2
    at = pl.ds(pl.multiple_of((shard & (half - 1)) * plan.shard, plan.shard), plan.shard)
    low, high = refs[2 * part][at, :], refs[2 * part + 1][at, :]
    store(jnp.where(shard >= half, high.astype(f32), low.astype(f32)))


def dense_place_kernel(
    shard, each, held, table_ref, info_ref, all_ref, down_ref, up_ref, vec_ref, pool_ref, hold_ref, word_ref, sems, word_sem
):
    step, steps = pl.program_id(0), pl.num_programs(0)
    width = down_ref.shape[1]
    parts = width // shard

    def fetch(block, slot):
        for i in range(parts):
            at = pl.multiple_of(table_ref[block * parts + i], SHARD_STEP)
            pltpu.make_async_copy(
                all_ref.at[pl.ds(at, shard)],
                hold_ref.at[slot, pl.ds(i * shard, shard)],
                sems.at[slot],
            ).start()

    def words(device):
        return pltpu.make_async_copy(
            all_ref.at[pl.ds(device * each + each - 2 * SUM_ROWS, 2 * SUM_ROWS)],
            word_ref.at[device],
            word_sem,
        )

    devices = word_ref.shape[0]

    @pl.when(step == 0)
    def _():
        fetch(0, 0)
        for device in range(devices):
            words(device).start()

    @pl.when(step + 1 < steps)
    def _():
        fetch(step + 1, (step + 1) % 2)

    slot = step % 2
    pltpu.make_async_copy(all_ref.at[pl.ds(0, width)], hold_ref.at[slot], sems.at[slot]).wait()

    @pl.when(step < steps // 2)
    def _():
        down_ref[...] = hold_ref[slot].astype(f32)

    @pl.when(step >= steps // 2)
    def _():
        up_ref[...] = hold_ref[slot].astype(f32)

    @pl.when(step == steps - 1)
    def _():
        pltpu.make_async_copy(word_ref, word_ref, word_sem).wait()

        def both(device):
            return word_ref[device, :SUM_ROWS].astype(f32) + word_ref[device, SUM_ROWS:].astype(f32)

        vec_ref[...] = lax.fori_loop(
            0, devices, lambda i, total: total + both(i), jnp.zeros(vec_ref.shape, f32)
        )
        group = pool_ref.shape[0]
        for i in range(group):
            pool_ref[i] = both(info_ref[held] + i)[POOL_ROW:]


def dense_place(plan, gathered, each, width, wide, devices, seq_count, group):
    table = jnp.array(plan.table(2 * wide, width, each), jnp.int32)
    return pl.pallas_call(
        functools.partial(dense_place_kernel, plan.shard, each, 0),
        grid_spec=pltpu.PrefetchScalarGridSpec(
            num_scalar_prefetch=2,
            grid=(2 * wide,),
            in_specs=[pl.BlockSpec(memory_space=pl.ANY)],
            out_specs=[
                pl.BlockSpec((width, width), lambda i, *_: (jnp.minimum(i, wide - 1), 0)),
                pl.BlockSpec((width, width), lambda i, *_: (0, jnp.maximum(i - wide, 0))),
                pl.BlockSpec((SUM_ROWS, width), lambda i, *_: (0, 0)),
                pl.BlockSpec((seq_count, SUM_ROWS - POOL_ROW, width), lambda i, *_: (0, 0, 0)),
            ],
            scratch_shapes=[
                pltpu.VMEM((2, width, width), bf16),
                pltpu.VMEM((devices, 2 * SUM_ROWS, width), bf16),
                pltpu.SemaphoreType.DMA((2,)),
                pltpu.SemaphoreType.DMA(()),
            ],
        ),
        out_shape=[
            jax.ShapeDtypeStruct((wide * width, width), f32),
            jax.ShapeDtypeStruct((width, wide * width), f32),
            jax.ShapeDtypeStruct((SUM_ROWS, width), f32),
            jax.ShapeDtypeStruct((seq_count, SUM_ROWS - POOL_ROW, width), f32),
        ],
        compiler_params=PARAMS,
        cost_estimate=cost(0, 12 * wide * width * width),
    )(table, group, gathered)


def attend_place_kernel(plan, first_code, at, flip, info_ref, *refs):
    sources, (hold_ref, sems) = refs[: 2 * PARTS], refs[-2:]
    outs = refs[-6:-2]
    codes = [info_ref[first_code + i] for i in range(PARTS)]
    own = info_ref[at] ^ flip
    width = hold_ref.shape[2]

    def move(block, act):
        for side in range(2):

            @pl.when(own == side)
            def _():
                act(pltpu.make_async_copy(hold_ref.at[block], outs[2 * side + block], sems.at[block]))

    for block in range(2):
        for row in range(0, width, plan.shard):

            def store(value, row=row):
                hold_ref[block, row : row + plan.shard, :] = value

            place(plan, sources, codes, block * width + row, store)
        move(block, lambda copy: copy.start())
    for block in range(2):
        move(block, lambda copy: copy.wait())


def attend_place(plan, first_code, at, flip, info, sources, width, before):
    kept = list(before)
    return pl.pallas_call(
        functools.partial(attend_place_kernel, plan, first_code, at, flip),
        grid_spec=pltpu.PrefetchScalarGridSpec(
            num_scalar_prefetch=1,
            grid=(1,),
            in_specs=[fixed(x.shape) for x in sources]
            + [pl.BlockSpec(memory_space=pl.ANY)] * len(kept),
            out_specs=[pl.BlockSpec(memory_space=pl.ANY)] * 4,
            scratch_shapes=[pltpu.VMEM((2, width, width), f32), pltpu.SemaphoreType.DMA((2,))],
        ),
        out_shape=[jax.ShapeDtypeStruct((width, width), f32)] * 4,
        input_output_aliases={1 + len(sources) + i: i for i in range(len(kept))},
        compiler_params=SMALL,
        cost_estimate=cost(0, 12 * width * width),
    )(info, *sources, *kept)


def shards(
    tokens,
    lengths,
    w_query,
    b_query,
    w_key,
    w_value,
    b_value,
    w_out,
    b_out,
    gain_one,
    shift_one,
    w_up,
    b_up,
    w_down,
    b_down,
    gain_two,
    shift_two,
    out_grad,
    pooled_grad,
):
    seq_count = lax.axis_size("seq")
    held, piece, width = tokens.shape
    full = piece * seq_count
    count = held // seq_count
    mine = lax.axis_index("seq")
    wide = w_up.shape[1] // width
    total = count * full

    def flat(value):
        return value.reshape(total, width)

    def split(value):
        return value.reshape(count, full, width)

    dense_plan = Plan(wide * width)
    outer_plan = Plan(2 * width)
    first = axis_bits("seq")[0]
    scalars = [mine, upper(first)] + dense_plan.codes() + outer_plan.codes()
    own_at, dense_at, outer_at = held + 1, held + 2, held + 2 + PARTS
    info = jnp.concatenate([lengths, jnp.stack([v.astype(jnp.int32) for v in scalars])])
    vecs = jnp.concatenate(
        [b_query, b_value, b_out, gain_one, shift_one, b_down, gain_two, shift_two, b_up]
    )
    vecs = vecs.astype(f32).reshape(-1, width)

    weights = [w_query, w_key, w_value, vecs]
    done = None
    source = tokens
    parts = []
    for passage in range(count):
        if parts:
            source = lax.optimization_barrier((tokens, parts))[0]
        parts = [
            exchange(
                lax.dynamic_slice_in_dim(source, (mine ^ mask) * count + passage, 1, 0), "seq", mask
            )
            for mask in range(1, seq_count)
        ]
        done = attend(passage, count, info, tokens, parts, weights, done)
    stacked, q, k, v, stat = done
    cot = to_passages(lax.optimization_barrier((out_grad, parts))[0])
    stacked = stacked.reshape(2, total, width)
    result, first_low, act, second, inner, branch_in, mixed_grad, sums = row_work(
        held, info, stacked, flat(cot), pooled_grad, w_out, w_up, w_down, vecs, count
    )
    chain = Chain()
    pieces = chain.mark(position_pieces(split(result)))
    out_pieces = traded(pieces)
    send = dense_outer(own_at, 1, info, *chain.tie((act, second, first_low, inner)))
    chain.mark(send)
    got = swap(send, first)
    keep = chain.mark(dense_outer(own_at, 0, info, *chain.tie((act, second, first_low, inner))))
    dense, shard, outer = [], [], []
    dense_steps = scatter_steps(dense_plan, chain, keep, got, dense)
    next(dense_steps)
    chain.mark((chain.token, out_pieces))
    block_out = to_positions(out_pieces)
    grads, words = attend_back(
        held,
        info,
        q,
        k,
        v,
        chain.tie(split(mixed_grad)),
        stacked.reshape(2, count, full, width),
        split(branch_in),
        stat,
        sums,
    )
    chain.mark(words)
    grads = grads.reshape(4, total, width)
    next(dense_steps)
    send = attend_outer(own_at, 1, info, stacked, chain.tie(grads))
    chain.mark(send)
    got = swap(send, first)
    keep = attend_outer(own_at, 0, info, stacked, chain.tie(grads))
    chain.mark(keep)
    next(dense_steps)
    outer_steps = scatter_steps(outer_plan, chain, keep, got, shard)
    next(outer_steps)
    input_low = input_grad(branch_in, chain.tie(grads), w_query, w_key, w_value)
    chain.mark(input_low)
    next(dense_steps)
    next(outer_steps)
    for _ in dense_steps:
        pass
    gathered = jnp.concatenate([dense[0], words], axis=0)
    each = gathered.shape[0]
    gathered = chain.mark(gathered)
    gathered = lax.all_gather(gathered, ("dp", "seq"), axis=0, tiled=True)
    next(outer_steps)
    next(outer_steps)
    pieces = chain.mark(position_pieces(split(chain.tie(input_low))))
    in_pieces = traded(pieces)
    for _ in outer_steps:
        pass
    outer_steps = gather_steps(outer_plan, chain, shard[0], outer)
    next(outer_steps)
    next(outer_steps)
    next(outer_steps)
    chain.mark((chain.token, in_pieces))
    tokens_grad = to_positions(in_pieces)
    for _ in outer_steps:
        pass
    group = (lax.axis_index("dp") * seq_count).astype(jnp.int32)[None]
    down_sum, up_sum, vectors, pooled = dense_place(
        dense_plan, chain.tie(gathered), each, width, wide, gathered.shape[0] // each, seq_count, group
    )
    pooled = pooled[:, :count].reshape(held, width)

    def place_outer(flip, before):
        pick = outer[2 * PARTS :] if flip else outer[: 2 * PARTS]
        return chain.mark(
            attend_place(outer_plan, outer_at, own_at, flip, info, chain.tie(pick), width, before)
        )

    placed = place_outer(0, [])
    outer = place_outer(1, placed)
    return (
        block_out,
        pooled,
        tokens_grad,
        outer[0],
        vectors[0],
        outer[1],
        outer[2],
        vectors[1],
        outer[3],
        vectors[2],
        vectors[3],
        vectors[4],
        up_sum,
        vectors[8 : 8 + wide].reshape(-1),
        down_sum,
        vectors[5],
        vectors[6],
        vectors[7],
    )


def solution(mesh):
    in_specs = (
        (P("dp", "seq", None), P("dp"))
        + (P(),) * 15
        + (P("dp", "seq", None), P("dp", None))
    )
    out_specs = (P("dp", "seq", None), P("dp", None), P("dp", "seq", None)) + (P(),) * 15
    return jax.shard_map(shards, mesh=mesh, in_specs=in_specs, out_specs=out_specs, check_vma=False)
```

```python
import functools

import jax
import jax.numpy as jnp
from jax import lax
from jax.experimental import pallas as pl
from jax.experimental.pallas import tpu as pltpu
from jax.sharding import PartitionSpec as P

HEADS = 12
HEAD_DIM = 64
PAIR = 2 * HEAD_DIM
PAIRS = HEADS // 2
SCALE = HEAD_DIM ** (-0.5)
ROWS = 512
BACK_ROWS = 256
STRIP = 32
TOGETHER = 1
BACK_TOGETHER = 3
STAT_ROWS = 16
CHUNK = 256
KEY_STEP = 128
VMEM_BYTES = 62 * 1024 * 1024
SMALL_BYTES = 40 * 1024 * 1024
SUM_ROWS = 16
POOL_ROW = 12

eps = 1e-06
root_half = 0.7071067811865476
inv_root_two_pi = 0.3989422804014327

f32 = jnp.float32
bf16 = jnp.bfloat16

NN = (((1,), (0,)), ((), ()))
NT = (((1,), (1,)), ((), ()))
TN = (((0,), (0,)), ((), ()))


def mul(left, right, dims=NN):
    return lax.dot_general(left, right, dims, preferred_element_type=f32)


def fixed(shape):
    return pl.BlockSpec(shape, lambda *_: (0,) * len(shape), pipeline_mode=pl.Buffered(1))


PARAMS = pltpu.CompilerParams(dimension_semantics=("arbitrary",), vmem_limit_bytes=VMEM_BYTES)
SMALL = pltpu.CompilerParams(dimension_semantics=("arbitrary",), vmem_limit_bytes=SMALL_BYTES)


def cost(flops, moved, exps=0):
    return pl.CostEstimate(flops=int(flops), bytes_accessed=int(moved), transcendentals=int(exps))


def over_extents(length, full, body):
    for extent in range(KEY_STEP, full + 1, KEY_STEP):
        pl.when((length > extent - KEY_STEP) & (length <= extent))(functools.partial(body, extent))


def by_eight(value):
    return value.reshape(value.shape[0] // 8, 8, value.shape[1])


def fill_dead(dead_ref, extent, length):
    key_at = lax.broadcasted_iota(jnp.int32, dead_ref.shape, 0) + (extent - KEY_STEP)
    dead_ref[...] = jnp.where(key_at < length, 0.0, -1e30)


def live_strip(scores, dead_ref, extent, row):
    strip = scores[row : row + STRIP]
    last = row - (extent - KEY_STEP)
    return strip + dead_ref[last : last + STRIP] if last >= 0 else strip


def attend_kernel(pieces, passage, count, held, info_ref, *refs):
    part_refs, refs = refs[:pieces], refs[pieces:]
    wq_ref, wk_ref, wv_ref, vec_ref = refs[:4]
    xm_ref, q_ref, k_ref, v_ref, stat_ref, prob_ref, dead_ref = refs[-7:]
    x_ref, mix_ref = xm_ref.at[0], xm_ref.at[1]
    mine = info_ref[held]
    length = info_ref[mine * count + passage]
    size = part_refs[0].shape[1]
    for mask, part_ref in enumerate(part_refs):
        x_ref[0, pl.ds(pl.multiple_of((mine ^ mask) * size, size), size)] = part_ref[0]

    def project(index, carry):
        at = pl.ds(pl.multiple_of(index * CHUNK, CHUNK), CHUNK)
        x = x_ref[0]
        q_ref[0, :, at] = (mul(x, wq_ref[:, at]) + vec_ref[0:1, at]).astype(bf16)
        k_ref[0, :, at] = mul(x, wk_ref[:, at]).astype(bf16)
        v_ref[0, :, at] = (mul(x, wv_ref[:, at]) + vec_ref[1:2, at]).astype(bf16)
        return carry

    lax.fori_loop(0, wq_ref.shape[1] // CHUNK, project, 0)
    stat_ref[0] = jnp.zeros(stat_ref.shape[1:], f32)
    full = size * pieces
    lane = lax.broadcasted_iota(jnp.int32, (1, PAIR), 1)

    def run(extent):
        fill_dead(dead_ref, extent, length)

        def head(at, number, half, slot):
            q, k = q_ref[0, :, at], k_ref[0, :extent, at]
            own = (lane >= half * HEAD_DIM) & (lane < (half + 1) * HEAD_DIM)
            scores = mul(jnp.where(own, k * SCALE, 0).astype(bf16), q, NT)
            top = jnp.full((8, full), -jnp.inf, f32)
            for row in range(0, extent, STRIP):
                top = jnp.maximum(top, by_eight(live_strip(scores, dead_ref, extent, row)).max(axis=0))
            top = jnp.max(top, axis=0, keepdims=True)
            total = jnp.zeros((8, full), f32)
            for row in range(0, extent, STRIP):
                expo = jnp.exp(live_strip(scores, dead_ref, extent, row) - top)
                total += by_eight(expo).sum(axis=0)
                prob_ref[slot, row : row + STRIP] = expo.astype(bf16)
            total = jnp.sum(total, axis=0, keepdims=True)
            stat_ref[0, pl.ds(number, 1), :] = top + jnp.log(total)
            return 1.0 / total

        def group(index, carry):
            for i in range(TOGETHER):
                pair = index * TOGETHER + i
                at = pl.ds(pl.multiple_of(pair * PAIR, PAIR), PAIR)
                values = v_ref[0, :extent, at].T
                mixed = []
                for half in range(2):
                    slot = 2 * i + half
                    scale = head(at, pair * 2 + half, half, slot)
                    own = values[half * HEAD_DIM : (half + 1) * HEAD_DIM]
                    mixed.append(mul(own, prob_ref[slot, :extent]) * scale)
                mix_ref[0, :, at] = jnp.concatenate(mixed, axis=0).T.astype(bf16)
            return carry

        lax.fori_loop(0, PAIRS // TOGETHER, group, 0)

    over_extents(length, full, run)


def attend(passage, count, info, tokens, parts, weights, before):
    held, piece, width = tokens.shape
    pieces = len(parts) + 1
    full = piece * pieces
    rows = pl.BlockSpec((1, full, width), lambda i, s: (passage, 0, 0))
    act = jax.ShapeDtypeStruct((count, full, width), bf16)
    got = pl.BlockSpec((1, piece, width), lambda i, s: (0, 0, 0))
    kept = [] if before is None else list(before)
    first_kept = 1 + pieces + len(weights)
    return pl.pallas_call(
        functools.partial(attend_kernel, pieces, passage, count, held),
        grid_spec=pltpu.PrefetchScalarGridSpec(
            num_scalar_prefetch=1,
            grid=(1,),
            in_specs=[pl.BlockSpec((1, piece, width), lambda i, s: (s[held] * count + passage, 0, 0))]
            + [got] * len(parts)
            + [fixed(w.shape) for w in weights]
            + [pl.BlockSpec(memory_space=pl.ANY)] * len(kept),
            out_specs=[pl.BlockSpec((2, 1, full, width), lambda i, s: (0, passage, 0, 0))]
            + [rows] * 3
            + [pl.BlockSpec((1, STAT_ROWS, full), lambda i, s: (passage, 0, 0))],
            scratch_shapes=[
                pltpu.VMEM((2 * TOGETHER, full, full), bf16),
                pltpu.VMEM((KEY_STEP, full), f32),
            ],
        ),
        out_shape=[jax.ShapeDtypeStruct((2, count, full, width), bf16)]
        + [act] * 3
        + [jax.ShapeDtypeStruct((count, STAT_ROWS, full), f32)],
        input_output_aliases={first_kept + i: i for i in range(len(kept))},
        compiler_params=PARAMS,
        cost_estimate=cost(
            2 * full * (3 * width * width + 4 * 2 * full * width),
            12 * full * width + 6 * width * width,
        ),
    )(info, tokens, *parts, *weights, *kept)


def attend_back_kernel(
    held,
    info_ref,
    q_ref,
    k_ref,
    v_ref,
    mg_ref,
    mix_ref,
    branch_ref,
    stat_ref,
    sum_ref,
    grads_ref,
    word_ref,
    bias_ref,
    along_ref,
    prob_ref,
    score_ref,
    dead_ref,
):
    dq_ref, dk_ref, dv_ref = (grads_ref.at[i] for i in range(3))
    grads_ref[3] = branch_ref[...].astype(bf16)
    full, width = q_ref.shape[1:]
    length = info_ref[info_ref[held] * pl.num_programs(0) + pl.program_id(0)]
    lane = lax.broadcasted_iota(jnp.int32, (1, PAIR), 1)
    row = lax.broadcasted_iota(jnp.int32, (8, 1), 0)

    @pl.when(pl.program_id(0) == 0)
    def _():
        bias_ref[...] = sum_ref[...]

    feature = lax.broadcasted_iota(jnp.int32, (STAT_ROWS, width), 1)
    number = lax.broadcasted_iota(jnp.int32, (STAT_ROWS, width), 0)
    ours = jnp.where(
        (feature >= number * HEAD_DIM) & (feature < (number + 1) * HEAD_DIM), 1.0, 0.0
    ).astype(bf16)
    product = mg_ref[0].astype(f32) * mix_ref[0, 0].astype(f32)
    high = product.astype(bf16)
    low = (product - high.astype(f32)).astype(bf16)
    along_ref[...] = mul(ours, high, NT) + mul(ours, low, NT)

    def run(extent):
        fill_dead(dead_ref, extent, length)
        if extent < full:
            dk_ref[0, extent:] = jnp.zeros((full - extent, width), bf16)
            dv_ref[0, extent:] = jnp.zeros((full - extent, width), bf16)

        def group(index, carry):
            for i in range(BACK_TOGETHER):
                pair = index * BACK_TOGETHER + i
                at = pl.ds(pl.multiple_of(pair * PAIR, PAIR), PAIR)
                q, mg = q_ref[0, :, at], mg_ref[0, :, at]
                k, v = k_ref[0, :extent, at], v_ref[0, :extent, at]
                keys = k.T
                dq, dk, dv = [], [], []
                for half in range(2):
                    slot = 2 * i + half
                    own = (lane >= half * HEAD_DIM) & (lane < (half + 1) * HEAD_DIM)
                    scores = mul(jnp.where(own, k * SCALE, 0).astype(bf16), q, NT)
                    prob_grad = mul(jnp.where(own, v, 0).astype(bf16), mg, NT)
                    log_row = stat_ref[0, pl.ds(pair * 2 + half, 1), :]
                    along = along_ref[pl.ds(pair * 2 + half, 1), :]
                    for at_row in range(0, extent, STRIP):
                        rows = slice(at_row, at_row + STRIP)
                        probs = jnp.exp(live_strip(scores, dead_ref, extent, at_row) - log_row)
                        prob_ref[slot, rows] = probs.astype(bf16)
                        score_ref[slot, rows] = (probs * (prob_grad[rows] - along)).astype(bf16)
                    score_grad = score_ref[slot, :extent]
                    dv.append(mul(prob_ref[slot, :extent], mg))
                    dk.append(mul(score_grad, q))
                    dq.append(mul(keys[half * HEAD_DIM : (half + 1) * HEAD_DIM], score_grad))
                first = lane < HEAD_DIM
                dq_pair = jnp.concatenate(dq, axis=0).T * SCALE
                dk_pair = jnp.where(first, dk[0], dk[1]) * SCALE
                dv_pair = jnp.where(first, dv[0], dv[1])
                dq_ref[0, :, at] = dq_pair.astype(bf16)
                dk_ref[0, :extent, at] = dk_pair.astype(bf16)
                dv_ref[0, :extent, at] = dv_pair.astype(bf16)
                sums = jnp.where(
                    row == 0,
                    jnp.sum(dq_pair, axis=0, keepdims=True),
                    jnp.where(row == 1, jnp.sum(dv_pair, axis=0, keepdims=True), 0.0),
                )
                bias_ref[0:8, at] += sums
            return carry

        lax.fori_loop(0, PAIRS // BACK_TOGETHER, group, 0)

    over_extents(length, full, run)

    @pl.when(pl.program_id(0) == pl.num_programs(0) - 1)
    def _():
        high = bias_ref[...].astype(bf16)
        word_ref[:SUM_ROWS] = high
        word_ref[SUM_ROWS:] = (bias_ref[...] - high.astype(f32)).astype(bf16)


def attend_back(held, info, q, k, v, mixed_grad, stacked, branch_in, stat, sums):
    count, full, width = q.shape
    rows = pl.BlockSpec((1, full, width), lambda i, *_: (i, 0, 0))
    return pl.pallas_call(
        functools.partial(attend_back_kernel, held),
        grid_spec=pltpu.PrefetchScalarGridSpec(
            num_scalar_prefetch=1,
            grid=(count,),
            in_specs=[rows] * 4
            + [
                pl.BlockSpec((1, 1, full, width), lambda i, *_: (1, i, 0, 0)),
                rows,
                pl.BlockSpec((1, STAT_ROWS, full), lambda i, *_: (i, 0, 0)),
                fixed(sums.shape),
            ],
            out_specs=[
                pl.BlockSpec((4, 1, full, width), lambda i, *_: (0, i, 0, 0)),
                pl.BlockSpec((2 * SUM_ROWS, width), lambda i, *_: (0, 0)),
            ],
            scratch_shapes=[
                pltpu.VMEM(sums.shape, f32),
                pltpu.VMEM((STAT_ROWS, full), f32),
                pltpu.VMEM((2 * BACK_TOGETHER, full, full), bf16),
                pltpu.VMEM((2 * BACK_TOGETHER, full, full), bf16),
                pltpu.VMEM((KEY_STEP, full), f32),
            ],
        ),
        out_shape=[
            jax.ShapeDtypeStruct((4, count, full, width), bf16),
            jax.ShapeDtypeStruct((2 * SUM_ROWS, width), bf16),
        ],
        compiler_params=PARAMS,
        cost_estimate=cost(
            2 * count * full * 10 * 2 * full * width, 16 * count * full * width
        ),
    )(info, q, k, v, mixed_grad, stacked, branch_in, stat, sums)


def norm_parts(hidden):
    centred = hidden - jnp.mean(hidden, axis=1, keepdims=True)
    inv_scale = lax.rsqrt(jnp.mean(centred * centred, axis=1, keepdims=True) + eps)
    return centred * inv_scale, inv_scale


def norm_back(scaled, normed, inv_scale):
    mean = jnp.mean(scaled, axis=1, keepdims=True)
    along = jnp.mean(scaled * normed, axis=1, keepdims=True)
    return (scaled - mean - normed * along) * inv_scale


def gelu_parts(u):
    expo = jnp.exp(u * u * -0.5)
    base = 1.0 + jnp.abs(u) * (0.3275911 * root_half)
    t = pl.reciprocal(base, approx=True)
    t = t * (2.0 - base * t)
    poly = t * (
        0.5 * 0.254829592
        + t
        * (
            0.5 * -0.284496736
            + t * (0.5 * 1.421413741 + t * (0.5 * -1.453152027 + t * (0.5 * 1.061405429)))
        )
    )
    tail = poly * expo
    return jnp.where(u >= 0, 1.0 - tail, tail), expo


def rows_kernel(
    blocks,
    count,
    held,
    info_ref,
    x_ref,
    mix_ref,
    cot_ref,
    pool_ref,
    wo_ref,
    vec_ref,
    wu_all,
    wd_all,
    out_ref,
    low_ref,
    act_all,
    second_ref,
    inner_all,
    branch_ref,
    mg_ref,
    sum_ref,
    wu_ref,
    wd_ref,
    act_ref,
    inner_ref,
    slope_ref,
    first_ref,
    normed_ref,
    total_ref,
    scale_ref,
    sems,
):
    step, steps = pl.program_id(0), pl.num_programs(0)
    rows, width = cot_ref.shape
    hidden_width = wu_ref.shape[1]
    b_out, gain_one, shift_one, b_down, gain_two, shift_two = (
        vec_ref[i : i + 1] for i in range(2, 8)
    )
    passage = info_ref[held] * count + step // blocks
    length = info_ref[passage]
    inv_length = 1.0 / jnp.full((1, width), length, jnp.int32).astype(f32)
    pool = pool_ref[pl.ds(passage, 1), :] * inv_length
    first_row = (step % blocks) * rows
    load_up = pltpu.make_async_copy(wu_all, wu_ref, sems.at[0])
    load_down = pltpu.make_async_copy(wd_all, wd_ref, sems.at[1])

    def give(source_ref, all_ref, at):
        return pltpu.make_async_copy(
            source_ref, all_ref.at[pl.ds(pl.multiple_of(at * rows, rows), rows)], sems.at[2 if source_ref is act_ref else 3]
        )

    @pl.when(step == 0)
    def _():
        load_up.start()
        load_down.start()
        sum_ref[...] = jnp.zeros(sum_ref.shape, f32)

    def tally(at, value, columns=slice(None)):
        sum_ref[at : at + 1, columns] += jnp.sum(value, axis=0, keepdims=True)

    def strips(size):
        return [slice(i, i + size) for i in range(0, rows, size)]

    groups = width // CHUNK
    chunks = hidden_width // CHUNK
    part = [slice(i * CHUNK, (i + 1) * CHUNK) for i in range(chunks)]
    whole = [slice(i * width, (i + 1) * width) for i in range(hidden_width // width)]
    lanes = scale_ref.shape[1]

    branch = mul(mix_ref[0], wo_ref[...])
    for at in strips(STRIP):
        normed, scale = norm_parts(x_ref[0, at].astype(f32) + branch[at] + b_out)
        first = normed * gain_one + shift_one
        normed_ref[at] = normed
        scale_ref[at] = jnp.broadcast_to(scale, (STRIP, lanes))
        first_ref[at] = first + b_down
        low_ref[at] = first.astype(bf16)

    @pl.when(step == 0)
    def _():
        load_up.wait()
        load_down.wait()

    @pl.when(step > 0)
    def _():
        give(act_ref, act_all, step - 1).wait()

    def up(i):
        return mul(low_ref[...], wu_ref[:, part[i]])

    pre = up(0)
    for i in range(chunks):
        ahead = up(i + 1) if i + 1 < chunks else None
        bias = vec_ref[8 + i // groups : 9 + i // groups, part[i % groups]]
        for at in strips(2 * STRIP):
            u = pre[at] + bias
            phi, expo = gelu_parts(u)
            act_ref[at, part[i]] = (u * phi).astype(bf16)
            slope_ref[at, part[i]] = phi + u * expo * inv_root_two_pi
        if i % groups == 0 and i:
            done = whole[i // groups - 1]
            first_ref[...] += mul(act_ref[:, done], wd_ref[done, :])
        pre = ahead
    last = mul(act_ref[:, whole[-1]], wd_ref[whole[-1], :])
    give(act_ref, act_all, step).start()

    pooled, shift, gain, down = (jnp.zeros((8, width), f32) for _ in range(4))
    for at in strips(STRIP):
        normed, scale = norm_parts(first_ref[at] + last[at])
        result = normed * gain_two + shift_two
        out_ref[at] = result.astype(bf16)
        row_at = lax.broadcasted_iota(jnp.int32, (STRIP, 1), 0) + (first_row + at.start)
        live = jnp.where(row_at < length, 1.0, 0.0)
        pooled += by_eight(result * live).sum(axis=0)
        upstream = cot_ref[at].astype(f32) + live * pool
        gain += by_eight(upstream * normed).sum(axis=0)
        shift += by_eight(upstream).sum(axis=0)
        second_in = norm_back(upstream * gain_two, normed, scale)
        down += by_eight(second_in).sum(axis=0)
        total_ref[at] = second_in
        second_ref[at] = second_in.astype(bf16)
    tally(6, gain)
    tally(7, shift)
    tally(5, down)
    sum_ref[pl.ds(POOL_ROW + step // blocks, 1), :] += (
        jnp.sum(pooled, axis=0, keepdims=True) * inv_length
    )

    @pl.when(step > 0)
    def _():
        give(inner_ref, inner_all, step - 1).wait()

    def back(i):
        return mul(second_ref[...], wd_ref[part[i], :], NT)

    grad = back(0)
    for i in range(chunks):
        ahead = back(i + 1) if i + 1 < chunks else None
        bias = jnp.zeros((8, CHUNK), f32)
        for at in strips(2 * STRIP):
            inner = grad[at] * slope_ref[at, part[i]]
            bias += by_eight(inner).sum(axis=0)
            inner_ref[at, part[i]] = inner.astype(bf16)
        tally(8 + i // groups, bias, part[i % groups])
        if i % groups == 0 and i:
            done = whole[i // groups - 1]
            total_ref[...] += mul(inner_ref[:, done], wu_ref[:, done], NT)
        grad = ahead
    last = mul(inner_ref[:, whole[-1]], wu_ref[:, whole[-1]], NT)
    give(inner_ref, inner_all, step).start()

    gain, shift, out = (jnp.zeros((8, width), f32) for _ in range(3))
    for at in strips(STRIP):
        first_up = total_ref[at] + last[at]
        normed = normed_ref[at]
        gain += by_eight(first_up * normed).sum(axis=0)
        shift += by_eight(first_up).sum(axis=0)
        branch_in = norm_back(first_up * gain_one, normed, scale_ref[at, :1])
        out += by_eight(branch_in).sum(axis=0)
        branch_ref[at] = branch_in
    tally(3, gain)
    tally(4, shift)
    tally(2, out)
    mg_ref[...] = mul(branch_ref[...].astype(bf16), wo_ref[...], NT).astype(bf16)

    @pl.when(step == steps - 1)
    def _():
        give(act_ref, act_all, step).wait()
        give(inner_ref, inner_all, step).wait()


def row_work(held, info, stacked, cot, pool, w_out, w_up, w_down, vecs, count):
    total, width = cot.shape
    full = total // count
    assert POOL_ROW + count <= SUM_ROWS
    hidden = w_up.shape[1]
    blocks = full // ROWS
    narrow = pl.BlockSpec((ROWS, width), lambda i, *_: (i, 0))
    anywhere = pl.BlockSpec(memory_space=pl.ANY)
    thin = jax.ShapeDtypeStruct((total, width), bf16)
    thick = jax.ShapeDtypeStruct((total, hidden), bf16)
    return pl.pallas_call(
        functools.partial(rows_kernel, blocks, count, held),
        grid_spec=pltpu.PrefetchScalarGridSpec(
            num_scalar_prefetch=1,
            grid=(total // ROWS,),
            in_specs=[
                pl.BlockSpec((1, ROWS, width), lambda i, *_: (0, i, 0)),
                pl.BlockSpec((1, ROWS, width), lambda i, *_: (1, i, 0)),
                narrow,
                fixed(pool.shape),
                fixed((width, width)),
                fixed(vecs.shape),
                anywhere,
                anywhere,
            ],
            out_specs=[
                narrow,
                narrow,
                anywhere,
                narrow,
                anywhere,
                narrow,
                narrow,
                pl.BlockSpec((SUM_ROWS, width), lambda i, *_: (0, 0)),
            ],
            scratch_shapes=[
                pltpu.VMEM((width, hidden), bf16),
                pltpu.VMEM((hidden, width), bf16),
                pltpu.VMEM((ROWS, hidden), bf16),
                pltpu.VMEM((ROWS, hidden), bf16),
                pltpu.VMEM((ROWS, hidden), f32),
                pltpu.VMEM((ROWS, width), f32),
                pltpu.VMEM((ROWS, width), f32),
                pltpu.VMEM((ROWS, width), f32),
                pltpu.VMEM((ROWS, PAIR), f32),
                pltpu.SemaphoreType.DMA((4,)),
            ],
        ),
        out_shape=[
            thin,
            thin,
            thick,
            thin,
            thick,
            jax.ShapeDtypeStruct((total, width), f32),
            thin,
            jax.ShapeDtypeStruct((SUM_ROWS, width), f32),
        ],
        compiler_params=PARAMS,
        cost_estimate=cost(
            4 * total * width * (width + 2 * hidden),
            2 * total * (8 * width + 2 * hidden) + 2 * width * (width + 2 * hidden),
        ),
    )(info, stacked, stacked, cot, pool, w_out, vecs, w_up, w_down)


def first_half(plan, info, first_code, part, keep):
    return (info[first_code + part] >> (plan.halved - 1)) & 1 ^ (1 - keep)


def outer_outputs(plan, separate, width):
    size = plan.rows // 2
    if separate:
        return (
            [pl.BlockSpec((size, width), lambda i, s: (0, 0))] * PARTS,
            [jax.ShapeDtypeStruct((size, width), bf16)] * PARTS,
        )
    return (
        [pl.BlockSpec((size, width), lambda i, s: (i, 0))],
        [jax.ShapeDtypeStruct((PARTS * size, width), bf16)],
    )


def give_outer(value, got_refs, out_refs):
    if not got_refs:
        out_refs[0][...] = value.astype(bf16)
        return
    value = (value + got_refs[0][...].astype(f32)).astype(bf16)
    for i, out_ref in enumerate(out_refs):

        @pl.when(pl.program_id(0) == i)
        def _(out_ref=out_ref):
            out_ref[...] = value


def dense_outer_kernel(plan, first_code, keep, shared, info_ref, act_ref, second_ref, low_ref, inner_ref, *refs):
    part = pl.program_id(0)
    piece = 2 * part + first_half(plan, info_ref, first_code, part, keep)
    got_refs, out_refs = refs[:shared], refs[shared:]

    @pl.when(piece < PARTS)
    def _():
        give_outer(mul(act_ref[...], second_ref[...], TN), got_refs, out_refs)

    @pl.when(piece >= PARTS)
    def _():
        give_outer(mul(inner_ref[...], low_ref[...], TN), got_refs, out_refs)


def dense_outer(plan, first_code, at, flip, keep, info, act, second, low, inner, got):
    total, width = second.shape
    size = plan.rows // 2
    shared = [] if got is None else [got]
    out_specs, out_shape = outer_outputs(plan, bool(shared), width)

    def piece(i, s):
        return 2 * i + first_half(plan, s, first_code, i, keep)

    def base(s):
        return (s[at] ^ flip) * PARTS

    return pl.pallas_call(
        functools.partial(dense_outer_kernel, plan, first_code, keep, len(shared)),
        grid_spec=pltpu.PrefetchScalarGridSpec(
            num_scalar_prefetch=1,
            grid=(PARTS,),
            in_specs=[
                pl.BlockSpec(
                    (total, size), lambda i, s: (0, base(s) + jnp.minimum(piece(i, s), PARTS - 1))
                ),
                fixed((total, width)),
                fixed((total, width)),
                pl.BlockSpec(
                    (total, size), lambda i, s: (0, base(s) + jnp.maximum(piece(i, s) - PARTS, 0))
                ),
            ]
            + [pl.BlockSpec((size, width), lambda i, s: (i, 0))] * len(shared),
            out_specs=out_specs,
        ),
        out_shape=out_shape,
        compiler_params=SMALL,
        cost_estimate=cost(
            2 * PARTS * total * size * width, 2 * total * (2 * width + PARTS * size) + 4 * PARTS * size * width
        ),
    )(info, act, second, low, inner, *shared)


def attend_outer_kernel(shared, info_ref, left_ref, right_ref, *refs):
    give_outer(mul(left_ref[0], right_ref[0], TN), refs[:shared], refs[shared:])


def attend_outer(plan, first_code, at, flip, keep, info, stacked, grads, got):
    total, width = stacked.shape[1:]
    size = plan.rows // 2
    steps = width // size
    shared = [] if got is None else [got]
    out_specs, out_shape = outer_outputs(plan, bool(shared), width)

    def piece(i, s):
        return 2 * i + first_half(plan, s, first_code, i, keep)

    def block(i, s):
        return (s[at] ^ flip) * 2 + piece(i, s) // steps

    return pl.pallas_call(
        functools.partial(attend_outer_kernel, len(shared)),
        grid_spec=pltpu.PrefetchScalarGridSpec(
            num_scalar_prefetch=1,
            grid=(PARTS,),
            in_specs=[
                pl.BlockSpec((1, total, size), lambda i, s: (block(i, s) // 3, 0, piece(i, s) % steps)),
                pl.BlockSpec((1, total, width), lambda i, s: (block(i, s), 0, 0)),
            ]
            + [pl.BlockSpec((size, width), lambda i, s: (i, 0))] * len(shared),
            out_specs=out_specs,
        ),
        out_shape=out_shape,
        compiler_params=SMALL,
        cost_estimate=cost(
            2 * PARTS * total * size * width, 2 * total * (2 * width + PARTS * size) + 4 * PARTS * size * width
        ),
    )(info, stacked, grads, *shared)


def input_kernel(branch_ref, dq_ref, dk_ref, dv_ref, wq_ref, wk_ref, wv_ref, out_ref):
    total = branch_ref[...] + mul(dq_ref[0], wq_ref[...], NT)
    total += mul(dk_ref[0], wk_ref[...], NT)
    total += mul(dv_ref[0], wv_ref[...], NT)
    out_ref[...] = total.astype(bf16)


def input_grad(branch_in, grads, w_query, w_key, w_value):
    total, width = branch_in.shape
    rows = pl.BlockSpec((BACK_ROWS, width), lambda i: (i, 0))
    return pl.pallas_call(
        input_kernel,
        grid=(total // BACK_ROWS,),
        in_specs=[rows]
        + [pl.BlockSpec((1, BACK_ROWS, width), lambda i, at=at: (at, i, 0)) for at in range(3)]
        + [fixed((width, width))] * 3,
        out_specs=rows,
        out_shape=jax.ShapeDtypeStruct((total, width), bf16),
        compiler_params=SMALL,
        cost_estimate=cost(6 * total * width * width, 12 * total * width + 6 * width * width),
    )(branch_in, grads, grads, grads, w_query, w_key, w_value)


def exchange(value, axis, mask):
    count = lax.axis_size(axis)
    return lax.ppermute(value, axis, [(i, i ^ mask) for i in range(count)])


def to_passages(value):
    count = lax.axis_size("seq")
    mine = lax.axis_index("seq")
    held, piece, width = value.shape
    own = held // count
    whole = jnp.zeros((own, piece * count, width), value.dtype)
    for mask in range(count):
        peer = mine ^ mask
        part = lax.dynamic_slice_in_dim(value, peer * own, own, 0)
        if mask:
            part = exchange(part, "seq", mask)
        whole = lax.dynamic_update_slice_in_dim(whole, part, peer * piece, 1)
    return whole


def position_pieces(value):
    count = lax.axis_size("seq")
    piece = value.shape[1] // count
    mine = lax.axis_index("seq")
    return [
        lax.dynamic_slice_in_dim(value, (mine ^ mask) * piece, piece, 1) for mask in range(count)
    ]


def traded(pieces):
    return [exchange(part, "seq", mask) if mask else part for mask, part in enumerate(pieces)]


def to_positions(pieces):
    mine = lax.axis_index("seq")
    own, piece, width = pieces[0].shape
    result = jnp.zeros((own * len(pieces), piece, width), pieces[0].dtype)
    for mask, part in enumerate(pieces):
        result = lax.dynamic_update_slice_in_dim(result, part, (mine ^ mask) * own, 0)
    return result


def axis_bits(axis):
    return [(axis, 1 << i) for i in range(lax.axis_size(axis).bit_length() - 1)]


def upper(dim):
    axis, mask = dim
    return (lax.axis_index(axis) & mask) // mask


def swap(value, dim):
    return exchange(value, dim[0], dim[1])


def total_of(parts):
    total = parts[0].astype(f32)
    for part in parts[1:]:
        total += part.astype(f32)
    return total.astype(bf16)


PARTS = 3
SHARD_STEP = 16


class Plan:
    def __init__(self, rows):
        dims = axis_bits("seq") + axis_bits("dp")
        self.first = dims[0]
        rest = dims[1:]
        self.rows = rows // PARTS
        halved = 0
        while halved < len(rest) and (self.rows >> (halved + 1)) % SHARD_STEP == 0:
            halved += 1
        self.halved = halved
        self.last = rest[halved - 1]
        self.plain = rest[halved:]
        split = rest[: halved - 1]
        self.orders = [split[i % len(split) :] + split[: i % len(split)] for i in range(PARTS)]
        self.shards = 1 << halved
        self.shard = self.rows >> halved

    def table(self, each):
        places = {}
        devices = 1
        weight = {}
        for axis in ("seq", "dp"):
            for _, mask in axis_bits(axis):
                weight[(axis, mask)] = devices
                devices *= 2
        for side in range(2):
            for part, order in enumerate(self.orders):
                dims = [self.last] + order[::-1]
                for code in range(self.shards):
                    device = side * weight[self.first]
                    device += sum(weight[d] for i, d in enumerate(dims) if (code >> i) & 1)
                    row = (side * PARTS + part) * self.rows + code * self.shard
                    places[row] = device * each + part * self.shard
        return [places[row] for row in sorted(places)]

    def codes(self):
        found = []
        for order in self.orders:
            code = upper(self.last)
            for at, dim in enumerate(reversed(order)):
                code += upper(dim) << (at + 1)
            found.append(code)
        return [code.astype(jnp.int32) for code in found]


class Chain:
    def __init__(self):
        self.token = None

    def tie(self, values):
        if self.token is None:
            return values
        return lax.optimization_barrier((values, self.token))[0]

    def mark(self, values):
        self.token = values
        return values


def scatter_steps(plan, chain, keeps, sends, found):
    pairs = [[k, swap(s, order[0])] for k, s, order in zip(keeps, sends, plan.orders)]
    size = plan.rows // 2
    for step in range(1, len(plan.orders[0])):
        pairs = chain.tie(pairs)
        size //= 2
        dims = [order[step] for order in plan.orders]

        def halves(pair, at):
            return total_of([lax.dynamic_slice_in_dim(p, at * size, size, 0) for p in pair])

        sends = [halves(p, 1 - upper(d)) for p, d in zip(pairs, dims)]
        chain.mark(sends)
        mine = [halves(p, upper(d)) for p, d in zip(pairs, dims)]
        pairs = [[m, swap(s, d)] for m, s, d in zip(mine, sends, dims)]
        yield
    size = plan.shard
    bit = upper(plan.last)
    pairs = chain.tie(pairs)

    def side(at):
        return jnp.concatenate(
            [total_of([lax.dynamic_slice_in_dim(p, at * size, size, 0) for p in pair]) for pair in pairs],
            axis=0,
        )

    send = chain.mark(side(1 - bit))
    shard = side(bit)
    got = swap(send, plan.last)
    yield
    shard, got = chain.tie((shard, got))
    shard = total_of([shard, got])
    for dim in plan.plain:
        shard = total_of([shard, swap(shard, dim)])
    found.append(chain.mark(shard))
    yield


def gather_steps(plan, chain, shard, found):
    size = plan.shard
    got = swap(shard, plan.last)
    yield
    values = [(shard[i * size : (i + 1) * size], got[i * size : (i + 1) * size]) for i in range(PARTS)]
    for step in reversed(range(len(plan.orders[0]))):
        values = chain.tie(values)
        values = [jnp.concatenate(pair, axis=0) for pair in values]
        chain.mark(values)
        values = [(v, swap(v, order[step])) for v, order in zip(values, plan.orders)]
        yield
    values = chain.tie(values)
    chain.mark(values)
    found += [v for pair in values for v in pair]
    found += [swap(v, plan.first) for v in found]
    yield


def place(plan, refs, codes, row, store):
    part = row // plan.rows
    shard = ((row % plan.rows) // plan.shard) ^ codes[part]
    half = plan.shards // 2
    at = pl.ds(pl.multiple_of((shard & (half - 1)) * plan.shard, plan.shard), plan.shard)
    low, high = refs[2 * part][at, :], refs[2 * part + 1][at, :]
    store(jnp.where(shard >= half, high.astype(f32), low.astype(f32)))


def place(plan, refs, codes, row, store):
    part = row // plan.rows
    shard = ((row % plan.rows) // plan.shard) ^ codes[part]
    half = plan.shards // 2
    at = pl.ds(pl.multiple_of((shard & (half - 1)) * plan.shard, plan.shard), plan.shard)
    low, high = refs[2 * part][at, :], refs[2 * part + 1][at, :]
    store(jnp.where(shard >= half, high.astype(f32), low.astype(f32)))


def dense_place_kernel(plan, first_code, info_ref, *refs):
    sources, (down_ref, up_ref, hold_ref) = refs[: 2 * PARTS], refs[-3:]
    codes = [info_ref[first_code + i] for i in range(PARTS)]
    size = hold_ref.shape[0]
    for block in range(2 * PARTS):

        @pl.when(pl.program_id(0) == block)
        def _(block=block):
            out_ref = down_ref if block < PARTS else hold_ref
            for row in range(0, size, plan.shard):

                def store(value, row=row):
                    out_ref[row : row + plan.shard, :] = value

                place(plan, sources, codes, block * size + row, store)

    @pl.when(pl.program_id(0) >= PARTS)
    def _():
        up_ref[...] = hold_ref[...].T


def dense_place(plan, first_code, at, flip, info, sources, width, wide, before):
    kept = list(before)
    size = plan.rows // 2

    def spot(step, s):
        return (s[at] ^ flip) * PARTS + jnp.clip(step, 0, PARTS - 1)

    return pl.pallas_call(
        functools.partial(dense_place_kernel, plan, first_code),
        grid_spec=pltpu.PrefetchScalarGridSpec(
            num_scalar_prefetch=1,
            grid=(2 * PARTS,),
            in_specs=[fixed(x.shape) for x in sources]
            + [pl.BlockSpec(memory_space=pl.ANY)] * len(kept),
            out_specs=[
                pl.BlockSpec((size, width), lambda i, s: (spot(i, s), 0)),
                pl.BlockSpec((width, size), lambda i, s: (0, spot(i - PARTS, s))),
            ],
            scratch_shapes=[pltpu.VMEM((size, width), f32)],
        ),
        out_shape=[
            jax.ShapeDtypeStruct((wide * width, width), f32),
            jax.ShapeDtypeStruct((width, wide * width), f32),
        ],
        input_output_aliases={1 + len(sources) + i: i for i in range(len(kept))},
        compiler_params=SMALL,
        cost_estimate=cost(0, 6 * wide * width * width),
    )(info, *sources, *kept)


def attend_place_kernel(shard, each, steps, table_ref, group_ref, all_ref, *refs):
    outs, (vec_ref, pool_ref, hold_ref, word_ref, sems, word_sem) = refs[:4], refs[4:]
    step = pl.program_id(0)
    rows = hold_ref.shape[1]
    parts = rows // shard

    def fetch(block, slot):
        for i in range(parts):
            at = pl.multiple_of(table_ref[block * parts + i], SHARD_STEP)
            pltpu.make_async_copy(
                all_ref.at[pl.ds(at, shard)],
                hold_ref.at[slot, pl.ds(i * shard, shard)],
                sems.at[slot],
            ).start()

    devices = word_ref.shape[0]

    @pl.when(step == 0)
    def _():
        fetch(0, 0)
        for device in range(devices):
            pltpu.make_async_copy(
                all_ref.at[pl.ds(device * each + each - 2 * SUM_ROWS, 2 * SUM_ROWS)],
                word_ref.at[device],
                word_sem,
            ).start()

    @pl.when(step + 1 < 4 * steps)
    def _():
        fetch(step + 1, (step + 1) % 2)

    slot = step % 2
    pltpu.make_async_copy(all_ref.at[pl.ds(0, rows)], hold_ref.at[slot], sems.at[slot]).wait()
    for i, out_ref in enumerate(outs):

        @pl.when((step >= i * steps) & (step < (i + 1) * steps))
        def _(out_ref=out_ref):
            out_ref[...] = hold_ref[slot].astype(f32)

    @pl.when(step == 4 * steps - 1)
    def _():
        pltpu.make_async_copy(word_ref, word_ref, word_sem).wait()

        def both(device):
            return word_ref[device, :SUM_ROWS].astype(f32) + word_ref[device, SUM_ROWS:].astype(f32)

        vec_ref[...] = lax.fori_loop(
            0, devices, lambda i, total: total + both(i), jnp.zeros(vec_ref.shape, f32)
        )
        for i in range(pool_ref.shape[0]):
            pool_ref[i] = both(group_ref[0] + i)[POOL_ROW:]


def attend_place(plan, gathered, each, width, devices, seq_count, group):
    table = jnp.array(plan.table(each), jnp.int32)
    rows = plan.rows // 2
    steps = width // rows

    def out_spec(at):
        return pl.BlockSpec((rows, width), lambda i, *_: (jnp.clip(i - at * steps, 0, steps - 1), 0))

    return pl.pallas_call(
        functools.partial(attend_place_kernel, plan.shard, each, steps),
        grid_spec=pltpu.PrefetchScalarGridSpec(
            num_scalar_prefetch=2,
            grid=(4 * steps,),
            in_specs=[pl.BlockSpec(memory_space=pl.ANY)],
            out_specs=[out_spec(i) for i in range(4)]
            + [
                pl.BlockSpec((SUM_ROWS, width), lambda i, *_: (0, 0)),
                pl.BlockSpec((seq_count, SUM_ROWS - POOL_ROW, width), lambda i, *_: (0, 0, 0)),
            ],
            scratch_shapes=[
                pltpu.VMEM((2, rows, width), bf16),
                pltpu.VMEM((devices, 2 * SUM_ROWS, width), bf16),
                pltpu.SemaphoreType.DMA((2,)),
                pltpu.SemaphoreType.DMA(()),
            ],
        ),
        out_shape=[jax.ShapeDtypeStruct((width, width), f32)] * 4
        + [
            jax.ShapeDtypeStruct((SUM_ROWS, width), f32),
            jax.ShapeDtypeStruct((seq_count, SUM_ROWS - POOL_ROW, width), f32),
        ],
        compiler_params=PARAMS,
        cost_estimate=cost(0, 24 * width * width),
    )(table, group, gathered)


def shards(
    tokens,
    lengths,
    w_query,
    b_query,
    w_key,
    w_value,
    b_value,
    w_out,
    b_out,
    gain_one,
    shift_one,
    w_up,
    b_up,
    w_down,
    b_down,
    gain_two,
    shift_two,
    out_grad,
    pooled_grad,
):
    seq_count = lax.axis_size("seq")
    held, piece, width = tokens.shape
    full = piece * seq_count
    count = held // seq_count
    mine = lax.axis_index("seq")
    wide = w_up.shape[1] // width
    total = count * full

    def flat(value):
        return value.reshape(total, width)

    def split(value):
        return value.reshape(count, full, width)

    dense_plan = Plan(wide * width)
    outer_plan = Plan(2 * width)
    first = axis_bits("seq")[0]
    scalars = [mine, upper(first)] + dense_plan.codes() + outer_plan.codes()
    own_at, dense_at, outer_at = held + 1, held + 2, held + 2 + PARTS
    info = jnp.concatenate([lengths, jnp.stack([v.astype(jnp.int32) for v in scalars])])
    vecs = jnp.concatenate(
        [b_query, b_value, b_out, gain_one, shift_one, b_down, gain_two, shift_two, b_up]
    )
    vecs = vecs.astype(f32).reshape(-1, width)

    weights = [w_query, w_key, w_value, vecs]
    done = None
    source = tokens
    parts = []
    for passage in range(count):
        if parts:
            source = lax.optimization_barrier((tokens, parts))[0]
        parts = [
            exchange(
                lax.dynamic_slice_in_dim(source, (mine ^ mask) * count + passage, 1, 0), "seq", mask
            )
            for mask in range(1, seq_count)
        ]
        done = attend(passage, count, info, tokens, parts, weights, done)
    stacked, q, k, v, stat = done
    cot = to_passages(lax.optimization_barrier((out_grad, parts))[0])
    stacked = stacked.reshape(2, total, width)
    result, first_low, act, second, inner, branch_in, mixed_grad, sums = row_work(
        held, info, stacked, flat(cot), pooled_grad, w_out, w_up, w_down, vecs, count
    )
    chain = Chain()
    pieces = chain.mark(position_pieces(split(result)))
    out_pieces = traded(pieces)
    dense, shard, found = [], [], []

    def outer_part(flip, keep, got):
        made = dense_outer(
            dense_plan, dense_at, own_at, flip, keep, info, *chain.tie((act, second, first_low, inner)), got
        )
        return chain.mark(made)

    away = [swap(outer_part(1, keep, None)[0], first) for keep in range(2)]
    sends = outer_part(0, 0, away[0])
    keeps = outer_part(0, 1, away[1])
    dense_steps = scatter_steps(dense_plan, chain, keeps, sends, dense)
    chain.mark((chain.token, out_pieces))
    block_out = to_positions(out_pieces)
    grads, words = attend_back(
        held,
        info,
        q,
        k,
        v,
        chain.tie(split(mixed_grad)),
        stacked.reshape(2, count, full, width),
        split(branch_in),
        stat,
        sums,
    )
    chain.mark(words)
    grads = grads.reshape(4, total, width)
    next(dense_steps)

    def attend_part(flip, keep, got):
        made = attend_outer(
            outer_plan, outer_at, own_at, flip, keep, info, stacked, chain.tie(grads), got
        )
        return chain.mark(made)

    away = [swap(attend_part(1, keep, None)[0], first) for keep in range(2)]
    next(dense_steps)
    sends = attend_part(0, 0, away[0])
    keeps = attend_part(0, 1, away[1])
    outer_steps = scatter_steps(outer_plan, chain, keeps, sends, shard)
    input_low = input_grad(branch_in, chain.tie(grads), w_query, w_key, w_value)
    chain.mark(input_low)
    next(dense_steps)
    next(outer_steps)
    for _ in dense_steps:
        pass
    dense_steps = gather_steps(dense_plan, chain, dense[0], found)
    next(dense_steps)
    next(outer_steps)
    pieces = chain.mark(position_pieces(split(chain.tie(input_low))))
    in_pieces = traded(pieces)
    next(outer_steps)
    next(dense_steps)
    for _ in outer_steps:
        pass
    gathered = jnp.concatenate([shard[0], words], axis=0)
    each = gathered.shape[0]
    gathered = chain.mark(gathered)
    gathered = lax.all_gather(gathered, ("dp", "seq"), axis=0, tiled=True)
    next(dense_steps)
    chain.mark((chain.token, in_pieces))
    tokens_grad = to_positions(in_pieces)
    for _ in dense_steps:
        pass

    def place_dense(flip, before):
        pick = found[2 * PARTS :] if flip else found[: 2 * PARTS]
        return chain.mark(
            dense_place(
                dense_plan, dense_at, own_at, flip, info, chain.tie(pick), width, wide, before
            )
        )

    down_sum, up_sum = place_dense(1, place_dense(0, []))
    group = (lax.axis_index("dp") * seq_count).astype(jnp.int32)[None]
    *outer, vectors, pooled = attend_place(
        outer_plan, chain.tie(gathered), each, width, gathered.shape[0] // each, seq_count, group
    )
    pooled = pooled[:, :count].reshape(held, width)
    return (
        block_out,
        pooled,
        tokens_grad,
        outer[0],
        vectors[0],
        outer[1],
        outer[2],
        vectors[1],
        outer[3],
        vectors[2],
        vectors[3],
        vectors[4],
        up_sum,
        vectors[8 : 8 + wide].reshape(-1),
        down_sum,
        vectors[5],
        vectors[6],
        vectors[7],
    )


def solution(mesh):
    in_specs = (
        (P("dp", "seq", None), P("dp"))
        + (P(),) * 15
        + (P("dp", "seq", None), P("dp", None))
    )
    out_specs = (P("dp", "seq", None), P("dp", None), P("dp", "seq", None)) + (P(),) * 15
    return jax.shard_map(shards, mesh=mesh, in_specs=in_specs, out_specs=out_specs, check_vma=False)
```

```python
import functools

import jax
import jax.numpy as jnp
from jax import lax
from jax.experimental import pallas as pl
from jax.experimental.pallas import tpu as pltpu
from jax.sharding import PartitionSpec as P

HEADS = 12
HEAD_DIM = 64
PAIR = 2 * HEAD_DIM
PAIRS = HEADS // 2
SCALE = HEAD_DIM ** (-0.5)
ROWS = 512
BACK_ROWS = 256
STRIP = 32
TOGETHER = 1
BACK_TOGETHER = 3
STAT_ROWS = 16
CHUNK = 256
KEY_STEP = 128
VMEM_BYTES = 62 * 1024 * 1024
SMALL_BYTES = 40 * 1024 * 1024
SUM_ROWS = 16
POOL_ROW = 12

eps = 1e-06
root_half = 0.7071067811865476
inv_root_two_pi = 0.3989422804014327

f32 = jnp.float32
bf16 = jnp.bfloat16

NN = (((1,), (0,)), ((), ()))
NT = (((1,), (1,)), ((), ()))
TN = (((0,), (0,)), ((), ()))


def mul(left, right, dims=NN):
    return lax.dot_general(left, right, dims, preferred_element_type=f32)


def fixed(shape):
    return pl.BlockSpec(shape, lambda *_: (0,) * len(shape), pipeline_mode=pl.Buffered(1))


PARAMS = pltpu.CompilerParams(dimension_semantics=("arbitrary",), vmem_limit_bytes=VMEM_BYTES)
SMALL = pltpu.CompilerParams(dimension_semantics=("arbitrary",), vmem_limit_bytes=SMALL_BYTES)


def cost(flops, moved, exps=0):
    return pl.CostEstimate(flops=int(flops), bytes_accessed=int(moved), transcendentals=int(exps))


def over_extents(length, full, body):
    for extent in range(KEY_STEP, full + 1, KEY_STEP):
        pl.when((length > extent - KEY_STEP) & (length <= extent))(functools.partial(body, extent))


def by_eight(value):
    return value.reshape(value.shape[0] // 8, 8, value.shape[1])


def fill_dead(dead_ref, extent, length):
    key_at = lax.broadcasted_iota(jnp.int32, dead_ref.shape, 0) + (extent - KEY_STEP)
    dead_ref[...] = jnp.where(key_at < length, 0.0, -1e30)


def live_strip(scores, dead_ref, extent, row):
    strip = scores[row : row + STRIP]
    last = row - (extent - KEY_STEP)
    return strip + dead_ref[last : last + STRIP] if last >= 0 else strip


def attend_kernel(pieces, passage, count, held, info_ref, *refs):
    part_refs, refs = refs[:pieces], refs[pieces:]
    wq_ref, wk_ref, wv_ref, vec_ref = refs[:4]
    xm_ref, xmt_ref, q_ref, k_ref, v_ref, stat_ref, prob_ref, dead_ref = refs[-8:]
    x_ref, mix_ref = xm_ref.at[0], xm_ref.at[1]
    mine = info_ref[held]
    length = info_ref[mine * count + passage]
    size = part_refs[0].shape[1]
    for mask, part_ref in enumerate(part_refs):
        x_ref[0, pl.ds(pl.multiple_of((mine ^ mask) * size, size), size)] = part_ref[0]

    def project(index, carry):
        at = pl.ds(pl.multiple_of(index * CHUNK, CHUNK), CHUNK)
        x = x_ref[0]
        xmt_ref[0, at, :] = x_ref[0, :, at].T
        q_ref[0, :, at] = (mul(x, wq_ref[:, at]) + vec_ref[0:1, at]).astype(bf16)
        k_ref[0, :, at] = mul(x, wk_ref[:, at]).astype(bf16)
        v_ref[0, :, at] = (mul(x, wv_ref[:, at]) + vec_ref[1:2, at]).astype(bf16)
        return carry

    lax.fori_loop(0, wq_ref.shape[1] // CHUNK, project, 0)
    stat_ref[0] = jnp.zeros(stat_ref.shape[1:], f32)
    full = size * pieces
    lane = lax.broadcasted_iota(jnp.int32, (1, PAIR), 1)

    def run(extent):
        fill_dead(dead_ref, extent, length)

        def head(at, number, half, slot):
            q, k = q_ref[0, :, at], k_ref[0, :extent, at]
            own = (lane >= half * HEAD_DIM) & (lane < (half + 1) * HEAD_DIM)
            scores = mul(jnp.where(own, k * SCALE, 0).astype(bf16), q, NT)
            top = jnp.full((8, full), -jnp.inf, f32)
            for row in range(0, extent, STRIP):
                top = jnp.maximum(top, by_eight(live_strip(scores, dead_ref, extent, row)).max(axis=0))
            top = jnp.max(top, axis=0, keepdims=True)
            total = jnp.zeros((8, full), f32)
            for row in range(0, extent, STRIP):
                expo = jnp.exp(live_strip(scores, dead_ref, extent, row) - top)
                total += by_eight(expo).sum(axis=0)
                prob_ref[slot, row : row + STRIP] = expo.astype(bf16)
            total = jnp.sum(total, axis=0, keepdims=True)
            stat_ref[0, pl.ds(number, 1), :] = top + jnp.log(total)
            return 1.0 / total

        def group(index, carry):
            for i in range(TOGETHER):
                pair = index * TOGETHER + i
                at = pl.ds(pl.multiple_of(pair * PAIR, PAIR), PAIR)
                values = v_ref[0, :extent, at].T
                mixed = []
                for half in range(2):
                    slot = 2 * i + half
                    scale = head(at, pair * 2 + half, half, slot)
                    own = values[half * HEAD_DIM : (half + 1) * HEAD_DIM]
                    mixed.append(mul(own, prob_ref[slot, :extent]) * scale)
                mixed = jnp.concatenate(mixed, axis=0)
                xmt_ref[1, at, :] = mixed.astype(bf16)
                mix_ref[0, :, at] = mixed.T.astype(bf16)
            return carry

        lax.fori_loop(0, PAIRS // TOGETHER, group, 0)

    over_extents(length, full, run)


def attend(passage, count, info, tokens, parts, weights, before):
    held, piece, width = tokens.shape
    pieces = len(parts) + 1
    full = piece * pieces
    rows = pl.BlockSpec((1, full, width), lambda i, s: (passage, 0, 0))
    act = jax.ShapeDtypeStruct((count, full, width), bf16)
    got = pl.BlockSpec((1, piece, width), lambda i, s: (0, 0, 0))
    kept = [] if before is None else list(before)
    first_kept = 1 + pieces + len(weights)
    return pl.pallas_call(
        functools.partial(attend_kernel, pieces, passage, count, held),
        grid_spec=pltpu.PrefetchScalarGridSpec(
            num_scalar_prefetch=1,
            grid=(1,),
            in_specs=[pl.BlockSpec((1, piece, width), lambda i, s: (s[held] * count + passage, 0, 0))]
            + [got] * len(parts)
            + [fixed(w.shape) for w in weights]
            + [pl.BlockSpec(memory_space=pl.ANY)] * len(kept),
            out_specs=[
                pl.BlockSpec((2, 1, full, width), lambda i, s: (0, passage, 0, 0)),
                pl.BlockSpec((2, width, full), lambda i, s: (0, 0, passage)),
            ]
            + [rows] * 3
            + [pl.BlockSpec((1, STAT_ROWS, full), lambda i, s: (passage, 0, 0))],
            scratch_shapes=[
                pltpu.VMEM((2 * TOGETHER, full, full), bf16),
                pltpu.VMEM((KEY_STEP, full), f32),
            ],
        ),
        out_shape=[
            jax.ShapeDtypeStruct((2, count, full, width), bf16),
            jax.ShapeDtypeStruct((2, width, count * full), bf16),
        ]
        + [act] * 3
        + [jax.ShapeDtypeStruct((count, STAT_ROWS, full), f32)],
        input_output_aliases={first_kept + i: i for i in range(len(kept))},
        compiler_params=PARAMS,
        cost_estimate=cost(
            2 * full * (3 * width * width + 4 * 2 * full * width),
            12 * full * width + 6 * width * width,
        ),
    )(info, tokens, *parts, *weights, *kept)


def attend_back_kernel(
    held,
    info_ref,
    q_ref,
    k_ref,
    v_ref,
    mg_ref,
    mix_ref,
    branch_ref,
    stat_ref,
    sum_ref,
    grads_ref,
    word_ref,
    bias_ref,
    along_ref,
    prob_ref,
    score_ref,
    dead_ref,
):
    dq_ref, dk_ref, dv_ref = (grads_ref.at[i] for i in range(3))
    grads_ref[3] = branch_ref[...].astype(bf16)
    full, width = q_ref.shape[1:]
    length = info_ref[info_ref[held] * pl.num_programs(0) + pl.program_id(0)]
    lane = lax.broadcasted_iota(jnp.int32, (1, PAIR), 1)
    row = lax.broadcasted_iota(jnp.int32, (8, 1), 0)

    @pl.when(pl.program_id(0) == 0)
    def _():
        bias_ref[...] = sum_ref[...]

    feature = lax.broadcasted_iota(jnp.int32, (STAT_ROWS, width), 1)
    number = lax.broadcasted_iota(jnp.int32, (STAT_ROWS, width), 0)
    ours = jnp.where(
        (feature >= number * HEAD_DIM) & (feature < (number + 1) * HEAD_DIM), 1.0, 0.0
    ).astype(bf16)
    product = mg_ref[0].astype(f32) * mix_ref[0, 0].astype(f32)
    high = product.astype(bf16)
    low = (product - high.astype(f32)).astype(bf16)
    along_ref[...] = mul(ours, high, NT) + mul(ours, low, NT)

    def run(extent):
        fill_dead(dead_ref, extent, length)
        if extent < full:
            dk_ref[0, extent:] = jnp.zeros((full - extent, width), bf16)
            dv_ref[0, extent:] = jnp.zeros((full - extent, width), bf16)

        def group(index, carry):
            for i in range(BACK_TOGETHER):
                pair = index * BACK_TOGETHER + i
                at = pl.ds(pl.multiple_of(pair * PAIR, PAIR), PAIR)
                q, mg = q_ref[0, :, at], mg_ref[0, :, at]
                k, v = k_ref[0, :extent, at], v_ref[0, :extent, at]
                keys = k.T
                dq, dk, dv = [], [], []
                for half in range(2):
                    slot = 2 * i + half
                    own = (lane >= half * HEAD_DIM) & (lane < (half + 1) * HEAD_DIM)
                    scores = mul(jnp.where(own, k * SCALE, 0).astype(bf16), q, NT)
                    prob_grad = mul(jnp.where(own, v, 0).astype(bf16), mg, NT)
                    log_row = stat_ref[0, pl.ds(pair * 2 + half, 1), :]
                    along = along_ref[pl.ds(pair * 2 + half, 1), :]
                    for at_row in range(0, extent, STRIP):
                        rows = slice(at_row, at_row + STRIP)
                        probs = jnp.exp(live_strip(scores, dead_ref, extent, at_row) - log_row)
                        prob_ref[slot, rows] = probs.astype(bf16)
                        score_ref[slot, rows] = (probs * (prob_grad[rows] - along)).astype(bf16)
                    score_grad = score_ref[slot, :extent]
                    dv.append(mul(prob_ref[slot, :extent], mg))
                    dk.append(mul(score_grad, q))
                    dq.append(mul(keys[half * HEAD_DIM : (half + 1) * HEAD_DIM], score_grad))
                first = lane < HEAD_DIM
                dq_pair = jnp.concatenate(dq, axis=0).T * SCALE
                dk_pair = jnp.where(first, dk[0], dk[1]) * SCALE
                dv_pair = jnp.where(first, dv[0], dv[1])
                dq_ref[0, :, at] = dq_pair.astype(bf16)
                dk_ref[0, :extent, at] = dk_pair.astype(bf16)
                dv_ref[0, :extent, at] = dv_pair.astype(bf16)
                sums = jnp.where(
                    row == 0,
                    jnp.sum(dq_pair, axis=0, keepdims=True),
                    jnp.where(row == 1, jnp.sum(dv_pair, axis=0, keepdims=True), 0.0),
                )
                bias_ref[0:8, at] += sums
            return carry

        lax.fori_loop(0, PAIRS // BACK_TOGETHER, group, 0)

    over_extents(length, full, run)

    @pl.when(pl.program_id(0) == pl.num_programs(0) - 1)
    def _():
        high = bias_ref[...].astype(bf16)
        word_ref[:SUM_ROWS] = high
        word_ref[SUM_ROWS:] = (bias_ref[...] - high.astype(f32)).astype(bf16)


def attend_back(held, info, q, k, v, mixed_grad, stacked, branch_in, stat, sums):
    count, full, width = q.shape
    rows = pl.BlockSpec((1, full, width), lambda i, *_: (i, 0, 0))
    return pl.pallas_call(
        functools.partial(attend_back_kernel, held),
        grid_spec=pltpu.PrefetchScalarGridSpec(
            num_scalar_prefetch=1,
            grid=(count,),
            in_specs=[rows] * 4
            + [
                pl.BlockSpec((1, 1, full, width), lambda i, *_: (1, i, 0, 0)),
                rows,
                pl.BlockSpec((1, STAT_ROWS, full), lambda i, *_: (i, 0, 0)),
                fixed(sums.shape),
            ],
            out_specs=[
                pl.BlockSpec((4, 1, full, width), lambda i, *_: (0, i, 0, 0)),
                pl.BlockSpec((2 * SUM_ROWS, width), lambda i, *_: (0, 0)),
            ],
            scratch_shapes=[
                pltpu.VMEM(sums.shape, f32),
                pltpu.VMEM((STAT_ROWS, full), f32),
                pltpu.VMEM((2 * BACK_TOGETHER, full, full), bf16),
                pltpu.VMEM((2 * BACK_TOGETHER, full, full), bf16),
                pltpu.VMEM((KEY_STEP, full), f32),
            ],
        ),
        out_shape=[
            jax.ShapeDtypeStruct((4, count, full, width), bf16),
            jax.ShapeDtypeStruct((2 * SUM_ROWS, width), bf16),
        ],
        compiler_params=PARAMS,
        cost_estimate=cost(
            2 * count * full * 10 * 2 * full * width, 16 * count * full * width
        ),
    )(info, q, k, v, mixed_grad, stacked, branch_in, stat, sums)


def norm_parts(hidden):
    centred = hidden - jnp.mean(hidden, axis=1, keepdims=True)
    inv_scale = lax.rsqrt(jnp.mean(centred * centred, axis=1, keepdims=True) + eps)
    return centred * inv_scale, inv_scale


def norm_back(scaled, normed, inv_scale):
    mean = jnp.mean(scaled, axis=1, keepdims=True)
    along = jnp.mean(scaled * normed, axis=1, keepdims=True)
    return (scaled - mean - normed * along) * inv_scale


def gelu_parts(u):
    expo = jnp.exp(u * u * -0.5)
    base = 1.0 + jnp.abs(u) * (0.3275911 * root_half)
    t = pl.reciprocal(base, approx=True)
    t = t * (2.0 - base * t)
    poly = t * (
        0.5 * 0.254829592
        + t
        * (
            0.5 * -0.284496736
            + t * (0.5 * 1.421413741 + t * (0.5 * -1.453152027 + t * (0.5 * 1.061405429)))
        )
    )
    tail = poly * expo
    return jnp.where(u >= 0, 1.0 - tail, tail), expo


def rows_kernel(
    blocks,
    count,
    held,
    info_ref,
    x_ref,
    mix_ref,
    cot_ref,
    pool_ref,
    wo_ref,
    vec_ref,
    wu_all,
    wd_all,
    out_ref,
    lowt_ref,
    act_all,
    secondt_ref,
    inner_all,
    branch_ref,
    mg_ref,
    sum_ref,
    wu_ref,
    wd_ref,
    act_ref,
    inner_ref,
    slope_ref,
    first_ref,
    normed_ref,
    total_ref,
    scale_ref,
    low_ref,
    second_ref,
    sems,
):
    step, steps = pl.program_id(0), pl.num_programs(0)
    rows, width = cot_ref.shape
    hidden_width = wu_ref.shape[1]
    b_out, gain_one, shift_one, b_down, gain_two, shift_two = (
        vec_ref[i : i + 1] for i in range(2, 8)
    )
    passage = info_ref[held] * count + step // blocks
    length = info_ref[passage]
    inv_length = 1.0 / jnp.full((1, width), length, jnp.int32).astype(f32)
    pool = pool_ref[pl.ds(passage, 1), :] * inv_length
    first_row = (step % blocks) * rows
    load_up = pltpu.make_async_copy(wu_all, wu_ref, sems.at[0])
    load_down = pltpu.make_async_copy(wd_all, wd_ref, sems.at[1])

    def give(source_ref, all_ref, at):
        return pltpu.make_async_copy(
            source_ref, all_ref.at[pl.ds(pl.multiple_of(at * rows, rows), rows)], sems.at[2 if source_ref is act_ref else 3]
        )

    @pl.when(step == 0)
    def _():
        load_up.start()
        load_down.start()
        sum_ref[...] = jnp.zeros(sum_ref.shape, f32)

    def tally(at, value, columns=slice(None)):
        sum_ref[at : at + 1, columns] += jnp.sum(value, axis=0, keepdims=True)

    def strips(size):
        return [slice(i, i + size) for i in range(0, rows, size)]

    groups = width // CHUNK
    chunks = hidden_width // CHUNK
    part = [slice(i * CHUNK, (i + 1) * CHUNK) for i in range(chunks)]
    whole = [slice(i * width, (i + 1) * width) for i in range(hidden_width // width)]
    lanes = scale_ref.shape[1]

    branch = mul(mix_ref[0], wo_ref[...])
    for at in strips(STRIP):
        normed, scale = norm_parts(x_ref[0, at].astype(f32) + branch[at] + b_out)
        first = normed * gain_one + shift_one
        normed_ref[at] = normed
        scale_ref[at] = jnp.broadcast_to(scale, (STRIP, lanes))
        first_ref[at] = first + b_down
        low_ref[at] = first.astype(bf16)

    @pl.when(step == 0)
    def _():
        load_up.wait()
        load_down.wait()

    @pl.when(step > 0)
    def _():
        give(act_ref, act_all, step - 1).wait()

    def up(i):
        return mul(low_ref[...], wu_ref[:, part[i]])

    for at in range(0, width, CHUNK):
        lowt_ref[at : at + CHUNK, :] = low_ref[:, at : at + CHUNK].T
    pre = up(0)
    for i in range(chunks):
        ahead = up(i + 1) if i + 1 < chunks else None
        bias = vec_ref[8 + i // groups : 9 + i // groups, part[i % groups]]
        for at in strips(2 * STRIP):
            u = pre[at] + bias
            phi, expo = gelu_parts(u)
            act_ref[at, part[i]] = (u * phi).astype(bf16)
            slope_ref[at, part[i]] = phi + u * expo * inv_root_two_pi
        if i % groups == 0 and i:
            done = whole[i // groups - 1]
            first_ref[...] += mul(act_ref[:, done], wd_ref[done, :])
        pre = ahead
    last = mul(act_ref[:, whole[-1]], wd_ref[whole[-1], :])
    give(act_ref, act_all, step).start()

    pooled, shift, gain, down = (jnp.zeros((8, width), f32) for _ in range(4))
    for at in strips(STRIP):
        normed, scale = norm_parts(first_ref[at] + last[at])
        result = normed * gain_two + shift_two
        out_ref[at] = result.astype(bf16)
        row_at = lax.broadcasted_iota(jnp.int32, (STRIP, 1), 0) + (first_row + at.start)
        live = jnp.where(row_at < length, 1.0, 0.0)
        pooled += by_eight(result * live).sum(axis=0)
        upstream = cot_ref[at].astype(f32) + live * pool
        gain += by_eight(upstream * normed).sum(axis=0)
        shift += by_eight(upstream).sum(axis=0)
        second_in = norm_back(upstream * gain_two, normed, scale)
        down += by_eight(second_in).sum(axis=0)
        total_ref[at] = second_in
        second_ref[at] = second_in.astype(bf16)
    tally(6, gain)
    tally(7, shift)
    tally(5, down)
    sum_ref[pl.ds(POOL_ROW + step // blocks, 1), :] += (
        jnp.sum(pooled, axis=0, keepdims=True) * inv_length
    )

    @pl.when(step > 0)
    def _():
        give(inner_ref, inner_all, step - 1).wait()

    def back(i):
        return mul(second_ref[...], wd_ref[part[i], :], NT)

    for at in range(0, width, CHUNK):
        secondt_ref[at : at + CHUNK, :] = second_ref[:, at : at + CHUNK].T
    grad = back(0)
    for i in range(chunks):
        ahead = back(i + 1) if i + 1 < chunks else None
        bias = jnp.zeros((8, CHUNK), f32)
        for at in strips(2 * STRIP):
            inner = grad[at] * slope_ref[at, part[i]]
            bias += by_eight(inner).sum(axis=0)
            inner_ref[at, part[i]] = inner.astype(bf16)
        tally(8 + i // groups, bias, part[i % groups])
        if i % groups == 0 and i:
            done = whole[i // groups - 1]
            total_ref[...] += mul(inner_ref[:, done], wu_ref[:, done], NT)
        grad = ahead
    last = mul(inner_ref[:, whole[-1]], wu_ref[:, whole[-1]], NT)
    give(inner_ref, inner_all, step).start()

    gain, shift, out = (jnp.zeros((8, width), f32) for _ in range(3))
    for at in strips(STRIP):
        first_up = total_ref[at] + last[at]
        normed = normed_ref[at]
        gain += by_eight(first_up * normed).sum(axis=0)
        shift += by_eight(first_up).sum(axis=0)
        branch_in = norm_back(first_up * gain_one, normed, scale_ref[at, :1])
        out += by_eight(branch_in).sum(axis=0)
        branch_ref[at] = branch_in
    tally(3, gain)
    tally(4, shift)
    tally(2, out)
    mg_ref[...] = mul(branch_ref[...].astype(bf16), wo_ref[...], NT).astype(bf16)

    @pl.when(step == steps - 1)
    def _():
        give(act_ref, act_all, step).wait()
        give(inner_ref, inner_all, step).wait()


def row_work(held, info, stacked, cot, pool, w_out, w_up, w_down, vecs, count):
    total, width = cot.shape
    full = total // count
    assert POOL_ROW + count <= SUM_ROWS
    hidden = w_up.shape[1]
    blocks = full // ROWS
    narrow = pl.BlockSpec((ROWS, width), lambda i, *_: (i, 0))
    turned = pl.BlockSpec((width, ROWS), lambda i, *_: (0, i))
    anywhere = pl.BlockSpec(memory_space=pl.ANY)
    thin = jax.ShapeDtypeStruct((total, width), bf16)
    thick = jax.ShapeDtypeStruct((total, hidden), bf16)
    return pl.pallas_call(
        functools.partial(rows_kernel, blocks, count, held),
        grid_spec=pltpu.PrefetchScalarGridSpec(
            num_scalar_prefetch=1,
            grid=(total // ROWS,),
            in_specs=[
                pl.BlockSpec((1, ROWS, width), lambda i, *_: (0, i, 0)),
                pl.BlockSpec((1, ROWS, width), lambda i, *_: (1, i, 0)),
                narrow,
                fixed(pool.shape),
                fixed((width, width)),
                fixed(vecs.shape),
                anywhere,
                anywhere,
            ],
            out_specs=[
                narrow,
                turned,
                anywhere,
                turned,
                anywhere,
                narrow,
                narrow,
                pl.BlockSpec((SUM_ROWS, width), lambda i, *_: (0, 0)),
            ],
            scratch_shapes=[
                pltpu.VMEM((width, hidden), bf16),
                pltpu.VMEM((hidden, width), bf16),
                pltpu.VMEM((ROWS, hidden), bf16),
                pltpu.VMEM((ROWS, hidden), bf16),
                pltpu.VMEM((ROWS, hidden), f32),
                pltpu.VMEM((ROWS, width), f32),
                pltpu.VMEM((ROWS, width), f32),
                pltpu.VMEM((ROWS, width), f32),
                pltpu.VMEM((ROWS, PAIR), f32),
                pltpu.VMEM((ROWS, width), bf16),
                pltpu.VMEM((ROWS, width), bf16),
                pltpu.SemaphoreType.DMA((4,)),
            ],
        ),
        out_shape=[
            thin,
            jax.ShapeDtypeStruct((width, total), bf16),
            thick,
            jax.ShapeDtypeStruct((width, total), bf16),
            thick,
            jax.ShapeDtypeStruct((total, width), f32),
            thin,
            jax.ShapeDtypeStruct((SUM_ROWS, width), f32),
        ],
        compiler_params=PARAMS,
        cost_estimate=cost(
            4 * total * width * (width + 2 * hidden),
            2 * total * (8 * width + 2 * hidden) + 2 * width * (width + 2 * hidden),
        ),
    )(info, stacked, stacked, cot, pool, w_out, vecs, w_up, w_down)


def dense_outer_kernel(side_ref, act_ref, second_ref, low_ref, inner_ref, out_ref):
    step = pl.program_id(0)
    half = pl.num_programs(0) // 2

    @pl.when(step < half)
    def _():
        out_ref[0] = mul(second_ref[...], act_ref[...]).astype(bf16)

    @pl.when(step >= half)
    def _():
        out_ref[0] = mul(low_ref[...], inner_ref[...]).astype(bf16)


def dense_outer(at, flip, info, act, second, low, inner):
    width, total = second.shape
    wide = act.shape[1] // width
    half = wide // 2
    return pl.pallas_call(
        dense_outer_kernel,
        grid_spec=pltpu.PrefetchScalarGridSpec(
            num_scalar_prefetch=1,
            grid=(wide,),
            in_specs=[
                pl.BlockSpec(
                    (total, width), lambda i, s: (0, (s[at] ^ flip) * half + jnp.minimum(i, half - 1))
                ),
                fixed((width, total)),
                fixed((width, total)),
                pl.BlockSpec(
                    (total, width), lambda i, s: (0, (s[at] ^ flip) * half + jnp.maximum(i - half, 0))
                ),
            ],
            out_specs=pl.BlockSpec((1, width, width), lambda i, s: (i, 0, 0)),
        ),
        out_shape=jax.ShapeDtypeStruct((wide, width, width), bf16),
        compiler_params=SMALL,
        cost_estimate=cost(
            2 * total * width * width * wide, 2 * (wide + 2) * total * width + 2 * wide * width * width
        ),
    )(info, act, second, low, inner).reshape(wide * width, width)


def attend_outer_kernel(side_ref, left_ref, right_ref, out_ref):
    out_ref[0] = mul(left_ref[0], right_ref[0]).astype(bf16)


def attend_outer(at, flip, info, turned, grads):
    width, total = turned.shape[1:]
    return pl.pallas_call(
        attend_outer_kernel,
        grid_spec=pltpu.PrefetchScalarGridSpec(
            num_scalar_prefetch=1,
            grid=(2,),
            in_specs=[
                pl.BlockSpec((1, width, total), lambda i, s: (((s[at] ^ flip) * 2 + i) // 3, 0, 0)),
                pl.BlockSpec((1, total, width), lambda i, s: ((s[at] ^ flip) * 2 + i, 0, 0)),
            ],
            out_specs=pl.BlockSpec((1, width, width), lambda i, s: (i, 0, 0)),
        ),
        out_shape=jax.ShapeDtypeStruct((2, width, width), bf16),
        compiler_params=SMALL,
        cost_estimate=cost(4 * total * width * width, 8 * total * width + 4 * width * width),
    )(info, turned, grads).reshape(2 * width, width)


def input_kernel(branch_ref, dq_ref, dk_ref, dv_ref, wq_ref, wk_ref, wv_ref, out_ref):
    total = branch_ref[...] + mul(dq_ref[0], wq_ref[...], NT)
    total += mul(dk_ref[0], wk_ref[...], NT)
    total += mul(dv_ref[0], wv_ref[...], NT)
    out_ref[...] = total.astype(bf16)


def input_grad(branch_in, grads, w_query, w_key, w_value):
    total, width = branch_in.shape
    rows = pl.BlockSpec((BACK_ROWS, width), lambda i: (i, 0))
    return pl.pallas_call(
        input_kernel,
        grid=(total // BACK_ROWS,),
        in_specs=[rows]
        + [pl.BlockSpec((1, BACK_ROWS, width), lambda i, at=at: (at, i, 0)) for at in range(3)]
        + [fixed((width, width))] * 3,
        out_specs=rows,
        out_shape=jax.ShapeDtypeStruct((total, width), bf16),
        compiler_params=SMALL,
        cost_estimate=cost(6 * total * width * width, 12 * total * width + 6 * width * width),
    )(branch_in, grads, grads, grads, w_query, w_key, w_value)


def exchange(value, axis, mask):
    count = lax.axis_size(axis)
    return lax.ppermute(value, axis, [(i, i ^ mask) for i in range(count)])


def to_passages(value):
    count = lax.axis_size("seq")
    mine = lax.axis_index("seq")
    held, piece, width = value.shape
    own = held // count
    whole = jnp.zeros((own, piece * count, width), value.dtype)
    for mask in range(count):
        peer = mine ^ mask
        part = lax.dynamic_slice_in_dim(value, peer * own, own, 0)
        if mask:
            part = exchange(part, "seq", mask)
        whole = lax.dynamic_update_slice_in_dim(whole, part, peer * piece, 1)
    return whole


def position_pieces(value):
    count = lax.axis_size("seq")
    piece = value.shape[1] // count
    mine = lax.axis_index("seq")
    return [
        lax.dynamic_slice_in_dim(value, (mine ^ mask) * piece, piece, 1) for mask in range(count)
    ]


def traded(pieces):
    return [exchange(part, "seq", mask) if mask else part for mask, part in enumerate(pieces)]


def to_positions(pieces):
    mine = lax.axis_index("seq")
    own, piece, width = pieces[0].shape
    result = jnp.zeros((own * len(pieces), piece, width), pieces[0].dtype)
    for mask, part in enumerate(pieces):
        result = lax.dynamic_update_slice_in_dim(result, part, (mine ^ mask) * own, 0)
    return result


def axis_bits(axis):
    return [(axis, 1 << i) for i in range(lax.axis_size(axis).bit_length() - 1)]


def upper(dim):
    axis, mask = dim
    return (lax.axis_index(axis) & mask) // mask


def swap(value, dim):
    return exchange(value, dim[0], dim[1])


def total_of(parts):
    total = parts[0].astype(f32)
    for part in parts[1:]:
        total += part.astype(f32)
    return total.astype(bf16)


PARTS = 3
SHARD_STEP = 16


class Plan:
    def __init__(self, rows):
        dims = axis_bits("seq") + axis_bits("dp")
        self.first = dims[0]
        rest = dims[1:]
        self.rows = rows // PARTS
        halved = 0
        while halved < len(rest) and (self.rows >> (halved + 1)) % SHARD_STEP == 0:
            halved += 1
        self.last = rest[halved - 1]
        self.plain = rest[halved:]
        split = rest[: halved - 1]
        self.orders = [split[i % len(split) :] + split[: i % len(split)] for i in range(PARTS)]
        self.shards = 1 << halved
        self.shard = self.rows >> halved

    def table(self, blocks, width, each):
        places = {}
        devices = 1
        weight = {}
        for axis in ("seq", "dp"):
            for _, mask in axis_bits(axis):
                weight[(axis, mask)] = devices
                devices *= 2
        for side in range(2):
            for part, order in enumerate(self.orders):
                dims = [self.last] + order[::-1]
                for code in range(self.shards):
                    device = side * weight[self.first]
                    device += sum(weight[d] for i, d in enumerate(dims) if (code >> i) & 1)
                    row = part * self.rows + code * self.shard
                    places[side, row] = device * each + part * self.shard
        half = blocks // 4
        found = []
        for block in range(blocks):
            side = block % (2 * half) // half
            local = block // (2 * half) * half + block % half
            for row in range(0, width, self.shard):
                found.append(places[side, local * width + row])
        return found

    def codes(self):
        found = []
        for order in self.orders:
            code = upper(self.last)
            for at, dim in enumerate(reversed(order)):
                code += upper(dim) << (at + 1)
            found.append(code)
        return [code.astype(jnp.int32) for code in found]


class Chain:
    def __init__(self):
        self.token = None

    def tie(self, values):
        if self.token is None:
            return values
        return lax.optimization_barrier((values, self.token))[0]

    def mark(self, values):
        self.token = values
        return values


def scatter_steps(plan, chain, keep, got, found):
    pairs = [[keep, got]] * PARTS
    bases = [i * plan.rows for i in range(PARTS)]
    size = plan.rows
    for step in range(len(plan.orders[0])):
        pairs = chain.tie(pairs)
        size //= 2
        dims = [order[step] for order in plan.orders]

        def halves(pair, base, at):
            return total_of([lax.dynamic_slice_in_dim(p, base + at * size, size, 0) for p in pair])

        sends = [halves(p, base, 1 - upper(d)) for p, base, d in zip(pairs, bases, dims)]
        chain.mark(sends)
        mine = [halves(p, base, upper(d)) for p, base, d in zip(pairs, bases, dims)]
        pairs = [[m, swap(s, d)] for m, s, d in zip(mine, sends, dims)]
        bases = [0] * PARTS
        yield
    size = plan.shard
    bit = upper(plan.last)
    pairs = chain.tie(pairs)

    def side(at):
        return jnp.concatenate(
            [total_of([lax.dynamic_slice_in_dim(p, at * size, size, 0) for p in pair]) for pair in pairs],
            axis=0,
        )

    send = chain.mark(side(1 - bit))
    shard = side(bit)
    got = swap(send, plan.last)
    yield
    shard, got = chain.tie((shard, got))
    shard = total_of([shard, got])
    for dim in plan.plain:
        shard = total_of([shard, swap(shard, dim)])
    found.append(chain.mark(shard))
    yield


def gather_steps(plan, chain, shard, found):
    size = plan.shard
    got = swap(shard, plan.last)
    yield
    values = [(shard[i * size : (i + 1) * size], got[i * size : (i + 1) * size]) for i in range(PARTS)]
    for step in reversed(range(len(plan.orders[0]))):
        values = chain.tie(values)
        values = [jnp.concatenate(pair, axis=0) for pair in values]
        chain.mark(values)
        values = [(v, swap(v, order[step])) for v, order in zip(values, plan.orders)]
        yield
    values = chain.tie(values)
    chain.mark(values)
    found += [v for pair in values for v in pair]
    found += [swap(v, plan.first) for v in found]
    yield


def place(plan, refs, codes, row, store):
    part = row // plan.rows
    shard = ((row % plan.rows) // plan.shard) ^ codes[part]
    half = plan.shards // 2
    at = pl.ds(pl.multiple_of((shard & (half - 1)) * plan.shard, plan.shard), plan.shard)
    low, high = refs[2 * part][at, :], refs[2 * part + 1][at, :]
    store(jnp.where(shard >= half, high.astype(f32), low.astype(f32)))


def dense_place_kernel(
    shard, each, table_ref, group_ref, all_ref, down_ref, up_ref, vec_ref, pool_ref, hold_ref, word_ref, sems, word_sem
):
    step, steps = pl.program_id(0), pl.num_programs(0)
    width = down_ref.shape[1]
    parts = width // shard
    devices = word_ref.shape[0]

    @pl.when(step == 0)
    def _():
        def fetch(block, carry):
            for i in range(parts):
                at = pl.multiple_of(table_ref[block * parts + i], SHARD_STEP)
                pltpu.make_async_copy(
                    all_ref.at[pl.ds(at, shard)],
                    hold_ref.at[block, pl.ds(i * shard, shard)],
                    sems.at[block],
                ).start()
            return carry

        lax.fori_loop(0, steps, fetch, 0)

        def words(device, carry):
            pltpu.make_async_copy(
                all_ref.at[pl.ds(pl.multiple_of(device * each + each - 2 * SUM_ROWS, SHARD_STEP), 2 * SUM_ROWS)],
                word_ref.at[device],
                word_sem,
            ).start()
            return carry

        lax.fori_loop(0, devices, words, 0)

    pltpu.make_async_copy(all_ref.at[pl.ds(0, width)], hold_ref.at[step], sems.at[step]).wait()

    @pl.when(step < steps // 2)
    def _():
        for at in range(0, width, CHUNK):
            down_ref[at : at + CHUNK, :] = hold_ref[step, :, at : at + CHUNK].T.astype(f32)

    @pl.when(step >= steps // 2)
    def _():
        up_ref[...] = hold_ref[step].astype(f32)

    @pl.when(step == steps - 1)
    def _():
        pltpu.make_async_copy(word_ref, word_ref, word_sem).wait()

        def both(device):
            return word_ref[device, :SUM_ROWS].astype(f32) + word_ref[device, SUM_ROWS:].astype(f32)

        vec_ref[...] = lax.fori_loop(
            0, devices, lambda i, total: total + both(i), jnp.zeros(vec_ref.shape, f32)
        )
        for i in range(pool_ref.shape[0]):
            pool_ref[i] = both(group_ref[0] + i)[POOL_ROW:]


def dense_place(plan, gathered, each, width, wide, devices, seq_count, group):
    table = jnp.array(plan.table(2 * wide, width, each), jnp.int32)
    return pl.pallas_call(
        functools.partial(dense_place_kernel, plan.shard, each),
        grid_spec=pltpu.PrefetchScalarGridSpec(
            num_scalar_prefetch=2,
            grid=(2 * wide,),
            in_specs=[pl.BlockSpec(memory_space=pl.ANY)],
            out_specs=[
                pl.BlockSpec((width, width), lambda i, *_: (jnp.minimum(i, wide - 1), 0)),
                pl.BlockSpec((width, width), lambda i, *_: (0, jnp.maximum(i - wide, 0))),
                pl.BlockSpec((SUM_ROWS, width), lambda i, *_: (0, 0)),
                pl.BlockSpec((seq_count, SUM_ROWS - POOL_ROW, width), lambda i, *_: (0, 0, 0)),
            ],
            scratch_shapes=[
                pltpu.VMEM((2 * wide, width, width), bf16),
                pltpu.VMEM((devices, 2 * SUM_ROWS, width), bf16),
                pltpu.SemaphoreType.DMA((2 * wide,)),
                pltpu.SemaphoreType.DMA(()),
            ],
        ),
        out_shape=[
            jax.ShapeDtypeStruct((wide * width, width), f32),
            jax.ShapeDtypeStruct((width, wide * width), f32),
            jax.ShapeDtypeStruct((SUM_ROWS, width), f32),
            jax.ShapeDtypeStruct((seq_count, SUM_ROWS - POOL_ROW, width), f32),
        ],
        compiler_params=PARAMS,
        cost_estimate=cost(0, 12 * wide * width * width),
    )(table, group, gathered)


def attend_place_kernel(plan, first_code, at, flip, info_ref, *refs):
    sources, (hold_ref, sems) = refs[: 2 * PARTS], refs[-2:]
    outs = refs[-6:-2]
    codes = [info_ref[first_code + i] for i in range(PARTS)]
    own = info_ref[at] ^ flip
    width = hold_ref.shape[2]

    def move(block, act):
        for side in range(2):

            @pl.when(own == side)
            def _():
                act(pltpu.make_async_copy(hold_ref.at[block], outs[2 * side + block], sems.at[block]))

    for block in range(2):
        for row in range(0, width, plan.shard):

            def store(value, row=row):
                hold_ref[block, row : row + plan.shard, :] = value

            place(plan, sources, codes, block * width + row, store)
        move(block, lambda copy: copy.start())
    for block in range(2):
        move(block, lambda copy: copy.wait())


def attend_place(plan, first_code, at, flip, info, sources, width, before):
    kept = list(before)
    return pl.pallas_call(
        functools.partial(attend_place_kernel, plan, first_code, at, flip),
        grid_spec=pltpu.PrefetchScalarGridSpec(
            num_scalar_prefetch=1,
            grid=(1,),
            in_specs=[fixed(x.shape) for x in sources]
            + [pl.BlockSpec(memory_space=pl.ANY)] * len(kept),
            out_specs=[pl.BlockSpec(memory_space=pl.ANY)] * 4,
            scratch_shapes=[pltpu.VMEM((2, width, width), f32), pltpu.SemaphoreType.DMA((2,))],
        ),
        out_shape=[jax.ShapeDtypeStruct((width, width), f32)] * 4,
        input_output_aliases={1 + len(sources) + i: i for i in range(len(kept))},
        compiler_params=SMALL,
        cost_estimate=cost(0, 12 * width * width),
    )(info, *sources, *kept)


def shards(
    tokens,
    lengths,
    w_query,
    b_query,
    w_key,
    w_value,
    b_value,
    w_out,
    b_out,
    gain_one,
    shift_one,
    w_up,
    b_up,
    w_down,
    b_down,
    gain_two,
    shift_two,
    out_grad,
    pooled_grad,
):
    seq_count = lax.axis_size("seq")
    held, piece, width = tokens.shape
    full = piece * seq_count
    count = held // seq_count
    mine = lax.axis_index("seq")
    wide = w_up.shape[1] // width
    total = count * full

    def flat(value):
        return value.reshape(total, width)

    def split(value):
        return value.reshape(count, full, width)

    dense_plan = Plan(wide * width)
    outer_plan = Plan(2 * width)
    first = axis_bits("seq")[0]
    scalars = [mine, upper(first)] + dense_plan.codes() + outer_plan.codes()
    own_at, dense_at, outer_at = held + 1, held + 2, held + 2 + PARTS
    info = jnp.concatenate([lengths, jnp.stack([v.astype(jnp.int32) for v in scalars])])
    vecs = jnp.concatenate(
        [b_query, b_value, b_out, gain_one, shift_one, b_down, gain_two, shift_two, b_up]
    )
    vecs = vecs.astype(f32).reshape(-1, width)

    weights = [w_query, w_key, w_value, vecs]
    done = None
    source = tokens
    parts = []
    for passage in range(count):
        if parts:
            source = lax.optimization_barrier((tokens, parts))[0]
        parts = [
            exchange(
                lax.dynamic_slice_in_dim(source, (mine ^ mask) * count + passage, 1, 0), "seq", mask
            )
            for mask in range(1, seq_count)
        ]
        done = attend(passage, count, info, tokens, parts, weights, done)
    stacked, turned, q, k, v, stat = done
    cot = to_passages(lax.optimization_barrier((out_grad, parts))[0])
    stacked = stacked.reshape(2, total, width)
    result, first_low, act, second, inner, branch_in, mixed_grad, sums = row_work(
        held, info, stacked, flat(cot), pooled_grad, w_out, w_up, w_down, vecs, count
    )
    chain = Chain()
    pieces = chain.mark(position_pieces(split(result)))
    out_pieces = traded(pieces)
    send = dense_outer(own_at, 1, info, *chain.tie((act, second, first_low, inner)))
    chain.mark(send)
    got = swap(send, first)
    keep = chain.mark(dense_outer(own_at, 0, info, *chain.tie((act, second, first_low, inner))))
    dense, shard, outer = [], [], []
    dense_steps = scatter_steps(dense_plan, chain, keep, got, dense)
    next(dense_steps)
    chain.mark((chain.token, out_pieces))
    block_out = to_positions(out_pieces)
    grads, words = attend_back(
        held,
        info,
        q,
        k,
        v,
        chain.tie(split(mixed_grad)),
        stacked.reshape(2, count, full, width),
        split(branch_in),
        stat,
        sums,
    )
    chain.mark(words)
    grads = grads.reshape(4, total, width)
    next(dense_steps)
    send = attend_outer(own_at, 1, info, turned, chain.tie(grads))
    chain.mark(send)
    got = swap(send, first)
    next(dense_steps)
    keep = attend_outer(own_at, 0, info, turned, chain.tie(grads))
    chain.mark(keep)
    outer_steps = scatter_steps(outer_plan, chain, keep, got, shard)
    next(outer_steps)
    next(dense_steps)
    input_low = input_grad(branch_in, chain.tie(grads), w_query, w_key, w_value)
    chain.mark(input_low)
    for _ in dense_steps:
        pass
    gathered = jnp.concatenate([dense[0], words], axis=0)
    each = gathered.shape[0]
    gathered = chain.mark(gathered)
    gathered = lax.all_gather(gathered, ("dp", "seq"), axis=0, tiled=True)
    next(outer_steps)
    next(outer_steps)
    next(outer_steps)
    pieces = chain.mark(position_pieces(split(chain.tie(input_low))))
    in_pieces = traded(pieces)
    for _ in outer_steps:
        pass
    outer_steps = gather_steps(outer_plan, chain, shard[0], outer)
    next(outer_steps)
    next(outer_steps)
    next(outer_steps)
    chain.mark((chain.token, in_pieces))
    next(outer_steps)
    tokens_grad = to_positions(in_pieces)
    chain.mark((chain.token, tokens_grad, block_out))
    for _ in outer_steps:
        pass
    group = (lax.axis_index("dp") * seq_count).astype(jnp.int32)[None]

    def place_outer(flip, before):
        pick = outer[2 * PARTS :] if flip else outer[: 2 * PARTS]
        return chain.mark(
            attend_place(outer_plan, outer_at, own_at, flip, info, chain.tie(pick), width, before)
        )

    placed = place_outer(0, [])
    outer = place_outer(1, placed)
    down_sum, up_sum, vectors, pooled = dense_place(
        dense_plan, chain.tie(gathered), each, width, wide, gathered.shape[0] // each, seq_count, group
    )
    pooled = pooled[:, :count].reshape(held, width)
    return (
        block_out,
        pooled,
        tokens_grad,
        outer[0],
        vectors[0],
        outer[1],
        outer[2],
        vectors[1],
        outer[3],
        vectors[2],
        vectors[3],
        vectors[4],
        up_sum,
        vectors[8 : 8 + wide].reshape(-1),
        down_sum,
        vectors[5],
        vectors[6],
        vectors[7],
    )


def solution(mesh):
    in_specs = (
        (P("dp", "seq", None), P("dp"))
        + (P(),) * 15
        + (P("dp", "seq", None), P("dp", None))
    )
    out_specs = (P("dp", "seq", None), P("dp", None), P("dp", "seq", None)) + (P(),) * 15
    return jax.shard_map(shards, mesh=mesh, in_specs=in_specs, out_specs=out_specs, check_vma=False)
```

```python
import functools

import jax
import jax.numpy as jnp
from jax import lax
from jax.experimental import pallas as pl
from jax.experimental.pallas import tpu as pltpu
from jax.sharding import PartitionSpec as P

HEADS = 12
HEAD_DIM = 64
PAIR = 2 * HEAD_DIM
PAIRS = HEADS // 2
SCALE = HEAD_DIM ** (-0.5)
ROWS = 512
BACK_ROWS = 256
STRIP = 32
TOGETHER = 1
BACK_TOGETHER = 3
STAT_ROWS = 16
CHUNK = 256
KEY_STEP = 128
VMEM_BYTES = 62 * 1024 * 1024
SMALL_BYTES = 40 * 1024 * 1024
SUM_ROWS = 16
POOL_ROW = 12

eps = 1e-06
root_half = 0.7071067811865476
inv_root_two_pi = 0.3989422804014327

f32 = jnp.float32
bf16 = jnp.bfloat16

NN = (((1,), (0,)), ((), ()))
NT = (((1,), (1,)), ((), ()))
TN = (((0,), (0,)), ((), ()))


def mul(left, right, dims=NN):
    return lax.dot_general(left, right, dims, preferred_element_type=f32)


def fixed(shape):
    return pl.BlockSpec(shape, lambda *_: (0,) * len(shape), pipeline_mode=pl.Buffered(1))


PARAMS = pltpu.CompilerParams(dimension_semantics=("arbitrary",), vmem_limit_bytes=VMEM_BYTES)
SMALL = pltpu.CompilerParams(dimension_semantics=("arbitrary",), vmem_limit_bytes=SMALL_BYTES)


def cost(flops, moved, exps=0):
    return pl.CostEstimate(flops=int(flops), bytes_accessed=int(moved), transcendentals=int(exps))


def over_extents(length, full, body):
    for extent in range(KEY_STEP, full + 1, KEY_STEP):
        pl.when((length > extent - KEY_STEP) & (length <= extent))(functools.partial(body, extent))


def by_eight(value):
    return value.reshape(value.shape[0] // 8, 8, value.shape[1])


def fill_dead(dead_ref, extent, length):
    key_at = lax.broadcasted_iota(jnp.int32, dead_ref.shape, 0) + (extent - KEY_STEP)
    dead_ref[...] = jnp.where(key_at < length, 0.0, -1e30)


def live_strip(scores, dead_ref, extent, row):
    strip = scores[row : row + STRIP]
    last = row - (extent - KEY_STEP)
    return strip + dead_ref[last : last + STRIP] if last >= 0 else strip


def attend_kernel(pieces, passage, count, held, info_ref, *refs):
    part_refs, refs = refs[:pieces], refs[pieces:]
    wq_ref, wk_ref, wv_ref, vec_ref = refs[:4]
    xm_ref, q_ref, k_ref, v_ref, stat_ref, prob_ref, dead_ref = refs[-7:]
    x_ref, mix_ref = xm_ref.at[0], xm_ref.at[1]
    mine = info_ref[held]
    length = info_ref[mine * count + passage]
    size = part_refs[0].shape[1]
    for mask, part_ref in enumerate(part_refs):
        x_ref[0, pl.ds(pl.multiple_of((mine ^ mask) * size, size), size)] = part_ref[0]

    def project(index, carry):
        at = pl.ds(pl.multiple_of(index * CHUNK, CHUNK), CHUNK)
        x = x_ref[0]
        q_ref[0, :, at] = (mul(x, wq_ref[:, at]) + vec_ref[0:1, at]).astype(bf16)
        k_ref[0, :, at] = mul(x, wk_ref[:, at]).astype(bf16)
        v_ref[0, :, at] = (mul(x, wv_ref[:, at]) + vec_ref[1:2, at]).astype(bf16)
        return carry

    lax.fori_loop(0, wq_ref.shape[1] // CHUNK, project, 0)
    stat_ref[0] = jnp.zeros(stat_ref.shape[1:], f32)
    full = size * pieces
    lane = lax.broadcasted_iota(jnp.int32, (1, PAIR), 1)

    def run(extent):
        fill_dead(dead_ref, extent, length)

        def head(at, number, half, slot):
            q, k = q_ref[0, :, at], k_ref[0, :extent, at]
            own = (lane >= half * HEAD_DIM) & (lane < (half + 1) * HEAD_DIM)
            scores = mul(jnp.where(own, k * SCALE, 0).astype(bf16), q, NT)
            top = jnp.full((8, full), -jnp.inf, f32)
            for row in range(0, extent, STRIP):
                top = jnp.maximum(top, by_eight(live_strip(scores, dead_ref, extent, row)).max(axis=0))
            top = jnp.max(top, axis=0, keepdims=True)
            total = jnp.zeros((8, full), f32)
            for row in range(0, extent, STRIP):
                expo = jnp.exp(live_strip(scores, dead_ref, extent, row) - top)
                total += by_eight(expo).sum(axis=0)
                prob_ref[slot, row : row + STRIP] = expo.astype(bf16)
            total = jnp.sum(total, axis=0, keepdims=True)
            stat_ref[0, pl.ds(number, 1), :] = top + jnp.log(total)
            return 1.0 / total

        def group(index, carry):
            for i in range(TOGETHER):
                pair = index * TOGETHER + i
                at = pl.ds(pl.multiple_of(pair * PAIR, PAIR), PAIR)
                values = v_ref[0, :extent, at].T
                mixed = []
                for half in range(2):
                    slot = 2 * i + half
                    scale = head(at, pair * 2 + half, half, slot)
                    own = values[half * HEAD_DIM : (half + 1) * HEAD_DIM]
                    mixed.append(mul(own, prob_ref[slot, :extent]) * scale)
                mix_ref[0, :, at] = jnp.concatenate(mixed, axis=0).T.astype(bf16)
            return carry

        lax.fori_loop(0, PAIRS // TOGETHER, group, 0)

    over_extents(length, full, run)


def attend(passage, count, info, tokens, parts, weights, before):
    held, piece, width = tokens.shape
    pieces = len(parts) + 1
    full = piece * pieces
    rows = pl.BlockSpec((1, full, width), lambda i, s: (passage, 0, 0))
    act = jax.ShapeDtypeStruct((count, full, width), bf16)
    got = pl.BlockSpec((1, piece, width), lambda i, s: (0, 0, 0))
    kept = [] if before is None else list(before)
    first_kept = 1 + pieces + len(weights)
    return pl.pallas_call(
        functools.partial(attend_kernel, pieces, passage, count, held),
        grid_spec=pltpu.PrefetchScalarGridSpec(
            num_scalar_prefetch=1,
            grid=(1,),
            in_specs=[pl.BlockSpec((1, piece, width), lambda i, s: (s[held] * count + passage, 0, 0))]
            + [got] * len(parts)
            + [fixed(w.shape) for w in weights]
            + [pl.BlockSpec(memory_space=pl.ANY)] * len(kept),
            out_specs=[pl.BlockSpec((2, 1, full, width), lambda i, s: (0, passage, 0, 0))]
            + [rows] * 3
            + [pl.BlockSpec((1, STAT_ROWS, full), lambda i, s: (passage, 0, 0))],
            scratch_shapes=[
                pltpu.VMEM((2 * TOGETHER, full, full), bf16),
                pltpu.VMEM((KEY_STEP, full), f32),
            ],
        ),
        out_shape=[jax.ShapeDtypeStruct((2, count, full, width), bf16)]
        + [act] * 3
        + [jax.ShapeDtypeStruct((count, STAT_ROWS, full), f32)],
        input_output_aliases={first_kept + i: i for i in range(len(kept))},
        compiler_params=PARAMS,
        cost_estimate=cost(
            2 * full * (3 * width * width + 4 * 2 * full * width),
            12 * full * width + 6 * width * width,
        ),
    )(info, tokens, *parts, *weights, *kept)


def attend_back_kernel(
    held,
    info_ref,
    q_ref,
    k_ref,
    v_ref,
    mg_ref,
    mix_ref,
    branch_ref,
    stat_ref,
    sum_ref,
    grads_ref,
    word_ref,
    bias_ref,
    along_ref,
    prob_ref,
    score_ref,
    dead_ref,
):
    dq_ref, dk_ref, dv_ref = (grads_ref.at[i] for i in range(3))
    grads_ref[3] = branch_ref[...].astype(bf16)
    full, width = q_ref.shape[1:]
    length = info_ref[info_ref[held] * pl.num_programs(0) + pl.program_id(0)]
    lane = lax.broadcasted_iota(jnp.int32, (1, PAIR), 1)
    row = lax.broadcasted_iota(jnp.int32, (8, 1), 0)

    @pl.when(pl.program_id(0) == 0)
    def _():
        bias_ref[...] = sum_ref[...]

    feature = lax.broadcasted_iota(jnp.int32, (STAT_ROWS, width), 1)
    number = lax.broadcasted_iota(jnp.int32, (STAT_ROWS, width), 0)
    ours = jnp.where(
        (feature >= number * HEAD_DIM) & (feature < (number + 1) * HEAD_DIM), 1.0, 0.0
    ).astype(bf16)
    product = mg_ref[0].astype(f32) * mix_ref[0, 0].astype(f32)
    high = product.astype(bf16)
    low = (product - high.astype(f32)).astype(bf16)
    along_ref[...] = mul(ours, high, NT) + mul(ours, low, NT)

    def run(extent):
        fill_dead(dead_ref, extent, length)
        if extent < full:
            dk_ref[0, extent:] = jnp.zeros((full - extent, width), bf16)
            dv_ref[0, extent:] = jnp.zeros((full - extent, width), bf16)

        def group(index, carry):
            for i in range(BACK_TOGETHER):
                pair = index * BACK_TOGETHER + i
                at = pl.ds(pl.multiple_of(pair * PAIR, PAIR), PAIR)
                q, mg = q_ref[0, :, at], mg_ref[0, :, at]
                k, v = k_ref[0, :extent, at], v_ref[0, :extent, at]
                keys = k.T
                dq, dk, dv = [], [], []
                for half in range(2):
                    slot = 2 * i + half
                    own = (lane >= half * HEAD_DIM) & (lane < (half + 1) * HEAD_DIM)
                    scores = mul(jnp.where(own, k * SCALE, 0).astype(bf16), q, NT)
                    prob_grad = mul(jnp.where(own, v, 0).astype(bf16), mg, NT)
                    log_row = stat_ref[0, pl.ds(pair * 2 + half, 1), :]
                    along = along_ref[pl.ds(pair * 2 + half, 1), :]
                    for at_row in range(0, extent, STRIP):
                        rows = slice(at_row, at_row + STRIP)
                        probs = jnp.exp(live_strip(scores, dead_ref, extent, at_row) - log_row)
                        prob_ref[slot, rows] = probs.astype(bf16)
                        score_ref[slot, rows] = (probs * (prob_grad[rows] - along)).astype(bf16)
                    score_grad = score_ref[slot, :extent]
                    dv.append(mul(prob_ref[slot, :extent], mg))
                    dk.append(mul(score_grad, q))
                    dq.append(mul(keys[half * HEAD_DIM : (half + 1) * HEAD_DIM], score_grad))
                first = lane < HEAD_DIM
                dq_pair = jnp.concatenate(dq, axis=0).T * SCALE
                dk_pair = jnp.where(first, dk[0], dk[1]) * SCALE
                dv_pair = jnp.where(first, dv[0], dv[1])
                dq_ref[0, :, at] = dq_pair.astype(bf16)
                dk_ref[0, :extent, at] = dk_pair.astype(bf16)
                dv_ref[0, :extent, at] = dv_pair.astype(bf16)
                sums = jnp.where(
                    row == 0,
                    jnp.sum(dq_pair, axis=0, keepdims=True),
                    jnp.where(row == 1, jnp.sum(dv_pair, axis=0, keepdims=True), 0.0),
                )
                bias_ref[0:8, at] += sums
            return carry

        lax.fori_loop(0, PAIRS // BACK_TOGETHER, group, 0)

    over_extents(length, full, run)

    @pl.when(pl.program_id(0) == pl.num_programs(0) - 1)
    def _():
        high = bias_ref[...].astype(bf16)
        word_ref[:SUM_ROWS] = high
        word_ref[SUM_ROWS:] = (bias_ref[...] - high.astype(f32)).astype(bf16)


def attend_back(held, info, q, k, v, mixed_grad, stacked, branch_in, stat, sums):
    count, full, width = q.shape
    rows = pl.BlockSpec((1, full, width), lambda i, *_: (i, 0, 0))
    return pl.pallas_call(
        functools.partial(attend_back_kernel, held),
        grid_spec=pltpu.PrefetchScalarGridSpec(
            num_scalar_prefetch=1,
            grid=(count,),
            in_specs=[rows] * 4
            + [
                pl.BlockSpec((1, 1, full, width), lambda i, *_: (1, i, 0, 0)),
                rows,
                pl.BlockSpec((1, STAT_ROWS, full), lambda i, *_: (i, 0, 0)),
                fixed(sums.shape),
            ],
            out_specs=[
                pl.BlockSpec((4, 1, full, width), lambda i, *_: (0, i, 0, 0)),
                pl.BlockSpec((2 * SUM_ROWS, width), lambda i, *_: (0, 0)),
            ],
            scratch_shapes=[
                pltpu.VMEM(sums.shape, f32),
                pltpu.VMEM((STAT_ROWS, full), f32),
                pltpu.VMEM((2 * BACK_TOGETHER, full, full), bf16),
                pltpu.VMEM((2 * BACK_TOGETHER, full, full), bf16),
                pltpu.VMEM((KEY_STEP, full), f32),
            ],
        ),
        out_shape=[
            jax.ShapeDtypeStruct((4, count, full, width), bf16),
            jax.ShapeDtypeStruct((2 * SUM_ROWS, width), bf16),
        ],
        compiler_params=PARAMS,
        cost_estimate=cost(
            2 * count * full * 10 * 2 * full * width, 16 * count * full * width
        ),
    )(info, q, k, v, mixed_grad, stacked, branch_in, stat, sums)


def norm_parts(hidden):
    centred = hidden - jnp.mean(hidden, axis=1, keepdims=True)
    inv_scale = lax.rsqrt(jnp.mean(centred * centred, axis=1, keepdims=True) + eps)
    return centred * inv_scale, inv_scale


def norm_back(scaled, normed, inv_scale):
    mean = jnp.mean(scaled, axis=1, keepdims=True)
    along = jnp.mean(scaled * normed, axis=1, keepdims=True)
    return (scaled - mean - normed * along) * inv_scale


def gelu_parts(u):
    expo = jnp.exp(u * u * -0.5)
    base = 1.0 + jnp.abs(u) * (0.3275911 * root_half)
    t = pl.reciprocal(base, approx=True)
    t = t * (2.0 - base * t)
    poly = t * (
        0.5 * 0.254829592
        + t
        * (
            0.5 * -0.284496736
            + t * (0.5 * 1.421413741 + t * (0.5 * -1.453152027 + t * (0.5 * 1.061405429)))
        )
    )
    tail = poly * expo
    return jnp.where(u >= 0, 1.0 - tail, tail), expo


def rows_kernel(
    blocks,
    count,
    held,
    info_ref,
    x_ref,
    mix_ref,
    cot_ref,
    pool_ref,
    wo_ref,
    vec_ref,
    wu_all,
    wd_all,
    out_ref,
    low_ref,
    act_all,
    second_ref,
    inner_all,
    branch_ref,
    mg_ref,
    sum_ref,
    wu_ref,
    wd_ref,
    act_ref,
    inner_ref,
    slope_ref,
    first_ref,
    normed_ref,
    total_ref,
    scale_ref,
    sems,
):
    step, steps = pl.program_id(0), pl.num_programs(0)
    rows, width = cot_ref.shape
    hidden_width = wu_ref.shape[1]
    b_out, gain_one, shift_one, b_down, gain_two, shift_two = (
        vec_ref[i : i + 1] for i in range(2, 8)
    )
    passage = info_ref[held] * count + step // blocks
    length = info_ref[passage]
    inv_length = 1.0 / jnp.full((1, width), length, jnp.int32).astype(f32)
    pool = pool_ref[pl.ds(passage, 1), :] * inv_length
    first_row = (step % blocks) * rows
    load_up = pltpu.make_async_copy(wu_all, wu_ref, sems.at[0])
    load_down = pltpu.make_async_copy(wd_all, wd_ref, sems.at[1])

    def give(source_ref, all_ref, at):
        return pltpu.make_async_copy(
            source_ref, all_ref.at[pl.ds(pl.multiple_of(at * rows, rows), rows)], sems.at[2 if source_ref is act_ref else 3]
        )

    @pl.when(step == 0)
    def _():
        load_up.start()
        load_down.start()
        sum_ref[...] = jnp.zeros(sum_ref.shape, f32)

    def tally(at, value, columns=slice(None)):
        sum_ref[at : at + 1, columns] += jnp.sum(value, axis=0, keepdims=True)

    def strips(size):
        return [slice(i, i + size) for i in range(0, rows, size)]

    groups = width // CHUNK
    chunks = hidden_width // CHUNK
    part = [slice(i * CHUNK, (i + 1) * CHUNK) for i in range(chunks)]
    whole = [slice(i * width, (i + 1) * width) for i in range(hidden_width // width)]
    lanes = scale_ref.shape[1]

    branch = mul(mix_ref[0], wo_ref[...])
    for at in strips(STRIP):
        normed, scale = norm_parts(x_ref[0, at].astype(f32) + branch[at] + b_out)
        first = normed * gain_one + shift_one
        normed_ref[at] = normed
        scale_ref[at] = jnp.broadcast_to(scale, (STRIP, lanes))
        first_ref[at] = first + b_down
        low_ref[at] = first.astype(bf16)

    @pl.when(step == 0)
    def _():
        load_up.wait()
        load_down.wait()

    @pl.when(step > 0)
    def _():
        give(act_ref, act_all, step - 1).wait()

    def up(i):
        return mul(low_ref[...], wu_ref[:, part[i]])

    pre = up(0)
    for i in range(chunks):
        ahead = up(i + 1) if i + 1 < chunks else None
        bias = vec_ref[8 + i // groups : 9 + i // groups, part[i % groups]]
        for at in strips(2 * STRIP):
            u = pre[at] + bias
            phi, expo = gelu_parts(u)
            act_ref[at, part[i]] = (u * phi).astype(bf16)
            slope_ref[at, part[i]] = phi + u * expo * inv_root_two_pi
        if i % groups == 0 and i:
            done = whole[i // groups - 1]
            first_ref[...] += mul(act_ref[:, done], wd_ref[done, :])
        pre = ahead
    last = mul(act_ref[:, whole[-1]], wd_ref[whole[-1], :])
    give(act_ref, act_all, step).start()

    pooled, shift, gain, down = (jnp.zeros((8, width), f32) for _ in range(4))
    for at in strips(STRIP):
        normed, scale = norm_parts(first_ref[at] + last[at])
        result = normed * gain_two + shift_two
        out_ref[at] = result.astype(bf16)
        row_at = lax.broadcasted_iota(jnp.int32, (STRIP, 1), 0) + (first_row + at.start)
        live = jnp.where(row_at < length, 1.0, 0.0)
        pooled += by_eight(result * live).sum(axis=0)
        upstream = cot_ref[at].astype(f32) + live * pool
        gain += by_eight(upstream * normed).sum(axis=0)
        shift += by_eight(upstream).sum(axis=0)
        second_in = norm_back(upstream * gain_two, normed, scale)
        down += by_eight(second_in).sum(axis=0)
        total_ref[at] = second_in
        second_ref[at] = second_in.astype(bf16)
    tally(6, gain)
    tally(7, shift)
    tally(5, down)
    sum_ref[pl.ds(POOL_ROW + step // blocks, 1), :] += (
        jnp.sum(pooled, axis=0, keepdims=True) * inv_length
    )

    @pl.when(step > 0)
    def _():
        give(inner_ref, inner_all, step - 1).wait()

    def back(i):
        return mul(second_ref[...], wd_ref[part[i], :], NT)

    grad = back(0)
    for i in range(chunks):
        ahead = back(i + 1) if i + 1 < chunks else None
        bias = jnp.zeros((8, CHUNK), f32)
        for at in strips(2 * STRIP):
            inner = grad[at] * slope_ref[at, part[i]]
            bias += by_eight(inner).sum(axis=0)
            inner_ref[at, part[i]] = inner.astype(bf16)
        tally(8 + i // groups, bias, part[i % groups])
        if i % groups == 0 and i:
            done = whole[i // groups - 1]
            total_ref[...] += mul(inner_ref[:, done], wu_ref[:, done], NT)
        grad = ahead
    last = mul(inner_ref[:, whole[-1]], wu_ref[:, whole[-1]], NT)
    give(inner_ref, inner_all, step).start()

    gain, shift, out = (jnp.zeros((8, width), f32) for _ in range(3))
    for at in strips(STRIP):
        first_up = total_ref[at] + last[at]
        normed = normed_ref[at]
        gain += by_eight(first_up * normed).sum(axis=0)
        shift += by_eight(first_up).sum(axis=0)
        branch_in = norm_back(first_up * gain_one, normed, scale_ref[at, :1])
        out += by_eight(branch_in).sum(axis=0)
        branch_ref[at] = branch_in
    tally(3, gain)
    tally(4, shift)
    tally(2, out)
    mg_ref[...] = mul(branch_ref[...].astype(bf16), wo_ref[...], NT).astype(bf16)

    @pl.when(step == steps - 1)
    def _():
        give(act_ref, act_all, step).wait()
        give(inner_ref, inner_all, step).wait()


def row_work(held, info, stacked, cot, pool, w_out, w_up, w_down, vecs, count):
    total, width = cot.shape
    full = total // count
    assert POOL_ROW + count <= SUM_ROWS
    hidden = w_up.shape[1]
    blocks = full // ROWS
    narrow = pl.BlockSpec((ROWS, width), lambda i, *_: (i, 0))
    anywhere = pl.BlockSpec(memory_space=pl.ANY)
    thin = jax.ShapeDtypeStruct((total, width), bf16)
    thick = jax.ShapeDtypeStruct((total, hidden), bf16)
    return pl.pallas_call(
        functools.partial(rows_kernel, blocks, count, held),
        grid_spec=pltpu.PrefetchScalarGridSpec(
            num_scalar_prefetch=1,
            grid=(total // ROWS,),
            in_specs=[
                pl.BlockSpec((1, ROWS, width), lambda i, *_: (0, i, 0)),
                pl.BlockSpec((1, ROWS, width), lambda i, *_: (1, i, 0)),
                narrow,
                fixed(pool.shape),
                fixed((width, width)),
                fixed(vecs.shape),
                anywhere,
                anywhere,
            ],
            out_specs=[
                narrow,
                narrow,
                anywhere,
                narrow,
                anywhere,
                narrow,
                narrow,
                pl.BlockSpec((SUM_ROWS, width), lambda i, *_: (0, 0)),
            ],
            scratch_shapes=[
                pltpu.VMEM((width, hidden), bf16),
                pltpu.VMEM((hidden, width), bf16),
                pltpu.VMEM((ROWS, hidden), bf16),
                pltpu.VMEM((ROWS, hidden), bf16),
                pltpu.VMEM((ROWS, hidden), f32),
                pltpu.VMEM((ROWS, width), f32),
                pltpu.VMEM((ROWS, width), f32),
                pltpu.VMEM((ROWS, width), f32),
                pltpu.VMEM((ROWS, PAIR), f32),
                pltpu.SemaphoreType.DMA((4,)),
            ],
        ),
        out_shape=[
            thin,
            thin,
            thick,
            thin,
            thick,
            jax.ShapeDtypeStruct((total, width), f32),
            thin,
            jax.ShapeDtypeStruct((SUM_ROWS, width), f32),
        ],
        compiler_params=PARAMS,
        cost_estimate=cost(
            4 * total * width * (width + 2 * hidden),
            2 * total * (8 * width + 2 * hidden) + 2 * width * (width + 2 * hidden),
        ),
    )(info, stacked, stacked, cot, pool, w_out, vecs, w_up, w_down)


def dense_outer_kernel(side_ref, act_ref, second_ref, low_ref, inner_ref, out_ref):
    step = pl.program_id(0)
    half = pl.num_programs(0) // 2

    @pl.when(step < half)
    def _():
        out_ref[0] = mul(act_ref[...], second_ref[...], TN).astype(bf16)

    @pl.when(step >= half)
    def _():
        out_ref[0] = mul(low_ref[...], inner_ref[...], TN).astype(bf16)


def dense_outer(at, flip, info, act, second, low, inner):
    total, width = second.shape
    wide = act.shape[1] // width
    half = wide // 2
    return pl.pallas_call(
        dense_outer_kernel,
        grid_spec=pltpu.PrefetchScalarGridSpec(
            num_scalar_prefetch=1,
            grid=(wide,),
            in_specs=[
                pl.BlockSpec(
                    (total, width), lambda i, s: (0, (s[at] ^ flip) * half + jnp.minimum(i, half - 1))
                ),
                fixed((total, width)),
                fixed((total, width)),
                pl.BlockSpec(
                    (total, width), lambda i, s: (0, (s[at] ^ flip) * half + jnp.maximum(i - half, 0))
                ),
            ],
            out_specs=pl.BlockSpec((1, width, width), lambda i, s: (i, 0, 0)),
        ),
        out_shape=jax.ShapeDtypeStruct((wide, width, width), bf16),
        compiler_params=SMALL,
        cost_estimate=cost(
            2 * total * width * width * wide, 2 * (wide + 2) * total * width + 2 * wide * width * width
        ),
    )(info, act, second, low, inner).reshape(wide * width, width)


def attend_outer_kernel(side_ref, left_ref, right_ref, out_ref):
    out_ref[0] = mul(left_ref[0], right_ref[0], TN).astype(bf16)


def attend_outer(at, flip, info, stacked, grads):
    total, width = stacked.shape[1:]
    return pl.pallas_call(
        attend_outer_kernel,
        grid_spec=pltpu.PrefetchScalarGridSpec(
            num_scalar_prefetch=1,
            grid=(2,),
            in_specs=[
                pl.BlockSpec((1, total, width), lambda i, s: (((s[at] ^ flip) * 2 + i) // 3, 0, 0)),
                pl.BlockSpec((1, total, width), lambda i, s: ((s[at] ^ flip) * 2 + i, 0, 0)),
            ],
            out_specs=pl.BlockSpec((1, width, width), lambda i, s: (i, 0, 0)),
        ),
        out_shape=jax.ShapeDtypeStruct((2, width, width), bf16),
        compiler_params=SMALL,
        cost_estimate=cost(4 * total * width * width, 8 * total * width + 4 * width * width),
    )(info, stacked, grads).reshape(2 * width, width)


def input_kernel(branch_ref, dq_ref, dk_ref, dv_ref, wq_ref, wk_ref, wv_ref, out_ref):
    total = branch_ref[...] + mul(dq_ref[0], wq_ref[...], NT)
    total += mul(dk_ref[0], wk_ref[...], NT)
    total += mul(dv_ref[0], wv_ref[...], NT)
    out_ref[...] = total.astype(bf16)


def input_grad(branch_in, grads, w_query, w_key, w_value):
    total, width = branch_in.shape
    rows = pl.BlockSpec((BACK_ROWS, width), lambda i: (i, 0))
    return pl.pallas_call(
        input_kernel,
        grid=(total // BACK_ROWS,),
        in_specs=[rows]
        + [pl.BlockSpec((1, BACK_ROWS, width), lambda i, at=at: (at, i, 0)) for at in range(3)]
        + [fixed((width, width))] * 3,
        out_specs=rows,
        out_shape=jax.ShapeDtypeStruct((total, width), bf16),
        compiler_params=SMALL,
        cost_estimate=cost(6 * total * width * width, 12 * total * width + 6 * width * width),
    )(branch_in, grads, grads, grads, w_query, w_key, w_value)


def exchange(value, axis, mask):
    count = lax.axis_size(axis)
    return lax.ppermute(value, axis, [(i, i ^ mask) for i in range(count)])


def to_passages(value):
    count = lax.axis_size("seq")
    mine = lax.axis_index("seq")
    held, piece, width = value.shape
    own = held // count
    whole = jnp.zeros((own, piece * count, width), value.dtype)
    for mask in range(count):
        peer = mine ^ mask
        part = lax.dynamic_slice_in_dim(value, peer * own, own, 0)
        if mask:
            part = exchange(part, "seq", mask)
        whole = lax.dynamic_update_slice_in_dim(whole, part, peer * piece, 1)
    return whole


def position_pieces(value):
    count = lax.axis_size("seq")
    piece = value.shape[1] // count
    mine = lax.axis_index("seq")
    return [
        lax.dynamic_slice_in_dim(value, (mine ^ mask) * piece, piece, 1) for mask in range(count)
    ]


def traded(pieces):
    return [exchange(part, "seq", mask) if mask else part for mask, part in enumerate(pieces)]


def to_positions(pieces):
    mine = lax.axis_index("seq")
    own, piece, width = pieces[0].shape
    result = jnp.zeros((own * len(pieces), piece, width), pieces[0].dtype)
    for mask, part in enumerate(pieces):
        result = lax.dynamic_update_slice_in_dim(result, part, (mine ^ mask) * own, 0)
    return result


def axis_bits(axis):
    return [(axis, 1 << i) for i in range(lax.axis_size(axis).bit_length() - 1)]


def upper(dim):
    axis, mask = dim
    return (lax.axis_index(axis) & mask) // mask


def swap(value, dim):
    return exchange(value, dim[0], dim[1])


def total_of(parts):
    total = parts[0].astype(f32)
    for part in parts[1:]:
        total += part.astype(f32)
    return total.astype(bf16)


PARTS = 3
SHARD_STEP = 16


class Plan:
    def __init__(self, rows):
        dims = axis_bits("seq") + axis_bits("dp")
        self.first = dims[0]
        rest = dims[1:]
        self.rows = rows // PARTS
        halved = 0
        while halved < len(rest) and (self.rows >> (halved + 1)) % SHARD_STEP == 0:
            halved += 1
        self.last = rest[halved - 1]
        self.plain = rest[halved:]
        split = rest[: halved - 1]
        self.orders = [split[i % len(split) :] + split[: i % len(split)] for i in range(PARTS)]
        self.shards = 1 << halved
        self.shard = self.rows >> halved

    def table(self, blocks, width, each):
        places = {}
        devices = 1
        weight = {}
        for axis in ("seq", "dp"):
            for _, mask in axis_bits(axis):
                weight[(axis, mask)] = devices
                devices *= 2
        for side in range(2):
            for part, order in enumerate(self.orders):
                dims = [self.last] + order[::-1]
                for code in range(self.shards):
                    device = side * weight[self.first]
                    device += sum(weight[d] for i, d in enumerate(dims) if (code >> i) & 1)
                    row = part * self.rows + code * self.shard
                    places[side, row] = device * each + part * self.shard
        half = blocks // 4
        found = []
        for block in range(blocks):
            side = block % (2 * half) // half
            local = block // (2 * half) * half + block % half
            for row in range(0, width, self.shard):
                found.append(places[side, local * width + row])
        return found

    def codes(self):
        found = []
        for order in self.orders:
            code = upper(self.last)
            for at, dim in enumerate(reversed(order)):
                code += upper(dim) << (at + 1)
            found.append(code)
        return [code.astype(jnp.int32) for code in found]


class Chain:
    def __init__(self):
        self.token = None

    def tie(self, values):
        if self.token is None:
            return values
        return lax.optimization_barrier((values, self.token))[0]

    def mark(self, values):
        self.token = values
        return values


def scatter_steps(plan, chain, keep, got, found):
    pairs = [[keep, got]] * PARTS
    bases = [i * plan.rows for i in range(PARTS)]
    size = plan.rows
    for step in range(len(plan.orders[0])):
        pairs = chain.tie(pairs)
        size //= 2
        dims = [order[step] for order in plan.orders]

        def halves(pair, base, at):
            return total_of([lax.dynamic_slice_in_dim(p, base + at * size, size, 0) for p in pair])

        sends = [halves(p, base, 1 - upper(d)) for p, base, d in zip(pairs, bases, dims)]
        chain.mark(sends)
        mine = [halves(p, base, upper(d)) for p, base, d in zip(pairs, bases, dims)]
        pairs = [[m, swap(s, d)] for m, s, d in zip(mine, sends, dims)]
        bases = [0] * PARTS
        yield
    size = plan.shard
    bit = upper(plan.last)
    pairs = chain.tie(pairs)

    def side(at):
        return jnp.concatenate(
            [total_of([lax.dynamic_slice_in_dim(p, at * size, size, 0) for p in pair]) for pair in pairs],
            axis=0,
        )

    send = chain.mark(side(1 - bit))
    shard = side(bit)
    got = swap(send, plan.last)
    yield
    shard, got = chain.tie((shard, got))
    shard = total_of([shard, got])
    for dim in plan.plain:
        shard = total_of([shard, swap(shard, dim)])
    found.append(chain.mark(shard))
    yield


def gather_steps(plan, chain, shard, found):
    size = plan.shard
    got = swap(shard, plan.last)
    yield
    values = [(shard[i * size : (i + 1) * size], got[i * size : (i + 1) * size]) for i in range(PARTS)]
    for step in reversed(range(len(plan.orders[0]))):
        values = chain.tie(values)
        values = [jnp.concatenate(pair, axis=0) for pair in values]
        chain.mark(values)
        values = [(v, swap(v, order[step])) for v, order in zip(values, plan.orders)]
        yield
    values = chain.tie(values)
    chain.mark(values)
    found += [v for pair in values for v in pair]
    found += [swap(v, plan.first) for v in found]
    yield


def place(plan, refs, codes, row, store):
    part = row // plan.rows
    shard = ((row % plan.rows) // plan.shard) ^ codes[part]
    half = plan.shards // 2
    at = pl.ds(pl.multiple_of((shard & (half - 1)) * plan.shard, plan.shard), plan.shard)
    low, high = refs[2 * part][at, :], refs[2 * part + 1][at, :]
    store(jnp.where(shard >= half, high.astype(f32), low.astype(f32)))


def dense_place_kernel(
    shard, each, table_ref, group_ref, all_ref, down_ref, up_ref, vec_ref, pool_ref, hold_ref, word_ref, sems, word_sem
):
    step, steps = pl.program_id(0), pl.num_programs(0)
    width = down_ref.shape[1]
    parts = width // shard
    devices = word_ref.shape[0]

    @pl.when(step == 0)
    def _():
        def fetch(block, carry):
            for i in range(parts):
                at = pl.multiple_of(table_ref[block * parts + i], SHARD_STEP)
                pltpu.make_async_copy(
                    all_ref.at[pl.ds(at, shard)],
                    hold_ref.at[block, pl.ds(i * shard, shard)],
                    sems.at[block],
                ).start()
            return carry

        lax.fori_loop(0, steps, fetch, 0)

        def words(device, carry):
            pltpu.make_async_copy(
                all_ref.at[pl.ds(pl.multiple_of(device * each + each - 2 * SUM_ROWS, SHARD_STEP), 2 * SUM_ROWS)],
                word_ref.at[device],
                word_sem,
            ).start()
            return carry

        lax.fori_loop(0, devices, words, 0)

    pltpu.make_async_copy(all_ref.at[pl.ds(0, width)], hold_ref.at[step], sems.at[step]).wait()

    @pl.when(step < steps // 2)
    def _():
        down_ref[...] = hold_ref[step].astype(f32)

    @pl.when(step >= steps // 2)
    def _():
        up_ref[...] = hold_ref[step].astype(f32)

    @pl.when(step == steps - 1)
    def _():
        pltpu.make_async_copy(word_ref, word_ref, word_sem).wait()

        def both(device):
            return word_ref[device, :SUM_ROWS].astype(f32) + word_ref[device, SUM_ROWS:].astype(f32)

        vec_ref[...] = lax.fori_loop(
            0, devices, lambda i, total: total + both(i), jnp.zeros(vec_ref.shape, f32)
        )
        for i in range(pool_ref.shape[0]):
            pool_ref[i] = both(group_ref[0] + i)[POOL_ROW:]


def dense_place(plan, gathered, each, width, wide, devices, seq_count, group):
    table = jnp.array(plan.table(2 * wide, width, each), jnp.int32)
    return pl.pallas_call(
        functools.partial(dense_place_kernel, plan.shard, each),
        grid_spec=pltpu.PrefetchScalarGridSpec(
            num_scalar_prefetch=2,
            grid=(2 * wide,),
            in_specs=[pl.BlockSpec(memory_space=pl.ANY)],
            out_specs=[
                pl.BlockSpec((width, width), lambda i, *_: (jnp.minimum(i, wide - 1), 0)),
                pl.BlockSpec((width, width), lambda i, *_: (0, jnp.maximum(i - wide, 0))),
                pl.BlockSpec((SUM_ROWS, width), lambda i, *_: (0, 0)),
                pl.BlockSpec((seq_count, SUM_ROWS - POOL_ROW, width), lambda i, *_: (0, 0, 0)),
            ],
            scratch_shapes=[
                pltpu.VMEM((2 * wide, width, width), bf16),
                pltpu.VMEM((devices, 2 * SUM_ROWS, width), bf16),
                pltpu.SemaphoreType.DMA((2 * wide,)),
                pltpu.SemaphoreType.DMA(()),
            ],
        ),
        out_shape=[
            jax.ShapeDtypeStruct((wide * width, width), f32),
            jax.ShapeDtypeStruct((width, wide * width), f32),
            jax.ShapeDtypeStruct((SUM_ROWS, width), f32),
            jax.ShapeDtypeStruct((seq_count, SUM_ROWS - POOL_ROW, width), f32),
        ],
        compiler_params=PARAMS,
        cost_estimate=cost(0, 12 * wide * width * width),
    )(table, group, gathered)


def attend_place_kernel(plan, first_code, at, flip, info_ref, *refs):
    sources, (hold_ref, sems) = refs[: 2 * PARTS], refs[-2:]
    outs = refs[-6:-2]
    codes = [info_ref[first_code + i] for i in range(PARTS)]
    own = info_ref[at] ^ flip
    width = hold_ref.shape[2]

    def move(block, act):
        for side in range(2):

            @pl.when(own == side)
            def _():
                act(pltpu.make_async_copy(hold_ref.at[block], outs[2 * side + block], sems.at[block]))

    for block in range(2):
        for row in range(0, width, plan.shard):

            def store(value, row=row):
                hold_ref[block, row : row + plan.shard, :] = value

            place(plan, sources, codes, block * width + row, store)
        move(block, lambda copy: copy.start())
    for block in range(2):
        move(block, lambda copy: copy.wait())


def attend_place(plan, first_code, at, flip, info, sources, width, before):
    kept = list(before)
    return pl.pallas_call(
        functools.partial(attend_place_kernel, plan, first_code, at, flip),
        grid_spec=pltpu.PrefetchScalarGridSpec(
            num_scalar_prefetch=1,
            grid=(1,),
            in_specs=[fixed(x.shape) for x in sources]
            + [pl.BlockSpec(memory_space=pl.ANY)] * len(kept),
            out_specs=[pl.BlockSpec(memory_space=pl.ANY)] * 4,
            scratch_shapes=[pltpu.VMEM((2, width, width), f32), pltpu.SemaphoreType.DMA((2,))],
        ),
        out_shape=[jax.ShapeDtypeStruct((width, width), f32)] * 4,
        input_output_aliases={1 + len(sources) + i: i for i in range(len(kept))},
        compiler_params=SMALL,
        cost_estimate=cost(0, 12 * width * width),
    )(info, *sources, *kept)


def shards(
    tokens,
    lengths,
    w_query,
    b_query,
    w_key,
    w_value,
    b_value,
    w_out,
    b_out,
    gain_one,
    shift_one,
    w_up,
    b_up,
    w_down,
    b_down,
    gain_two,
    shift_two,
    out_grad,
    pooled_grad,
):
    seq_count = lax.axis_size("seq")
    held, piece, width = tokens.shape
    full = piece * seq_count
    count = held // seq_count
    mine = lax.axis_index("seq")
    wide = w_up.shape[1] // width
    total = count * full

    def flat(value):
        return value.reshape(total, width)

    def split(value):
        return value.reshape(count, full, width)

    dense_plan = Plan(wide * width)
    outer_plan = Plan(2 * width)
    first = axis_bits("seq")[0]
    scalars = [mine, upper(first)] + dense_plan.codes() + outer_plan.codes()
    own_at, dense_at, outer_at = held + 1, held + 2, held + 2 + PARTS
    info = jnp.concatenate([lengths, jnp.stack([v.astype(jnp.int32) for v in scalars])])
    vecs = jnp.concatenate(
        [b_query, b_value, b_out, gain_one, shift_one, b_down, gain_two, shift_two, b_up]
    )
    vecs = vecs.astype(f32).reshape(-1, width)

    weights = [w_query, w_key, w_value, vecs]
    done = None
    source = tokens
    parts = []
    for passage in range(count):
        if parts:
            source = lax.optimization_barrier((tokens, parts))[0]
        parts = [
            exchange(
                lax.dynamic_slice_in_dim(source, (mine ^ mask) * count + passage, 1, 0), "seq", mask
            )
            for mask in range(1, seq_count)
        ]
        done = attend(passage, count, info, tokens, parts, weights, done)
    stacked, q, k, v, stat = done
    cot = to_passages(lax.optimization_barrier((out_grad, parts))[0])
    stacked = stacked.reshape(2, total, width)
    result, first_low, act, second, inner, branch_in, mixed_grad, sums = row_work(
        held, info, stacked, flat(cot), pooled_grad, w_out, w_up, w_down, vecs, count
    )
    chain = Chain()
    pieces = chain.mark(position_pieces(split(result)))
    out_pieces = traded(pieces)
    send = dense_outer(own_at, 1, info, *chain.tie((act, second, first_low, inner)))
    chain.mark(send)
    got = swap(send, first)
    keep = chain.mark(dense_outer(own_at, 0, info, *chain.tie((act, second, first_low, inner))))
    dense, shard, outer = [], [], []
    dense_steps = scatter_steps(dense_plan, chain, keep, got, dense)
    next(dense_steps)
    chain.mark((chain.token, out_pieces))
    block_out = to_positions(out_pieces)
    grads, words = attend_back(
        held,
        info,
        q,
        k,
        v,
        chain.tie(split(mixed_grad)),
        stacked.reshape(2, count, full, width),
        split(branch_in),
        stat,
        sums,
    )
    chain.mark(words)
    grads = grads.reshape(4, total, width)
    next(dense_steps)
    send = attend_outer(own_at, 1, info, stacked, chain.tie(grads))
    chain.mark(send)
    got = swap(send, first)
    keep = attend_outer(own_at, 0, info, stacked, chain.tie(grads))
    chain.mark(keep)
    next(dense_steps)
    outer_steps = scatter_steps(outer_plan, chain, keep, got, shard)
    next(outer_steps)
    input_low = input_grad(branch_in, chain.tie(grads), w_query, w_key, w_value)
    chain.mark(input_low)
    next(dense_steps)
    next(outer_steps)
    for _ in dense_steps:
        pass
    gathered = jnp.concatenate([dense[0], words], axis=0)
    each = gathered.shape[0]
    gathered = chain.mark(gathered)
    gathered = lax.all_gather(gathered, ("dp", "seq"), axis=0, tiled=True)
    next(outer_steps)
    next(outer_steps)
    pieces = chain.mark(position_pieces(split(chain.tie(input_low))))
    in_pieces = traded(pieces)
    for _ in outer_steps:
        pass
    outer_steps = gather_steps(outer_plan, chain, shard[0], outer)
    next(outer_steps)
    next(outer_steps)
    next(outer_steps)
    chain.mark((chain.token, in_pieces))
    next(outer_steps)
    tokens_grad = to_positions(in_pieces)
    chain.mark((chain.token, tokens_grad, block_out))
    for _ in outer_steps:
        pass
    group = (lax.axis_index("dp") * seq_count).astype(jnp.int32)[None]

    def place_outer(flip, before):
        pick = outer[2 * PARTS :] if flip else outer[: 2 * PARTS]
        return chain.mark(
            attend_place(outer_plan, outer_at, own_at, flip, info, chain.tie(pick), width, before)
        )

    placed = place_outer(0, [])
    outer = place_outer(1, placed)
    down_sum, up_sum, vectors, pooled = dense_place(
        dense_plan, chain.tie(gathered), each, width, wide, gathered.shape[0] // each, seq_count, group
    )
    pooled = pooled[:, :count].reshape(held, width)
    return (
        block_out,
        pooled,
        tokens_grad,
        outer[0],
        vectors[0],
        outer[1],
        outer[2],
        vectors[1],
        outer[3],
        vectors[2],
        vectors[3],
        vectors[4],
        up_sum,
        vectors[8 : 8 + wide].reshape(-1),
        down_sum,
        vectors[5],
        vectors[6],
        vectors[7],
    )


def solution(mesh):
    in_specs = (
        (P("dp", "seq", None), P("dp"))
        + (P(),) * 15
        + (P("dp", "seq", None), P("dp", None))
    )
    out_specs = (P("dp", "seq", None), P("dp", None), P("dp", "seq", None)) + (P(),) * 15
    return jax.shard_map(shards, mesh=mesh, in_specs=in_specs, out_specs=out_specs, check_vma=False)
```

```python
import functools

import jax
import jax.numpy as jnp
from jax import lax
from jax.experimental import pallas as pl
from jax.experimental.pallas import tpu as pltpu
from jax.sharding import PartitionSpec as P

HEADS = 12
HEAD_DIM = 64
PAIR = 2 * HEAD_DIM
PAIRS = HEADS // 2
SCALE = HEAD_DIM ** (-0.5)
ROWS = 256
BACK_ROWS = 256
STRIP = 32
TOGETHER = 1
BACK_TOGETHER = 1
STAT_ROWS = 16
CHUNK = 256
KEY_STEP = 128
VMEM_BYTES = 62 * 1024 * 1024
SMALL_BYTES = 40 * 1024 * 1024
SUM_ROWS = 16
POOL_ROW = 12

eps = 1e-06
root_half = 0.7071067811865476
inv_root_two_pi = 0.3989422804014327

f32 = jnp.float32
bf16 = jnp.bfloat16

NN = (((1,), (0,)), ((), ()))
NT = (((1,), (1,)), ((), ()))
TN = (((0,), (0,)), ((), ()))


def mul(left, right, dims=NN):
    return lax.dot_general(left, right, dims, preferred_element_type=f32)


def fixed(shape):
    return pl.BlockSpec(shape, lambda *_: (0,) * len(shape), pipeline_mode=pl.Buffered(1))


PARAMS = pltpu.CompilerParams(dimension_semantics=("arbitrary",), vmem_limit_bytes=VMEM_BYTES)
SMALL = pltpu.CompilerParams(dimension_semantics=("arbitrary",), vmem_limit_bytes=SMALL_BYTES)


def cost(flops, moved, exps=0):
    return pl.CostEstimate(flops=int(flops), bytes_accessed=int(moved), transcendentals=int(exps))


def over_extents(length, full, body):
    for extent in range(KEY_STEP, full + 1, KEY_STEP):
        pl.when((length > extent - KEY_STEP) & (length <= extent))(functools.partial(body, extent))


def by_eight(value):
    return value.reshape(value.shape[0] // 8, 8, value.shape[1])


def fill_dead(dead_ref, extent, length):
    key_at = lax.broadcasted_iota(jnp.int32, dead_ref.shape, 0) + (extent - KEY_STEP)
    dead_ref[...] = jnp.where(key_at < length, 0.0, -1e30)


def live_strip(scores, dead_ref, extent, row):
    strip = scores[row : row + STRIP]
    last = row - (extent - KEY_STEP)
    return strip + dead_ref[last : last + STRIP] if last >= 0 else strip


def attend_kernel(pieces, passage, count, held, info_ref, *refs):
    part_refs, refs = refs[:pieces], refs[pieces:]
    wq_ref, wk_ref, wv_ref, vec_ref = refs[:4]
    xm_ref, q_ref, k_ref, v_ref, stat_ref, prob_ref, dead_ref = refs[-7:]
    x_ref, mix_ref = xm_ref.at[0], xm_ref.at[1]
    mine = info_ref[held]
    length = info_ref[mine * count + passage]
    size = part_refs[0].shape[1]
    for mask, part_ref in enumerate(part_refs):
        x_ref[0, pl.ds(pl.multiple_of((mine ^ mask) * size, size), size)] = part_ref[0]

    def project(index, carry):
        at = pl.ds(pl.multiple_of(index * CHUNK, CHUNK), CHUNK)
        x = x_ref[0]
        q_ref[0, :, at] = (mul(x, wq_ref[:, at]) + vec_ref[0:1, at]).astype(bf16)
        k_ref[0, :, at] = mul(x, wk_ref[:, at]).astype(bf16)
        v_ref[0, :, at] = (mul(x, wv_ref[:, at]) + vec_ref[1:2, at]).astype(bf16)
        return carry

    lax.fori_loop(0, wq_ref.shape[1] // CHUNK, project, 0)
    stat_ref[0] = jnp.zeros(stat_ref.shape[1:], f32)
    full = size * pieces
    lane = lax.broadcasted_iota(jnp.int32, (1, PAIR), 1)

    def run(extent):
        fill_dead(dead_ref, extent, length)

        def head(at, number, half, slot):
            q, k = q_ref[0, :, at], k_ref[0, :extent, at]
            own = (lane >= half * HEAD_DIM) & (lane < (half + 1) * HEAD_DIM)
            scores = mul(jnp.where(own, k * SCALE, 0).astype(bf16), q, NT)
            top = jnp.full((8, full), -jnp.inf, f32)
            for row in range(0, extent, STRIP):
                top = jnp.maximum(top, by_eight(live_strip(scores, dead_ref, extent, row)).max(axis=0))
            top = jnp.max(top, axis=0, keepdims=True)
            total = jnp.zeros((8, full), f32)
            for row in range(0, extent, STRIP):
                expo = jnp.exp(live_strip(scores, dead_ref, extent, row) - top)
                total += by_eight(expo).sum(axis=0)
                prob_ref[slot, row : row + STRIP] = expo.astype(bf16)
            total = jnp.sum(total, axis=0, keepdims=True)
            stat_ref[0, pl.ds(number, 1), :] = top + jnp.log(total)
            return 1.0 / total

        def group(index, carry):
            for i in range(TOGETHER):
                pair = index * TOGETHER + i
                at = pl.ds(pl.multiple_of(pair * PAIR, PAIR), PAIR)
                values = v_ref[0, :extent, at].T
                mixed = []
                for half in range(2):
                    slot = 2 * i + half
                    scale = head(at, pair * 2 + half, half, slot)
                    own = values[half * HEAD_DIM : (half + 1) * HEAD_DIM]
                    mixed.append(mul(own, prob_ref[slot, :extent]) * scale)
                mix_ref[0, :, at] = jnp.concatenate(mixed, axis=0).T.astype(bf16)
            return carry

        lax.fori_loop(0, PAIRS // TOGETHER, group, 0)

    over_extents(length, full, run)


def attend(passage, count, info, tokens, parts, weights, before):
    held, piece, width = tokens.shape
    pieces = len(parts) + 1
    full = piece * pieces
    rows = pl.BlockSpec((1, full, width), lambda i, s: (passage, 0, 0))
    act = jax.ShapeDtypeStruct((count, full, width), bf16)
    got = pl.BlockSpec((1, piece, width), lambda i, s: (0, 0, 0))
    kept = [] if before is None else list(before)
    first_kept = 1 + pieces + len(weights)
    return pl.pallas_call(
        functools.partial(attend_kernel, pieces, passage, count, held),
        grid_spec=pltpu.PrefetchScalarGridSpec(
            num_scalar_prefetch=1,
            grid=(1,),
            in_specs=[pl.BlockSpec((1, piece, width), lambda i, s: (s[held] * count + passage, 0, 0))]
            + [got] * len(parts)
            + [fixed(w.shape) for w in weights]
            + [pl.BlockSpec(memory_space=pl.ANY)] * len(kept),
            out_specs=[pl.BlockSpec((2, 1, full, width), lambda i, s: (0, passage, 0, 0))]
            + [rows] * 3
            + [pl.BlockSpec((1, STAT_ROWS, full), lambda i, s: (passage, 0, 0))],
            scratch_shapes=[
                pltpu.VMEM((2 * TOGETHER, full, full), bf16),
                pltpu.VMEM((KEY_STEP, full), f32),
            ],
        ),
        out_shape=[jax.ShapeDtypeStruct((2, count, full, width), bf16)]
        + [act] * 3
        + [jax.ShapeDtypeStruct((count, STAT_ROWS, full), f32)],
        input_output_aliases={first_kept + i: i for i in range(len(kept))},
        compiler_params=PARAMS,
        cost_estimate=cost(
            2 * full * (3 * width * width + 4 * 2 * full * width),
            12 * full * width + 6 * width * width,
        ),
    )(info, tokens, *parts, *weights, *kept)


def attend_back_kernel(
    held,
    info_ref,
    q_ref,
    k_ref,
    v_ref,
    mg_ref,
    mix_ref,
    branch_ref,
    stat_ref,
    sum_ref,
    grads_ref,
    word_ref,
    bias_ref,
    along_ref,
    prob_ref,
    score_ref,
    dead_ref,
):
    dq_ref, dk_ref, dv_ref = (grads_ref.at[i] for i in range(3))
    grads_ref[3] = branch_ref[...].astype(bf16)
    full, width = q_ref.shape[1:]
    length = info_ref[info_ref[held] * pl.num_programs(0) + pl.program_id(0)]
    lane = lax.broadcasted_iota(jnp.int32, (1, PAIR), 1)
    row = lax.broadcasted_iota(jnp.int32, (8, 1), 0)

    @pl.when(pl.program_id(0) == 0)
    def _():
        bias_ref[...] = sum_ref[...]

    feature = lax.broadcasted_iota(jnp.int32, (STAT_ROWS, width), 1)
    number = lax.broadcasted_iota(jnp.int32, (STAT_ROWS, width), 0)
    ours = jnp.where(
        (feature >= number * HEAD_DIM) & (feature < (number + 1) * HEAD_DIM), 1.0, 0.0
    ).astype(bf16)
    product = mg_ref[0].astype(f32) * mix_ref[0, 0].astype(f32)
    high = product.astype(bf16)
    low = (product - high.astype(f32)).astype(bf16)
    along_ref[...] = mul(ours, high, NT) + mul(ours, low, NT)

    def run(extent):
        fill_dead(dead_ref, extent, length)
        if extent < full:
            dk_ref[0, extent:] = jnp.zeros((full - extent, width), bf16)
            dv_ref[0, extent:] = jnp.zeros((full - extent, width), bf16)

        def group(index, carry):
            for i in range(BACK_TOGETHER):
                pair = index * BACK_TOGETHER + i
                at = pl.ds(pl.multiple_of(pair * PAIR, PAIR), PAIR)
                q, mg = q_ref[0, :, at], mg_ref[0, :, at]
                k, v = k_ref[0, :extent, at], v_ref[0, :extent, at]
                keys = k.T
                dq, dk, dv = [], [], []
                for half in range(2):
                    slot = 2 * i + half
                    own = (lane >= half * HEAD_DIM) & (lane < (half + 1) * HEAD_DIM)
                    scores = mul(jnp.where(own, k * SCALE, 0).astype(bf16), q, NT)
                    prob_grad = mul(jnp.where(own, v, 0).astype(bf16), mg, NT)
                    log_row = stat_ref[0, pl.ds(pair * 2 + half, 1), :]
                    along = along_ref[pl.ds(pair * 2 + half, 1), :]
                    for at_row in range(0, extent, STRIP):
                        rows = slice(at_row, at_row + STRIP)
                        probs = jnp.exp(live_strip(scores, dead_ref, extent, at_row) - log_row)
                        prob_ref[slot, rows] = probs.astype(bf16)
                        score_ref[slot, rows] = (probs * (prob_grad[rows] - along)).astype(bf16)
                    score_grad = score_ref[slot, :extent]
                    dv.append(mul(prob_ref[slot, :extent], mg))
                    dk.append(mul(score_grad, q))
                    dq.append(mul(keys[half * HEAD_DIM : (half + 1) * HEAD_DIM], score_grad))
                first = lane < HEAD_DIM
                dq_pair = jnp.concatenate(dq, axis=0).T * SCALE
                dk_pair = jnp.where(first, dk[0], dk[1]) * SCALE
                dv_pair = jnp.where(first, dv[0], dv[1])
                dq_ref[0, :, at] = dq_pair.astype(bf16)
                dk_ref[0, :extent, at] = dk_pair.astype(bf16)
                dv_ref[0, :extent, at] = dv_pair.astype(bf16)
                sums = jnp.where(
                    row == 0,
                    jnp.sum(dq_pair, axis=0, keepdims=True),
                    jnp.where(row == 1, jnp.sum(dv_pair, axis=0, keepdims=True), 0.0),
                )
                bias_ref[0:8, at] += sums
            return carry

        lax.fori_loop(0, PAIRS // BACK_TOGETHER, group, 0)

    over_extents(length, full, run)

    @pl.when(pl.program_id(0) == pl.num_programs(0) - 1)
    def _():
        high = bias_ref[...].astype(bf16)
        word_ref[:SUM_ROWS] = high
        word_ref[SUM_ROWS:] = (bias_ref[...] - high.astype(f32)).astype(bf16)


def attend_back(held, info, q, k, v, mixed_grad, stacked, branch_in, stat, sums):
    count, full, width = q.shape
    rows = pl.BlockSpec((1, full, width), lambda i, *_: (i, 0, 0))
    return pl.pallas_call(
        functools.partial(attend_back_kernel, held),
        grid_spec=pltpu.PrefetchScalarGridSpec(
            num_scalar_prefetch=1,
            grid=(count,),
            in_specs=[rows] * 4
            + [
                pl.BlockSpec((1, 1, full, width), lambda i, *_: (1, i, 0, 0)),
                rows,
                pl.BlockSpec((1, STAT_ROWS, full), lambda i, *_: (i, 0, 0)),
                fixed(sums.shape),
            ],
            out_specs=[
                pl.BlockSpec((4, 1, full, width), lambda i, *_: (0, i, 0, 0)),
                pl.BlockSpec((2 * SUM_ROWS, width), lambda i, *_: (0, 0)),
            ],
            scratch_shapes=[
                pltpu.VMEM(sums.shape, f32),
                pltpu.VMEM((STAT_ROWS, full), f32),
                pltpu.VMEM((2 * BACK_TOGETHER, full, full), bf16),
                pltpu.VMEM((2 * BACK_TOGETHER, full, full), bf16),
                pltpu.VMEM((KEY_STEP, full), f32),
            ],
        ),
        out_shape=[
            jax.ShapeDtypeStruct((4, count, full, width), bf16),
            jax.ShapeDtypeStruct((2 * SUM_ROWS, width), bf16),
        ],
        compiler_params=PARAMS,
        cost_estimate=cost(
            2 * count * full * 10 * 2 * full * width, 16 * count * full * width
        ),
    )(info, q, k, v, mixed_grad, stacked, branch_in, stat, sums)


def norm_parts(hidden):
    centred = hidden - jnp.mean(hidden, axis=1, keepdims=True)
    inv_scale = lax.rsqrt(jnp.mean(centred * centred, axis=1, keepdims=True) + eps)
    return centred * inv_scale, inv_scale


def norm_back(scaled, normed, inv_scale):
    mean = jnp.mean(scaled, axis=1, keepdims=True)
    along = jnp.mean(scaled * normed, axis=1, keepdims=True)
    return (scaled - mean - normed * along) * inv_scale


def gelu_parts(u):
    expo = jnp.exp(u * u * -0.5)
    base = 1.0 + jnp.abs(u) * (0.3275911 * root_half)
    t = pl.reciprocal(base, approx=True)
    t = t * (2.0 - base * t)
    poly = t * (
        0.5 * 0.254829592
        + t
        * (
            0.5 * -0.284496736
            + t * (0.5 * 1.421413741 + t * (0.5 * -1.453152027 + t * (0.5 * 1.061405429)))
        )
    )
    tail = poly * expo
    return jnp.where(u >= 0, 1.0 - tail, tail), expo


def rows_kernel(
    blocks,
    count,
    held,
    info_ref,
    x_ref,
    mix_ref,
    cot_ref,
    pool_ref,
    wo_ref,
    vec_ref,
    wu_all,
    wd_all,
    out_ref,
    low_ref,
    act_all,
    second_ref,
    inner_all,
    branch_ref,
    mg_ref,
    sum_ref,
    wu_ref,
    wd_ref,
    act_ref,
    inner_ref,
    slope_ref,
    first_ref,
    normed_ref,
    total_ref,
    scale_ref,
    sems,
):
    step, steps = pl.program_id(0), pl.num_programs(0)
    rows, width = cot_ref.shape
    hidden_width = wu_ref.shape[1]
    b_out, gain_one, shift_one, b_down, gain_two, shift_two = (
        vec_ref[i : i + 1] for i in range(2, 8)
    )
    passage = info_ref[held] * count + step // blocks
    length = info_ref[passage]
    inv_length = 1.0 / jnp.full((1, width), length, jnp.int32).astype(f32)
    pool = pool_ref[pl.ds(passage, 1), :] * inv_length
    first_row = (step % blocks) * rows
    load_up = pltpu.make_async_copy(wu_all, wu_ref, sems.at[0])
    load_down = pltpu.make_async_copy(wd_all, wd_ref, sems.at[1])

    def give(source_ref, all_ref, at):
        return pltpu.make_async_copy(
            source_ref, all_ref.at[pl.ds(pl.multiple_of(at * rows, rows), rows)], sems.at[2 if source_ref is act_ref else 3]
        )

    @pl.when(step == 0)
    def _():
        load_up.start()
        load_down.start()
        sum_ref[...] = jnp.zeros(sum_ref.shape, f32)

    def tally(at, value, columns=slice(None)):
        sum_ref[at : at + 1, columns] += jnp.sum(value, axis=0, keepdims=True)

    def strips(size):
        return [slice(i, i + size) for i in range(0, rows, size)]

    groups = width // CHUNK
    chunks = hidden_width // CHUNK
    part = [slice(i * CHUNK, (i + 1) * CHUNK) for i in range(chunks)]
    whole = [slice(i * width, (i + 1) * width) for i in range(hidden_width // width)]
    lanes = scale_ref.shape[1]

    branch = mul(mix_ref[0], wo_ref[...])
    for at in strips(STRIP):
        normed, scale = norm_parts(x_ref[0, at].astype(f32) + branch[at] + b_out)
        first = normed * gain_one + shift_one
        normed_ref[at] = normed
        scale_ref[at] = jnp.broadcast_to(scale, (STRIP, lanes))
        first_ref[at] = first + b_down
        low_ref[at] = first.astype(bf16)

    @pl.when(step == 0)
    def _():
        load_up.wait()
        load_down.wait()

    @pl.when(step > 0)
    def _():
        give(act_ref, act_all, step - 1).wait()

    def up(i):
        return mul(low_ref[...], wu_ref[:, part[i]])

    pre = up(0)
    for i in range(chunks):
        ahead = up(i + 1) if i + 1 < chunks else None
        bias = vec_ref[8 + i // groups : 9 + i // groups, part[i % groups]]
        for at in strips(2 * STRIP):
            u = pre[at] + bias
            phi, expo = gelu_parts(u)
            act_ref[at, part[i]] = (u * phi).astype(bf16)
            slope_ref[at, part[i]] = phi + u * expo * inv_root_two_pi
        if i % groups == 0 and i:
            done = whole[i // groups - 1]
            first_ref[...] += mul(act_ref[:, done], wd_ref[done, :])
        pre = ahead
    last = mul(act_ref[:, whole[-1]], wd_ref[whole[-1], :])
    give(act_ref, act_all, step).start()

    pooled, shift, gain, down = (jnp.zeros((8, width), f32) for _ in range(4))
    for at in strips(STRIP):
        normed, scale = norm_parts(first_ref[at] + last[at])
        result = normed * gain_two + shift_two
        out_ref[at] = result.astype(bf16)
        row_at = lax.broadcasted_iota(jnp.int32, (STRIP, 1), 0) + (first_row + at.start)
        live = jnp.where(row_at < length, 1.0, 0.0)
        pooled += by_eight(result * live).sum(axis=0)
        upstream = cot_ref[at].astype(f32) + live * pool
        gain += by_eight(upstream * normed).sum(axis=0)
        shift += by_eight(upstream).sum(axis=0)
        second_in = norm_back(upstream * gain_two, normed, scale)
        down += by_eight(second_in).sum(axis=0)
        total_ref[at] = second_in
        second_ref[at] = second_in.astype(bf16)
    tally(6, gain)
    tally(7, shift)
    tally(5, down)
    sum_ref[pl.ds(POOL_ROW + step // blocks, 1), :] += (
        jnp.sum(pooled, axis=0, keepdims=True) * inv_length
    )

    @pl.when(step > 0)
    def _():
        give(inner_ref, inner_all, step - 1).wait()

    def back(i):
        return mul(second_ref[...], wd_ref[part[i], :], NT)

    grad = back(0)
    for i in range(chunks):
        ahead = back(i + 1) if i + 1 < chunks else None
        bias = jnp.zeros((8, CHUNK), f32)
        for at in strips(2 * STRIP):
            inner = grad[at] * slope_ref[at, part[i]]
            bias += by_eight(inner).sum(axis=0)
            inner_ref[at, part[i]] = inner.astype(bf16)
        tally(8 + i // groups, bias, part[i % groups])
        if i % groups == 0 and i:
            done = whole[i // groups - 1]
            total_ref[...] += mul(inner_ref[:, done], wu_ref[:, done], NT)
        grad = ahead
    last = mul(inner_ref[:, whole[-1]], wu_ref[:, whole[-1]], NT)
    give(inner_ref, inner_all, step).start()

    gain, shift, out = (jnp.zeros((8, width), f32) for _ in range(3))
    for at in strips(STRIP):
        first_up = total_ref[at] + last[at]
        normed = normed_ref[at]
        gain += by_eight(first_up * normed).sum(axis=0)
        shift += by_eight(first_up).sum(axis=0)
        branch_in = norm_back(first_up * gain_one, normed, scale_ref[at, :1])
        out += by_eight(branch_in).sum(axis=0)
        branch_ref[at] = branch_in
    tally(3, gain)
    tally(4, shift)
    tally(2, out)
    mg_ref[...] = mul(branch_ref[...].astype(bf16), wo_ref[...], NT).astype(bf16)

    @pl.when(step == steps - 1)
    def _():
        give(act_ref, act_all, step).wait()
        give(inner_ref, inner_all, step).wait()


def row_work(held, info, stacked, cot, pool, w_out, w_up, w_down, vecs, count):
    total, width = cot.shape
    full = total // count
    assert POOL_ROW + count <= SUM_ROWS
    hidden = w_up.shape[1]
    blocks = full // ROWS
    narrow = pl.BlockSpec((ROWS, width), lambda i, *_: (i, 0))
    anywhere = pl.BlockSpec(memory_space=pl.ANY)
    thin = jax.ShapeDtypeStruct((total, width), bf16)
    thick = jax.ShapeDtypeStruct((total, hidden), bf16)
    return pl.pallas_call(
        functools.partial(rows_kernel, blocks, count, held),
        grid_spec=pltpu.PrefetchScalarGridSpec(
            num_scalar_prefetch=1,
            grid=(total // ROWS,),
            in_specs=[
                pl.BlockSpec((1, ROWS, width), lambda i, *_: (0, i, 0)),
                pl.BlockSpec((1, ROWS, width), lambda i, *_: (1, i, 0)),
                narrow,
                fixed(pool.shape),
                fixed((width, width)),
                fixed(vecs.shape),
                anywhere,
                anywhere,
            ],
            out_specs=[
                narrow,
                narrow,
                anywhere,
                narrow,
                anywhere,
                narrow,
                narrow,
                pl.BlockSpec((SUM_ROWS, width), lambda i, *_: (0, 0)),
            ],
            scratch_shapes=[
                pltpu.VMEM((width, hidden), bf16),
                pltpu.VMEM((hidden, width), bf16),
                pltpu.VMEM((ROWS, hidden), bf16),
                pltpu.VMEM((ROWS, hidden), bf16),
                pltpu.VMEM((ROWS, hidden), f32),
                pltpu.VMEM((ROWS, width), f32),
                pltpu.VMEM((ROWS, width), f32),
                pltpu.VMEM((ROWS, width), f32),
                pltpu.VMEM((ROWS, PAIR), f32),
                pltpu.SemaphoreType.DMA((4,)),
            ],
        ),
        out_shape=[
            thin,
            thin,
            thick,
            thin,
            thick,
            jax.ShapeDtypeStruct((total, width), f32),
            thin,
            jax.ShapeDtypeStruct((SUM_ROWS, width), f32),
        ],
        compiler_params=PARAMS,
        cost_estimate=cost(
            4 * total * width * (width + 2 * hidden),
            2 * total * (8 * width + 2 * hidden) + 2 * width * (width + 2 * hidden),
        ),
    )(info, stacked, stacked, cot, pool, w_out, vecs, w_up, w_down)


def dense_outer_kernel(side_ref, act_ref, second_ref, low_ref, inner_ref, out_ref):
    step = pl.program_id(0)
    half = pl.num_programs(0) // 2

    @pl.when(step < half)
    def _():
        out_ref[0] = mul(act_ref[...], second_ref[...], TN).astype(bf16)

    @pl.when(step >= half)
    def _():
        out_ref[0] = mul(low_ref[...], inner_ref[...], TN).astype(bf16)


def dense_outer(at, flip, info, act, second, low, inner):
    total, width = second.shape
    wide = act.shape[1] // width
    half = wide // 2
    return pl.pallas_call(
        dense_outer_kernel,
        grid_spec=pltpu.PrefetchScalarGridSpec(
            num_scalar_prefetch=1,
            grid=(wide,),
            in_specs=[
                pl.BlockSpec(
                    (total, width), lambda i, s: (0, (s[at] ^ flip) * half + jnp.minimum(i, half - 1))
                ),
                fixed((total, width)),
                fixed((total, width)),
                pl.BlockSpec(
                    (total, width), lambda i, s: (0, (s[at] ^ flip) * half + jnp.maximum(i - half, 0))
                ),
            ],
            out_specs=pl.BlockSpec((1, width, width), lambda i, s: (i, 0, 0)),
        ),
        out_shape=jax.ShapeDtypeStruct((wide, width, width), bf16),
        compiler_params=SMALL,
        cost_estimate=cost(
            2 * total * width * width * wide, 2 * (wide + 2) * total * width + 2 * wide * width * width
        ),
    )(info, act, second, low, inner).reshape(wide * width, width)


def attend_outer_kernel(side_ref, left_ref, right_ref, out_ref):
    out_ref[0] = mul(left_ref[0], right_ref[0], TN).astype(bf16)


def attend_outer(at, flip, info, stacked, grads):
    total, width = stacked.shape[1:]
    return pl.pallas_call(
        attend_outer_kernel,
        grid_spec=pltpu.PrefetchScalarGridSpec(
            num_scalar_prefetch=1,
            grid=(2,),
            in_specs=[
                pl.BlockSpec((1, total, width), lambda i, s: (((s[at] ^ flip) * 2 + i) // 3, 0, 0)),
                pl.BlockSpec((1, total, width), lambda i, s: ((s[at] ^ flip) * 2 + i, 0, 0)),
            ],
            out_specs=pl.BlockSpec((1, width, width), lambda i, s: (i, 0, 0)),
        ),
        out_shape=jax.ShapeDtypeStruct((2, width, width), bf16),
        compiler_params=SMALL,
        cost_estimate=cost(4 * total * width * width, 8 * total * width + 4 * width * width),
    )(info, stacked, grads).reshape(2 * width, width)


def input_kernel(branch_ref, dq_ref, dk_ref, dv_ref, wq_ref, wk_ref, wv_ref, out_ref):
    total = branch_ref[...] + mul(dq_ref[0], wq_ref[...], NT)
    total += mul(dk_ref[0], wk_ref[...], NT)
    total += mul(dv_ref[0], wv_ref[...], NT)
    out_ref[...] = total.astype(bf16)


def input_grad(branch_in, grads, w_query, w_key, w_value):
    total, width = branch_in.shape
    rows = pl.BlockSpec((BACK_ROWS, width), lambda i: (i, 0))
    return pl.pallas_call(
        input_kernel,
        grid=(total // BACK_ROWS,),
        in_specs=[rows]
        + [pl.BlockSpec((1, BACK_ROWS, width), lambda i, at=at: (at, i, 0)) for at in range(3)]
        + [fixed((width, width))] * 3,
        out_specs=rows,
        out_shape=jax.ShapeDtypeStruct((total, width), bf16),
        compiler_params=SMALL,
        cost_estimate=cost(6 * total * width * width, 12 * total * width + 6 * width * width),
    )(branch_in, grads, grads, grads, w_query, w_key, w_value)


def exchange(value, axis, mask):
    count = lax.axis_size(axis)
    return lax.ppermute(value, axis, [(i, i ^ mask) for i in range(count)])


def to_passages(value):
    count = lax.axis_size("seq")
    mine = lax.axis_index("seq")
    held, piece, width = value.shape
    own = held // count
    whole = jnp.zeros((own, piece * count, width), value.dtype)
    for mask in range(count):
        peer = mine ^ mask
        part = lax.dynamic_slice_in_dim(value, peer * own, own, 0)
        if mask:
            part = exchange(part, "seq", mask)
        whole = lax.dynamic_update_slice_in_dim(whole, part, peer * piece, 1)
    return whole


def position_pieces(value):
    count = lax.axis_size("seq")
    piece = value.shape[1] // count
    mine = lax.axis_index("seq")
    return [
        lax.dynamic_slice_in_dim(value, (mine ^ mask) * piece, piece, 1) for mask in range(count)
    ]


def traded(pieces):
    return [exchange(part, "seq", mask) if mask else part for mask, part in enumerate(pieces)]


def to_positions(pieces):
    mine = lax.axis_index("seq")
    own, piece, width = pieces[0].shape
    result = jnp.zeros((own * len(pieces), piece, width), pieces[0].dtype)
    for mask, part in enumerate(pieces):
        result = lax.dynamic_update_slice_in_dim(result, part, (mine ^ mask) * own, 0)
    return result


def axis_bits(axis):
    return [(axis, 1 << i) for i in range(lax.axis_size(axis).bit_length() - 1)]


def upper(dim):
    axis, mask = dim
    return (lax.axis_index(axis) & mask) // mask


def swap(value, dim):
    return exchange(value, dim[0], dim[1])


def total_of(parts):
    total = parts[0].astype(f32)
    for part in parts[1:]:
        total += part.astype(f32)
    return total.astype(bf16)


PARTS = 3
SHARD_STEP = 16


class Plan:
    def __init__(self, rows):
        dims = axis_bits("seq") + axis_bits("dp")
        self.first = dims[0]
        rest = dims[1:]
        self.rows = rows // PARTS
        halved = 0
        while halved < len(rest) and (self.rows >> (halved + 1)) % SHARD_STEP == 0:
            halved += 1
        self.last = rest[halved - 1]
        self.plain = rest[halved:]
        split = rest[: halved - 1]
        self.orders = [split[i % len(split) :] + split[: i % len(split)] for i in range(PARTS)]
        self.shards = 1 << halved
        self.shard = self.rows >> halved

    def table(self, blocks, width, each):
        places = {}
        devices = 1
        weight = {}
        for axis in ("seq", "dp"):
            for _, mask in axis_bits(axis):
                weight[(axis, mask)] = devices
                devices *= 2
        for side in range(2):
            for part, order in enumerate(self.orders):
                dims = [self.last] + order[::-1]
                for code in range(self.shards):
                    device = side * weight[self.first]
                    device += sum(weight[d] for i, d in enumerate(dims) if (code >> i) & 1)
                    row = part * self.rows + code * self.shard
                    places[side, row] = device * each + part * self.shard
        half = blocks // 4
        found = []
        for block in range(blocks):
            side = block % (2 * half) // half
            local = block // (2 * half) * half + block % half
            for row in range(0, width, self.shard):
                found.append(places[side, local * width + row])
        return found

    def codes(self):
        found = []
        for order in self.orders:
            code = upper(self.last)
            for at, dim in enumerate(reversed(order)):
                code += upper(dim) << (at + 1)
            found.append(code)
        return [code.astype(jnp.int32) for code in found]


class Chain:
    def __init__(self):
        self.token = None

    def tie(self, values):
        if self.token is None:
            return values
        return lax.optimization_barrier((values, self.token))[0]

    def mark(self, values):
        self.token = values
        return values


def scatter_steps(plan, chain, keep, got, found):
    pairs = [[keep, got]] * PARTS
    bases = [i * plan.rows for i in range(PARTS)]
    size = plan.rows
    for step in range(len(plan.orders[0])):
        pairs = chain.tie(pairs)
        size //= 2
        dims = [order[step] for order in plan.orders]

        def halves(pair, base, at):
            return total_of([lax.dynamic_slice_in_dim(p, base + at * size, size, 0) for p in pair])

        sends = [halves(p, base, 1 - upper(d)) for p, base, d in zip(pairs, bases, dims)]
        chain.mark(sends)
        mine = [halves(p, base, upper(d)) for p, base, d in zip(pairs, bases, dims)]
        pairs = [[m, swap(s, d)] for m, s, d in zip(mine, sends, dims)]
        bases = [0] * PARTS
        yield
    size = plan.shard
    bit = upper(plan.last)
    pairs = chain.tie(pairs)

    def side(at):
        return jnp.concatenate(
            [total_of([lax.dynamic_slice_in_dim(p, at * size, size, 0) for p in pair]) for pair in pairs],
            axis=0,
        )

    send = chain.mark(side(1 - bit))
    shard = side(bit)
    got = swap(send, plan.last)
    yield
    shard, got = chain.tie((shard, got))
    shard = total_of([shard, got])
    for dim in plan.plain:
        shard = total_of([shard, swap(shard, dim)])
    found.append(chain.mark(shard))
    yield


def gather_steps(plan, chain, shard, found):
    size = plan.shard
    got = swap(shard, plan.last)
    yield
    values = [(shard[i * size : (i + 1) * size], got[i * size : (i + 1) * size]) for i in range(PARTS)]
    for step in reversed(range(len(plan.orders[0]))):
        values = chain.tie(values)
        values = [jnp.concatenate(pair, axis=0) for pair in values]
        chain.mark(values)
        values = [(v, swap(v, order[step])) for v, order in zip(values, plan.orders)]
        yield
    values = chain.tie(values)
    chain.mark(values)
    found += [v for pair in values for v in pair]
    found += [swap(v, plan.first) for v in found]
    yield


def place(plan, refs, codes, row, store):
    part = row // plan.rows
    shard = ((row % plan.rows) // plan.shard) ^ codes[part]
    half = plan.shards // 2
    at = pl.ds(pl.multiple_of((shard & (half - 1)) * plan.shard, plan.shard), plan.shard)
    low, high = refs[2 * part][at, :], refs[2 * part + 1][at, :]
    store(jnp.where(shard >= half, high.astype(f32), low.astype(f32)))


def dense_place_kernel(
    shard, each, table_ref, group_ref, all_ref, down_ref, up_ref, vec_ref, pool_ref, hold_ref, word_ref, sems, word_sem
):
    step, steps = pl.program_id(0), pl.num_programs(0)
    width = down_ref.shape[1]
    parts = width // shard
    devices = word_ref.shape[0]

    @pl.when(step == 0)
    def _():
        def fetch(block, carry):
            for i in range(parts):
                at = pl.multiple_of(table_ref[block * parts + i], SHARD_STEP)
                pltpu.make_async_copy(
                    all_ref.at[pl.ds(at, shard)],
                    hold_ref.at[block, pl.ds(i * shard, shard)],
                    sems.at[block],
                ).start()
            return carry

        lax.fori_loop(0, steps, fetch, 0)

        def words(device, carry):
            pltpu.make_async_copy(
                all_ref.at[pl.ds(pl.multiple_of(device * each + each - 2 * SUM_ROWS, SHARD_STEP), 2 * SUM_ROWS)],
                word_ref.at[device],
                word_sem,
            ).start()
            return carry

        lax.fori_loop(0, devices, words, 0)

    pltpu.make_async_copy(all_ref.at[pl.ds(0, width)], hold_ref.at[step], sems.at[step]).wait()

    @pl.when(step < steps // 2)
    def _():
        down_ref[...] = hold_ref[step].astype(f32)

    @pl.when(step >= steps // 2)
    def _():
        up_ref[...] = hold_ref[step].astype(f32)

    @pl.when(step == steps - 1)
    def _():
        pltpu.make_async_copy(word_ref, word_ref, word_sem).wait()

        def both(device):
            return word_ref[device, :SUM_ROWS].astype(f32) + word_ref[device, SUM_ROWS:].astype(f32)

        vec_ref[...] = lax.fori_loop(
            0, devices, lambda i, total: total + both(i), jnp.zeros(vec_ref.shape, f32)
        )
        for i in range(pool_ref.shape[0]):
            pool_ref[i] = both(group_ref[0] + i)[POOL_ROW:]


def dense_place(plan, gathered, each, width, wide, devices, seq_count, group):
    table = jnp.array(plan.table(2 * wide, width, each), jnp.int32)
    return pl.pallas_call(
        functools.partial(dense_place_kernel, plan.shard, each),
        grid_spec=pltpu.PrefetchScalarGridSpec(
            num_scalar_prefetch=2,
            grid=(2 * wide,),
            in_specs=[pl.BlockSpec(memory_space=pl.ANY)],
            out_specs=[
                pl.BlockSpec((width, width), lambda i, *_: (jnp.minimum(i, wide - 1), 0)),
                pl.BlockSpec((width, width), lambda i, *_: (0, jnp.maximum(i - wide, 0))),
                pl.BlockSpec((SUM_ROWS, width), lambda i, *_: (0, 0)),
                pl.BlockSpec((seq_count, SUM_ROWS - POOL_ROW, width), lambda i, *_: (0, 0, 0)),
            ],
            scratch_shapes=[
                pltpu.VMEM((2 * wide, width, width), bf16),
                pltpu.VMEM((devices, 2 * SUM_ROWS, width), bf16),
                pltpu.SemaphoreType.DMA((2 * wide,)),
                pltpu.SemaphoreType.DMA(()),
            ],
        ),
        out_shape=[
            jax.ShapeDtypeStruct((wide * width, width), f32),
            jax.ShapeDtypeStruct((width, wide * width), f32),
            jax.ShapeDtypeStruct((SUM_ROWS, width), f32),
            jax.ShapeDtypeStruct((seq_count, SUM_ROWS - POOL_ROW, width), f32),
        ],
        compiler_params=PARAMS,
        cost_estimate=cost(0, 12 * wide * width * width),
    )(table, group, gathered)


def attend_place_kernel(plan, first_code, at, flip, info_ref, *refs):
    sources, (hold_ref, sems) = refs[: 2 * PARTS], refs[-2:]
    outs = refs[-6:-2]
    codes = [info_ref[first_code + i] for i in range(PARTS)]
    own = info_ref[at] ^ flip
    width = hold_ref.shape[2]

    def move(block, act):
        for side in range(2):

            @pl.when(own == side)
            def _():
                act(pltpu.make_async_copy(hold_ref.at[block], outs[2 * side + block], sems.at[block]))

    for block in range(2):
        for row in range(0, width, plan.shard):

            def store(value, row=row):
                hold_ref[block, row : row + plan.shard, :] = value

            place(plan, sources, codes, block * width + row, store)
        move(block, lambda copy: copy.start())
    for block in range(2):
        move(block, lambda copy: copy.wait())


def attend_place(plan, first_code, at, flip, info, sources, width, before):
    kept = list(before)
    return pl.pallas_call(
        functools.partial(attend_place_kernel, plan, first_code, at, flip),
        grid_spec=pltpu.PrefetchScalarGridSpec(
            num_scalar_prefetch=1,
            grid=(1,),
            in_specs=[fixed(x.shape) for x in sources]
            + [pl.BlockSpec(memory_space=pl.ANY)] * len(kept),
            out_specs=[pl.BlockSpec(memory_space=pl.ANY)] * 4,
            scratch_shapes=[pltpu.VMEM((2, width, width), f32), pltpu.SemaphoreType.DMA((2,))],
        ),
        out_shape=[jax.ShapeDtypeStruct((width, width), f32)] * 4,
        input_output_aliases={1 + len(sources) + i: i for i in range(len(kept))},
        compiler_params=SMALL,
        cost_estimate=cost(0, 12 * width * width),
    )(info, *sources, *kept)


def shards(
    tokens,
    lengths,
    w_query,
    b_query,
    w_key,
    w_value,
    b_value,
    w_out,
    b_out,
    gain_one,
    shift_one,
    w_up,
    b_up,
    w_down,
    b_down,
    gain_two,
    shift_two,
    out_grad,
    pooled_grad,
):
    seq_count = lax.axis_size("seq")
    held, piece, width = tokens.shape
    full = piece * seq_count
    count = held // seq_count
    mine = lax.axis_index("seq")
    wide = w_up.shape[1] // width
    total = count * full

    def flat(value):
        return value.reshape(total, width)

    def split(value):
        return value.reshape(count, full, width)

    dense_plan = Plan(wide * width)
    outer_plan = Plan(2 * width)
    first = axis_bits("seq")[0]
    scalars = [mine, upper(first)] + dense_plan.codes() + outer_plan.codes()
    own_at, dense_at, outer_at = held + 1, held + 2, held + 2 + PARTS
    info = jnp.concatenate([lengths, jnp.stack([v.astype(jnp.int32) for v in scalars])])
    vecs = jnp.concatenate(
        [b_query, b_value, b_out, gain_one, shift_one, b_down, gain_two, shift_two, b_up]
    )
    vecs = vecs.astype(f32).reshape(-1, width)

    weights = [w_query, w_key, w_value, vecs]
    done = None
    source = tokens
    parts = []
    for passage in range(count):
        if parts:
            source = lax.optimization_barrier((tokens, parts))[0]
        parts = [
            exchange(
                lax.dynamic_slice_in_dim(source, (mine ^ mask) * count + passage, 1, 0), "seq", mask
            )
            for mask in range(1, seq_count)
        ]
        done = attend(passage, count, info, tokens, parts, weights, done)
    stacked, q, k, v, stat = done
    cot = to_passages(lax.optimization_barrier((out_grad, parts))[0])
    stacked = stacked.reshape(2, total, width)
    result, first_low, act, second, inner, branch_in, mixed_grad, sums = row_work(
        held, info, stacked, flat(cot), pooled_grad, w_out, w_up, w_down, vecs, count
    )
    chain = Chain()
    pieces = chain.mark(position_pieces(split(result)))
    out_pieces = traded(pieces)
    send = dense_outer(own_at, 1, info, *chain.tie((act, second, first_low, inner)))
    chain.mark(send)
    got = swap(send, first)
    keep = chain.mark(dense_outer(own_at, 0, info, *chain.tie((act, second, first_low, inner))))
    dense, shard, outer = [], [], []
    dense_steps = scatter_steps(dense_plan, chain, keep, got, dense)
    next(dense_steps)
    chain.mark((chain.token, out_pieces))
    block_out = to_positions(out_pieces)
    grads, words = attend_back(
        held,
        info,
        q,
        k,
        v,
        chain.tie(split(mixed_grad)),
        stacked.reshape(2, count, full, width),
        split(branch_in),
        stat,
        sums,
    )
    chain.mark(words)
    grads = grads.reshape(4, total, width)
    next(dense_steps)
    send = attend_outer(own_at, 1, info, stacked, chain.tie(grads))
    chain.mark(send)
    got = swap(send, first)
    keep = attend_outer(own_at, 0, info, stacked, chain.tie(grads))
    chain.mark(keep)
    next(dense_steps)
    outer_steps = scatter_steps(outer_plan, chain, keep, got, shard)
    next(outer_steps)
    input_low = input_grad(branch_in, chain.tie(grads), w_query, w_key, w_value)
    chain.mark(input_low)
    next(dense_steps)
    next(outer_steps)
    for _ in dense_steps:
        pass
    gathered = jnp.concatenate([dense[0], words], axis=0)
    each = gathered.shape[0]
    gathered = chain.mark(gathered)
    gathered = lax.all_gather(gathered, ("dp", "seq"), axis=0, tiled=True)
    next(outer_steps)
    next(outer_steps)
    pieces = chain.mark(position_pieces(split(chain.tie(input_low))))
    in_pieces = traded(pieces)
    for _ in outer_steps:
        pass
    outer_steps = gather_steps(outer_plan, chain, shard[0], outer)
    next(outer_steps)
    next(outer_steps)
    next(outer_steps)
    chain.mark((chain.token, in_pieces))
    next(outer_steps)
    tokens_grad = to_positions(in_pieces)
    chain.mark((chain.token, tokens_grad, block_out))
    for _ in outer_steps:
        pass
    group = (lax.axis_index("dp") * seq_count).astype(jnp.int32)[None]

    def place_outer(flip, before):
        pick = outer[2 * PARTS :] if flip else outer[: 2 * PARTS]
        return chain.mark(
            attend_place(outer_plan, outer_at, own_at, flip, info, chain.tie(pick), width, before)
        )

    placed = place_outer(0, [])
    outer = place_outer(1, placed)
    down_sum, up_sum, vectors, pooled = dense_place(
        dense_plan, chain.tie(gathered), each, width, wide, gathered.shape[0] // each, seq_count, group
    )
    pooled = pooled[:, :count].reshape(held, width)
    return (
        block_out,
        pooled,
        tokens_grad,
        outer[0],
        vectors[0],
        outer[1],
        outer[2],
        vectors[1],
        outer[3],
        vectors[2],
        vectors[3],
        vectors[4],
        up_sum,
        vectors[8 : 8 + wide].reshape(-1),
        down_sum,
        vectors[5],
        vectors[6],
        vectors[7],
    )


def solution(mesh):
    in_specs = (
        (P("dp", "seq", None), P("dp"))
        + (P(),) * 15
        + (P("dp", "seq", None), P("dp", None))
    )
    out_specs = (P("dp", "seq", None), P("dp", None), P("dp", "seq", None)) + (P(),) * 15
    return jax.shard_map(shards, mesh=mesh, in_specs=in_specs, out_specs=out_specs, check_vma=False)
```

```python
import functools

import jax
import jax.numpy as jnp
from jax import lax
from jax.experimental import pallas as pl
from jax.experimental.pallas import tpu as pltpu
from jax.sharding import PartitionSpec as P

HEADS = 12
HEAD_DIM = 64
PAIR = 2 * HEAD_DIM
PAIRS = HEADS // 2
SCALE = HEAD_DIM ** (-0.5)
ROWS = 256
BACK_ROWS = 256
STRIP = 32
TOGETHER = 1
BACK_TOGETHER = 1
STAT_ROWS = 16
CHUNK = 256
KEY_STEP = 128
VMEM_BYTES = 62 * 1024 * 1024
SMALL_BYTES = 40 * 1024 * 1024
SUM_ROWS = 16
POOL_ROW = 12

eps = 1e-06
root_half = 0.7071067811865476
inv_root_two_pi = 0.3989422804014327

f32 = jnp.float32
bf16 = jnp.bfloat16

NN = (((1,), (0,)), ((), ()))
NT = (((1,), (1,)), ((), ()))
TN = (((0,), (0,)), ((), ()))


def mul(left, right, dims=NN):
    return lax.dot_general(left, right, dims, preferred_element_type=f32)


def fixed(shape):
    return pl.BlockSpec(shape, lambda *_: (0,) * len(shape), pipeline_mode=pl.Buffered(1))


PARAMS = pltpu.CompilerParams(dimension_semantics=("arbitrary",), vmem_limit_bytes=VMEM_BYTES)
SMALL = pltpu.CompilerParams(dimension_semantics=("arbitrary",), vmem_limit_bytes=SMALL_BYTES)


def cost(flops, moved, exps=0):
    return pl.CostEstimate(flops=int(flops), bytes_accessed=int(moved), transcendentals=int(exps))


def over_extents(length, full, body):
    for extent in range(KEY_STEP, full + 1, KEY_STEP):
        pl.when((length > extent - KEY_STEP) & (length <= extent))(functools.partial(body, extent))


def by_eight(value):
    return value.reshape(value.shape[0] // 8, 8, value.shape[1])


def fill_dead(dead_ref, extent, length):
    key_at = lax.broadcasted_iota(jnp.int32, dead_ref.shape, 0) + (extent - KEY_STEP)
    dead_ref[...] = jnp.where(key_at < length, 0.0, -1e30)


def live_strip(scores, dead_ref, extent, row):
    strip = scores[row : row + STRIP]
    last = row - (extent - KEY_STEP)
    return strip + dead_ref[last : last + STRIP] if last >= 0 else strip


def attend_kernel(pieces, passage, count, held, info_ref, *refs):
    part_refs, refs = refs[:pieces], refs[pieces:]
    wq_ref, wk_ref, wv_ref, vec_ref = refs[:4]
    xm_ref, q_ref, k_ref, v_ref, stat_ref, prob_ref, dead_ref = refs[-7:]
    x_ref, mix_ref = xm_ref.at[0], xm_ref.at[1]
    mine = info_ref[held]
    length = info_ref[mine * count + passage]
    size = part_refs[0].shape[1]
    for mask, part_ref in enumerate(part_refs):
        x_ref[0, pl.ds(pl.multiple_of((mine ^ mask) * size, size), size)] = part_ref[0]

    def project(index, carry):
        at = pl.ds(pl.multiple_of(index * CHUNK, CHUNK), CHUNK)
        x = x_ref[0]
        q_ref[0, :, at] = (mul(x, wq_ref[:, at]) + vec_ref[0:1, at]).astype(bf16)
        k_ref[0, :, at] = mul(x, wk_ref[:, at]).astype(bf16)
        v_ref[0, :, at] = (mul(x, wv_ref[:, at]) + vec_ref[1:2, at]).astype(bf16)
        return carry

    lax.fori_loop(0, wq_ref.shape[1] // CHUNK, project, 0)
    stat_ref[0] = jnp.zeros(stat_ref.shape[1:], f32)
    full = size * pieces
    lane = lax.broadcasted_iota(jnp.int32, (1, PAIR), 1)

    def run(extent):
        fill_dead(dead_ref, extent, length)

        def head(at, number, half, slot):
            q, k = q_ref[0, :, at], k_ref[0, :extent, at]
            own = (lane >= half * HEAD_DIM) & (lane < (half + 1) * HEAD_DIM)
            scores = mul(jnp.where(own, k * SCALE, 0).astype(bf16), q, NT)
            top = jnp.full((8, full), -jnp.inf, f32)
            for row in range(0, extent, STRIP):
                top = jnp.maximum(top, by_eight(live_strip(scores, dead_ref, extent, row)).max(axis=0))
            top = jnp.max(top, axis=0, keepdims=True)
            total = jnp.zeros((8, full), f32)
            for row in range(0, extent, STRIP):
                expo = jnp.exp(live_strip(scores, dead_ref, extent, row) - top)
                total += by_eight(expo).sum(axis=0)
                prob_ref[slot, row : row + STRIP] = expo.astype(bf16)
            total = jnp.sum(total, axis=0, keepdims=True)
            stat_ref[0, pl.ds(number, 1), :] = top + jnp.log(total)
            return 1.0 / total

        def group(index, carry):
            for i in range(TOGETHER):
                pair = index * TOGETHER + i
                at = pl.ds(pl.multiple_of(pair * PAIR, PAIR), PAIR)
                values = v_ref[0, :extent, at].T
                mixed = []
                for half in range(2):
                    slot = 2 * i + half
                    scale = head(at, pair * 2 + half, half, slot)
                    own = values[half * HEAD_DIM : (half + 1) * HEAD_DIM]
                    mixed.append(mul(own, prob_ref[slot, :extent]) * scale)
                mix_ref[0, :, at] = jnp.concatenate(mixed, axis=0).T.astype(bf16)
            return carry

        lax.fori_loop(0, PAIRS // TOGETHER, group, 0)

    over_extents(length, full, run)


def attend(passage, count, info, tokens, parts, weights, before):
    held, piece, width = tokens.shape
    pieces = len(parts) + 1
    full = piece * pieces
    rows = pl.BlockSpec((1, full, width), lambda i, s: (passage, 0, 0))
    act = jax.ShapeDtypeStruct((count, full, width), bf16)
    got = pl.BlockSpec((1, piece, width), lambda i, s: (0, 0, 0))
    kept = [] if before is None else list(before)
    first_kept = 1 + pieces + len(weights)
    return pl.pallas_call(
        functools.partial(attend_kernel, pieces, passage, count, held),
        grid_spec=pltpu.PrefetchScalarGridSpec(
            num_scalar_prefetch=1,
            grid=(1,),
            in_specs=[pl.BlockSpec((1, piece, width), lambda i, s: (s[held] * count + passage, 0, 0))]
            + [got] * len(parts)
            + [fixed(w.shape) for w in weights]
            + [pl.BlockSpec(memory_space=pl.ANY)] * len(kept),
            out_specs=[pl.BlockSpec((2, 1, full, width), lambda i, s: (0, passage, 0, 0))]
            + [rows] * 3
            + [pl.BlockSpec((1, STAT_ROWS, full), lambda i, s: (passage, 0, 0))],
            scratch_shapes=[
                pltpu.VMEM((2 * TOGETHER, full, full), bf16),
                pltpu.VMEM((KEY_STEP, full), f32),
            ],
        ),
        out_shape=[jax.ShapeDtypeStruct((2, count, full, width), bf16)]
        + [act] * 3
        + [jax.ShapeDtypeStruct((count, STAT_ROWS, full), f32)],
        input_output_aliases={first_kept + i: i for i in range(len(kept))},
        compiler_params=PARAMS,
        cost_estimate=cost(
            2 * full * (3 * width * width + 4 * 2 * full * width),
            12 * full * width + 6 * width * width,
        ),
    )(info, tokens, *parts, *weights, *kept)


def attend_back_kernel(
    held,
    info_ref,
    q_ref,
    k_ref,
    v_ref,
    mg_ref,
    mix_ref,
    branch_ref,
    stat_ref,
    sum_ref,
    grads_ref,
    word_ref,
    bias_ref,
    along_ref,
    prob_ref,
    score_ref,
    dead_ref,
):
    dq_ref, dk_ref, dv_ref = (grads_ref.at[i] for i in range(3))
    grads_ref[3] = branch_ref[...].astype(bf16)
    full, width = q_ref.shape[1:]
    length = info_ref[info_ref[held] * pl.num_programs(0) + pl.program_id(0)]
    lane = lax.broadcasted_iota(jnp.int32, (1, PAIR), 1)
    row = lax.broadcasted_iota(jnp.int32, (8, 1), 0)

    @pl.when(pl.program_id(0) == 0)
    def _():
        bias_ref[...] = sum_ref[...]

    feature = lax.broadcasted_iota(jnp.int32, (STAT_ROWS, width), 1)
    number = lax.broadcasted_iota(jnp.int32, (STAT_ROWS, width), 0)
    ours = jnp.where(
        (feature >= number * HEAD_DIM) & (feature < (number + 1) * HEAD_DIM), 1.0, 0.0
    ).astype(bf16)
    product = mg_ref[0].astype(f32) * mix_ref[0, 0].astype(f32)
    high = product.astype(bf16)
    low = (product - high.astype(f32)).astype(bf16)
    along_ref[...] = mul(ours, high, NT) + mul(ours, low, NT)

    def run(extent):
        fill_dead(dead_ref, extent, length)
        if extent < full:
            dk_ref[0, extent:] = jnp.zeros((full - extent, width), bf16)
            dv_ref[0, extent:] = jnp.zeros((full - extent, width), bf16)

        def group(index, carry):
            for i in range(BACK_TOGETHER):
                pair = index * BACK_TOGETHER + i
                at = pl.ds(pl.multiple_of(pair * PAIR, PAIR), PAIR)
                q, mg = q_ref[0, :, at], mg_ref[0, :, at]
                k, v = k_ref[0, :extent, at], v_ref[0, :extent, at]
                keys = k.T
                dq, dk, dv = [], [], []
                for half in range(2):
                    slot = 2 * i + half
                    own = (lane >= half * HEAD_DIM) & (lane < (half + 1) * HEAD_DIM)
                    scores = mul(jnp.where(own, k * SCALE, 0).astype(bf16), q, NT)
                    prob_grad = mul(jnp.where(own, v, 0).astype(bf16), mg, NT)
                    log_row = stat_ref[0, pl.ds(pair * 2 + half, 1), :]
                    along = along_ref[pl.ds(pair * 2 + half, 1), :]
                    for at_row in range(0, extent, STRIP):
                        rows = slice(at_row, at_row + STRIP)
                        probs = jnp.exp(live_strip(scores, dead_ref, extent, at_row) - log_row)
                        prob_ref[slot, rows] = probs.astype(bf16)
                        score_ref[slot, rows] = (probs * (prob_grad[rows] - along)).astype(bf16)
                    score_grad = score_ref[slot, :extent]
                    dv.append(mul(prob_ref[slot, :extent], mg))
                    dk.append(mul(score_grad, q))
                    dq.append(mul(keys[half * HEAD_DIM : (half + 1) * HEAD_DIM], score_grad))
                first = lane < HEAD_DIM
                dq_pair = jnp.concatenate(dq, axis=0).T * SCALE
                dk_pair = jnp.where(first, dk[0], dk[1]) * SCALE
                dv_pair = jnp.where(first, dv[0], dv[1])
                dq_ref[0, :, at] = dq_pair.astype(bf16)
                dk_ref[0, :extent, at] = dk_pair.astype(bf16)
                dv_ref[0, :extent, at] = dv_pair.astype(bf16)
                sums = jnp.where(
                    row == 0,
                    jnp.sum(dq_pair, axis=0, keepdims=True),
                    jnp.where(row == 1, jnp.sum(dv_pair, axis=0, keepdims=True), 0.0),
                )
                bias_ref[0:8, at] += sums
            return carry

        lax.fori_loop(0, PAIRS // BACK_TOGETHER, group, 0)

    over_extents(length, full, run)

    @pl.when(pl.program_id(0) == pl.num_programs(0) - 1)
    def _():
        high = bias_ref[...].astype(bf16)
        word_ref[:SUM_ROWS] = high
        word_ref[SUM_ROWS:] = (bias_ref[...] - high.astype(f32)).astype(bf16)


def attend_back(held, info, q, k, v, mixed_grad, stacked, branch_in, stat, sums):
    count, full, width = q.shape
    rows = pl.BlockSpec((1, full, width), lambda i, *_: (i, 0, 0))
    return pl.pallas_call(
        functools.partial(attend_back_kernel, held),
        grid_spec=pltpu.PrefetchScalarGridSpec(
            num_scalar_prefetch=1,
            grid=(count,),
            in_specs=[rows] * 4
            + [
                pl.BlockSpec((1, 1, full, width), lambda i, *_: (1, i, 0, 0)),
                rows,
                pl.BlockSpec((1, STAT_ROWS, full), lambda i, *_: (i, 0, 0)),
                fixed(sums.shape),
            ],
            out_specs=[
                pl.BlockSpec((4, 1, full, width), lambda i, *_: (0, i, 0, 0)),
                pl.BlockSpec((2 * SUM_ROWS, width), lambda i, *_: (0, 0)),
            ],
            scratch_shapes=[
                pltpu.VMEM(sums.shape, f32),
                pltpu.VMEM((STAT_ROWS, full), f32),
                pltpu.VMEM((2 * BACK_TOGETHER, full, full), bf16),
                pltpu.VMEM((2 * BACK_TOGETHER, full, full), bf16),
                pltpu.VMEM((KEY_STEP, full), f32),
            ],
        ),
        out_shape=[
            jax.ShapeDtypeStruct((4, count, full, width), bf16),
            jax.ShapeDtypeStruct((2 * SUM_ROWS, width), bf16),
        ],
        compiler_params=PARAMS,
        cost_estimate=cost(
            2 * count * full * 10 * 2 * full * width, 16 * count * full * width
        ),
    )(info, q, k, v, mixed_grad, stacked, branch_in, stat, sums)


def norm_parts(hidden):
    centred = hidden - jnp.mean(hidden, axis=1, keepdims=True)
    inv_scale = lax.rsqrt(jnp.mean(centred * centred, axis=1, keepdims=True) + eps)
    return centred * inv_scale, inv_scale


def norm_back(scaled, normed, inv_scale):
    mean = jnp.mean(scaled, axis=1, keepdims=True)
    along = jnp.mean(scaled * normed, axis=1, keepdims=True)
    return (scaled - mean - normed * along) * inv_scale


def gelu_parts(u):
    expo = jnp.exp(u * u * -0.5)
    base = 1.0 + jnp.abs(u) * (0.3275911 * root_half)
    t = pl.reciprocal(base, approx=True)
    t = t * (2.0 - base * t)
    poly = t * (
        0.5 * 0.254829592
        + t
        * (
            0.5 * -0.284496736
            + t * (0.5 * 1.421413741 + t * (0.5 * -1.453152027 + t * (0.5 * 1.061405429)))
        )
    )
    tail = poly * expo
    return jnp.where(u >= 0, 1.0 - tail, tail), expo


def rows_kernel(
    blocks,
    count,
    held,
    info_ref,
    x_ref,
    mix_ref,
    cot_ref,
    pool_ref,
    wo_ref,
    vec_ref,
    wu_all,
    wd_all,
    out_ref,
    low_ref,
    act_all,
    second_ref,
    inner_all,
    branch_ref,
    mg_ref,
    sum_ref,
    wu_ref,
    wd_ref,
    act_ref,
    inner_ref,
    slope_ref,
    first_ref,
    normed_ref,
    total_ref,
    scale_ref,
    sems,
):
    step, steps = pl.program_id(0), pl.num_programs(0)
    rows, width = cot_ref.shape
    hidden_width = wu_ref.shape[1]
    b_out, gain_one, shift_one, b_down, gain_two, shift_two = (
        vec_ref[i : i + 1] for i in range(2, 8)
    )
    passage = info_ref[held] * count + step // blocks
    length = info_ref[passage]
    inv_length = 1.0 / jnp.full((1, width), length, jnp.int32).astype(f32)
    pool = pool_ref[pl.ds(passage, 1), :] * inv_length
    first_row = (step % blocks) * rows
    load_up = pltpu.make_async_copy(wu_all, wu_ref, sems.at[0])
    load_down = pltpu.make_async_copy(wd_all, wd_ref, sems.at[1])

    def give(source_ref, all_ref, at):
        return pltpu.make_async_copy(
            source_ref, all_ref.at[pl.ds(pl.multiple_of(at * rows, rows), rows)], sems.at[2 if source_ref is act_ref else 3]
        )

    @pl.when(step == 0)
    def _():
        load_up.start()
        load_down.start()
        sum_ref[...] = jnp.zeros(sum_ref.shape, f32)

    def tally(at, value, columns=slice(None)):
        sum_ref[at : at + 1, columns] += jnp.sum(value, axis=0, keepdims=True)

    def strips(size):
        return [slice(i, i + size) for i in range(0, rows, size)]

    groups = width // CHUNK
    chunks = hidden_width // CHUNK
    part = [slice(i * CHUNK, (i + 1) * CHUNK) for i in range(chunks)]
    whole = [slice(i * width, (i + 1) * width) for i in range(hidden_width // width)]
    lanes = scale_ref.shape[1]

    branch = mul(mix_ref[0], wo_ref[...])
    for at in strips(STRIP):
        normed, scale = norm_parts(x_ref[0, at].astype(f32) + branch[at] + b_out)
        first = normed * gain_one + shift_one
        normed_ref[at] = normed
        scale_ref[at] = jnp.broadcast_to(scale, (STRIP, lanes))
        first_ref[at] = first + b_down
        low_ref[at] = first.astype(bf16)

    @pl.when(step == 0)
    def _():
        load_up.wait()
        load_down.wait()

    @pl.when(step > 0)
    def _():
        give(act_ref, act_all, step - 1).wait()

    def up(i):
        return mul(low_ref[...], wu_ref[:, part[i]])

    pre = up(0)
    for i in range(chunks):
        ahead = up(i + 1) if i + 1 < chunks else None
        bias = vec_ref[8 + i // groups : 9 + i // groups, part[i % groups]]
        for at in strips(2 * STRIP):
            u = pre[at] + bias
            phi, expo = gelu_parts(u)
            act_ref[at, part[i]] = (u * phi).astype(bf16)
            slope_ref[at, part[i]] = phi + u * expo * inv_root_two_pi
        if i % groups == 0 and i:
            done = whole[i // groups - 1]
            first_ref[...] += mul(act_ref[:, done], wd_ref[done, :])
        pre = ahead
    last = mul(act_ref[:, whole[-1]], wd_ref[whole[-1], :])
    give(act_ref, act_all, step).start()

    pooled, shift, gain, down = (jnp.zeros((8, width), f32) for _ in range(4))
    for at in strips(STRIP):
        normed, scale = norm_parts(first_ref[at] + last[at])
        result = normed * gain_two + shift_two
        out_ref[at] = result.astype(bf16)
        row_at = lax.broadcasted_iota(jnp.int32, (STRIP, 1), 0) + (first_row + at.start)
        live = jnp.where(row_at < length, 1.0, 0.0)
        pooled += by_eight(result * live).sum(axis=0)
        upstream = cot_ref[at].astype(f32) + live * pool
        gain += by_eight(upstream * normed).sum(axis=0)
        shift += by_eight(upstream).sum(axis=0)
        second_in = norm_back(upstream * gain_two, normed, scale)
        down += by_eight(second_in).sum(axis=0)
        total_ref[at] = second_in
        second_ref[at] = second_in.astype(bf16)
    tally(6, gain)
    tally(7, shift)
    tally(5, down)
    sum_ref[pl.ds(POOL_ROW + step // blocks, 1), :] += (
        jnp.sum(pooled, axis=0, keepdims=True) * inv_length
    )

    @pl.when(step > 0)
    def _():
        give(inner_ref, inner_all, step - 1).wait()

    def back(i):
        return mul(second_ref[...], wd_ref[part[i], :], NT)

    grad = back(0)
    for i in range(chunks):
        ahead = back(i + 1) if i + 1 < chunks else None
        bias = jnp.zeros((8, CHUNK), f32)
        for at in strips(2 * STRIP):
            inner = grad[at] * slope_ref[at, part[i]]
            bias += by_eight(inner).sum(axis=0)
            inner_ref[at, part[i]] = inner.astype(bf16)
        tally(8 + i // groups, bias, part[i % groups])
        if i % groups == 0 and i:
            done = whole[i // groups - 1]
            total_ref[...] += mul(inner_ref[:, done], wu_ref[:, done], NT)
        grad = ahead
    last = mul(inner_ref[:, whole[-1]], wu_ref[:, whole[-1]], NT)
    give(inner_ref, inner_all, step).start()

    gain, shift, out = (jnp.zeros((8, width), f32) for _ in range(3))
    for at in strips(STRIP):
        first_up = total_ref[at] + last[at]
        normed = normed_ref[at]
        gain += by_eight(first_up * normed).sum(axis=0)
        shift += by_eight(first_up).sum(axis=0)
        branch_in = norm_back(first_up * gain_one, normed, scale_ref[at, :1])
        out += by_eight(branch_in).sum(axis=0)
        branch_ref[at] = branch_in
    tally(3, gain)
    tally(4, shift)
    tally(2, out)
    mg_ref[...] = mul(branch_ref[...].astype(bf16), wo_ref[...], NT).astype(bf16)

    @pl.when(step == steps - 1)
    def _():
        give(act_ref, act_all, step).wait()
        give(inner_ref, inner_all, step).wait()


def row_work(held, info, stacked, cot, pool, w_out, w_up, w_down, vecs, count):
    total, width = cot.shape
    full = total // count
    assert POOL_ROW + count <= SUM_ROWS
    hidden = w_up.shape[1]
    blocks = full // ROWS
    narrow = pl.BlockSpec((ROWS, width), lambda i, *_: (i, 0))
    anywhere = pl.BlockSpec(memory_space=pl.ANY)
    thin = jax.ShapeDtypeStruct((total, width), bf16)
    thick = jax.ShapeDtypeStruct((total, hidden), bf16)
    return pl.pallas_call(
        functools.partial(rows_kernel, blocks, count, held),
        grid_spec=pltpu.PrefetchScalarGridSpec(
            num_scalar_prefetch=1,
            grid=(total // ROWS,),
            in_specs=[
                pl.BlockSpec((1, ROWS, width), lambda i, *_: (0, i, 0)),
                pl.BlockSpec((1, ROWS, width), lambda i, *_: (1, i, 0)),
                narrow,
                fixed(pool.shape),
                fixed((width, width)),
                fixed(vecs.shape),
                anywhere,
                anywhere,
            ],
            out_specs=[
                narrow,
                narrow,
                anywhere,
                narrow,
                anywhere,
                narrow,
                narrow,
                pl.BlockSpec((SUM_ROWS, width), lambda i, *_: (0, 0)),
            ],
            scratch_shapes=[
                pltpu.VMEM((width, hidden), bf16),
                pltpu.VMEM((hidden, width), bf16),
                pltpu.VMEM((ROWS, hidden), bf16),
                pltpu.VMEM((ROWS, hidden), bf16),
                pltpu.VMEM((ROWS, hidden), f32),
                pltpu.VMEM((ROWS, width), f32),
                pltpu.VMEM((ROWS, width), f32),
                pltpu.VMEM((ROWS, width), f32),
                pltpu.VMEM((ROWS, PAIR), f32),
                pltpu.SemaphoreType.DMA((4,)),
            ],
        ),
        out_shape=[
            thin,
            thin,
            thick,
            thin,
            thick,
            jax.ShapeDtypeStruct((total, width), f32),
            thin,
            jax.ShapeDtypeStruct((SUM_ROWS, width), f32),
        ],
        compiler_params=PARAMS,
        cost_estimate=cost(
            4 * total * width * (width + 2 * hidden),
            2 * total * (8 * width + 2 * hidden) + 2 * width * (width + 2 * hidden),
        ),
    )(info, stacked, stacked, cot, pool, w_out, vecs, w_up, w_down)


def dense_outer_kernel(side_ref, act_ref, second_ref, low_ref, inner_ref, out_ref):
    step = pl.program_id(0)
    half = pl.num_programs(0) // 2

    @pl.when(step < half)
    def _():
        out_ref[0] = mul(act_ref[...], second_ref[...], TN).astype(bf16)

    @pl.when(step >= half)
    def _():
        out_ref[0] = mul(low_ref[...], inner_ref[...], TN).astype(bf16)


def dense_outer(at, flip, info, act, second, low, inner):
    total, width = second.shape
    wide = act.shape[1] // width
    half = wide // 2
    return pl.pallas_call(
        dense_outer_kernel,
        grid_spec=pltpu.PrefetchScalarGridSpec(
            num_scalar_prefetch=1,
            grid=(wide,),
            in_specs=[
                pl.BlockSpec(
                    (total, width), lambda i, s: (0, (s[at] ^ flip) * half + jnp.minimum(i, half - 1))
                ),
                fixed((total, width)),
                fixed((total, width)),
                pl.BlockSpec(
                    (total, width), lambda i, s: (0, (s[at] ^ flip) * half + jnp.maximum(i - half, 0))
                ),
            ],
            out_specs=pl.BlockSpec((1, width, width), lambda i, s: (i, 0, 0)),
        ),
        out_shape=jax.ShapeDtypeStruct((wide, width, width), bf16),
        compiler_params=PARAMS,
        cost_estimate=cost(
            2 * total * width * width * wide, 2 * (wide + 2) * total * width + 2 * wide * width * width
        ),
    )(info, act, second, low, inner).reshape(wide * width, width)


def attend_outer_kernel(side_ref, left_ref, right_ref, out_ref):
    out_ref[0] = mul(left_ref[0], right_ref[0], TN).astype(bf16)


def attend_outer(at, flip, info, stacked, grads):
    total, width = stacked.shape[1:]
    return pl.pallas_call(
        attend_outer_kernel,
        grid_spec=pltpu.PrefetchScalarGridSpec(
            num_scalar_prefetch=1,
            grid=(2,),
            in_specs=[
                pl.BlockSpec((1, total, width), lambda i, s: (((s[at] ^ flip) * 2 + i) // 3, 0, 0)),
                pl.BlockSpec((1, total, width), lambda i, s: ((s[at] ^ flip) * 2 + i, 0, 0)),
            ],
            out_specs=pl.BlockSpec((1, width, width), lambda i, s: (i, 0, 0)),
        ),
        out_shape=jax.ShapeDtypeStruct((2, width, width), bf16),
        compiler_params=PARAMS,
        cost_estimate=cost(4 * total * width * width, 8 * total * width + 4 * width * width),
    )(info, stacked, grads).reshape(2 * width, width)


def input_kernel(branch_ref, dq_ref, dk_ref, dv_ref, wq_ref, wk_ref, wv_ref, out_ref):
    total = branch_ref[...] + mul(dq_ref[0], wq_ref[...], NT)
    total += mul(dk_ref[0], wk_ref[...], NT)
    total += mul(dv_ref[0], wv_ref[...], NT)
    out_ref[...] = total.astype(bf16)


def input_grad(branch_in, grads, w_query, w_key, w_value):
    total, width = branch_in.shape
    rows = pl.BlockSpec((BACK_ROWS, width), lambda i: (i, 0))
    return pl.pallas_call(
        input_kernel,
        grid=(total // BACK_ROWS,),
        in_specs=[rows]
        + [pl.BlockSpec((1, BACK_ROWS, width), lambda i, at=at: (at, i, 0)) for at in range(3)]
        + [fixed((width, width))] * 3,
        out_specs=rows,
        out_shape=jax.ShapeDtypeStruct((total, width), bf16),
        compiler_params=SMALL,
        cost_estimate=cost(6 * total * width * width, 12 * total * width + 6 * width * width),
    )(branch_in, grads, grads, grads, w_query, w_key, w_value)


def exchange(value, axis, mask):
    count = lax.axis_size(axis)
    return lax.ppermute(value, axis, [(i, i ^ mask) for i in range(count)])


def to_passages(value):
    count = lax.axis_size("seq")
    mine = lax.axis_index("seq")
    held, piece, width = value.shape
    own = held // count
    whole = jnp.zeros((own, piece * count, width), value.dtype)
    for mask in range(count):
        peer = mine ^ mask
        part = lax.dynamic_slice_in_dim(value, peer * own, own, 0)
        if mask:
            part = exchange(part, "seq", mask)
        whole = lax.dynamic_update_slice_in_dim(whole, part, peer * piece, 1)
    return whole


def position_pieces(value):
    count = lax.axis_size("seq")
    piece = value.shape[1] // count
    mine = lax.axis_index("seq")
    return [
        lax.dynamic_slice_in_dim(value, (mine ^ mask) * piece, piece, 1) for mask in range(count)
    ]


def traded(pieces):
    return [exchange(part, "seq", mask) if mask else part for mask, part in enumerate(pieces)]


def to_positions(pieces):
    mine = lax.axis_index("seq")
    own, piece, width = pieces[0].shape
    result = jnp.zeros((own * len(pieces), piece, width), pieces[0].dtype)
    for mask, part in enumerate(pieces):
        result = lax.dynamic_update_slice_in_dim(result, part, (mine ^ mask) * own, 0)
    return result


def axis_bits(axis):
    return [(axis, 1 << i) for i in range(lax.axis_size(axis).bit_length() - 1)]


def upper(dim):
    axis, mask = dim
    return (lax.axis_index(axis) & mask) // mask


def swap(value, dim):
    return exchange(value, dim[0], dim[1])


def total_of(parts):
    total = parts[0].astype(f32)
    for part in parts[1:]:
        total += part.astype(f32)
    return total.astype(bf16)


PARTS = 3
SHARD_STEP = 16


class Plan:
    def __init__(self, rows):
        dims = axis_bits("seq") + axis_bits("dp")
        self.first = dims[0]
        rest = dims[1:]
        self.rows = rows // PARTS
        halved = 0
        while halved < len(rest) and (self.rows >> (halved + 1)) % SHARD_STEP == 0:
            halved += 1
        self.last = rest[halved - 1]
        self.plain = rest[halved:]
        split = rest[: halved - 1]
        self.orders = [split[i % len(split) :] + split[: i % len(split)] for i in range(PARTS)]
        self.shards = 1 << halved
        self.shard = self.rows >> halved

    def table(self, blocks, width, each):
        places = {}
        devices = 1
        weight = {}
        for axis in ("seq", "dp"):
            for _, mask in axis_bits(axis):
                weight[(axis, mask)] = devices
                devices *= 2
        for side in range(2):
            for part, order in enumerate(self.orders):
                dims = [self.last] + order[::-1]
                for code in range(self.shards):
                    device = side * weight[self.first]
                    device += sum(weight[d] for i, d in enumerate(dims) if (code >> i) & 1)
                    row = part * self.rows + code * self.shard
                    places[side, row] = device * each + part * self.shard
        half = blocks // 4
        found = []
        for block in range(blocks):
            side = block % (2 * half) // half
            local = block // (2 * half) * half + block % half
            for row in range(0, width, self.shard):
                found.append(places[side, local * width + row])
        return found

    def codes(self):
        found = []
        for order in self.orders:
            code = upper(self.last)
            for at, dim in enumerate(reversed(order)):
                code += upper(dim) << (at + 1)
            found.append(code)
        return [code.astype(jnp.int32) for code in found]


class Chain:
    def __init__(self):
        self.token = None

    def tie(self, values):
        if self.token is None:
            return values
        return lax.optimization_barrier((values, self.token))[0]

    def mark(self, values):
        self.token = values
        return values


def scatter_steps(plan, chain, keep, got, found):
    pairs = [[keep, got]] * PARTS
    bases = [i * plan.rows for i in range(PARTS)]
    size = plan.rows
    for step in range(len(plan.orders[0])):
        pairs = chain.tie(pairs)
        size //= 2
        dims = [order[step] for order in plan.orders]

        def halves(pair, base, at):
            return total_of([lax.dynamic_slice_in_dim(p, base + at * size, size, 0) for p in pair])

        sends = [halves(p, base, 1 - upper(d)) for p, base, d in zip(pairs, bases, dims)]
        chain.mark(sends)
        mine = [halves(p, base, upper(d)) for p, base, d in zip(pairs, bases, dims)]
        pairs = [[m, swap(s, d)] for m, s, d in zip(mine, sends, dims)]
        bases = [0] * PARTS
        yield
    size = plan.shard
    bit = upper(plan.last)
    pairs = chain.tie(pairs)

    def side(at):
        return jnp.concatenate(
            [total_of([lax.dynamic_slice_in_dim(p, at * size, size, 0) for p in pair]) for pair in pairs],
            axis=0,
        )

    send = chain.mark(side(1 - bit))
    shard = side(bit)
    got = swap(send, plan.last)
    yield
    shard, got = chain.tie((shard, got))
    shard = total_of([shard, got])
    for dim in plan.plain:
        shard = total_of([shard, swap(shard, dim)])
    found.append(chain.mark(shard))
    yield


def gather_steps(plan, chain, shard, found):
    size = plan.shard
    got = swap(shard, plan.last)
    yield
    values = [(shard[i * size : (i + 1) * size], got[i * size : (i + 1) * size]) for i in range(PARTS)]
    for step in reversed(range(len(plan.orders[0]))):
        values = chain.tie(values)
        values = [jnp.concatenate(pair, axis=0) for pair in values]
        chain.mark(values)
        values = [(v, swap(v, order[step])) for v, order in zip(values, plan.orders)]
        yield
    values = chain.tie(values)
    chain.mark(values)
    found += [v for pair in values for v in pair]
    found += [swap(v, plan.first) for v in found]
    yield


def place(plan, refs, codes, row, store):
    part = row // plan.rows
    shard = ((row % plan.rows) // plan.shard) ^ codes[part]
    half = plan.shards // 2
    at = pl.ds(pl.multiple_of((shard & (half - 1)) * plan.shard, plan.shard), plan.shard)
    low, high = refs[2 * part][at, :], refs[2 * part + 1][at, :]
    store(jnp.where(shard >= half, high.astype(f32), low.astype(f32)))


def dense_place_kernel(
    shard, each, table_ref, group_ref, all_ref, down_ref, up_ref, vec_ref, pool_ref, hold_ref, word_ref, sems, word_sem
):
    step, steps = pl.program_id(0), pl.num_programs(0)
    width = down_ref.shape[1]
    parts = width // shard
    devices = word_ref.shape[0]

    @pl.when(step == 0)
    def _():
        def fetch(block, carry):
            for i in range(parts):
                at = pl.multiple_of(table_ref[block * parts + i], SHARD_STEP)
                pltpu.make_async_copy(
                    all_ref.at[pl.ds(at, shard)],
                    hold_ref.at[block, pl.ds(i * shard, shard)],
                    sems.at[block],
                ).start()
            return carry

        lax.fori_loop(0, steps, fetch, 0)

        def words(device, carry):
            pltpu.make_async_copy(
                all_ref.at[pl.ds(pl.multiple_of(device * each + each - 2 * SUM_ROWS, SHARD_STEP), 2 * SUM_ROWS)],
                word_ref.at[device],
                word_sem,
            ).start()
            return carry

        lax.fori_loop(0, devices, words, 0)

    pltpu.make_async_copy(all_ref.at[pl.ds(0, width)], hold_ref.at[step], sems.at[step]).wait()

    @pl.when(step < steps // 2)
    def _():
        down_ref[...] = hold_ref[step].astype(f32)

    @pl.when(step >= steps // 2)
    def _():
        up_ref[...] = hold_ref[step].astype(f32)

    @pl.when(step == steps - 1)
    def _():
        pltpu.make_async_copy(word_ref, word_ref, word_sem).wait()

        def both(device):
            return word_ref[device, :SUM_ROWS].astype(f32) + word_ref[device, SUM_ROWS:].astype(f32)

        vec_ref[...] = lax.fori_loop(
            0, devices, lambda i, total: total + both(i), jnp.zeros(vec_ref.shape, f32)
        )
        for i in range(pool_ref.shape[0]):
            pool_ref[i] = both(group_ref[0] + i)[POOL_ROW:]


def dense_place(plan, gathered, each, width, wide, devices, seq_count, group):
    table = jnp.array(plan.table(2 * wide, width, each), jnp.int32)
    return pl.pallas_call(
        functools.partial(dense_place_kernel, plan.shard, each),
        grid_spec=pltpu.PrefetchScalarGridSpec(
            num_scalar_prefetch=2,
            grid=(2 * wide,),
            in_specs=[pl.BlockSpec(memory_space=pl.ANY)],
            out_specs=[
                pl.BlockSpec((width, width), lambda i, *_: (jnp.minimum(i, wide - 1), 0)),
                pl.BlockSpec((width, width), lambda i, *_: (0, jnp.maximum(i - wide, 0))),
                pl.BlockSpec((SUM_ROWS, width), lambda i, *_: (0, 0)),
                pl.BlockSpec((seq_count, SUM_ROWS - POOL_ROW, width), lambda i, *_: (0, 0, 0)),
            ],
            scratch_shapes=[
                pltpu.VMEM((2 * wide, width, width), bf16),
                pltpu.VMEM((devices, 2 * SUM_ROWS, width), bf16),
                pltpu.SemaphoreType.DMA((2 * wide,)),
                pltpu.SemaphoreType.DMA(()),
            ],
        ),
        out_shape=[
            jax.ShapeDtypeStruct((wide * width, width), f32),
            jax.ShapeDtypeStruct((width, wide * width), f32),
            jax.ShapeDtypeStruct((SUM_ROWS, width), f32),
            jax.ShapeDtypeStruct((seq_count, SUM_ROWS - POOL_ROW, width), f32),
        ],
        compiler_params=PARAMS,
        cost_estimate=cost(0, 12 * wide * width * width),
    )(table, group, gathered)


def attend_place_kernel(plan, first_code, at, flip, info_ref, *refs):
    sources, (hold_ref, sems) = refs[: 2 * PARTS], refs[-2:]
    outs = refs[-6:-2]
    codes = [info_ref[first_code + i] for i in range(PARTS)]
    own = info_ref[at] ^ flip
    width = hold_ref.shape[2]

    def move(block, act):
        for side in range(2):

            @pl.when(own == side)
            def _():
                act(pltpu.make_async_copy(hold_ref.at[block], outs[2 * side + block], sems.at[block]))

    for block in range(2):
        for row in range(0, width, plan.shard):

            def store(value, row=row):
                hold_ref[block, row : row + plan.shard, :] = value

            place(plan, sources, codes, block * width + row, store)
        move(block, lambda copy: copy.start())
    for block in range(2):
        move(block, lambda copy: copy.wait())


def attend_place(plan, first_code, at, flip, info, sources, width, before):
    kept = list(before)
    return pl.pallas_call(
        functools.partial(attend_place_kernel, plan, first_code, at, flip),
        grid_spec=pltpu.PrefetchScalarGridSpec(
            num_scalar_prefetch=1,
            grid=(1,),
            in_specs=[fixed(x.shape) for x in sources]
            + [pl.BlockSpec(memory_space=pl.ANY)] * len(kept),
            out_specs=[pl.BlockSpec(memory_space=pl.ANY)] * 4,
            scratch_shapes=[pltpu.VMEM((2, width, width), f32), pltpu.SemaphoreType.DMA((2,))],
        ),
        out_shape=[jax.ShapeDtypeStruct((width, width), f32)] * 4,
        input_output_aliases={1 + len(sources) + i: i for i in range(len(kept))},
        compiler_params=SMALL,
        cost_estimate=cost(0, 12 * width * width),
    )(info, *sources, *kept)


def shards(
    tokens,
    lengths,
    w_query,
    b_query,
    w_key,
    w_value,
    b_value,
    w_out,
    b_out,
    gain_one,
    shift_one,
    w_up,
    b_up,
    w_down,
    b_down,
    gain_two,
    shift_two,
    out_grad,
    pooled_grad,
):
    seq_count = lax.axis_size("seq")
    held, piece, width = tokens.shape
    full = piece * seq_count
    count = held // seq_count
    mine = lax.axis_index("seq")
    wide = w_up.shape[1] // width
    total = count * full

    def flat(value):
        return value.reshape(total, width)

    def split(value):
        return value.reshape(count, full, width)

    dense_plan = Plan(wide * width)
    outer_plan = Plan(2 * width)
    first = axis_bits("seq")[0]
    scalars = [mine, upper(first)] + dense_plan.codes() + outer_plan.codes()
    own_at, dense_at, outer_at = held + 1, held + 2, held + 2 + PARTS
    info = jnp.concatenate([lengths, jnp.stack([v.astype(jnp.int32) for v in scalars])])
    vecs = jnp.concatenate(
        [b_query, b_value, b_out, gain_one, shift_one, b_down, gain_two, shift_two, b_up]
    )
    vecs = vecs.astype(f32).reshape(-1, width)

    weights = [w_query, w_key, w_value, vecs]
    done = None
    source = tokens
    parts = []
    for passage in range(count):
        if parts:
            source = lax.optimization_barrier((tokens, parts))[0]
        slices = [
            lax.dynamic_slice_in_dim(source, (mine ^ mask) * count + passage, 1, 0)
            for mask in range(1, seq_count)
        ]
        parts = [exchange(value, "seq", mask + 1) for mask, value in enumerate(slices)]
        done = attend(passage, count, info, tokens, parts, weights, done)
    stacked, q, k, v, stat = done
    cot = to_passages(lax.optimization_barrier((out_grad, slices))[0])
    stacked = stacked.reshape(2, total, width)
    result, first_low, act, second, inner, branch_in, mixed_grad, sums = row_work(
        held, info, stacked, flat(cot), pooled_grad, w_out, w_up, w_down, vecs, count
    )
    chain = Chain()
    pieces = chain.mark(position_pieces(split(result)))
    out_pieces = traded(pieces)
    send = dense_outer(own_at, 1, info, *chain.tie((act, second, first_low, inner)))
    chain.mark(send)
    got = swap(send, first)
    keep = chain.mark(dense_outer(own_at, 0, info, *chain.tie((act, second, first_low, inner))))
    dense, shard, outer = [], [], []
    dense_steps = scatter_steps(dense_plan, chain, keep, got, dense)
    next(dense_steps)
    chain.mark((chain.token, out_pieces))
    block_out = to_positions(out_pieces)
    grads, words = attend_back(
        held,
        info,
        q,
        k,
        v,
        chain.tie(split(mixed_grad)),
        stacked.reshape(2, count, full, width),
        split(branch_in),
        stat,
        sums,
    )
    chain.mark(words)
    grads = grads.reshape(4, total, width)
    next(dense_steps)
    send = attend_outer(own_at, 1, info, stacked, chain.tie(grads))
    chain.mark(send)
    got = swap(send, first)
    keep = attend_outer(own_at, 0, info, stacked, chain.tie(grads))
    chain.mark(keep)
    next(dense_steps)
    outer_steps = scatter_steps(outer_plan, chain, keep, got, shard)
    next(outer_steps)
    input_low = input_grad(branch_in, chain.tie(grads), w_query, w_key, w_value)
    chain.mark(input_low)
    next(dense_steps)
    next(outer_steps)
    for _ in dense_steps:
        pass
    gathered = jnp.concatenate([dense[0], words], axis=0)
    each = gathered.shape[0]
    gathered = chain.mark(gathered)
    gathered = lax.all_gather(gathered, ("dp", "seq"), axis=0, tiled=True)
    next(outer_steps)
    next(outer_steps)
    pieces = chain.mark(position_pieces(split(chain.tie(input_low))))
    in_pieces = traded(pieces)
    for _ in outer_steps:
        pass
    outer_steps = gather_steps(outer_plan, chain, shard[0], outer)
    next(outer_steps)
    chain.mark((chain.token, in_pieces))
    next(outer_steps)
    next(outer_steps)
    next(outer_steps)
    tokens_grad = to_positions(in_pieces)
    chain.mark((chain.token, tokens_grad, block_out))
    for _ in outer_steps:
        pass
    group = (lax.axis_index("dp") * seq_count).astype(jnp.int32)[None]

    def place_outer(flip, before):
        pick = outer[2 * PARTS :] if flip else outer[: 2 * PARTS]
        return chain.mark(
            attend_place(outer_plan, outer_at, own_at, flip, info, chain.tie(pick), width, before)
        )

    placed = place_outer(0, [])
    outer = place_outer(1, placed)
    down_sum, up_sum, vectors, pooled = dense_place(
        dense_plan, chain.tie(gathered), each, width, wide, gathered.shape[0] // each, seq_count, group
    )
    pooled = pooled[:, :count].reshape(held, width)
    return (
        block_out,
        pooled,
        tokens_grad,
        outer[0],
        vectors[0],
        outer[1],
        outer[2],
        vectors[1],
        outer[3],
        vectors[2],
        vectors[3],
        vectors[4],
        up_sum,
        vectors[8 : 8 + wide].reshape(-1),
        down_sum,
        vectors[5],
        vectors[6],
        vectors[7],
    )


def solution(mesh):
    in_specs = (
        (P("dp", "seq", None), P("dp"))
        + (P(),) * 15
        + (P("dp", "seq", None), P("dp", None))
    )
    out_specs = (P("dp", "seq", None), P("dp", None), P("dp", "seq", None)) + (P(),) * 15
    return jax.shard_map(shards, mesh=mesh, in_specs=in_specs, out_specs=out_specs, check_vma=False)
```

```python
import functools

import jax
import jax.numpy as jnp
from jax import lax
from jax.experimental import pallas as pl
from jax.experimental.pallas import tpu as pltpu
from jax.sharding import PartitionSpec as P

HEADS = 12
HEAD_DIM = 64
PAIR = 2 * HEAD_DIM
PAIRS = HEADS // 2
SCALE = HEAD_DIM ** (-0.5)
ROWS = 256
BACK_ROWS = 256
STRIP = 32
TOGETHER = 1
BACK_TOGETHER = 1
STAT_ROWS = 16
CHUNK = 256
KEY_STEP = 128
VMEM_BYTES = 62 * 1024 * 1024
SMALL_BYTES = 40 * 1024 * 1024
SUM_ROWS = 16
POOL_ROW = 12

eps = 1e-06
root_half = 0.7071067811865476
inv_root_two_pi = 0.3989422804014327

f32 = jnp.float32
bf16 = jnp.bfloat16

NN = (((1,), (0,)), ((), ()))
NT = (((1,), (1,)), ((), ()))
TN = (((0,), (0,)), ((), ()))


def mul(left, right, dims=NN):
    return lax.dot_general(left, right, dims, preferred_element_type=f32)


def fixed(shape):
    return pl.BlockSpec(shape, lambda *_: (0,) * len(shape), pipeline_mode=pl.Buffered(1))


PARAMS = pltpu.CompilerParams(dimension_semantics=("arbitrary",), vmem_limit_bytes=VMEM_BYTES)
SMALL = pltpu.CompilerParams(dimension_semantics=("arbitrary",), vmem_limit_bytes=SMALL_BYTES)


def cost(flops, moved, exps=0):
    return pl.CostEstimate(flops=int(flops), bytes_accessed=int(moved), transcendentals=int(exps))


def over_extents(length, full, body):
    for extent in range(KEY_STEP, full + 1, KEY_STEP):
        pl.when((length > extent - KEY_STEP) & (length <= extent))(functools.partial(body, extent))


def by_eight(value):
    return value.reshape(value.shape[0] // 8, 8, value.shape[1])


def fill_dead(dead_ref, extent, length):
    key_at = lax.broadcasted_iota(jnp.int32, dead_ref.shape, 0) + (extent - KEY_STEP)
    dead_ref[...] = jnp.where(key_at < length, 0.0, -1e30)


def live_strip(scores, dead_ref, extent, row):
    strip = scores[row : row + STRIP]
    last = row - (extent - KEY_STEP)
    return strip + dead_ref[last : last + STRIP] if last >= 0 else strip


def attend_kernel(pieces, passage, count, held, info_ref, *refs):
    part_refs, refs = refs[:pieces], refs[pieces:]
    wq_ref, wk_ref, wv_ref, vec_ref = refs[:4]
    xm_ref, q_ref, k_ref, v_ref, stat_ref, prob_ref, dead_ref = refs[-7:]
    x_ref, mix_ref = xm_ref.at[0], xm_ref.at[1]
    mine = info_ref[held]
    length = info_ref[mine * count + passage]
    size = part_refs[0].shape[1]
    for mask, part_ref in enumerate(part_refs):
        x_ref[0, pl.ds(pl.multiple_of((mine ^ mask) * size, size), size)] = part_ref[0]

    def project(index, carry):
        at = pl.ds(pl.multiple_of(index * CHUNK, CHUNK), CHUNK)
        x = x_ref[0]
        q_ref[0, :, at] = (mul(x, wq_ref[:, at]) + vec_ref[0:1, at]).astype(bf16)
        k_ref[0, :, at] = mul(x, wk_ref[:, at]).astype(bf16)
        v_ref[0, :, at] = (mul(x, wv_ref[:, at]) + vec_ref[1:2, at]).astype(bf16)
        return carry

    lax.fori_loop(0, wq_ref.shape[1] // CHUNK, project, 0)
    stat_ref[0] = jnp.zeros(stat_ref.shape[1:], f32)
    full = size * pieces
    lane = lax.broadcasted_iota(jnp.int32, (1, PAIR), 1)

    def run(extent):
        fill_dead(dead_ref, extent, length)

        def head(at, number, half, slot):
            q, k = q_ref[0, :, at], k_ref[0, :extent, at]
            own = (lane >= half * HEAD_DIM) & (lane < (half + 1) * HEAD_DIM)
            scores = mul(jnp.where(own, k * SCALE, 0).astype(bf16), q, NT)
            top = jnp.full((8, full), -jnp.inf, f32)
            for row in range(0, extent, STRIP):
                top = jnp.maximum(top, by_eight(live_strip(scores, dead_ref, extent, row)).max(axis=0))
            top = jnp.max(top, axis=0, keepdims=True)
            total = jnp.zeros((8, full), f32)
            for row in range(0, extent, STRIP):
                expo = jnp.exp(live_strip(scores, dead_ref, extent, row) - top)
                total += by_eight(expo).sum(axis=0)
                prob_ref[slot, row : row + STRIP] = expo.astype(bf16)
            total = jnp.sum(total, axis=0, keepdims=True)
            stat_ref[0, pl.ds(number, 1), :] = top + jnp.log(total)
            return 1.0 / total

        def group(index, carry):
            for i in range(TOGETHER):
                pair = index * TOGETHER + i
                at = pl.ds(pl.multiple_of(pair * PAIR, PAIR), PAIR)
                values = v_ref[0, :extent, at].T
                mixed = []
                for half in range(2):
                    slot = 2 * i + half
                    scale = head(at, pair * 2 + half, half, slot)
                    own = values[half * HEAD_DIM : (half + 1) * HEAD_DIM]
                    mixed.append(mul(own, prob_ref[slot, :extent]) * scale)
                mix_ref[0, :, at] = jnp.concatenate(mixed, axis=0).T.astype(bf16)
            return carry

        lax.fori_loop(0, PAIRS // TOGETHER, group, 0)

    over_extents(length, full, run)


def attend(passage, count, info, tokens, parts, weights, before):
    held, piece, width = tokens.shape
    pieces = len(parts) + 1
    full = piece * pieces
    rows = pl.BlockSpec((1, full, width), lambda i, s: (passage, 0, 0))
    act = jax.ShapeDtypeStruct((count, full, width), bf16)
    got = pl.BlockSpec((1, piece, width), lambda i, s: (0, 0, 0))
    kept = [] if before is None else list(before)
    first_kept = 1 + pieces + len(weights)
    return pl.pallas_call(
        functools.partial(attend_kernel, pieces, passage, count, held),
        grid_spec=pltpu.PrefetchScalarGridSpec(
            num_scalar_prefetch=1,
            grid=(1,),
            in_specs=[pl.BlockSpec((1, piece, width), lambda i, s: (s[held] * count + passage, 0, 0))]
            + [got] * len(parts)
            + [fixed(w.shape) for w in weights]
            + [pl.BlockSpec(memory_space=pl.ANY)] * len(kept),
            out_specs=[pl.BlockSpec((2, 1, full, width), lambda i, s: (0, passage, 0, 0))]
            + [rows] * 3
            + [pl.BlockSpec((1, STAT_ROWS, full), lambda i, s: (passage, 0, 0))],
            scratch_shapes=[
                pltpu.VMEM((2 * TOGETHER, full, full), bf16),
                pltpu.VMEM((KEY_STEP, full), f32),
            ],
        ),
        out_shape=[jax.ShapeDtypeStruct((2, count, full, width), bf16)]
        + [act] * 3
        + [jax.ShapeDtypeStruct((count, STAT_ROWS, full), f32)],
        input_output_aliases={first_kept + i: i for i in range(len(kept))},
        compiler_params=PARAMS,
        cost_estimate=cost(
            2 * full * (3 * width * width + 4 * 2 * full * width),
            12 * full * width + 6 * width * width,
        ),
    )(info, tokens, *parts, *weights, *kept)


def attend_back_kernel(
    held,
    info_ref,
    q_ref,
    k_ref,
    v_ref,
    mg_ref,
    mix_ref,
    branch_ref,
    stat_ref,
    sum_ref,
    grads_ref,
    word_ref,
    bias_ref,
    along_ref,
    prob_ref,
    score_ref,
    dead_ref,
):
    dq_ref, dk_ref, dv_ref = (grads_ref.at[i] for i in range(3))
    grads_ref[3] = branch_ref[...].astype(bf16)
    full, width = q_ref.shape[1:]
    length = info_ref[info_ref[held] * pl.num_programs(0) + pl.program_id(0)]
    lane = lax.broadcasted_iota(jnp.int32, (1, PAIR), 1)
    row = lax.broadcasted_iota(jnp.int32, (8, 1), 0)

    @pl.when(pl.program_id(0) == 0)
    def _():
        bias_ref[...] = sum_ref[...]

    feature = lax.broadcasted_iota(jnp.int32, (STAT_ROWS, width), 1)
    number = lax.broadcasted_iota(jnp.int32, (STAT_ROWS, width), 0)
    ours = jnp.where(
        (feature >= number * HEAD_DIM) & (feature < (number + 1) * HEAD_DIM), 1.0, 0.0
    ).astype(bf16)
    product = mg_ref[0].astype(f32) * mix_ref[0, 0].astype(f32)
    high = product.astype(bf16)
    low = (product - high.astype(f32)).astype(bf16)
    along_ref[...] = mul(ours, high, NT) + mul(ours, low, NT)

    def run(extent):
        fill_dead(dead_ref, extent, length)
        if extent < full:
            dk_ref[0, extent:] = jnp.zeros((full - extent, width), bf16)
            dv_ref[0, extent:] = jnp.zeros((full - extent, width), bf16)

        def group(index, carry):
            for i in range(BACK_TOGETHER):
                pair = index * BACK_TOGETHER + i
                at = pl.ds(pl.multiple_of(pair * PAIR, PAIR), PAIR)
                q, mg = q_ref[0, :, at], mg_ref[0, :, at]
                k, v = k_ref[0, :extent, at], v_ref[0, :extent, at]
                keys = k.T
                dq, dk, dv = [], [], []
                for half in range(2):
                    slot = 2 * i + half
                    own = (lane >= half * HEAD_DIM) & (lane < (half + 1) * HEAD_DIM)
                    scores = mul(jnp.where(own, k * SCALE, 0).astype(bf16), q, NT)
                    prob_grad = mul(jnp.where(own, v, 0).astype(bf16), mg, NT)
                    log_row = stat_ref[0, pl.ds(pair * 2 + half, 1), :]
                    along = along_ref[pl.ds(pair * 2 + half, 1), :]
                    for at_row in range(0, extent, STRIP):
                        rows = slice(at_row, at_row + STRIP)
                        probs = jnp.exp(live_strip(scores, dead_ref, extent, at_row) - log_row)
                        prob_ref[slot, rows] = probs.astype(bf16)
                        score_ref[slot, rows] = (probs * (prob_grad[rows] - along)).astype(bf16)
                    score_grad = score_ref[slot, :extent]
                    dv.append(mul(prob_ref[slot, :extent], mg))
                    dk.append(mul(score_grad, q))
                    dq.append(mul(keys[half * HEAD_DIM : (half + 1) * HEAD_DIM], score_grad))
                first = lane < HEAD_DIM
                dq_pair = jnp.concatenate(dq, axis=0).T * SCALE
                dk_pair = jnp.where(first, dk[0], dk[1]) * SCALE
                dv_pair = jnp.where(first, dv[0], dv[1])
                dq_ref[0, :, at] = dq_pair.astype(bf16)
                dk_ref[0, :extent, at] = dk_pair.astype(bf16)
                dv_ref[0, :extent, at] = dv_pair.astype(bf16)
                sums = jnp.where(
                    row == 0,
                    jnp.sum(dq_pair, axis=0, keepdims=True),
                    jnp.where(row == 1, jnp.sum(dv_pair, axis=0, keepdims=True), 0.0),
                )
                bias_ref[0:8, at] += sums
            return carry

        lax.fori_loop(0, PAIRS // BACK_TOGETHER, group, 0)

    over_extents(length, full, run)

    @pl.when(pl.program_id(0) == pl.num_programs(0) - 1)
    def _():
        high = bias_ref[...].astype(bf16)
        word_ref[:SUM_ROWS] = high
        word_ref[SUM_ROWS:] = (bias_ref[...] - high.astype(f32)).astype(bf16)


def attend_back(held, info, q, k, v, mixed_grad, stacked, branch_in, stat, sums):
    count, full, width = q.shape
    rows = pl.BlockSpec((1, full, width), lambda i, *_: (i, 0, 0))
    return pl.pallas_call(
        functools.partial(attend_back_kernel, held),
        grid_spec=pltpu.PrefetchScalarGridSpec(
            num_scalar_prefetch=1,
            grid=(count,),
            in_specs=[rows] * 4
            + [
                pl.BlockSpec((1, 1, full, width), lambda i, *_: (1, i, 0, 0)),
                rows,
                pl.BlockSpec((1, STAT_ROWS, full), lambda i, *_: (i, 0, 0)),
                fixed(sums.shape),
            ],
            out_specs=[
                pl.BlockSpec((4, 1, full, width), lambda i, *_: (0, i, 0, 0)),
                pl.BlockSpec((2 * SUM_ROWS, width), lambda i, *_: (0, 0)),
            ],
            scratch_shapes=[
                pltpu.VMEM(sums.shape, f32),
                pltpu.VMEM((STAT_ROWS, full), f32),
                pltpu.VMEM((2 * BACK_TOGETHER, full, full), bf16),
                pltpu.VMEM((2 * BACK_TOGETHER, full, full), bf16),
                pltpu.VMEM((KEY_STEP, full), f32),
            ],
        ),
        out_shape=[
            jax.ShapeDtypeStruct((4, count, full, width), bf16),
            jax.ShapeDtypeStruct((2 * SUM_ROWS, width), bf16),
        ],
        compiler_params=PARAMS,
        cost_estimate=cost(
            2 * count * full * 10 * 2 * full * width, 16 * count * full * width
        ),
    )(info, q, k, v, mixed_grad, stacked, branch_in, stat, sums)


def norm_parts(hidden):
    centred = hidden - jnp.mean(hidden, axis=1, keepdims=True)
    inv_scale = lax.rsqrt(jnp.mean(centred * centred, axis=1, keepdims=True) + eps)
    return centred * inv_scale, inv_scale


def norm_back(scaled, normed, inv_scale):
    mean = jnp.mean(scaled, axis=1, keepdims=True)
    along = jnp.mean(scaled * normed, axis=1, keepdims=True)
    return (scaled - mean - normed * along) * inv_scale


def gelu_parts(u):
    expo = jnp.exp(u * u * -0.5)
    base = 1.0 + jnp.abs(u) * (0.3275911 * root_half)
    t = pl.reciprocal(base, approx=True)
    t = t * (2.0 - base * t)
    poly = t * (
        0.5 * 0.254829592
        + t
        * (
            0.5 * -0.284496736
            + t * (0.5 * 1.421413741 + t * (0.5 * -1.453152027 + t * (0.5 * 1.061405429)))
        )
    )
    tail = poly * expo
    return jnp.where(u >= 0, 1.0 - tail, tail), expo


def rows_kernel(
    blocks,
    count,
    held,
    info_ref,
    x_ref,
    mix_ref,
    cot_ref,
    pool_ref,
    wo_ref,
    vec_ref,
    wu_all,
    wd_all,
    out_ref,
    low_ref,
    act_all,
    second_ref,
    inner_all,
    branch_ref,
    mg_ref,
    sum_ref,
    wu_ref,
    wd_ref,
    act_ref,
    inner_ref,
    slope_ref,
    first_ref,
    normed_ref,
    total_ref,
    scale_ref,
    sems,
):
    step, steps = pl.program_id(0), pl.num_programs(0)
    rows, width = cot_ref.shape
    hidden_width = wu_ref.shape[1]
    b_out, gain_one, shift_one, b_down, gain_two, shift_two = (
        vec_ref[i : i + 1] for i in range(2, 8)
    )
    passage = info_ref[held] * count + step // blocks
    length = info_ref[passage]
    inv_length = 1.0 / jnp.full((1, width), length, jnp.int32).astype(f32)
    pool = pool_ref[pl.ds(passage, 1), :] * inv_length
    first_row = (step % blocks) * rows
    load_up = pltpu.make_async_copy(wu_all, wu_ref, sems.at[0])
    load_down = pltpu.make_async_copy(wd_all, wd_ref, sems.at[1])

    def give(source_ref, all_ref, at):
        return pltpu.make_async_copy(
            source_ref, all_ref.at[pl.ds(pl.multiple_of(at * rows, rows), rows)], sems.at[2 if source_ref is act_ref else 3]
        )

    @pl.when(step == 0)
    def _():
        load_up.start()
        load_down.start()
        sum_ref[...] = jnp.zeros(sum_ref.shape, f32)

    def tally(at, value, columns=slice(None)):
        sum_ref[at : at + 1, columns] += jnp.sum(value, axis=0, keepdims=True)

    def strips(size):
        return [slice(i, i + size) for i in range(0, rows, size)]

    groups = width // CHUNK
    chunks = hidden_width // CHUNK
    part = [slice(i * CHUNK, (i + 1) * CHUNK) for i in range(chunks)]
    whole = [slice(i * width, (i + 1) * width) for i in range(hidden_width // width)]
    lanes = scale_ref.shape[1]

    branch = mul(mix_ref[0], wo_ref[...])
    for at in strips(STRIP):
        normed, scale = norm_parts(x_ref[0, at].astype(f32) + branch[at] + b_out)
        first = normed * gain_one + shift_one
        normed_ref[at] = normed
        scale_ref[at] = jnp.broadcast_to(scale, (STRIP, lanes))
        first_ref[at] = first + b_down
        low_ref[at] = first.astype(bf16)

    @pl.when(step == 0)
    def _():
        load_up.wait()
        load_down.wait()

    @pl.when(step > 0)
    def _():
        give(act_ref, act_all, step - 1).wait()

    def up(i):
        return mul(low_ref[...], wu_ref[:, part[i]])

    pre = up(0)
    for i in range(chunks):
        ahead = up(i + 1) if i + 1 < chunks else None
        bias = vec_ref[8 + i // groups : 9 + i // groups, part[i % groups]]
        for at in strips(2 * STRIP):
            u = pre[at] + bias
            phi, expo = gelu_parts(u)
            act_ref[at, part[i]] = (u * phi).astype(bf16)
            slope_ref[at, part[i]] = phi + u * expo * inv_root_two_pi
        if i % groups == 0 and i:
            done = whole[i // groups - 1]
            first_ref[...] += mul(act_ref[:, done], wd_ref[done, :])
        pre = ahead
    last = mul(act_ref[:, whole[-1]], wd_ref[whole[-1], :])
    give(act_ref, act_all, step).start()

    pooled, shift, gain, down = (jnp.zeros((8, width), f32) for _ in range(4))
    for at in strips(STRIP):
        normed, scale = norm_parts(first_ref[at] + last[at])
        result = normed * gain_two + shift_two
        out_ref[at] = result.astype(bf16)
        row_at = lax.broadcasted_iota(jnp.int32, (STRIP, 1), 0) + (first_row + at.start)
        live = jnp.where(row_at < length, 1.0, 0.0)
        pooled += by_eight(result * live).sum(axis=0)
        upstream = cot_ref[at].astype(f32) + live * pool
        gain += by_eight(upstream * normed).sum(axis=0)
        shift += by_eight(upstream).sum(axis=0)
        second_in = norm_back(upstream * gain_two, normed, scale)
        down += by_eight(second_in).sum(axis=0)
        total_ref[at] = second_in
        second_ref[at] = second_in.astype(bf16)
    tally(6, gain)
    tally(7, shift)
    tally(5, down)
    sum_ref[pl.ds(POOL_ROW + step // blocks, 1), :] += (
        jnp.sum(pooled, axis=0, keepdims=True) * inv_length
    )

    @pl.when(step > 0)
    def _():
        give(inner_ref, inner_all, step - 1).wait()

    def back(i):
        return mul(second_ref[...], wd_ref[part[i], :], NT)

    grad = back(0)
    for i in range(chunks):
        ahead = back(i + 1) if i + 1 < chunks else None
        bias = jnp.zeros((8, CHUNK), f32)
        for at in strips(2 * STRIP):
            inner = grad[at] * slope_ref[at, part[i]]
            bias += by_eight(inner).sum(axis=0)
            inner_ref[at, part[i]] = inner.astype(bf16)
        tally(8 + i // groups, bias, part[i % groups])
        if i % groups == 0 and i:
            done = whole[i // groups - 1]
            total_ref[...] += mul(inner_ref[:, done], wu_ref[:, done], NT)
        grad = ahead
    last = mul(inner_ref[:, whole[-1]], wu_ref[:, whole[-1]], NT)
    give(inner_ref, inner_all, step).start()

    gain, shift, out = (jnp.zeros((8, width), f32) for _ in range(3))
    for at in strips(STRIP):
        first_up = total_ref[at] + last[at]
        normed = normed_ref[at]
        gain += by_eight(first_up * normed).sum(axis=0)
        shift += by_eight(first_up).sum(axis=0)
        branch_in = norm_back(first_up * gain_one, normed, scale_ref[at, :1])
        out += by_eight(branch_in).sum(axis=0)
        branch_ref[at] = branch_in
    tally(3, gain)
    tally(4, shift)
    tally(2, out)
    mg_ref[...] = mul(branch_ref[...].astype(bf16), wo_ref[...], NT).astype(bf16)

    @pl.when(step == steps - 1)
    def _():
        give(act_ref, act_all, step).wait()
        give(inner_ref, inner_all, step).wait()


def row_work(held, info, stacked, cot, pool, w_out, w_up, w_down, vecs, count):
    total, width = cot.shape
    full = total // count
    assert POOL_ROW + count <= SUM_ROWS
    hidden = w_up.shape[1]
    blocks = full // ROWS
    narrow = pl.BlockSpec((ROWS, width), lambda i, *_: (i, 0))
    anywhere = pl.BlockSpec(memory_space=pl.ANY)
    thin = jax.ShapeDtypeStruct((total, width), bf16)
    thick = jax.ShapeDtypeStruct((total, hidden), bf16)
    return pl.pallas_call(
        functools.partial(rows_kernel, blocks, count, held),
        grid_spec=pltpu.PrefetchScalarGridSpec(
            num_scalar_prefetch=1,
            grid=(total // ROWS,),
            in_specs=[
                pl.BlockSpec((1, ROWS, width), lambda i, *_: (0, i, 0)),
                pl.BlockSpec((1, ROWS, width), lambda i, *_: (1, i, 0)),
                narrow,
                fixed(pool.shape),
                fixed((width, width)),
                fixed(vecs.shape),
                anywhere,
                anywhere,
            ],
            out_specs=[
                narrow,
                narrow,
                anywhere,
                narrow,
                anywhere,
                narrow,
                narrow,
                pl.BlockSpec((SUM_ROWS, width), lambda i, *_: (0, 0)),
            ],
            scratch_shapes=[
                pltpu.VMEM((width, hidden), bf16),
                pltpu.VMEM((hidden, width), bf16),
                pltpu.VMEM((ROWS, hidden), bf16),
                pltpu.VMEM((ROWS, hidden), bf16),
                pltpu.VMEM((ROWS, hidden), f32),
                pltpu.VMEM((ROWS, width), f32),
                pltpu.VMEM((ROWS, width), f32),
                pltpu.VMEM((ROWS, width), f32),
                pltpu.VMEM((ROWS, PAIR), f32),
                pltpu.SemaphoreType.DMA((4,)),
            ],
        ),
        out_shape=[
            thin,
            thin,
            thick,
            thin,
            thick,
            jax.ShapeDtypeStruct((total, width), f32),
            thin,
            jax.ShapeDtypeStruct((SUM_ROWS, width), f32),
        ],
        compiler_params=PARAMS,
        cost_estimate=cost(
            4 * total * width * (width + 2 * hidden),
            2 * total * (8 * width + 2 * hidden) + 2 * width * (width + 2 * hidden),
        ),
    )(info, stacked, stacked, cot, pool, w_out, vecs, w_up, w_down)


def dense_outer_kernel(side_ref, act_ref, second_ref, low_ref, inner_ref, out_ref):
    step = pl.program_id(0)
    half = pl.num_programs(0) // 2

    @pl.when(step < half)
    def _():
        out_ref[0] = mul(act_ref[...], second_ref[...], TN).astype(bf16)

    @pl.when(step >= half)
    def _():
        out_ref[0] = mul(low_ref[...], inner_ref[...], TN).astype(bf16)


def dense_outer(at, flip, info, act, second, low, inner):
    total, width = second.shape
    wide = act.shape[1] // width
    half = wide // 2
    return pl.pallas_call(
        dense_outer_kernel,
        grid_spec=pltpu.PrefetchScalarGridSpec(
            num_scalar_prefetch=1,
            grid=(wide,),
            in_specs=[
                pl.BlockSpec(
                    (total, width), lambda i, s: (0, (s[at] ^ flip) * half + jnp.minimum(i, half - 1))
                ),
                fixed((total, width)),
                fixed((total, width)),
                pl.BlockSpec(
                    (total, width), lambda i, s: (0, (s[at] ^ flip) * half + jnp.maximum(i - half, 0))
                ),
            ],
            out_specs=pl.BlockSpec((1, width, width), lambda i, s: (i, 0, 0)),
        ),
        out_shape=jax.ShapeDtypeStruct((wide, width, width), bf16),
        compiler_params=PARAMS,
        cost_estimate=cost(
            2 * total * width * width * wide, 2 * (wide + 2) * total * width + 2 * wide * width * width
        ),
    )(info, act, second, low, inner).reshape(wide * width, width)


def attend_outer_kernel(side_ref, left_ref, right_ref, out_ref):
    out_ref[0] = mul(left_ref[0], right_ref[0], TN).astype(bf16)


def attend_outer(at, flip, info, stacked, grads):
    total, width = stacked.shape[1:]
    return pl.pallas_call(
        attend_outer_kernel,
        grid_spec=pltpu.PrefetchScalarGridSpec(
            num_scalar_prefetch=1,
            grid=(2,),
            in_specs=[
                pl.BlockSpec((1, total, width), lambda i, s: (((s[at] ^ flip) * 2 + i) // 3, 0, 0)),
                pl.BlockSpec((1, total, width), lambda i, s: ((s[at] ^ flip) * 2 + i, 0, 0)),
            ],
            out_specs=pl.BlockSpec((1, width, width), lambda i, s: (i, 0, 0)),
        ),
        out_shape=jax.ShapeDtypeStruct((2, width, width), bf16),
        compiler_params=PARAMS,
        cost_estimate=cost(4 * total * width * width, 8 * total * width + 4 * width * width),
    )(info, stacked, grads).reshape(2 * width, width)


def input_kernel(branch_ref, dq_ref, dk_ref, dv_ref, wq_ref, wk_ref, wv_ref, out_ref):
    total = branch_ref[...] + mul(dq_ref[0], wq_ref[...], NT)
    total += mul(dk_ref[0], wk_ref[...], NT)
    total += mul(dv_ref[0], wv_ref[...], NT)
    out_ref[...] = total.astype(bf16)


def input_grad(branch_in, grads, w_query, w_key, w_value):
    total, width = branch_in.shape
    rows = pl.BlockSpec((BACK_ROWS, width), lambda i: (i, 0))
    return pl.pallas_call(
        input_kernel,
        grid=(total // BACK_ROWS,),
        in_specs=[rows]
        + [pl.BlockSpec((1, BACK_ROWS, width), lambda i, at=at: (at, i, 0)) for at in range(3)]
        + [fixed((width, width))] * 3,
        out_specs=rows,
        out_shape=jax.ShapeDtypeStruct((total, width), bf16),
        compiler_params=SMALL,
        cost_estimate=cost(6 * total * width * width, 12 * total * width + 6 * width * width),
    )(branch_in, grads, grads, grads, w_query, w_key, w_value)


def exchange(value, axis, mask):
    count = lax.axis_size(axis)
    return lax.ppermute(value, axis, [(i, i ^ mask) for i in range(count)])


def to_passages(value):
    count = lax.axis_size("seq")
    mine = lax.axis_index("seq")
    held, piece, width = value.shape
    own = held // count
    whole = jnp.zeros((own, piece * count, width), value.dtype)
    for mask in range(count):
        peer = mine ^ mask
        part = lax.dynamic_slice_in_dim(value, peer * own, own, 0)
        if mask:
            part = exchange(part, "seq", mask)
        whole = lax.dynamic_update_slice_in_dim(whole, part, peer * piece, 1)
    return whole


def position_pieces(value):
    count = lax.axis_size("seq")
    piece = value.shape[1] // count
    mine = lax.axis_index("seq")
    return [
        lax.dynamic_slice_in_dim(value, (mine ^ mask) * piece, piece, 1) for mask in range(count)
    ]


def traded(pieces):
    return [exchange(part, "seq", mask) if mask else part for mask, part in enumerate(pieces)]


def to_positions(pieces):
    mine = lax.axis_index("seq")
    own, piece, width = pieces[0].shape
    result = jnp.zeros((own * len(pieces), piece, width), pieces[0].dtype)
    for mask, part in enumerate(pieces):
        result = lax.dynamic_update_slice_in_dim(result, part, (mine ^ mask) * own, 0)
    return result


def axis_bits(axis):
    return [(axis, 1 << i) for i in range(lax.axis_size(axis).bit_length() - 1)]


def upper(dim):
    axis, mask = dim
    return (lax.axis_index(axis) & mask) // mask


def swap(value, dim):
    return exchange(value, dim[0], dim[1])


def total_of(parts):
    total = parts[0].astype(f32)
    for part in parts[1:]:
        total += part.astype(f32)
    return total.astype(bf16)


PARTS = 3
SHARD_STEP = 16


class Plan:
    def __init__(self, rows):
        dims = axis_bits("seq") + axis_bits("dp")
        self.first = dims[0]
        rest = dims[1:]
        self.rows = rows // PARTS
        halved = 0
        while halved < len(rest) and (self.rows >> (halved + 1)) % SHARD_STEP == 0:
            halved += 1
        self.last = rest[halved - 1]
        self.plain = rest[halved:]
        split = rest[: halved - 1]
        self.orders = [split[i % len(split) :] + split[: i % len(split)] for i in range(PARTS)]
        self.shards = 1 << halved
        self.shard = self.rows >> halved

    def table(self, blocks, width, each):
        places = {}
        devices = 1
        weight = {}
        for axis in ("seq", "dp"):
            for _, mask in axis_bits(axis):
                weight[(axis, mask)] = devices
                devices *= 2
        for side in range(2):
            for part, order in enumerate(self.orders):
                dims = [self.last] + order[::-1]
                for code in range(self.shards):
                    device = side * weight[self.first]
                    device += sum(weight[d] for i, d in enumerate(dims) if (code >> i) & 1)
                    row = part * self.rows + code * self.shard
                    places[side, row] = device * each + part * self.shard
        half = blocks // 4
        found = []
        for block in range(blocks):
            side = block % (2 * half) // half
            local = block // (2 * half) * half + block % half
            for row in range(0, width, self.shard):
                found.append(places[side, local * width + row])
        return found

    def codes(self):
        found = []
        for order in self.orders:
            code = upper(self.last)
            for at, dim in enumerate(reversed(order)):
                code += upper(dim) << (at + 1)
            found.append(code)
        return [code.astype(jnp.int32) for code in found]


class Chain:
    def __init__(self):
        self.token = None

    def tie(self, values):
        if self.token is None:
            return values
        return lax.optimization_barrier((values, self.token))[0]

    def mark(self, values):
        self.token = values
        return values


def scatter_steps(plan, chain, keep, got, found):
    pairs = [[keep, got]] * PARTS
    bases = [i * plan.rows for i in range(PARTS)]
    size = plan.rows
    for step in range(len(plan.orders[0])):
        pairs = chain.tie(pairs)
        size //= 2
        dims = [order[step] for order in plan.orders]

        def halves(pair, base, at):
            return total_of([lax.dynamic_slice_in_dim(p, base + at * size, size, 0) for p in pair])

        sends = [halves(p, base, 1 - upper(d)) for p, base, d in zip(pairs, bases, dims)]
        chain.mark(sends)
        mine = [halves(p, base, upper(d)) for p, base, d in zip(pairs, bases, dims)]
        pairs = [[m, swap(s, d)] for m, s, d in zip(mine, sends, dims)]
        bases = [0] * PARTS
        yield
    size = plan.shard
    bit = upper(plan.last)
    pairs = chain.tie(pairs)

    def side(at):
        return jnp.concatenate(
            [total_of([lax.dynamic_slice_in_dim(p, at * size, size, 0) for p in pair]) for pair in pairs],
            axis=0,
        )

    send = chain.mark(side(1 - bit))
    shard = side(bit)
    got = swap(send, plan.last)
    yield
    shard, got = chain.tie((shard, got))
    shard = total_of([shard, got])
    for dim in plan.plain:
        shard = total_of([shard, swap(shard, dim)])
    found.append(chain.mark(shard))
    yield


def gather_steps(plan, chain, shard, found):
    size = plan.shard
    got = swap(shard, plan.last)
    yield
    values = [(shard[i * size : (i + 1) * size], got[i * size : (i + 1) * size]) for i in range(PARTS)]
    for step in reversed(range(len(plan.orders[0]))):
        values = chain.tie(values)
        values = [jnp.concatenate(pair, axis=0) for pair in values]
        chain.mark(values)
        values = [(v, swap(v, order[step])) for v, order in zip(values, plan.orders)]
        yield
    values = chain.tie(values)
    chain.mark(values)
    found += [v for pair in values for v in pair]
    found += [swap(v, plan.first) for v in found]
    yield


def place(plan, refs, codes, row, store):
    part = row // plan.rows
    shard = ((row % plan.rows) // plan.shard) ^ codes[part]
    half = plan.shards // 2
    at = pl.ds(pl.multiple_of((shard & (half - 1)) * plan.shard, plan.shard), plan.shard)
    low, high = refs[2 * part][at, :], refs[2 * part + 1][at, :]
    store(jnp.where(shard >= half, high.astype(f32), low.astype(f32)))


def dense_place_kernel(
    shard, each, table_ref, group_ref, all_ref, down_ref, up_ref, vec_ref, pool_ref, hold_ref, word_ref, sems, word_sem
):
    step, steps = pl.program_id(0), pl.num_programs(0)
    width = down_ref.shape[1]
    parts = width // shard
    devices = word_ref.shape[0]

    @pl.when(step == 0)
    def _():
        def fetch(block, carry):
            for i in range(parts):
                at = pl.multiple_of(table_ref[block * parts + i], SHARD_STEP)
                pltpu.make_async_copy(
                    all_ref.at[pl.ds(at, shard)],
                    hold_ref.at[block, pl.ds(i * shard, shard)],
                    sems.at[block],
                ).start()
            return carry

        lax.fori_loop(0, steps, fetch, 0)

        def words(device, carry):
            pltpu.make_async_copy(
                all_ref.at[pl.ds(pl.multiple_of(device * each + each - 2 * SUM_ROWS, SHARD_STEP), 2 * SUM_ROWS)],
                word_ref.at[device],
                word_sem,
            ).start()
            return carry

        lax.fori_loop(0, devices, words, 0)

    pltpu.make_async_copy(all_ref.at[pl.ds(0, width)], hold_ref.at[step], sems.at[step]).wait()

    @pl.when(step < steps // 2)
    def _():
        down_ref[...] = hold_ref[step].astype(f32)

    @pl.when(step >= steps // 2)
    def _():
        up_ref[...] = hold_ref[step].astype(f32)

    @pl.when(step == steps - 1)
    def _():
        pltpu.make_async_copy(word_ref, word_ref, word_sem).wait()

        def both(device):
            return word_ref[device, :SUM_ROWS].astype(f32) + word_ref[device, SUM_ROWS:].astype(f32)

        vec_ref[...] = lax.fori_loop(
            0, devices, lambda i, total: total + both(i), jnp.zeros(vec_ref.shape, f32)
        )
        for i in range(pool_ref.shape[0]):
            pool_ref[i] = both(group_ref[0] + i)[POOL_ROW:]


def dense_place(plan, gathered, each, width, wide, devices, seq_count, group):
    table = jnp.array(plan.table(2 * wide, width, each), jnp.int32)
    return pl.pallas_call(
        functools.partial(dense_place_kernel, plan.shard, each),
        grid_spec=pltpu.PrefetchScalarGridSpec(
            num_scalar_prefetch=2,
            grid=(2 * wide,),
            in_specs=[pl.BlockSpec(memory_space=pl.ANY)],
            out_specs=[
                pl.BlockSpec((width, width), lambda i, *_: (jnp.minimum(i, wide - 1), 0)),
                pl.BlockSpec((width, width), lambda i, *_: (0, jnp.maximum(i - wide, 0))),
                pl.BlockSpec((SUM_ROWS, width), lambda i, *_: (0, 0)),
                pl.BlockSpec((seq_count, SUM_ROWS - POOL_ROW, width), lambda i, *_: (0, 0, 0)),
            ],
            scratch_shapes=[
                pltpu.VMEM((2 * wide, width, width), bf16),
                pltpu.VMEM((devices, 2 * SUM_ROWS, width), bf16),
                pltpu.SemaphoreType.DMA((2 * wide,)),
                pltpu.SemaphoreType.DMA(()),
            ],
        ),
        out_shape=[
            jax.ShapeDtypeStruct((wide * width, width), f32),
            jax.ShapeDtypeStruct((width, wide * width), f32),
            jax.ShapeDtypeStruct((SUM_ROWS, width), f32),
            jax.ShapeDtypeStruct((seq_count, SUM_ROWS - POOL_ROW, width), f32),
        ],
        compiler_params=PARAMS,
        cost_estimate=cost(0, 12 * wide * width * width),
    )(table, group, gathered)


def attend_place_kernel(plan, first_code, at, flip, info_ref, *refs):
    sources, (hold_ref, sems) = refs[: 2 * PARTS], refs[-2:]
    outs = refs[-6:-2]
    codes = [info_ref[first_code + i] for i in range(PARTS)]
    own = info_ref[at] ^ flip
    width = hold_ref.shape[2]

    def move(block, act):
        for side in range(2):

            @pl.when(own == side)
            def _():
                act(pltpu.make_async_copy(hold_ref.at[block], outs[2 * side + block], sems.at[block]))

    for block in range(2):
        for row in range(0, width, plan.shard):

            def store(value, row=row):
                hold_ref[block, row : row + plan.shard, :] = value

            place(plan, sources, codes, block * width + row, store)
        move(block, lambda copy: copy.start())
    for block in range(2):
        move(block, lambda copy: copy.wait())


def attend_place(plan, first_code, at, flip, info, sources, width, before):
    kept = list(before)
    return pl.pallas_call(
        functools.partial(attend_place_kernel, plan, first_code, at, flip),
        grid_spec=pltpu.PrefetchScalarGridSpec(
            num_scalar_prefetch=1,
            grid=(1,),
            in_specs=[fixed(x.shape) for x in sources]
            + [pl.BlockSpec(memory_space=pl.ANY)] * len(kept),
            out_specs=[pl.BlockSpec(memory_space=pl.ANY)] * 4,
            scratch_shapes=[pltpu.VMEM((2, width, width), f32), pltpu.SemaphoreType.DMA((2,))],
        ),
        out_shape=[jax.ShapeDtypeStruct((width, width), f32)] * 4,
        input_output_aliases={1 + len(sources) + i: i for i in range(len(kept))},
        compiler_params=SMALL,
        cost_estimate=cost(0, 12 * width * width),
    )(info, *sources, *kept)


def shards(
    tokens,
    lengths,
    w_query,
    b_query,
    w_key,
    w_value,
    b_value,
    w_out,
    b_out,
    gain_one,
    shift_one,
    w_up,
    b_up,
    w_down,
    b_down,
    gain_two,
    shift_two,
    out_grad,
    pooled_grad,
):
    seq_count = lax.axis_size("seq")
    held, piece, width = tokens.shape
    full = piece * seq_count
    count = held // seq_count
    mine = lax.axis_index("seq")
    wide = w_up.shape[1] // width
    total = count * full

    def flat(value):
        return value.reshape(total, width)

    def split(value):
        return value.reshape(count, full, width)

    dense_plan = Plan(wide * width)
    outer_plan = Plan(2 * width)
    first = axis_bits("seq")[0]
    scalars = [mine, upper(first)] + dense_plan.codes() + outer_plan.codes()
    own_at, dense_at, outer_at = held + 1, held + 2, held + 2 + PARTS
    info = jnp.concatenate([lengths, jnp.stack([v.astype(jnp.int32) for v in scalars])])
    vecs = jnp.concatenate(
        [b_query, b_value, b_out, gain_one, shift_one, b_down, gain_two, shift_two, b_up]
    )
    vecs = vecs.astype(f32).reshape(-1, width)

    weights = [w_query, w_key, w_value, vecs]
    done = None
    source = tokens
    parts = []
    for passage in range(count):
        if parts:
            source = lax.optimization_barrier((tokens, parts))[0]
        slices = [
            lax.dynamic_slice_in_dim(source, (mine ^ mask) * count + passage, 1, 0)
            for mask in range(1, seq_count)
        ]
        parts = [exchange(value, "seq", mask + 1) for mask, value in enumerate(slices)]
        done = attend(passage, count, info, tokens, parts, weights, done)
    stacked, q, k, v, stat = done
    cot = to_passages(lax.optimization_barrier((out_grad, slices))[0])
    stacked = stacked.reshape(2, total, width)
    result, first_low, act, second, inner, branch_in, mixed_grad, sums = row_work(
        held, info, stacked, flat(cot), pooled_grad, w_out, w_up, w_down, vecs, count
    )
    chain = Chain()
    pieces = chain.mark(position_pieces(split(result)))
    out_pieces = traded(pieces)
    send = dense_outer(own_at, 1, info, *chain.tie((act, second, first_low, inner)))
    chain.mark(send)
    got = swap(send, first)
    keep = chain.mark(dense_outer(own_at, 0, info, *chain.tie((act, second, first_low, inner))))
    dense, shard, outer = [], [], []
    dense_steps = scatter_steps(dense_plan, chain, keep, got, dense)
    next(dense_steps)
    chain.mark((chain.token, out_pieces))
    block_out = to_positions(out_pieces)
    grads, words = attend_back(
        held,
        info,
        q,
        k,
        v,
        chain.tie(split(mixed_grad)),
        stacked.reshape(2, count, full, width),
        split(branch_in),
        stat,
        sums,
    )
    chain.mark(words)
    grads = grads.reshape(4, total, width)
    next(dense_steps)
    send = attend_outer(own_at, 1, info, stacked, chain.tie(grads))
    chain.mark(send)
    got = swap(send, first)
    keep = attend_outer(own_at, 0, info, stacked, chain.tie(grads))
    chain.mark(keep)
    next(dense_steps)
    outer_steps = scatter_steps(outer_plan, chain, keep, got, shard)
    next(outer_steps)
    next(dense_steps)
    input_low = input_grad(branch_in, chain.tie(grads), w_query, w_key, w_value)
    chain.mark(input_low)
    next(outer_steps)
    for _ in dense_steps:
        pass
    gathered = jnp.concatenate([dense[0], words], axis=0)
    each = gathered.shape[0]
    gathered = chain.mark(gathered)
    gathered = lax.all_gather(gathered, ("dp", "seq"), axis=0, tiled=True)
    next(outer_steps)
    next(outer_steps)
    pieces = chain.mark(position_pieces(split(chain.tie(input_low))))
    in_pieces = traded(pieces)
    for _ in outer_steps:
        pass
    outer_steps = gather_steps(outer_plan, chain, shard[0], outer)
    next(outer_steps)
    chain.mark((chain.token, in_pieces))
    next(outer_steps)
    next(outer_steps)
    next(outer_steps)
    tokens_grad = to_positions(in_pieces)
    chain.mark((chain.token, tokens_grad, block_out))
    for _ in outer_steps:
        pass
    group = (lax.axis_index("dp") * seq_count).astype(jnp.int32)[None]

    def place_outer(flip, before):
        pick = outer[2 * PARTS :] if flip else outer[: 2 * PARTS]
        return chain.mark(
            attend_place(outer_plan, outer_at, own_at, flip, info, chain.tie(pick), width, before)
        )

    placed = place_outer(0, [])
    outer = place_outer(1, placed)
    down_sum, up_sum, vectors, pooled = dense_place(
        dense_plan, chain.tie(gathered), each, width, wide, gathered.shape[0] // each, seq_count, group
    )
    pooled = pooled[:, :count].reshape(held, width)
    return (
        block_out,
        pooled,
        tokens_grad,
        outer[0],
        vectors[0],
        outer[1],
        outer[2],
        vectors[1],
        outer[3],
        vectors[2],
        vectors[3],
        vectors[4],
        up_sum,
        vectors[8 : 8 + wide].reshape(-1),
        down_sum,
        vectors[5],
        vectors[6],
        vectors[7],
    )


def solution(mesh):
    in_specs = (
        (P("dp", "seq", None), P("dp"))
        + (P(),) * 15
        + (P("dp", "seq", None), P("dp", None))
    )
    out_specs = (P("dp", "seq", None), P("dp", None), P("dp", "seq", None)) + (P(),) * 15
    return jax.shard_map(shards, mesh=mesh, in_specs=in_specs, out_specs=out_specs, check_vma=False)
```

```python
import functools

import jax
import jax.numpy as jnp
from jax import lax
from jax.experimental import pallas as pl
from jax.experimental.pallas import tpu as pltpu
from jax.sharding import PartitionSpec as P

HEADS = 12
HEAD_DIM = 64
PAIR = 2 * HEAD_DIM
PAIRS = HEADS // 2
SCALE = HEAD_DIM ** (-0.5)
ROWS = 256
BACK_ROWS = 256
STRIP = 32
TOGETHER = 1
BACK_TOGETHER = 1
STAT_ROWS = 16
CHUNK = 256
ROW_CHUNK = 768
KEY_STEP = 128
VMEM_BYTES = 62 * 1024 * 1024
SMALL_BYTES = 40 * 1024 * 1024
SUM_ROWS = 16
POOL_ROW = 12

eps = 1e-06
root_half = 0.7071067811865476
inv_root_two_pi = 0.3989422804014327

f32 = jnp.float32
bf16 = jnp.bfloat16

NN = (((1,), (0,)), ((), ()))
NT = (((1,), (1,)), ((), ()))
TN = (((0,), (0,)), ((), ()))


def mul(left, right, dims=NN):
    return lax.dot_general(left, right, dims, preferred_element_type=f32)


def fixed(shape):
    return pl.BlockSpec(shape, lambda *_: (0,) * len(shape), pipeline_mode=pl.Buffered(1))


PARAMS = pltpu.CompilerParams(dimension_semantics=("arbitrary",), vmem_limit_bytes=VMEM_BYTES)
SMALL = pltpu.CompilerParams(dimension_semantics=("arbitrary",), vmem_limit_bytes=SMALL_BYTES)


def cost(flops, moved, exps=0):
    return pl.CostEstimate(flops=int(flops), bytes_accessed=int(moved), transcendentals=int(exps))


def over_extents(length, full, body):
    for extent in range(KEY_STEP, full + 1, KEY_STEP):
        pl.when((length > extent - KEY_STEP) & (length <= extent))(functools.partial(body, extent))


def by_eight(value):
    return value.reshape(value.shape[0] // 8, 8, value.shape[1])


def fill_dead(dead_ref, extent, length):
    key_at = lax.broadcasted_iota(jnp.int32, dead_ref.shape, 0) + (extent - KEY_STEP)
    dead_ref[...] = jnp.where(key_at < length, 0.0, -1e30)


def live_strip(scores, dead_ref, extent, row):
    strip = scores[row : row + STRIP]
    last = row - (extent - KEY_STEP)
    return strip + dead_ref[last : last + STRIP] if last >= 0 else strip


def attend_kernel(pieces, passage, count, held, info_ref, *refs):
    part_refs, refs = refs[:pieces], refs[pieces:]
    wq_ref, wk_ref, wv_ref, vec_ref = refs[:4]
    xm_ref, q_ref, k_ref, v_ref, stat_ref, prob_ref, dead_ref = refs[-7:]
    x_ref, mix_ref = xm_ref.at[0], xm_ref.at[1]
    mine = info_ref[held]
    length = info_ref[mine * count + passage]
    size = part_refs[0].shape[1]
    for mask, part_ref in enumerate(part_refs):
        x_ref[0, pl.ds(pl.multiple_of((mine ^ mask) * size, size), size)] = part_ref[0]

    def project(index, carry):
        at = pl.ds(pl.multiple_of(index * CHUNK, CHUNK), CHUNK)
        x = x_ref[0]
        q_ref[0, :, at] = (mul(x, wq_ref[:, at]) + vec_ref[0:1, at]).astype(bf16)
        k_ref[0, :, at] = mul(x, wk_ref[:, at]).astype(bf16)
        v_ref[0, :, at] = (mul(x, wv_ref[:, at]) + vec_ref[1:2, at]).astype(bf16)
        return carry

    lax.fori_loop(0, wq_ref.shape[1] // CHUNK, project, 0)
    stat_ref[0] = jnp.zeros(stat_ref.shape[1:], f32)
    full = size * pieces
    lane = lax.broadcasted_iota(jnp.int32, (1, PAIR), 1)

    def run(extent):
        fill_dead(dead_ref, extent, length)

        def head(at, number, half, slot):
            q, k = q_ref[0, :, at], k_ref[0, :extent, at]
            own = (lane >= half * HEAD_DIM) & (lane < (half + 1) * HEAD_DIM)
            scores = mul(jnp.where(own, k * SCALE, 0).astype(bf16), q, NT)
            top = jnp.full((8, full), -jnp.inf, f32)
            for row in range(0, extent, STRIP):
                top = jnp.maximum(top, by_eight(live_strip(scores, dead_ref, extent, row)).max(axis=0))
            top = jnp.max(top, axis=0, keepdims=True)
            total = jnp.zeros((8, full), f32)
            for row in range(0, extent, STRIP):
                expo = jnp.exp(live_strip(scores, dead_ref, extent, row) - top)
                total += by_eight(expo).sum(axis=0)
                prob_ref[slot, row : row + STRIP] = expo.astype(bf16)
            total = jnp.sum(total, axis=0, keepdims=True)
            stat_ref[0, pl.ds(number, 1), :] = top + jnp.log(total)
            return 1.0 / total

        def group(index, carry):
            for i in range(TOGETHER):
                pair = index * TOGETHER + i
                at = pl.ds(pl.multiple_of(pair * PAIR, PAIR), PAIR)
                values = v_ref[0, :extent, at].T
                mixed = []
                for half in range(2):
                    slot = 2 * i + half
                    scale = head(at, pair * 2 + half, half, slot)
                    own = values[half * HEAD_DIM : (half + 1) * HEAD_DIM]
                    mixed.append(mul(own, prob_ref[slot, :extent]) * scale)
                mix_ref[0, :, at] = jnp.concatenate(mixed, axis=0).T.astype(bf16)
            return carry

        lax.fori_loop(0, PAIRS // TOGETHER, group, 0)

    over_extents(length, full, run)


def attend(passage, count, info, tokens, parts, weights, before):
    held, piece, width = tokens.shape
    pieces = len(parts) + 1
    full = piece * pieces
    rows = pl.BlockSpec((1, full, width), lambda i, s: (passage, 0, 0))
    act = jax.ShapeDtypeStruct((count, full, width), bf16)
    got = pl.BlockSpec((1, piece, width), lambda i, s: (0, 0, 0))
    kept = [] if before is None else list(before)
    first_kept = 1 + pieces + len(weights)
    return pl.pallas_call(
        functools.partial(attend_kernel, pieces, passage, count, held),
        grid_spec=pltpu.PrefetchScalarGridSpec(
            num_scalar_prefetch=1,
            grid=(1,),
            in_specs=[pl.BlockSpec((1, piece, width), lambda i, s: (s[held] * count + passage, 0, 0))]
            + [got] * len(parts)
            + [fixed(w.shape) for w in weights]
            + [pl.BlockSpec(memory_space=pl.ANY)] * len(kept),
            out_specs=[pl.BlockSpec((2, 1, full, width), lambda i, s: (0, passage, 0, 0))]
            + [rows] * 3
            + [pl.BlockSpec((1, STAT_ROWS, full), lambda i, s: (passage, 0, 0))],
            scratch_shapes=[
                pltpu.VMEM((2 * TOGETHER, full, full), bf16),
                pltpu.VMEM((KEY_STEP, full), f32),
            ],
        ),
        out_shape=[jax.ShapeDtypeStruct((2, count, full, width), bf16)]
        + [act] * 3
        + [jax.ShapeDtypeStruct((count, STAT_ROWS, full), f32)],
        input_output_aliases={first_kept + i: i for i in range(len(kept))},
        compiler_params=PARAMS,
        cost_estimate=cost(
            2 * full * (3 * width * width + 4 * 2 * full * width),
            12 * full * width + 6 * width * width,
        ),
    )(info, tokens, *parts, *weights, *kept)


def attend_back_kernel(
    held,
    info_ref,
    q_ref,
    k_ref,
    v_ref,
    mg_ref,
    mix_ref,
    branch_ref,
    stat_ref,
    sum_ref,
    grads_ref,
    word_ref,
    bias_ref,
    along_ref,
    prob_ref,
    score_ref,
    dead_ref,
):
    dq_ref, dk_ref, dv_ref = (grads_ref.at[i] for i in range(3))
    grads_ref[3] = branch_ref[...].astype(bf16)
    full, width = q_ref.shape[1:]
    length = info_ref[info_ref[held] * pl.num_programs(0) + pl.program_id(0)]
    lane = lax.broadcasted_iota(jnp.int32, (1, PAIR), 1)
    row = lax.broadcasted_iota(jnp.int32, (8, 1), 0)

    @pl.when(pl.program_id(0) == 0)
    def _():
        bias_ref[...] = sum_ref[...]

    feature = lax.broadcasted_iota(jnp.int32, (STAT_ROWS, width), 1)
    number = lax.broadcasted_iota(jnp.int32, (STAT_ROWS, width), 0)
    ours = jnp.where(
        (feature >= number * HEAD_DIM) & (feature < (number + 1) * HEAD_DIM), 1.0, 0.0
    ).astype(bf16)
    product = mg_ref[0].astype(f32) * mix_ref[0, 0].astype(f32)
    high = product.astype(bf16)
    low = (product - high.astype(f32)).astype(bf16)
    along_ref[...] = mul(ours, high, NT) + mul(ours, low, NT)

    def run(extent):
        fill_dead(dead_ref, extent, length)
        if extent < full:
            dk_ref[0, extent:] = jnp.zeros((full - extent, width), bf16)
            dv_ref[0, extent:] = jnp.zeros((full - extent, width), bf16)

        def group(index, carry):
            for i in range(BACK_TOGETHER):
                pair = index * BACK_TOGETHER + i
                at = pl.ds(pl.multiple_of(pair * PAIR, PAIR), PAIR)
                q, mg = q_ref[0, :, at], mg_ref[0, :, at]
                k, v = k_ref[0, :extent, at], v_ref[0, :extent, at]
                keys = k.T
                dq, dk, dv = [], [], []
                for half in range(2):
                    slot = 2 * i + half
                    own = (lane >= half * HEAD_DIM) & (lane < (half + 1) * HEAD_DIM)
                    scores = mul(jnp.where(own, k * SCALE, 0).astype(bf16), q, NT)
                    prob_grad = mul(jnp.where(own, v, 0).astype(bf16), mg, NT)
                    log_row = stat_ref[0, pl.ds(pair * 2 + half, 1), :]
                    along = along_ref[pl.ds(pair * 2 + half, 1), :]
                    for at_row in range(0, extent, STRIP):
                        rows = slice(at_row, at_row + STRIP)
                        probs = jnp.exp(live_strip(scores, dead_ref, extent, at_row) - log_row)
                        prob_ref[slot, rows] = probs.astype(bf16)
                        score_ref[slot, rows] = (probs * (prob_grad[rows] - along)).astype(bf16)
                    score_grad = score_ref[slot, :extent]
                    dv.append(mul(prob_ref[slot, :extent], mg))
                    dk.append(mul(score_grad, q))
                    dq.append(mul(keys[half * HEAD_DIM : (half + 1) * HEAD_DIM], score_grad))
                first = lane < HEAD_DIM
                dq_pair = jnp.concatenate(dq, axis=0).T * SCALE
                dk_pair = jnp.where(first, dk[0], dk[1]) * SCALE
                dv_pair = jnp.where(first, dv[0], dv[1])
                dq_ref[0, :, at] = dq_pair.astype(bf16)
                dk_ref[0, :extent, at] = dk_pair.astype(bf16)
                dv_ref[0, :extent, at] = dv_pair.astype(bf16)
                sums = jnp.where(
                    row == 0,
                    jnp.sum(dq_pair, axis=0, keepdims=True),
                    jnp.where(row == 1, jnp.sum(dv_pair, axis=0, keepdims=True), 0.0),
                )
                bias_ref[0:8, at] += sums
            return carry

        lax.fori_loop(0, PAIRS // BACK_TOGETHER, group, 0)

    over_extents(length, full, run)

    @pl.when(pl.program_id(0) == pl.num_programs(0) - 1)
    def _():
        high = bias_ref[...].astype(bf16)
        word_ref[:SUM_ROWS] = high
        word_ref[SUM_ROWS:] = (bias_ref[...] - high.astype(f32)).astype(bf16)


def attend_back(held, info, q, k, v, mixed_grad, stacked, branch_in, stat, sums):
    count, full, width = q.shape
    rows = pl.BlockSpec((1, full, width), lambda i, *_: (i, 0, 0))
    return pl.pallas_call(
        functools.partial(attend_back_kernel, held),
        grid_spec=pltpu.PrefetchScalarGridSpec(
            num_scalar_prefetch=1,
            grid=(count,),
            in_specs=[rows] * 4
            + [
                pl.BlockSpec((1, 1, full, width), lambda i, *_: (1, i, 0, 0)),
                rows,
                pl.BlockSpec((1, STAT_ROWS, full), lambda i, *_: (i, 0, 0)),
                fixed(sums.shape),
            ],
            out_specs=[
                pl.BlockSpec((4, 1, full, width), lambda i, *_: (0, i, 0, 0)),
                pl.BlockSpec((2 * SUM_ROWS, width), lambda i, *_: (0, 0)),
            ],
            scratch_shapes=[
                pltpu.VMEM(sums.shape, f32),
                pltpu.VMEM((STAT_ROWS, full), f32),
                pltpu.VMEM((2 * BACK_TOGETHER, full, full), bf16),
                pltpu.VMEM((2 * BACK_TOGETHER, full, full), bf16),
                pltpu.VMEM((KEY_STEP, full), f32),
            ],
        ),
        out_shape=[
            jax.ShapeDtypeStruct((4, count, full, width), bf16),
            jax.ShapeDtypeStruct((2 * SUM_ROWS, width), bf16),
        ],
        compiler_params=PARAMS,
        cost_estimate=cost(
            2 * count * full * 10 * 2 * full * width, 16 * count * full * width
        ),
    )(info, q, k, v, mixed_grad, stacked, branch_in, stat, sums)


def norm_parts(hidden):
    centred = hidden - jnp.mean(hidden, axis=1, keepdims=True)
    inv_scale = lax.rsqrt(jnp.mean(centred * centred, axis=1, keepdims=True) + eps)
    return centred * inv_scale, inv_scale


def norm_back(scaled, normed, inv_scale):
    mean = jnp.mean(scaled, axis=1, keepdims=True)
    along = jnp.mean(scaled * normed, axis=1, keepdims=True)
    return (scaled - mean - normed * along) * inv_scale


def gelu_parts(u):
    expo = jnp.exp(u * u * -0.5)
    base = 1.0 + jnp.abs(u) * (0.3275911 * root_half)
    t = pl.reciprocal(base, approx=True)
    t = t * (2.0 - base * t)
    poly = t * (
        0.5 * 0.254829592
        + t
        * (
            0.5 * -0.284496736
            + t * (0.5 * 1.421413741 + t * (0.5 * -1.453152027 + t * (0.5 * 1.061405429)))
        )
    )
    tail = poly * expo
    return jnp.where(u >= 0, 1.0 - tail, tail), expo


def rows_kernel(
    blocks,
    count,
    held,
    info_ref,
    x_ref,
    mix_ref,
    cot_ref,
    pool_ref,
    wo_ref,
    vec_ref,
    wu_all,
    wd_all,
    out_ref,
    low_ref,
    act_all,
    second_ref,
    inner_all,
    branch_ref,
    mg_ref,
    sum_ref,
    wu_ref,
    wd_ref,
    act_ref,
    inner_ref,
    slope_ref,
    first_ref,
    normed_ref,
    total_ref,
    scale_ref,
    sems,
):
    step, steps = pl.program_id(0), pl.num_programs(0)
    rows, width = cot_ref.shape
    hidden_width = wu_ref.shape[1]
    b_out, gain_one, shift_one, b_down, gain_two, shift_two = (
        vec_ref[i : i + 1] for i in range(2, 8)
    )
    passage = info_ref[held] * count + step // blocks
    length = info_ref[passage]
    inv_length = 1.0 / jnp.full((1, width), length, jnp.int32).astype(f32)
    pool = pool_ref[pl.ds(passage, 1), :] * inv_length
    first_row = (step % blocks) * rows
    load_up = pltpu.make_async_copy(wu_all, wu_ref, sems.at[0])
    load_down = pltpu.make_async_copy(wd_all, wd_ref, sems.at[1])

    def give(source_ref, all_ref, at):
        return pltpu.make_async_copy(
            source_ref, all_ref.at[pl.ds(pl.multiple_of(at * rows, rows), rows)], sems.at[2 if source_ref is act_ref else 3]
        )

    @pl.when(step == 0)
    def _():
        load_up.start()
        load_down.start()
        sum_ref[...] = jnp.zeros(sum_ref.shape, f32)

    def tally(at, value, columns=slice(None)):
        sum_ref[at : at + 1, columns] += jnp.sum(value, axis=0, keepdims=True)

    def strips(size):
        return [slice(i, i + size) for i in range(0, rows, size)]

    groups = width // ROW_CHUNK
    chunks = hidden_width // ROW_CHUNK
    part = [slice(i * ROW_CHUNK, (i + 1) * ROW_CHUNK) for i in range(chunks)]
    whole = [slice(i * width, (i + 1) * width) for i in range(hidden_width // width)]
    lanes = scale_ref.shape[1]

    branch = mul(mix_ref[0], wo_ref[...])
    for at in strips(STRIP):
        normed, scale = norm_parts(x_ref[0, at].astype(f32) + branch[at] + b_out)
        first = normed * gain_one + shift_one
        normed_ref[at] = normed
        scale_ref[at] = jnp.broadcast_to(scale, (STRIP, lanes))
        first_ref[at] = first + b_down
        low_ref[at] = first.astype(bf16)

    @pl.when(step == 0)
    def _():
        load_up.wait()
        load_down.wait()

    @pl.when(step > 0)
    def _():
        give(act_ref, act_all, step - 1).wait()

    def up(i):
        return mul(low_ref[...], wu_ref[:, part[i]])

    pre = up(0)
    for i in range(chunks):
        ahead = up(i + 1) if i + 1 < chunks else None
        bias = vec_ref[8 + i // groups : 9 + i // groups, part[i % groups]]
        for at in strips(STRIP):
            u = pre[at] + bias
            phi, expo = gelu_parts(u)
            act_ref[at, part[i]] = (u * phi).astype(bf16)
            slope_ref[at, part[i]] = phi + u * expo * inv_root_two_pi
        if i % groups == 0 and i:
            done = whole[i // groups - 1]
            first_ref[...] += mul(act_ref[:, done], wd_ref[done, :])
        pre = ahead
    last = mul(act_ref[:, whole[-1]], wd_ref[whole[-1], :])
    give(act_ref, act_all, step).start()

    pooled, shift, gain, down = (jnp.zeros((8, width), f32) for _ in range(4))
    for at in strips(STRIP):
        normed, scale = norm_parts(first_ref[at] + last[at])
        result = normed * gain_two + shift_two
        out_ref[at] = result.astype(bf16)
        row_at = lax.broadcasted_iota(jnp.int32, (STRIP, 1), 0) + (first_row + at.start)
        live = jnp.where(row_at < length, 1.0, 0.0)
        pooled += by_eight(result * live).sum(axis=0)
        upstream = cot_ref[at].astype(f32) + live * pool
        gain += by_eight(upstream * normed).sum(axis=0)
        shift += by_eight(upstream).sum(axis=0)
        second_in = norm_back(upstream * gain_two, normed, scale)
        down += by_eight(second_in).sum(axis=0)
        total_ref[at] = second_in
        second_ref[at] = second_in.astype(bf16)
    tally(6, gain)
    tally(7, shift)
    tally(5, down)
    sum_ref[pl.ds(POOL_ROW + step // blocks, 1), :] += (
        jnp.sum(pooled, axis=0, keepdims=True) * inv_length
    )

    @pl.when(step > 0)
    def _():
        give(inner_ref, inner_all, step - 1).wait()

    def back(i):
        return mul(second_ref[...], wd_ref[part[i], :], NT)

    grad = back(0)
    for i in range(chunks):
        ahead = back(i + 1) if i + 1 < chunks else None
        bias = jnp.zeros((8, ROW_CHUNK), f32)
        for at in strips(STRIP):
            inner = grad[at] * slope_ref[at, part[i]]
            bias += by_eight(inner).sum(axis=0)
            inner_ref[at, part[i]] = inner.astype(bf16)
        tally(8 + i // groups, bias, part[i % groups])
        if i % groups == 0 and i:
            done = whole[i // groups - 1]
            total_ref[...] += mul(inner_ref[:, done], wu_ref[:, done], NT)
        grad = ahead
    last = mul(inner_ref[:, whole[-1]], wu_ref[:, whole[-1]], NT)
    give(inner_ref, inner_all, step).start()

    gain, shift, out = (jnp.zeros((8, width), f32) for _ in range(3))
    for at in strips(STRIP):
        first_up = total_ref[at] + last[at]
        normed = normed_ref[at]
        gain += by_eight(first_up * normed).sum(axis=0)
        shift += by_eight(first_up).sum(axis=0)
        branch_in = norm_back(first_up * gain_one, normed, scale_ref[at, :1])
        out += by_eight(branch_in).sum(axis=0)
        branch_ref[at] = branch_in
    tally(3, gain)
    tally(4, shift)
    tally(2, out)
    mg_ref[...] = mul(branch_ref[...].astype(bf16), wo_ref[...], NT).astype(bf16)

    @pl.when(step == steps - 1)
    def _():
        give(act_ref, act_all, step).wait()
        give(inner_ref, inner_all, step).wait()


def row_work(held, info, stacked, cot, pool, w_out, w_up, w_down, vecs, count):
    total, width = cot.shape
    full = total // count
    assert POOL_ROW + count <= SUM_ROWS
    hidden = w_up.shape[1]
    blocks = full // ROWS
    narrow = pl.BlockSpec((ROWS, width), lambda i, *_: (i, 0))
    anywhere = pl.BlockSpec(memory_space=pl.ANY)
    thin = jax.ShapeDtypeStruct((total, width), bf16)
    thick = jax.ShapeDtypeStruct((total, hidden), bf16)
    return pl.pallas_call(
        functools.partial(rows_kernel, blocks, count, held),
        grid_spec=pltpu.PrefetchScalarGridSpec(
            num_scalar_prefetch=1,
            grid=(total // ROWS,),
            in_specs=[
                pl.BlockSpec((1, ROWS, width), lambda i, *_: (0, i, 0)),
                pl.BlockSpec((1, ROWS, width), lambda i, *_: (1, i, 0)),
                narrow,
                fixed(pool.shape),
                fixed((width, width)),
                fixed(vecs.shape),
                anywhere,
                anywhere,
            ],
            out_specs=[
                narrow,
                narrow,
                anywhere,
                narrow,
                anywhere,
                narrow,
                narrow,
                pl.BlockSpec((SUM_ROWS, width), lambda i, *_: (0, 0)),
            ],
            scratch_shapes=[
                pltpu.VMEM((width, hidden), bf16),
                pltpu.VMEM((hidden, width), bf16),
                pltpu.VMEM((ROWS, hidden), bf16),
                pltpu.VMEM((ROWS, hidden), bf16),
                pltpu.VMEM((ROWS, hidden), f32),
                pltpu.VMEM((ROWS, width), f32),
                pltpu.VMEM((ROWS, width), f32),
                pltpu.VMEM((ROWS, width), f32),
                pltpu.VMEM((ROWS, PAIR), f32),
                pltpu.SemaphoreType.DMA((4,)),
            ],
        ),
        out_shape=[
            thin,
            thin,
            thick,
            thin,
            thick,
            jax.ShapeDtypeStruct((total, width), f32),
            thin,
            jax.ShapeDtypeStruct((SUM_ROWS, width), f32),
        ],
        compiler_params=PARAMS,
        cost_estimate=cost(
            4 * total * width * (width + 2 * hidden),
            2 * total * (8 * width + 2 * hidden) + 2 * width * (width + 2 * hidden),
        ),
    )(info, stacked, stacked, cot, pool, w_out, vecs, w_up, w_down)


def dense_outer_kernel(side_ref, act_ref, second_ref, low_ref, inner_ref, out_ref):
    step = pl.program_id(0)
    half = pl.num_programs(0) // 2

    @pl.when(step < half)
    def _():
        out_ref[0] = mul(act_ref[...], second_ref[...], TN).astype(bf16)

    @pl.when(step >= half)
    def _():
        out_ref[0] = mul(low_ref[...], inner_ref[...], TN).astype(bf16)


def dense_outer(at, flip, info, act, second, low, inner):
    total, width = second.shape
    wide = act.shape[1] // width
    half = wide // 2
    return pl.pallas_call(
        dense_outer_kernel,
        grid_spec=pltpu.PrefetchScalarGridSpec(
            num_scalar_prefetch=1,
            grid=(wide,),
            in_specs=[
                pl.BlockSpec(
                    (total, width), lambda i, s: (0, (s[at] ^ flip) * half + jnp.minimum(i, half - 1))
                ),
                fixed((total, width)),
                fixed((total, width)),
                pl.BlockSpec(
                    (total, width), lambda i, s: (0, (s[at] ^ flip) * half + jnp.maximum(i - half, 0))
                ),
            ],
            out_specs=pl.BlockSpec((1, width, width), lambda i, s: (i, 0, 0)),
        ),
        out_shape=jax.ShapeDtypeStruct((wide, width, width), bf16),
        compiler_params=PARAMS,
        cost_estimate=cost(
            2 * total * width * width * wide, 2 * (wide + 2) * total * width + 2 * wide * width * width
        ),
    )(info, act, second, low, inner).reshape(wide * width, width)


def attend_outer_kernel(side_ref, left_ref, right_ref, out_ref):
    out_ref[0] = mul(left_ref[0], right_ref[0], TN).astype(bf16)


def attend_outer(at, flip, info, stacked, grads):
    total, width = stacked.shape[1:]
    return pl.pallas_call(
        attend_outer_kernel,
        grid_spec=pltpu.PrefetchScalarGridSpec(
            num_scalar_prefetch=1,
            grid=(2,),
            in_specs=[
                pl.BlockSpec((1, total, width), lambda i, s: (((s[at] ^ flip) * 2 + i) // 3, 0, 0)),
                pl.BlockSpec((1, total, width), lambda i, s: ((s[at] ^ flip) * 2 + i, 0, 0)),
            ],
            out_specs=pl.BlockSpec((1, width, width), lambda i, s: (i, 0, 0)),
        ),
        out_shape=jax.ShapeDtypeStruct((2, width, width), bf16),
        compiler_params=PARAMS,
        cost_estimate=cost(4 * total * width * width, 8 * total * width + 4 * width * width),
    )(info, stacked, grads).reshape(2 * width, width)


def input_kernel(branch_ref, dq_ref, dk_ref, dv_ref, wq_ref, wk_ref, wv_ref, out_ref):
    total = branch_ref[...] + mul(dq_ref[0], wq_ref[...], NT)
    total += mul(dk_ref[0], wk_ref[...], NT)
    total += mul(dv_ref[0], wv_ref[...], NT)
    out_ref[...] = total.astype(bf16)


def input_grad(branch_in, grads, w_query, w_key, w_value):
    total, width = branch_in.shape
    rows = pl.BlockSpec((BACK_ROWS, width), lambda i: (i, 0))
    return pl.pallas_call(
        input_kernel,
        grid=(total // BACK_ROWS,),
        in_specs=[rows]
        + [pl.BlockSpec((1, BACK_ROWS, width), lambda i, at=at: (at, i, 0)) for at in range(3)]
        + [fixed((width, width))] * 3,
        out_specs=rows,
        out_shape=jax.ShapeDtypeStruct((total, width), bf16),
        compiler_params=SMALL,
        cost_estimate=cost(6 * total * width * width, 12 * total * width + 6 * width * width),
    )(branch_in, grads, grads, grads, w_query, w_key, w_value)


def exchange(value, axis, mask):
    count = lax.axis_size(axis)
    return lax.ppermute(value, axis, [(i, i ^ mask) for i in range(count)])


def to_passages(value):
    count = lax.axis_size("seq")
    mine = lax.axis_index("seq")
    held, piece, width = value.shape
    own = held // count
    whole = jnp.zeros((own, piece * count, width), value.dtype)
    for mask in range(count):
        peer = mine ^ mask
        part = lax.dynamic_slice_in_dim(value, peer * own, own, 0)
        if mask:
            part = exchange(part, "seq", mask)
        whole = lax.dynamic_update_slice_in_dim(whole, part, peer * piece, 1)
    return whole


def position_pieces(value):
    count = lax.axis_size("seq")
    piece = value.shape[1] // count
    mine = lax.axis_index("seq")
    return [
        lax.dynamic_slice_in_dim(value, (mine ^ mask) * piece, piece, 1) for mask in range(count)
    ]


def traded(pieces):
    return [exchange(part, "seq", mask) if mask else part for mask, part in enumerate(pieces)]


def to_positions(pieces):
    mine = lax.axis_index("seq")
    own, piece, width = pieces[0].shape
    result = jnp.zeros((own * len(pieces), piece, width), pieces[0].dtype)
    for mask, part in enumerate(pieces):
        result = lax.dynamic_update_slice_in_dim(result, part, (mine ^ mask) * own, 0)
    return result


def axis_bits(axis):
    return [(axis, 1 << i) for i in range(lax.axis_size(axis).bit_length() - 1)]


def upper(dim):
    axis, mask = dim
    return (lax.axis_index(axis) & mask) // mask


def swap(value, dim):
    return exchange(value, dim[0], dim[1])


def total_of(parts):
    total = parts[0].astype(f32)
    for part in parts[1:]:
        total += part.astype(f32)
    return total.astype(bf16)


PARTS = 3
SHARD_STEP = 16


class Plan:
    def __init__(self, rows):
        dims = axis_bits("seq") + axis_bits("dp")
        self.first = dims[0]
        rest = dims[1:]
        self.rows = rows // PARTS
        halved = 0
        while halved < len(rest) and (self.rows >> (halved + 1)) % SHARD_STEP == 0:
            halved += 1
        self.last = rest[halved - 1]
        self.plain = rest[halved:]
        split = rest[: halved - 1]
        self.orders = [split[i % len(split) :] + split[: i % len(split)] for i in range(PARTS)]
        self.shards = 1 << halved
        self.shard = self.rows >> halved

    def table(self, blocks, width, each):
        places = {}
        devices = 1
        weight = {}
        for axis in ("seq", "dp"):
            for _, mask in axis_bits(axis):
                weight[(axis, mask)] = devices
                devices *= 2
        for side in range(2):
            for part, order in enumerate(self.orders):
                dims = [self.last] + order[::-1]
                for code in range(self.shards):
                    device = side * weight[self.first]
                    device += sum(weight[d] for i, d in enumerate(dims) if (code >> i) & 1)
                    row = part * self.rows + code * self.shard
                    places[side, row] = device * each + part * self.shard
        half = blocks // 4
        found = []
        for block in range(blocks):
            side = block % (2 * half) // half
            local = block // (2 * half) * half + block % half
            for row in range(0, width, self.shard):
                found.append(places[side, local * width + row])
        return found

    def codes(self):
        found = []
        for order in self.orders:
            code = upper(self.last)
            for at, dim in enumerate(reversed(order)):
                code += upper(dim) << (at + 1)
            found.append(code)
        return [code.astype(jnp.int32) for code in found]


class Chain:
    def __init__(self):
        self.token = None

    def tie(self, values):
        if self.token is None:
            return values
        return lax.optimization_barrier((values, self.token))[0]

    def mark(self, values):
        self.token = values
        return values


def scatter_steps(plan, chain, keep, got, found):
    pairs = [[keep, got]] * PARTS
    bases = [i * plan.rows for i in range(PARTS)]
    size = plan.rows
    for step in range(len(plan.orders[0])):
        pairs = chain.tie(pairs)
        size //= 2
        dims = [order[step] for order in plan.orders]

        def halves(pair, base, at):
            return total_of([lax.dynamic_slice_in_dim(p, base + at * size, size, 0) for p in pair])

        sends = [halves(p, base, 1 - upper(d)) for p, base, d in zip(pairs, bases, dims)]
        chain.mark(sends)
        mine = [halves(p, base, upper(d)) for p, base, d in zip(pairs, bases, dims)]
        pairs = [[m, swap(s, d)] for m, s, d in zip(mine, sends, dims)]
        bases = [0] * PARTS
        yield
    size = plan.shard
    bit = upper(plan.last)
    pairs = chain.tie(pairs)

    def side(at):
        return jnp.concatenate(
            [total_of([lax.dynamic_slice_in_dim(p, at * size, size, 0) for p in pair]) for pair in pairs],
            axis=0,
        )

    send = chain.mark(side(1 - bit))
    shard = side(bit)
    got = swap(send, plan.last)
    yield
    shard, got = chain.tie((shard, got))
    shard = total_of([shard, got])
    for dim in plan.plain:
        shard = total_of([shard, swap(shard, dim)])
    found.append(chain.mark(shard))
    yield


def gather_steps(plan, chain, shard, found):
    size = plan.shard
    got = swap(shard, plan.last)
    yield
    values = [(shard[i * size : (i + 1) * size], got[i * size : (i + 1) * size]) for i in range(PARTS)]
    for step in reversed(range(len(plan.orders[0]))):
        values = chain.tie(values)
        values = [jnp.concatenate(pair, axis=0) for pair in values]
        chain.mark(values)
        values = [(v, swap(v, order[step])) for v, order in zip(values, plan.orders)]
        yield
    values = chain.tie(values)
    chain.mark(values)
    found += [v for pair in values for v in pair]
    found += [swap(v, plan.first) for v in found]
    yield


def place(plan, refs, codes, row, store):
    part = row // plan.rows
    shard = ((row % plan.rows) // plan.shard) ^ codes[part]
    half = plan.shards // 2
    at = pl.ds(pl.multiple_of((shard & (half - 1)) * plan.shard, plan.shard), plan.shard)
    low, high = refs[2 * part][at, :], refs[2 * part + 1][at, :]
    store(jnp.where(shard >= half, high.astype(f32), low.astype(f32)))


def dense_place_kernel(
    shard, each, table_ref, group_ref, all_ref, down_ref, up_ref, vec_ref, pool_ref, hold_ref, word_ref, sems, word_sem
):
    step, steps = pl.program_id(0), pl.num_programs(0)
    width = down_ref.shape[1]
    parts = width // shard
    devices = word_ref.shape[0]

    @pl.when(step == 0)
    def _():
        def fetch(block, carry):
            for i in range(parts):
                at = pl.multiple_of(table_ref[block * parts + i], SHARD_STEP)
                pltpu.make_async_copy(
                    all_ref.at[pl.ds(at, shard)],
                    hold_ref.at[block, pl.ds(i * shard, shard)],
                    sems.at[block],
                ).start()
            return carry

        lax.fori_loop(0, steps, fetch, 0)

        def words(device, carry):
            pltpu.make_async_copy(
                all_ref.at[pl.ds(pl.multiple_of(device * each + each - 2 * SUM_ROWS, SHARD_STEP), 2 * SUM_ROWS)],
                word_ref.at[device],
                word_sem,
            ).start()
            return carry

        lax.fori_loop(0, devices, words, 0)

    pltpu.make_async_copy(all_ref.at[pl.ds(0, width)], hold_ref.at[step], sems.at[step]).wait()

    @pl.when(step < steps // 2)
    def _():
        down_ref[...] = hold_ref[step].astype(f32)

    @pl.when(step >= steps // 2)
    def _():
        up_ref[...] = hold_ref[step].astype(f32)

    @pl.when(step == steps - 1)
    def _():
        pltpu.make_async_copy(word_ref, word_ref, word_sem).wait()

        def both(device):
            return word_ref[device, :SUM_ROWS].astype(f32) + word_ref[device, SUM_ROWS:].astype(f32)

        vec_ref[...] = lax.fori_loop(
            0, devices, lambda i, total: total + both(i), jnp.zeros(vec_ref.shape, f32)
        )
        for i in range(pool_ref.shape[0]):
            pool_ref[i] = both(group_ref[0] + i)[POOL_ROW:]


def dense_place(plan, gathered, each, width, wide, devices, seq_count, group):
    table = jnp.array(plan.table(2 * wide, width, each), jnp.int32)
    return pl.pallas_call(
        functools.partial(dense_place_kernel, plan.shard, each),
        grid_spec=pltpu.PrefetchScalarGridSpec(
            num_scalar_prefetch=2,
            grid=(2 * wide,),
            in_specs=[pl.BlockSpec(memory_space=pl.ANY)],
            out_specs=[
                pl.BlockSpec((width, width), lambda i, *_: (jnp.minimum(i, wide - 1), 0)),
                pl.BlockSpec((width, width), lambda i, *_: (0, jnp.maximum(i - wide, 0))),
                pl.BlockSpec((SUM_ROWS, width), lambda i, *_: (0, 0)),
                pl.BlockSpec((seq_count, SUM_ROWS - POOL_ROW, width), lambda i, *_: (0, 0, 0)),
            ],
            scratch_shapes=[
                pltpu.VMEM((2 * wide, width, width), bf16),
                pltpu.VMEM((devices, 2 * SUM_ROWS, width), bf16),
                pltpu.SemaphoreType.DMA((2 * wide,)),
                pltpu.SemaphoreType.DMA(()),
            ],
        ),
        out_shape=[
            jax.ShapeDtypeStruct((wide * width, width), f32),
            jax.ShapeDtypeStruct((width, wide * width), f32),
            jax.ShapeDtypeStruct((SUM_ROWS, width), f32),
            jax.ShapeDtypeStruct((seq_count, SUM_ROWS - POOL_ROW, width), f32),
        ],
        compiler_params=PARAMS,
        cost_estimate=cost(0, 12 * wide * width * width),
    )(table, group, gathered)


def attend_place_kernel(plan, first_code, at, flip, info_ref, *refs):
    sources, (hold_ref, sems) = refs[: 2 * PARTS], refs[-2:]
    outs = refs[-6:-2]
    codes = [info_ref[first_code + i] for i in range(PARTS)]
    own = info_ref[at] ^ flip
    width = hold_ref.shape[2]

    def move(block, act):
        for side in range(2):

            @pl.when(own == side)
            def _():
                act(pltpu.make_async_copy(hold_ref.at[block], outs[2 * side + block], sems.at[block]))

    for block in range(2):
        for row in range(0, width, plan.shard):

            def store(value, row=row):
                hold_ref[block, row : row + plan.shard, :] = value

            place(plan, sources, codes, block * width + row, store)
        move(block, lambda copy: copy.start())
    for block in range(2):
        move(block, lambda copy: copy.wait())


def attend_place(plan, first_code, at, flip, info, sources, width, before):
    kept = list(before)
    return pl.pallas_call(
        functools.partial(attend_place_kernel, plan, first_code, at, flip),
        grid_spec=pltpu.PrefetchScalarGridSpec(
            num_scalar_prefetch=1,
            grid=(1,),
            in_specs=[fixed(x.shape) for x in sources]
            + [pl.BlockSpec(memory_space=pl.ANY)] * len(kept),
            out_specs=[pl.BlockSpec(memory_space=pl.ANY)] * 4,
            scratch_shapes=[pltpu.VMEM((2, width, width), f32), pltpu.SemaphoreType.DMA((2,))],
        ),
        out_shape=[jax.ShapeDtypeStruct((width, width), f32)] * 4,
        input_output_aliases={1 + len(sources) + i: i for i in range(len(kept))},
        compiler_params=SMALL,
        cost_estimate=cost(0, 12 * width * width),
    )(info, *sources, *kept)


def shards(
    tokens,
    lengths,
    w_query,
    b_query,
    w_key,
    w_value,
    b_value,
    w_out,
    b_out,
    gain_one,
    shift_one,
    w_up,
    b_up,
    w_down,
    b_down,
    gain_two,
    shift_two,
    out_grad,
    pooled_grad,
):
    seq_count = lax.axis_size("seq")
    held, piece, width = tokens.shape
    full = piece * seq_count
    count = held // seq_count
    mine = lax.axis_index("seq")
    wide = w_up.shape[1] // width
    total = count * full

    def flat(value):
        return value.reshape(total, width)

    def split(value):
        return value.reshape(count, full, width)

    dense_plan = Plan(wide * width)
    outer_plan = Plan(2 * width)
    first = axis_bits("seq")[0]
    scalars = [mine, upper(first)] + dense_plan.codes() + outer_plan.codes()
    own_at, dense_at, outer_at = held + 1, held + 2, held + 2 + PARTS
    info = jnp.concatenate([lengths, jnp.stack([v.astype(jnp.int32) for v in scalars])])
    vecs = jnp.concatenate(
        [b_query, b_value, b_out, gain_one, shift_one, b_down, gain_two, shift_two, b_up]
    )
    vecs = vecs.astype(f32).reshape(-1, width)

    weights = [w_query, w_key, w_value, vecs]
    done = None
    source = tokens
    parts = []
    for passage in range(count):
        if parts:
            source = lax.optimization_barrier((tokens, parts))[0]
        slices = [
            lax.dynamic_slice_in_dim(source, (mine ^ mask) * count + passage, 1, 0)
            for mask in range(1, seq_count)
        ]
        parts = [exchange(value, "seq", mask + 1) for mask, value in enumerate(slices)]
        done = attend(passage, count, info, tokens, parts, weights, done)
    stacked, q, k, v, stat = done
    cot = to_passages(lax.optimization_barrier((out_grad, slices))[0])
    stacked = stacked.reshape(2, total, width)
    result, first_low, act, second, inner, branch_in, mixed_grad, sums = row_work(
        held, info, stacked, flat(cot), pooled_grad, w_out, w_up, w_down, vecs, count
    )
    chain = Chain()
    pieces = chain.mark(position_pieces(split(result)))
    out_pieces = traded(pieces)
    send = dense_outer(own_at, 1, info, *chain.tie((act, second, first_low, inner)))
    chain.mark(send)
    got = swap(send, first)
    keep = chain.mark(dense_outer(own_at, 0, info, *chain.tie((act, second, first_low, inner))))
    dense, shard, outer = [], [], []
    dense_steps = scatter_steps(dense_plan, chain, keep, got, dense)
    next(dense_steps)
    chain.mark((chain.token, out_pieces))
    block_out = to_positions(out_pieces)
    grads, words = attend_back(
        held,
        info,
        q,
        k,
        v,
        chain.tie(split(mixed_grad)),
        stacked.reshape(2, count, full, width),
        split(branch_in),
        stat,
        sums,
    )
    chain.mark(words)
    grads = grads.reshape(4, total, width)
    next(dense_steps)
    send = attend_outer(own_at, 1, info, stacked, chain.tie(grads))
    chain.mark(send)
    got = swap(send, first)
    keep = attend_outer(own_at, 0, info, stacked, chain.tie(grads))
    chain.mark(keep)
    next(dense_steps)
    outer_steps = scatter_steps(outer_plan, chain, keep, got, shard)
    next(outer_steps)
    next(dense_steps)
    input_low = input_grad(branch_in, chain.tie(grads), w_query, w_key, w_value)
    chain.mark(input_low)
    next(outer_steps)
    for _ in dense_steps:
        pass
    gathered = jnp.concatenate([dense[0], words], axis=0)
    each = gathered.shape[0]
    gathered = chain.mark(gathered)
    gathered = lax.all_gather(gathered, ("dp", "seq"), axis=0, tiled=True)
    next(outer_steps)
    next(outer_steps)
    pieces = chain.mark(position_pieces(split(chain.tie(input_low))))
    in_pieces = traded(pieces)
    for _ in outer_steps:
        pass
    outer_steps = gather_steps(outer_plan, chain, shard[0], outer)
    next(outer_steps)
    chain.mark((chain.token, in_pieces))
    next(outer_steps)
    next(outer_steps)
    next(outer_steps)
    tokens_grad = to_positions(in_pieces)
    chain.mark((chain.token, tokens_grad, block_out))
    for _ in outer_steps:
        pass
    group = (lax.axis_index("dp") * seq_count).astype(jnp.int32)[None]

    def place_outer(flip, before):
        pick = outer[2 * PARTS :] if flip else outer[: 2 * PARTS]
        return chain.mark(
            attend_place(outer_plan, outer_at, own_at, flip, info, chain.tie(pick), width, before)
        )

    placed = place_outer(0, [])
    outer = place_outer(1, placed)
    down_sum, up_sum, vectors, pooled = dense_place(
        dense_plan, chain.tie(gathered), each, width, wide, gathered.shape[0] // each, seq_count, group
    )
    pooled = pooled[:, :count].reshape(held, width)
    return (
        block_out,
        pooled,
        tokens_grad,
        outer[0],
        vectors[0],
        outer[1],
        outer[2],
        vectors[1],
        outer[3],
        vectors[2],
        vectors[3],
        vectors[4],
        up_sum,
        vectors[8 : 8 + wide].reshape(-1),
        down_sum,
        vectors[5],
        vectors[6],
        vectors[7],
    )


def solution(mesh):
    in_specs = (
        (P("dp", "seq", None), P("dp"))
        + (P(),) * 15
        + (P("dp", "seq", None), P("dp", None))
    )
    out_specs = (P("dp", "seq", None), P("dp", None), P("dp", "seq", None)) + (P(),) * 15
    return jax.shard_map(shards, mesh=mesh, in_specs=in_specs, out_specs=out_specs, check_vma=False)
```
